32 devices in a mesh: date: 4 (over y, core), strip: 8 (over z, x).
Axes of the slice: x: 2, y: 2, z: 4, core: 2. Of those that a mesh axis runs over, the one named last changes fastest.
Arguments:
- stack: float32 [64, 512, 1024], P('date', 'strip'), may hold values from -6 to 6
- spatial_taps: float32 [13], replicated, may hold values from 0.2 to 1
- temporal_taps: float32 [2, 5], replicated, may hold values from -0.25 to 0.25
- foot_tile: int32 [1024], P(('date', 'strip')), may hold values from 0 to 1
- foot_row: int32 [1024], P(('date', 'strip')), may hold values from 0 to 63
- foot_count: int32 [1024], P(('date', 'strip')), may hold values from 1 to 128
- foot_owner: int32 [1024, 1], P(('date', 'strip')), may hold values from 0 to 31; in each aligned block of 32 rows (0 to 31, 32 to 63, ...) at most 2 rows name the same one
Outputs:
- residual: float32 [64, 512, 1024], P(None, 'strip', 'date')
- anomaly: float32 [32, 64, 64], P(('date', 'strip'))
- asset_series: float32 [32, 64], P(('date', 'strip'))
The draws below stay inside these ranges and needn't reach their ends.
Inputs may be any that keep to these rules, and one draw needn't show every extreme that they name: `foot_owner`: among the footprints of one block, no owner appears more than 2 times, a bound that some block reaches; every owner has some footprint.
All inputs are finite; a program needn't handle non-finite values.
Results may differ from the reference program's by a relative error of at most 0.000075.
Values sent between devices are 32-bit elements; how exact they have to be, the bound alone decides.
No kernel may reach another device: no remote copies, remote signals or barrier semaphores. Data moves between devices by JAX's collectives and lax.ppermute only.
A program may use at most 128 MiB of HBM per device.

```python
import math
import jax
import jax.numpy as jnp
import numpy as np
from jax import lax

DATES = 64
ROW_DEV = 64
TILE = 128
RADIUS = 6
REACH = 2
DILATION = 8
PAIR_CAP = 2
ROWS = 512
COLS = 1024
TILE_DEV = 2
FOOT_DEV = 32
FOOTS = 1024
N_DATE = 4
N_STRIP = 8
DEVICES = 32


def place_ends(entries, stream_key, smallest, high):
    extent = entries.shape
    place = [jax.random.randint(jax.random.fold_in(stream_key, axis), (), 0, extent[axis]) for axis in range(len(extent))]
    entries = entries.at[tuple(place)].set(smallest)
    longest = extent.index(max(extent))
    place[longest] = (place[longest] + 1) % extent[longest]
    return entries.at[tuple(place)].set(high)


def shard_levels(own_key, shape, shards, low, top_value):
    level = 1.0
    for dim, shards_of in shards:
        draws = jax.random.uniform(jax.random.fold_in(jax.random.fold_in(own_key, 6), dim), (shards_of,), jnp.float32, low / len(shards), top_value / len(shards))
        level = level * jnp.repeat(jnp.exp(draws), shape[dim] // shards_of).reshape((-1,) + (1,) * (len(shape) - 1 - dim))
    return level


def deal_out(own_key, own, number, rows, count, top, limit, lean):
    sequence = jax.random.permutation(own_key, count)
    heavy_load, common = portions_of(count, rows * top, limit, lean, True), portions_of(count, rows * top, limit, lean, False)
    places = jnp.arange(count)

    def named(sizes, rotation):
        used = int((sizes > 0).sum())
        fixed = max(1, used // 4)
        moved = fixed + (places - fixed + rotation * (used - fixed)) % max(1, count - fixed)
        return jnp.zeros((count,), jnp.int32).at[sequence[jnp.where(places < fixed, places, moved)]].set(jnp.asarray(sizes, jnp.int32))

    sizes = jnp.where(number % 4 == 0, named(heavy_load, number // 4), named(common, number - number // 4 - 1))
    mixed = jax.random.permutation(jax.random.fold_in(own, 3), count)
    giver, taker = mixed[0:count // 2 * 2:2], mixed[1:count // 2 * 2:2]
    room = jnp.minimum(sizes[giver] - 1, limit - sizes[taker]) // 2
    room = jnp.where((giver == sequence[0]) | (taker == sequence[0]) | (sizes[taker] == 0), 0, jnp.maximum(room, 0))
    moved = jax.random.randint(jax.random.fold_in(own, 4), (count // 2,), 0, 1 << 20) % (room + 1)
    sizes = sizes.at[giver].add(-moved).at[taker].add(moved)
    labels = jnp.searchsorted(jnp.cumsum(sizes), jnp.arange(rows * top), side="right").astype(jnp.int32)
    listing = labels.reshape(top, rows).T
    listing = listing[jax.random.permutation(jax.random.fold_in(own, 1), rows)]
    rotation = jax.random.randint(jax.random.fold_in(own, 2), (rows, 1), 0, top)
    return jnp.take_along_axis(listing, (jnp.arange(top)[None, :] + rotation) % top, axis=1)


def portions_of(count, total, reach, skew, full):
    weights = [(1 << 20) // math.isqrt(rank ** skew) + 1 for rank in range(1, count + 1)]
    largest = reach if full else min(reach, max(-(-total // count), total * weights[0] // sum(weights)))
    least = 1 if total - largest >= count - 1 else 0
    given, surplus = [largest] + [least] * (count - 1), total - largest - least * (count - 1)
    while surplus > 0:
        movable = [i for i in range(1, count) if given[i] < largest] or [i for i in range(1, count) if given[i] < reach]
        whole, left = sum([weights[i] for i in movable]), surplus
        for i in movable:
            more = min(reach - given[i], max(1, left * weights[i] // whole), surplus)
            given[i] = given[i] + more
            surplus = surplus - more
    return np.array(given)


def normal_values(own_key, extent, width, limit, split=(), kind=jnp.bfloat16):
    factor_of = shard_levels(own_key, extent, split, -0.22, 0.18) if split else 1.0
    values = jax.random.normal(own_key, extent, jnp.float32) * width * factor_of
    return jnp.minimum(jnp.maximum(values, -limit), limit).astype(kind)


def setup_inputs(seed: int = 0) -> dict:
    key_of = jax.random.split(jax.random.key(seed), 8)
    stack = normal_values(key_of[0], (DATES, ROWS, COLS), 1.0, 6.0, ((0, 4), (1, 8)), jnp.float32)
    spatial_taps = jnp.clip(jnp.exp(jax.random.uniform(key_of[1], (2 * RADIUS + 1,), jnp.float32, math.log(0.2), math.log(1.0))), 0.2, 1.0)
    temporal_taps = jnp.clip(jax.random.uniform(key_of[2], (2, 2 * REACH + 1), jnp.float32, -0.25, 0.25), -0.25, 0.25)
    foot_tile = place_ends(jax.random.randint(key_of[3], (FOOTS,), 0, TILE_DEV), jax.random.fold_in(key_of[3], 1), 0, TILE_DEV - 1).astype(jnp.int32)
    foot_row = place_ends(jax.random.randint(key_of[4], (FOOTS,), 0, ROW_DEV), jax.random.fold_in(key_of[4], 1), 0, ROW_DEV - 1).astype(jnp.int32)
    foot_count = place_ends(jax.random.randint(key_of[5], (FOOTS,), 1, TILE + 1), jax.random.fold_in(key_of[5], 1), 1, TILE).astype(jnp.int32)
    foot_owner_keys = jax.random.split(jax.random.fold_in(key_of[6], 1), FOOTS // FOOT_DEV)
    foot_owner_turns = jax.random.permutation(jax.random.fold_in(key_of[6], 3), FOOTS // FOOT_DEV)
    foot_owner = jax.vmap(lambda own, number: deal_out(jax.random.fold_in(key_of[6], 2), own, number, FOOT_DEV, DEVICES, 1, PAIR_CAP, 2))(foot_owner_keys, foot_owner_turns).reshape((FOOTS, 1))
    return dict(stack=stack, spatial_taps=spatial_taps, temporal_taps=temporal_taps, foot_tile=foot_tile, foot_row=foot_row, foot_count=foot_count, foot_owner=foot_owner)


def taps_pass(padded, weights, axis_num, length):
    summed = weights[0] * lax.slice_in_dim(padded, 0, length, axis=axis_num)
    for k in range(1, weights.shape[0]):
        summed = summed + weights[k] * lax.slice_in_dim(padded, k, k + length, axis=axis_num)
    return summed


def lowpass_image(image, weights):
    row_count, col_count = image.shape
    padded = jnp.pad(image, ((0, 0), (RADIUS, RADIUS)))
    across = taps_pass(padded, weights, 1, col_count)
    padded = jnp.pad(across, ((RADIUS, RADIUS), (0, 0)))
    return image - taps_pass(padded, weights, 0, row_count)


def temporal_filter(series, temporal_taps):
    date_count = series.shape[0]
    for level_idx, spacing in enumerate((1, DILATION)):
        margin = REACH * spacing
        padded = jnp.pad(series, ((margin, margin), (0, 0), (0, 0)))
        smooth_part = temporal_taps[level_idx, 0] * lax.slice_in_dim(padded, 0, date_count, axis=0)
        for k in range(1, 2 * REACH + 1):
            smooth_part = smooth_part + temporal_taps[level_idx, k] * lax.slice_in_dim(padded, k * spacing, k * spacing + date_count, axis=0)
        series = series - smooth_part
    return series


def reference(stack, spatial_taps, temporal_taps, foot_tile, foot_row, foot_count, foot_owner):
    weights = spatial_taps / jnp.sum(spatial_taps)
    corrected = lax.map(lambda image: lowpass_image(image, weights), stack)
    banded = jnp.moveaxis(corrected.reshape(DATES, N_STRIP, ROW_DEV, COLS), 1, 0)
    filtered = lax.map(lambda block: temporal_filter(block, temporal_taps), banded)
    residual = jnp.moveaxis(filtered, 0, 1).reshape(DATES, ROWS, COLS)
    devices_all = N_DATE * N_STRIP
    block_ids = jnp.arange(FOOT_DEV * devices_all, dtype=jnp.int32) // FOOT_DEV
    band_ids = block_ids % N_STRIP
    column_ids = block_ids // N_STRIP
    tile_view = residual.reshape(DATES, N_STRIP, ROW_DEV, N_DATE, TILE_DEV, TILE)
    picked = tile_view[:, band_ids, foot_row, column_ids, foot_tile, :]
    counts = foot_count.astype(jnp.float32)
    inside = (jnp.arange(TILE, dtype=jnp.int32)[None, :] < foot_count[:, None]).astype(jnp.float32)
    foot_mean = jnp.sum(picked * inside[None], axis=2) / counts[None, :]
    owners = foot_owner[:, 0].reshape(devices_all, FOOT_DEV)
    position = jnp.arange(FOOT_DEV, dtype=jnp.int32)
    earlier = (owners[:, :, None] == owners[:, None, :]) & (position[None, None, :] < position[None, :, None])
    slot_rank = jnp.sum(earlier.astype(jnp.int32), axis=2)
    dest_slot = owners * PAIR_CAP + slot_rank
    onehot = (dest_slot[:, :, None] == jnp.arange(devices_all * PAIR_CAP, dtype=jnp.int32)[None, None, :]).astype(jnp.float32)
    series_blocks = foot_mean.reshape(DATES, devices_all, FOOT_DEV)
    sent = jnp.einsum("bfk,tbf->bkt", onehot, series_blocks, precision=lax.Precision.HIGHEST)
    sent_weight = jnp.einsum("bfk,bf->bk", onehot, counts.reshape(devices_all, FOOT_DEV), precision=lax.Precision.HIGHEST)
    received = jnp.transpose(sent.reshape(devices_all, devices_all, PAIR_CAP, DATES), (1, 0, 2, 3))
    weight_in = jnp.transpose(sent_weight.reshape(devices_all, devices_all, PAIR_CAP), (1, 0, 2))
    total_weight = jnp.sum(weight_in, axis=(1, 2))
    asset_series = jnp.sum(weight_in[:, :, :, None] * received, axis=(1, 2)) / total_weight[:, None]
    anomaly = jnp.where(weight_in[:, :, :, None] > 0, received - asset_series[:, None, None, :], 0.0)
    return residual, anomaly.reshape(devices_all, devices_all * PAIR_CAP, DATES), asset_series
```

```python
import functools

import jax
import jax.numpy as jnp
from jax import lax
from jax.experimental import pallas as pl
from jax.experimental.pallas import tpu as pltpu
from jax.sharding import PartitionSpec as P

TILE = 128
RADIUS = 6
REACH = 2
DILATION = 8
PAIR_CAP = 2
LANES = 128
EDGE = 8
HIGHEST = lax.Precision.HIGHEST
VMEM_LIMIT = 48 * 1024 * 1024


def params(**more):
    return pltpu.CompilerParams(vmem_limit_bytes=VMEM_LIMIT, **more)


def cost(flops, bytes_accessed):
    return pl.CostEstimate(flops=flops, bytes_accessed=bytes_accessed, transcendentals=0)


def band(shape, offset, taps):
    at = lax.broadcasted_iota(jnp.int32, shape, 0) - lax.broadcasted_iota(jnp.int32, shape, 1) - offset
    return pick_taps(at, taps)


def pick_taps(at, taps):
    count = taps.shape[0]
    total = taps[0]
    for k in range(1, count):
        total = total + taps[k]
    out = jnp.zeros(at.shape, jnp.float32)
    for k in range(count):
        out = jnp.where(at == k, taps[k], out)
    return out / jnp.full(at.shape, total, jnp.float32)


def fill_columns(col_ref, taps):
    width = col_ref.shape[1]
    col_ref[...] = band((width + 2 * LANES, width), LANES - RADIUS, taps)


def fill_rows(row_ref, groups, out_rows, in_rows, first, taps):
    shape = (out_rows, groups * in_rows)
    lane = lax.broadcasted_iota(jnp.int32, shape, 1)
    group = lane // in_rows
    at = lane - group * in_rows - lax.broadcasted_iota(jnp.int32, shape, 0) - first
    values = pick_taps(at, taps)
    for g in range(groups):
        row_ref[g * out_rows:(g + 1) * out_rows, :] = jnp.where(group == g, values, 0.0)


def interior_kernel(offset, parts, place, taps, left_ref, mid_ref, right_ref, out_ref, col_ref, row_ref):
    dates, rows, width = mid_ref.shape
    inner = rows - 2 * EDGE

    @pl.when(pl.program_id(0) == 0)
    def _():
        fill_columns(col_ref, taps)
        fill_rows(row_ref, dates, inner, rows, EDGE - RADIUS, taps)

    block = place[0] ^ offset
    left = jnp.where(block > 0, left_ref[...], 0.0)
    right = jnp.where(block < parts - 1, right_ref[...], 0.0)
    mid = mid_ref[...]
    window = jnp.concatenate([left, mid, right], axis=2).reshape(dates * rows, width + 2 * LANES)
    across = jnp.dot(window, col_ref[...], precision=HIGHEST, preferred_element_type=jnp.float32)
    low = jnp.dot(row_ref[...], across, precision=HIGHEST, preferred_element_type=jnp.float32)
    out_ref[...] = mid[:, EDGE:rows - EDGE, :] - low.reshape(dates, inner, width)


def interior(stack, taps, place, offset, parts):
    dates, rows, cols = stack.shape
    width = cols // parts
    per = width // LANES
    group = min(4, dates)
    inner = rows - 2 * EDGE
    last = cols // LANES - 1
    return pl.pallas_call(
        functools.partial(interior_kernel, offset, parts),
        grid_spec=pltpu.PrefetchScalarGridSpec(
            num_scalar_prefetch=2,
            grid=(dates // group,),
            in_specs=[
                pl.BlockSpec((group, rows, LANES), lambda g, at, w: (g, 0, jnp.maximum((at[0] ^ offset) * per - 1, 0))),
                pl.BlockSpec((group, rows, width), lambda g, at, w: (g, 0, at[0] ^ offset)),
                pl.BlockSpec((group, rows, LANES), lambda g, at, w: (g, 0, jnp.minimum(((at[0] ^ offset) + 1) * per, last))),
            ],
            out_specs=pl.BlockSpec((group, inner, width), lambda g, at, w: (g, 0, 0)),
            scratch_shapes=[
                pltpu.VMEM((width + 2 * LANES, width), jnp.float32),
                pltpu.VMEM((group * inner, group * rows), jnp.float32),
            ],
        ),
        out_shape=jax.ShapeDtypeStruct((dates, inner, width), jnp.float32),
        compiler_params=params(),
        cost_estimate=cost(60 * dates * rows * width, 3 * 4 * dates * rows * width),
    )(place, taps, stack, stack, stack)


def edge_kernel(parts, place, taps, up_ref, top_ref, bottom_ref, down_ref, *rest):
    outs, (col_ref, row_ref) = rest[:parts], rest[parts:]
    dates, _, cols = top_ref.shape
    width = cols // parts
    span = 3 * EDGE

    @pl.when(pl.program_id(0) == 0)
    def _():
        fill_columns(col_ref, taps)
        fill_rows(row_ref, 2 * dates, EDGE, span, EDGE - RADIUS, taps)

    rim = jnp.concatenate([up_ref[...], top_ref[...], bottom_ref[...], down_ref[...]], axis=1)
    rim = rim.reshape(dates * 2 * span, cols)
    none = jnp.zeros((dates * 2 * span, LANES), jnp.float32)
    rim = jnp.concatenate([none, rim, none], axis=1)
    for c in range(parts):
        window = rim[:, c * width:(c + 1) * width + 2 * LANES]
        across = jnp.dot(window, col_ref[...], precision=HIGHEST, preferred_element_type=jnp.float32)
        low = jnp.dot(row_ref[...], across, precision=HIGHEST, preferred_element_type=jnp.float32)
        low = low.reshape(dates, 2 * EDGE, width)
        here = pl.ds(c * width, width)
        kept = jnp.concatenate([top_ref[:, 0:EDGE, here], bottom_ref[:, EDGE:2 * EDGE, here]], axis=1)
        done = kept - low
        for k in range(parts):
            @pl.when((place[0] ^ k) == c)
            def _():
                outs[k][...] = done


def edges(stack, up, down, taps, place, parts):
    dates, rows, cols = stack.shape
    width = cols // parts
    group = min(4, dates)
    ends = rows // (2 * EDGE) - 1
    return pl.pallas_call(
        functools.partial(edge_kernel, parts),
        grid_spec=pltpu.PrefetchScalarGridSpec(
            num_scalar_prefetch=2,
            grid=(dates // group,),
            in_specs=[
                pl.BlockSpec((group, EDGE, cols), lambda g, at, w: (g, 0, 0)),
                pl.BlockSpec((group, 2 * EDGE, cols), lambda g, at, w: (g, 0, 0)),
                pl.BlockSpec((group, 2 * EDGE, cols), lambda g, at, w: (g, ends, 0)),
                pl.BlockSpec((group, EDGE, cols), lambda g, at, w: (g, 0, 0)),
            ],
            out_specs=[pl.BlockSpec((group, 2 * EDGE, width), lambda g, at, w: (g, 0, 0))] * parts,
            scratch_shapes=[
                pltpu.VMEM((width + 2 * LANES, width), jnp.float32),
                pltpu.VMEM((group * 2 * EDGE, group * 6 * EDGE), jnp.float32),
            ],
        ),
        out_shape=[jax.ShapeDtypeStruct((dates, 2 * EDGE, width), jnp.float32)] * parts,
        compiler_params=params(),
        cost_estimate=cost(60 * dates * 48 * cols, 4 * dates * 64 * cols),
    )(place, taps, up, stack, stack, down)


def temporal_kernel(parts, with_base, place, taps, *rest):
    pieces = rest[:parts]
    out_ref, z_ref, f_ref = rest[parts + with_base:]
    local, rows, width = pieces[0].shape
    total = local * parts
    pad = REACH * DILATION
    step = 8

    @pl.when(pl.program_id(0) == 0)
    def _():
        none = jnp.zeros((REACH, rows, width), jnp.float32)
        z_ref[0:REACH] = none
        z_ref[REACH + total:REACH + total + REACH] = none
        wide = jnp.zeros((pad, rows, width), jnp.float32)
        f_ref[0:pad] = wide
        f_ref[pad + total:pad + total + pad] = wide

    for k in range(parts):
        z_ref[pl.ds(REACH + (place[0] ^ k) * local, local)] = pieces[k][...]

    def first(n, carry):
        t = n * step
        z = z_ref[pl.ds(t, step + 2 * REACH)]
        smooth = taps[0, 0] * z[0:step]
        for k in range(1, 2 * REACH + 1):
            smooth = smooth + taps[0, k] * z[k:k + step]
        f_ref[pl.ds(pad + t, step)] = z[REACH:REACH + step] - smooth
        return carry

    lax.fori_loop(0, total // step, first, 0)

    def second(n, carry):
        t = n * step
        smooth = taps[1, 0] * f_ref[pl.ds(t, step)]
        for k in range(1, 2 * REACH + 1):
            smooth = smooth + taps[1, k] * f_ref[pl.ds(t + k * DILATION, step)]
        out_ref[pl.ds(t, step)] = f_ref[pl.ds(pad + t, step)] - smooth
        return carry

    lax.fori_loop(0, total // step, second, 0)


def temporal(pieces, base, taps, place, tile_of, steps, rows):
    parts = len(pieces)
    local, _, width = pieces[0].shape
    total = local * parts
    extra = [] if base is None else [base]
    return pl.pallas_call(
        functools.partial(temporal_kernel, parts, len(extra)),
        grid_spec=pltpu.PrefetchScalarGridSpec(
            num_scalar_prefetch=2,
            grid=(steps,),
            in_specs=[pl.BlockSpec((local, EDGE, width), lambda i, at, w: (0, i, 0))] * parts
            + [pl.BlockSpec(memory_space=pl.ANY)] * len(extra),
            out_specs=pl.BlockSpec((total, EDGE, width), lambda i, at, w: (0, tile_of(i), 0)),
            scratch_shapes=[
                pltpu.VMEM((total + 2 * REACH, EDGE, width), jnp.float32),
                pltpu.VMEM((total + 2 * REACH * DILATION, EDGE, width), jnp.float32),
            ],
        ),
        out_shape=jax.ShapeDtypeStruct((total, rows, width), jnp.float32),
        input_output_aliases={} if base is None else {2 + parts: 0},
        compiler_params=params(),
        cost_estimate=cost(20 * total * EDGE * steps * width, 8 * total * EDGE * steps * width),
    )(place, taps, *pieces, *extra)


def footprint_kernel(parts, strips, feet, place, meta, *rest):
    inner, rim = rest[:parts], rest[parts:2 * parts]
    out_ref, x_ref, g_ref, seen, sem = rest[2 * parts:]
    per, dates, rows, _ = x_ref.shape
    per = per // parts
    owners = parts * strips
    copies = []
    for k in range(parts):
        for h in range(per):
            lanes = pl.ds(h * LANES, LANES)
            into = x_ref.at[k * per + h]
            copies.append(pltpu.make_async_copy(
                inner[k].at[:, :, lanes], into.at[:, EDGE:rows - EDGE, :], sem.at[3 * (k * per + h)]))
            copies.append(pltpu.make_async_copy(
                rim[k].at[:, 0:EDGE, lanes], into.at[:, 0:EDGE, :], sem.at[3 * (k * per + h) + 1]))
            copies.append(pltpu.make_async_copy(
                rim[k].at[:, EDGE:2 * EDGE, lanes], into.at[:, rows - EDGE:rows, :], sem.at[3 * (k * per + h) + 2]))
    for copy in copies:
        copy.start()

    def clear_seen(i, carry):
        seen[i] = 0
        return carry

    lax.fori_loop(0, parts * owners, clear_seen, 0)
    block_rows = parts * PAIR_CAP * dates

    def clear(i, carry):
        g_ref[pl.ds(pl.multiple_of(i * block_rows, block_rows), block_rows), :] = jnp.zeros((block_rows, LANES), jnp.float32)
        return carry

    lax.fori_loop(0, owners, clear, 0)
    for copy in copies:
        copy.wait()
    flat = x_ref.reshape(parts * per * dates * rows, LANES)
    lane = lax.broadcasted_iota(jnp.int32, (dates, LANES), 1)
    for block in range(parts):
        line = block * strips + place[1]
        slot_base = (block ^ place[0]) * per

        def take(f, carry):
            row = meta[line, f]
            tile = meta[line, feet + f]
            count = meta[line, 2 * feet + f]
            owner = meta[line, 3 * feet + f]
            slot = seen[block * owners + owner]
            seen[block * owners + owner] = slot + 1
            pixels = flat[pl.ds((slot_base + tile) * dates * rows + row, dates, stride=rows), :]
            to = ((owner * parts + block) * PAIR_CAP + slot) * dates
            g_ref[pl.ds(pl.multiple_of(to, dates), dates), :] = jnp.where(lane < count, pixels, 0.0)
            return carry

        lax.fori_loop(0, feet, take, 0)

    def total(o, carry):
        values = g_ref[pl.ds(pl.multiple_of(o * block_rows, block_rows), block_rows), :]
        out_ref[pl.ds(o, 1), :] = jnp.sum(values.T, axis=0, keepdims=True)
        return carry

    lax.fori_loop(0, owners, total, 0)


def footprints(inner, rim, meta, place, strips, feet):
    parts = len(inner)
    dates, inner_rows, width = inner[0].shape
    rows = inner_rows + 2 * EDGE
    per = width // LANES
    owners = parts * strips
    message = parts * PAIR_CAP * dates
    return pl.pallas_call(
        functools.partial(footprint_kernel, parts, strips, feet),
        grid_spec=pltpu.PrefetchScalarGridSpec(
            num_scalar_prefetch=2,
            grid=(),
            in_specs=[pl.BlockSpec(memory_space=pl.ANY)] * (2 * parts),
            out_specs=pl.BlockSpec(memory_space=pltpu.VMEM),
            scratch_shapes=[
                pltpu.VMEM((parts * per, dates, rows, LANES), jnp.float32),
                pltpu.VMEM((owners * message, LANES), jnp.float32),
                pltpu.SMEM((parts * owners,), jnp.int32),
                pltpu.SemaphoreType.DMA((3 * parts * per,)),
            ],
        ),
        out_shape=jax.ShapeDtypeStruct((owners, message), jnp.float32),
        compiler_params=params(),
        cost_estimate=cost(4 * owners * message * LANES, 8 * dates * rows * width * parts),
    )(place, meta, *inner, *rim)


def owner_kernel(parts, strips, feet, place, taps, meta_ref, sums_ref, anomaly_ref, series_ref):
    owners = parts * strips
    slots = owners * PAIR_CAP
    dates = sums_ref.shape[1] // PAIR_CAP
    local = dates // parts
    me = place[0] * strips + place[1]
    meta = meta_ref[...]
    counts = meta[:, 2 * feet:3 * feet].astype(jnp.float32)
    mine = (meta[:, 3 * feet:4 * feet] == me).astype(jnp.float32)
    shape = (feet, feet)
    before = (lax.broadcasted_iota(jnp.int32, shape, 0) < lax.broadcasted_iota(jnp.int32, shape, 1)).astype(jnp.float32)
    rank = jnp.dot(mine, before, precision=HIGHEST, preferred_element_type=jnp.float32)
    held = [
        jnp.sum(jnp.where((mine > 0) & (jnp.abs(rank - slot) < 0.5), counts, 0.0), axis=1, keepdims=True)
        for slot in range(PAIR_CAP)
    ]
    rows, weights = [], []
    for block in range(parts):
        for slot in range(PAIR_CAP):
            at = (block * PAIR_CAP + slot) * local
            rows.append(jnp.concatenate(
                [sums_ref[e * strips:(e + 1) * strips, at:at + local] for e in range(parts)], axis=1))
            weights.append(held[slot][block * strips:(block + 1) * strips])
    sums = jnp.concatenate(rows, axis=0)
    weight = jnp.concatenate(weights, axis=0)
    shape = (dates, dates)
    lag = lax.broadcasted_iota(jnp.int32, shape, 0) - lax.broadcasted_iota(jnp.int32, shape, 1)
    for level, spacing in ((0, 1), (1, DILATION)):
        filt = jnp.where(lag == 0, 1.0, 0.0)
        for k in range(2 * REACH + 1):
            filt = filt - jnp.where(lag == (k - REACH) * spacing, taps[level, k], 0.0)
        sums = jnp.dot(sums, filt, precision=HIGHEST, preferred_element_type=jnp.float32)
    mean = sums / jnp.where(weight > 0, weight, 1.0)
    asset = jnp.sum(weight * mean, axis=0, keepdims=True) / jnp.sum(weight, axis=0, keepdims=True)
    odd = jnp.where(weight > 0, mean - asset, 0.0)
    series_ref[...] = asset
    shape = (slots, slots)
    to = lax.broadcasted_iota(jnp.int32, shape, 0)
    source = lax.broadcasted_iota(jnp.int32, shape, 1)
    block, rest = source // (PAIR_CAP * strips), source % (PAIR_CAP * strips)
    place_of = block * (PAIR_CAP * strips) + (rest % strips) * PAIR_CAP + rest // strips
    order = jnp.where(to == place_of, 1.0, 0.0)
    anomaly_ref[0] = jnp.dot(order, odd, precision=HIGHEST, preferred_element_type=jnp.float32)


def owner_series(sums, meta, taps, place, parts, strips, feet):
    owners = parts * strips
    dates = sums.shape[1] // PAIR_CAP
    slots = owners * PAIR_CAP
    return pl.pallas_call(
        functools.partial(owner_kernel, parts, strips, feet),
        grid_spec=pltpu.PrefetchScalarGridSpec(
            num_scalar_prefetch=2,
            grid=(),
            in_specs=[pl.BlockSpec(memory_space=pltpu.VMEM)] * 2,
            out_specs=[pl.BlockSpec(memory_space=pltpu.VMEM)] * 2,
        ),
        out_shape=[
            jax.ShapeDtypeStruct((1, slots, dates), jnp.float32),
            jax.ShapeDtypeStruct((1, dates), jnp.float32),
        ],
        compiler_params=params(),
        cost_estimate=cost(4 * slots * dates * dates, 16 * slots * dates),
    )(place, taps, meta, sums)


def shards(stack, spatial_taps, temporal_taps, foot_tile, foot_row, foot_count, foot_owner):
    parts, strips = lax.axis_size("date"), lax.axis_size("strip")
    place = jnp.stack([lax.axis_index("date"), lax.axis_index("strip")]).astype(jnp.int32)
    rows = stack.shape[1]
    feet = foot_row.shape[0]
    own = jnp.concatenate([foot_row, foot_tile, foot_count, foot_owner[:, 0]])
    meta = lax.all_gather(own, ("date", "strip"))

    def swap(value, offset):
        return lax.ppermute(value, "date", [(i, i ^ offset) for i in range(parts)])

    order = [*range(2, parts), 1] if parts > 2 else [1]
    inner, far_inner = {}, {}
    up = lax.ppermute(stack[:, rows - EDGE:, :], "strip", [(i, i + 1) for i in range(strips - 1)])
    down = lax.ppermute(stack[:, :EDGE, :], "strip", [(i + 1, i) for i in range(strips - 1)])
    for offset in order:
        inner[offset] = interior(stack, spatial_taps, place, offset, parts)
        far_inner[offset] = swap(inner[offset], offset)
    inner[0] = interior(stack, spatial_taps, place, 0, parts)
    rim = edges(stack, up, down, spatial_taps, place, parts)
    far_rim = {offset: swap(rim[offset], offset) for offset in order}
    sums = footprints([inner[k] for k in range(parts)], rim, meta, place, strips, feet)
    got = lax.all_to_all(sums, ("date", "strip"), split_axis=0, concat_axis=0, tiled=True)
    anomaly, series = owner_series(got, meta, temporal_taps, place, parts, strips, feet)
    residual = temporal(
        [inner[0]] + [far_inner[k] for k in range(1, parts)], None, temporal_taps, place,
        lambda i: i + 1, rows // EDGE - 2, rows)
    residual = temporal(
        [rim[0]] + [far_rim[k] for k in range(1, parts)], residual, temporal_taps, place,
        lambda i: i * (rows // EDGE - 1), 2, rows)
    return residual, anomaly, series


def solution(mesh):
    placed = (
        P("date", "strip", None),
        P(),
        P(),
        P(("date", "strip")),
        P(("date", "strip")),
        P(("date", "strip")),
        P(("date", "strip"), None),
    )
    return jax.shard_map(
        shards,
        mesh=mesh,
        in_specs=placed,
        out_specs=(
            P(None, "strip", "date"),
            P(("date", "strip"), None, None),
            P(("date", "strip"), None),
        ),
        check_vma=False,
    )
```

```python
import functools

import jax
import jax.numpy as jnp
from jax import lax
from jax.experimental import pallas as pl
from jax.experimental.pallas import tpu as pltpu
from jax.sharding import PartitionSpec as P

TILE = 128
RADIUS = 6
REACH = 2
DILATION = 8
PAIR_CAP = 2
LANES = 128
EDGE = 8
HIGHEST = lax.Precision.HIGHEST


def params(mebibytes):
    return pltpu.CompilerParams(vmem_limit_bytes=mebibytes * 1024 * 1024)


def cost(flops, bytes_accessed):
    return pl.CostEstimate(flops=flops, bytes_accessed=bytes_accessed, transcendentals=0)


def pick_taps(at, taps):
    count = taps.shape[0]
    total = taps[0]
    for k in range(1, count):
        total = total + taps[k]
    out = jnp.zeros(at.shape, jnp.float32)
    for k in range(count):
        out = jnp.where(at == k, taps[k], out)
    return out / jnp.full(at.shape, total, jnp.float32)


def split(value, count):
    out = []
    for _ in range(count):
        piece = value.astype(jnp.bfloat16)
        out.append(piece)
        value = value - piece.astype(jnp.float32)
    return out


def spread(value, axis):
    high, mid = split(value, 2)
    return jnp.concatenate([high, high, high, mid], axis=axis)


def fill_columns(col_ref, taps):
    shape = (LANES, LANES)
    lag = lax.broadcasted_iota(jnp.int32, shape, 0) - lax.broadcasted_iota(jnp.int32, shape, 1)
    near = split(pick_taps(lag + RADIUS, taps), 3)
    far = pick_taps(jnp.where(lag > 0, lag + RADIUS - LANES, lag + RADIUS + LANES), taps)
    above = split(jnp.where(lag > 0, far, 0.0), 3)
    below = split(jnp.where(lag > 0, 0.0, far), 3)
    for n, piece in enumerate((0, 1, 2, 0)):
        at = n * 3 * LANES
        for i, pair in enumerate(((near, above), (below, near), (above, below))):
            for j, block in enumerate(pair):
                col_ref[at + i * LANES:at + (i + 1) * LANES, j * LANES:(j + 1) * LANES] = block[piece]


def row_band(out_rows, in_rows, taps):
    shape = (out_rows, 4 * in_rows)
    lane = lax.broadcasted_iota(jnp.int32, shape, 1)
    row = lax.broadcasted_iota(jnp.int32, shape, 0)
    part = jnp.zeros(shape, jnp.int32)
    for n in range(1, 4):
        part = jnp.where(lane >= n * in_rows, n, part)
    return lane - part * in_rows, row, part


def pieces_of(values, part):
    high, mid, low = [p.astype(jnp.float32) for p in split(values, 3)]
    return jnp.where(part == 1, mid, jnp.where(part == 2, low, high)).astype(jnp.bfloat16)


def filter_columns(mid, rim, col):
    rows = mid.shape[0]
    window = jnp.concatenate([mid, rim], axis=1)
    return jnp.dot(spread(window, 1), col, preferred_element_type=jnp.float32)


def rim_tile(left, right, block, parts):
    lane = lax.broadcasted_iota(jnp.int32, left.shape, len(left.shape) - 1)
    first = lane < LANES // 2
    keep = (first & (block < parts - 1)) | (~first & (block > 0))
    return jnp.where(keep, jnp.where(first, right, left), 0.0)


def interior_kernel(offset, parts, group, place, taps, stack, out, brim, mid_ref, left_ref, right_ref, out_ref, brim_ref,
                    col_ref, row_ref, in_sem, out_sem):
    dates, rows, width = mid_ref.shape
    inner = rows - 2 * EDGE
    cols = width * parts
    block = place[0] ^ offset
    start = block * width
    before = jnp.maximum(start - LANES, 0)
    after = jnp.minimum(start + width, cols - LANES)

    def load(g):
        at = pl.ds(g * group, group)
        return [
            pltpu.make_async_copy(stack.at[at, :, pl.ds(pl.multiple_of(first, LANES), span)], ref.at[at], in_sem.at[n, g])
            for n, (first, span, ref) in enumerate(((start, width, mid_ref), (before, LANES, left_ref), (after, LANES, right_ref)))
        ]

    def store(g):
        at = pl.ds(g * group, group)
        return [
            pltpu.make_async_copy(out_ref.at[at], out.at[at], out_sem.at[0, g]),
            pltpu.make_async_copy(brim_ref.at[at], brim.at[at], out_sem.at[1, g]),
        ]

    steps = dates // group
    for g in range(steps):
        for copy in load(g):
            copy.start()
    fill_columns(col_ref, taps)
    q, r, part = row_band(inner, rows, taps)
    row_ref[...] = pieces_of(pick_taps(q - r - (EDGE - RADIUS), taps), part)

    def step(g, carry):
        for copy in load(g):
            copy.wait()
        at = pl.ds(g * group, group)
        mid = mid_ref[at]
        rim = rim_tile(left_ref[at], right_ref[at], block, parts)
        across = filter_columns(mid.reshape(group * rows, width), rim.reshape(group * rows, LANES), col_ref[...])
        for t in range(group):
            one = across[t * rows:(t + 1) * rows]
            low = jnp.dot(row_ref[...], spread(one, 0), preferred_element_type=jnp.float32)
            out_ref[g * group + t] = mid[t, EDGE:rows - EDGE, :] - low
            brim_ref[g * group + t] = jnp.concatenate([one[:2 * EDGE], one[rows - 2 * EDGE:]], axis=0)
        for copy in store(g):
            copy.start()
        return carry

    lax.fori_loop(0, steps, step, 0)
    for g in range(steps):
        for copy in store(g):
            copy.wait()


def interior(stack, taps, place, offset, parts):
    dates, rows, cols = stack.shape
    width = cols // parts
    group = min(4, dates)
    inner = rows - 2 * EDGE
    anywhere = pl.BlockSpec(memory_space=pl.ANY)
    return pl.pallas_call(
        functools.partial(interior_kernel, offset, parts, group),
        grid_spec=pltpu.PrefetchScalarGridSpec(
            num_scalar_prefetch=2,
            grid=(),
            in_specs=[anywhere],
            out_specs=[anywhere] * 2,
            scratch_shapes=[
                pltpu.VMEM((dates, rows, width), jnp.float32),
                pltpu.VMEM((dates, rows, LANES), jnp.float32),
                pltpu.VMEM((dates, rows, LANES), jnp.float32),
                pltpu.VMEM((dates, inner, width), jnp.float32),
                pltpu.VMEM((dates, 4 * EDGE, width), jnp.float32),
                pltpu.VMEM((12 * LANES, width), jnp.bfloat16),
                pltpu.VMEM((inner, 4 * rows), jnp.bfloat16),
                pltpu.SemaphoreType.DMA((3, dates // group)),
                pltpu.SemaphoreType.DMA((2, dates // group)),
            ],
        ),
        out_shape=[
            jax.ShapeDtypeStruct((dates, inner, width), jnp.float32),
            jax.ShapeDtypeStruct((dates, 4 * EDGE, width), jnp.float32),
        ],
        compiler_params=params(60),
        cost_estimate=cost(60 * dates * rows * width, 3 * 4 * dates * rows * width),
    )(place, taps, stack)


def edge_kernel(parts, place, taps, stack, up, down, *rest):
    brims, outs = rest[:parts], rest[parts:2 * parts]
    x_ref, halo_ref, brim_ref, out_ref, col_ref, row_ref, in_sem, brim_sem, out_sem = rest[2 * parts:]
    dates, _, cols = halo_ref.shape
    rows = stack.shape[1]
    width = cols // parts
    span = 6 * EDGE
    low_half, high_half = pl.ds(0, EDGE), pl.ds(EDGE, EDGE)
    loads = [
        pltpu.make_async_copy(up, halo_ref.at[:, low_half, :], in_sem.at[0]),
        pltpu.make_async_copy(down, halo_ref.at[:, high_half, :], in_sem.at[1]),
        pltpu.make_async_copy(stack.at[:, low_half, :], x_ref.at[:, low_half, :], in_sem.at[2]),
        pltpu.make_async_copy(stack.at[:, pl.ds(rows - EDGE, EDGE), :], x_ref.at[:, high_half, :], in_sem.at[3]),
    ]
    kept = [pltpu.make_async_copy(brims[k], brim_ref.at[k], brim_sem.at[k]) for k in range(parts)]
    for copy in loads + kept:
        copy.start()
    fill_columns(col_ref, taps)
    q, r, part = row_band(2 * EDGE, span, taps)
    own = (q >= span // 2) == (r >= EDGE)
    at = jnp.where(own, (q % (span // 2)) - (r % EDGE) - (EDGE - RADIUS), -1)
    row_ref[...] = pieces_of(pick_taps(at, taps), part)
    for copy in loads:
        copy.wait()
    sends = []
    for k in range(parts):
        block = place[0] ^ k
        start = pl.multiple_of(block * width, LANES)
        before = pl.multiple_of(jnp.maximum(start - LANES, 0), LANES)
        after = pl.multiple_of(jnp.minimum(start + width, cols - LANES), LANES)
        kept[k].wait()
        mid = halo_ref[:, :, pl.ds(start, width)].reshape(dates * 2 * EDGE, width)
        rim = rim_tile(halo_ref[:, :, pl.ds(before, LANES)], halo_ref[:, :, pl.ds(after, LANES)], block, parts)
        across = filter_columns(mid, rim.reshape(dates * 2 * EDGE, LANES), col_ref[...])
        for t in range(dates):
            one = across[t * 2 * EDGE:(t + 1) * 2 * EDGE]
            one = jnp.concatenate([one[:EDGE], brim_ref[k, t], one[EDGE:]], axis=0)
            low = jnp.dot(row_ref[...], spread(one, 0), preferred_element_type=jnp.float32)
            out_ref[k, t] = x_ref[t, :, pl.ds(start, width)] - low
        sends.append(pltpu.make_async_copy(out_ref.at[k], outs[k], out_sem.at[k]))
        sends[-1].start()
    for copy in sends:
        copy.wait()


def edges(stack, up, down, brims, taps, place):
    parts = len(brims)
    dates, rows, cols = stack.shape
    width = cols // parts
    anywhere = pl.BlockSpec(memory_space=pl.ANY)
    return pl.pallas_call(
        functools.partial(edge_kernel, parts),
        grid_spec=pltpu.PrefetchScalarGridSpec(
            num_scalar_prefetch=2,
            grid=(),
            in_specs=[anywhere] * (3 + parts),
            out_specs=[anywhere] * parts,
            scratch_shapes=[
                pltpu.VMEM((dates, 2 * EDGE, cols), jnp.float32),
                pltpu.VMEM((dates, 2 * EDGE, cols), jnp.float32),
                pltpu.VMEM((parts, dates, 4 * EDGE, width), jnp.float32),
                pltpu.VMEM((parts, dates, 2 * EDGE, width), jnp.float32),
                pltpu.VMEM((12 * LANES, width), jnp.bfloat16),
                pltpu.VMEM((2 * EDGE, 24 * EDGE), jnp.bfloat16),
                pltpu.SemaphoreType.DMA((4,)),
                pltpu.SemaphoreType.DMA((parts,)),
                pltpu.SemaphoreType.DMA((parts,)),
            ],
        ),
        out_shape=[jax.ShapeDtypeStruct((dates, 2 * EDGE, width), jnp.float32)] * parts,
        compiler_params=params(60),
        cost_estimate=cost(60 * dates * 32 * cols, 4 * dates * 64 * cols),
    )(place, taps, stack, up, down, *brims)


def temporal_kernel(parts, with_base, tiles, place, taps, *rest):
    pieces = rest[:parts]
    out, z_ref, f_ref, out_ref, in_sem, out_sem = rest[parts + with_base:]
    _, total, _, width = out_ref.shape
    local = total // parts
    pad = REACH * DILATION
    step = 8
    loads = []
    for n in range(len(tiles)):
        for k in range(parts):
            into = z_ref.at[n, pl.ds(REACH + (place[0] ^ k) * local, local)]
            loads.append(pltpu.make_async_copy(pieces[k].at[:, pl.ds(n * EDGE, EDGE), :], into, in_sem.at[n, k]))
    for copy in loads:
        copy.start()
    none = jnp.zeros((REACH, EDGE, width), jnp.float32)
    for n in range(len(tiles)):
        z_ref[n, 0:REACH] = none
        z_ref[n, REACH + total:REACH + total + REACH] = none
    wide = jnp.zeros((pad, EDGE, width), jnp.float32)
    f_ref[0:pad] = wide
    f_ref[pad + total:pad + total + pad] = wide
    own = 1.0 - taps[0, REACH]
    own_wide = 1.0 - taps[1, REACH]
    others = [k for k in range(2 * REACH + 1) if k != REACH]
    sends = []
    for n, tile in enumerate(tiles):
        for k in range(parts):
            loads[n * parts + k].wait()

        def first(i, carry):
            t = i * step
            z = z_ref[n, pl.ds(t, step + 2 * REACH)]
            kept = own * z[REACH:REACH + step]
            for k in others:
                kept = kept - taps[0, k] * z[k:k + step]
            f_ref[pl.ds(pad + t, step)] = kept
            return carry

        lax.fori_loop(0, total // step, first, 0)

        def second(i, carry):
            t = i * step
            kept = own_wide * f_ref[pl.ds(pad + t, step)]
            for k in others:
                kept = kept - taps[1, k] * f_ref[pl.ds(t + k * DILATION, step)]
            out_ref[n, pl.ds(t, step)] = kept
            return carry

        lax.fori_loop(0, total // step, second, 0)
        sends.append(pltpu.make_async_copy(out_ref.at[n], out.at[:, pl.ds(tile * EDGE, EDGE), :], out_sem.at[n]))
        sends[-1].start()
    for copy in sends:
        copy.wait()


def temporal(pieces, base, taps, place, tiles, rows):
    parts = len(pieces)
    local, _, width = pieces[0].shape
    total = local * parts
    extra = [] if base is None else [base]
    count = len(tiles)
    anywhere = pl.BlockSpec(memory_space=pl.ANY)
    return pl.pallas_call(
        functools.partial(temporal_kernel, parts, len(extra), tiles),
        grid_spec=pltpu.PrefetchScalarGridSpec(
            num_scalar_prefetch=2,
            grid=(),
            in_specs=[anywhere] * (parts + len(extra)),
            out_specs=anywhere,
            scratch_shapes=[
                pltpu.VMEM((count, total + 2 * REACH, EDGE, width), jnp.float32),
                pltpu.VMEM((total + 2 * REACH * DILATION, EDGE, width), jnp.float32),
                pltpu.VMEM((count, total, EDGE, width), jnp.float32),
                pltpu.SemaphoreType.DMA((count, parts)),
                pltpu.SemaphoreType.DMA((count,)),
            ],
        ),
        out_shape=jax.ShapeDtypeStruct((total, rows, width), jnp.float32),
        input_output_aliases={} if base is None else {2 + parts: 0},
        compiler_params=params(20),
        cost_estimate=cost(20 * total * EDGE * count * width, 8 * total * EDGE * count * width),
    )(place, taps, *pieces, *extra)


def footprint_kernel(parts, feet, place, meta, *rest):
    inner, rim = rest[:parts], rest[parts:2 * parts]
    out_ref, x_ref, m_ref, n_ref, sem = rest[2 * parts:]
    per, dates, rows, _ = x_ref.shape
    per = per // parts
    copies = []
    for k in range(parts):
        for h in range(per):
            lanes = pl.ds(h * LANES, LANES)
            into = x_ref.at[k * per + h]
            copies.append(pltpu.make_async_copy(
                inner[k].at[:, :, lanes], into.at[:, EDGE:rows - EDGE, :], sem.at[3 * (k * per + h)]))
            copies.append(pltpu.make_async_copy(
                rim[k].at[:, 0:EDGE, lanes], into.at[:, 0:EDGE, :], sem.at[3 * (k * per + h) + 1]))
            copies.append(pltpu.make_async_copy(
                rim[k].at[:, EDGE:2 * EDGE, lanes], into.at[:, rows - EDGE:rows, :], sem.at[3 * (k * per + h) + 2]))
    for copy in copies:
        copy.start()
    m_ref[...] = jnp.zeros(m_ref.shape, jnp.float32)
    n_ref[...] = jnp.zeros(n_ref.shape, jnp.float32)
    for copy in copies:
        copy.wait()
    flat = x_ref.reshape(parts * per * dates * rows, LANES)
    lane = lax.broadcasted_iota(jnp.int32, (dates, LANES), 1)
    for block in range(parts):
        base = (block ^ place[0]) * per * dates * rows

        def take(f, carry):
            at = meta[block, f]
            count = meta[block, feet + f]
            owner = meta[block, 2 * feet + f]
            slot = meta[block, 3 * feet + f]
            pixels = flat[pl.ds(base + at, dates, stride=rows), :]
            total = jnp.sum(jnp.where(lane < count, pixels, 0.0), axis=1, keepdims=True)
            hit = lane == (owner & (LANES - 1))
            to = (owner // LANES, pl.ds(pl.multiple_of((block * PAIR_CAP + slot) * dates, dates), dates))
            m_ref[to] = jnp.where(hit, total, m_ref[to])
            n_ref[to] = jnp.where(hit, count.astype(jnp.float32), n_ref[to])
            return carry

        lax.fori_loop(0, feet, take, 0, unroll=8)
    for n in range(m_ref.shape[0]):
        owners = min(LANES, out_ref.shape[0] - n * LANES)
        out_ref[n * LANES:n * LANES + owners, 0, :] = m_ref[n].T[:owners]
        out_ref[n * LANES:n * LANES + owners, 1, :] = n_ref[n].T[:owners]


def footprints(inner, rim, meta, place, owners, feet):
    parts = len(inner)
    dates, inner_rows, width = inner[0].shape
    rows = inner_rows + 2 * EDGE
    per = width // LANES
    message = parts * PAIR_CAP * dates
    sets = -(-owners // LANES)
    return pl.pallas_call(
        functools.partial(footprint_kernel, parts, feet),
        grid_spec=pltpu.PrefetchScalarGridSpec(
            num_scalar_prefetch=2,
            grid=(),
            in_specs=[pl.BlockSpec(memory_space=pl.ANY)] * (2 * parts),
            out_specs=pl.BlockSpec(memory_space=pltpu.VMEM),
            scratch_shapes=[
                pltpu.VMEM((parts * per, dates, rows, LANES), jnp.float32),
                pltpu.VMEM((sets, message, LANES), jnp.float32),
                pltpu.VMEM((sets, message, LANES), jnp.float32),
                pltpu.SemaphoreType.DMA((3 * parts * per,)),
            ],
        ),
        out_shape=jax.ShapeDtypeStruct((owners, 2, message), jnp.float32),
        compiler_params=params(60),
        cost_estimate=cost(4 * owners * message * LANES, 8 * dates * rows * width * parts),
    )(place, meta, *inner, *rim)


def owner_kernel(parts, strips, taps, got_ref, anomaly_ref, series_ref):
    owners = parts * strips
    slots = owners * PAIR_CAP
    dates = got_ref.shape[2] // PAIR_CAP
    local = dates // parts
    sums, held = got_ref[:, 0, :], got_ref[:, 1, :]
    rows, weights = [], []
    for block in range(parts):
        for slot in range(PAIR_CAP):
            at = (block * PAIR_CAP + slot) * local
            rows.append(jnp.concatenate(
                [sums[e * strips:(e + 1) * strips, at:at + local] for e in range(parts)], axis=1))
            weights.append(held[0:strips, at:at + 1])
    sums = jnp.concatenate(rows, axis=0)
    weight = jnp.concatenate(weights, axis=0)
    shape = (dates, dates)
    lag = lax.broadcasted_iota(jnp.int32, shape, 0) - lax.broadcasted_iota(jnp.int32, shape, 1)
    for level, spacing in ((0, 1), (1, DILATION)):
        filt = jnp.where(lag == 0, 1.0, 0.0)
        for k in range(2 * REACH + 1):
            filt = filt - jnp.where(lag == (k - REACH) * spacing, taps[level, k], 0.0)
        sums = jnp.dot(sums, filt, precision=HIGHEST, preferred_element_type=jnp.float32)
    mean = sums / jnp.where(weight > 0, weight, 1.0)
    asset = jnp.sum(weight * mean, axis=0, keepdims=True) / jnp.sum(weight, axis=0, keepdims=True)
    odd = jnp.where(weight > 0, mean - asset, 0.0)
    series_ref[...] = asset
    shape = (slots, slots)
    to = lax.broadcasted_iota(jnp.int32, shape, 0)
    source = lax.broadcasted_iota(jnp.int32, shape, 1)
    block, rest = source // (PAIR_CAP * strips), source % (PAIR_CAP * strips)
    place_of = block * (PAIR_CAP * strips) + (rest % strips) * PAIR_CAP + rest // strips
    order = jnp.where(to == place_of, 1.0, 0.0)
    anomaly_ref[0] = jnp.dot(order, odd, precision=HIGHEST, preferred_element_type=jnp.float32)


def owner_series(got, taps, parts, strips):
    owners = parts * strips
    dates = got.shape[2] // PAIR_CAP
    slots = owners * PAIR_CAP
    return pl.pallas_call(
        functools.partial(owner_kernel, parts, strips),
        grid_spec=pltpu.PrefetchScalarGridSpec(
            num_scalar_prefetch=1,
            grid=(),
            in_specs=[pl.BlockSpec(memory_space=pltpu.VMEM)],
            out_specs=[pl.BlockSpec(memory_space=pltpu.VMEM)] * 2,
        ),
        out_shape=[
            jax.ShapeDtypeStruct((1, slots, dates), jnp.float32),
            jax.ShapeDtypeStruct((1, dates), jnp.float32),
        ],
        compiler_params=params(20),
        cost_estimate=cost(4 * slots * dates * dates, 16 * slots * dates),
    )(taps, got)


def shards(stack, spatial_taps, temporal_taps, foot_tile, foot_row, foot_count, foot_owner):
    parts, strips = lax.axis_size("date"), lax.axis_size("strip")
    place = lax.axis_index("date").astype(jnp.int32)[None]
    dates, rows, cols = stack.shape
    feet = foot_row.shape[0]
    owner = foot_owner[:, 0]
    position = jnp.arange(feet, dtype=jnp.int32)
    earlier = (owner[:, None] == owner[None, :]) & (position[None, :] < position[:, None])
    slot = jnp.sum(earlier.astype(jnp.int32), axis=1)
    own = jnp.concatenate([foot_tile * (dates * rows) + foot_row, foot_count, owner, slot])
    def swap(value, offset):
        return lax.ppermute(value, "date", [(i, i ^ offset) for i in range(parts)])

    order = [*range(2, parts), 1] if parts > 2 else [1]
    inner, far_inner, brim = {}, {}, {}
    up = lax.ppermute(stack[:, rows - EDGE:, :], "strip", [(i, i + 1) for i in range(strips - 1)])
    down = lax.ppermute(stack[:, :EDGE, :], "strip", [(i + 1, i) for i in range(strips - 1)])
    for offset in order:
        inner[offset], brim[offset] = interior(stack, spatial_taps, place, offset, parts)
        if offset == order[-1]:
            inner[offset], own = lax.optimization_barrier((inner[offset], own))
        far_inner[offset] = swap(inner[offset], offset)
    meta = lax.all_to_all(
        jnp.broadcast_to(own[None, None], (parts, 1, 4 * feet)), "date", split_axis=0, concat_axis=0, tiled=True)
    later, meta = lax.optimization_barrier((place, meta.reshape(parts, 4 * feet)))
    inner[0], brim[0] = interior(stack, spatial_taps, later, 0, parts)
    rim = edges(stack, up, down, [brim[k] for k in range(parts)], spatial_taps, place)
    far_rim = {offset: swap(rim[offset], offset) for offset in order}
    sums = footprints([inner[k] for k in range(parts)], rim, meta, place, parts * strips, feet)
    got = lax.all_to_all(sums, ("date", "strip"), split_axis=0, concat_axis=0, tiled=True)
    anomaly, series = owner_series(got, temporal_taps, parts, strips)
    last = rows // EDGE - 1
    residual = temporal(
        [inner[0]] + [far_inner[k] for k in range(1, parts)], None, temporal_taps, place, tuple(range(1, last)), rows)
    residual = temporal(
        [rim[0]] + [far_rim[k] for k in range(1, parts)], residual, temporal_taps, place, (0, last), rows)
    return residual, anomaly, series


def solution(mesh):
    placed = (
        P("date", "strip", None),
        P(),
        P(),
        P(("date", "strip")),
        P(("date", "strip")),
        P(("date", "strip")),
        P(("date", "strip"), None),
    )
    return jax.shard_map(
        shards,
        mesh=mesh,
        in_specs=placed,
        out_specs=(
            P(None, "strip", "date"),
            P(("date", "strip"), None, None),
            P(("date", "strip"), None),
        ),
        check_vma=False,
    )
```

```python
import functools

import jax
import jax.numpy as jnp
from jax import lax
from jax.experimental import pallas as pl
from jax.experimental.pallas import tpu as pltpu
from jax.sharding import PartitionSpec as P

TILE = 128
RADIUS = 6
REACH = 2
DILATION = 8
PAIR_CAP = 2
LANES = 128
EDGE = 8
HIGHEST = lax.Precision.HIGHEST


def params(mebibytes):
    return pltpu.CompilerParams(vmem_limit_bytes=mebibytes * 1024 * 1024)


def cost(flops, bytes_accessed):
    return pl.CostEstimate(flops=flops, bytes_accessed=bytes_accessed, transcendentals=0)


def pick_taps(at, taps):
    count = taps.shape[0]
    total = taps[0]
    for k in range(1, count):
        total = total + taps[k]
    out = jnp.zeros(at.shape, jnp.float32)
    for k in range(count):
        out = jnp.where(at == k, taps[k], out)
    return out / jnp.full(at.shape, total, jnp.float32)


def split(value, count):
    out = []
    for _ in range(count):
        piece = value.astype(jnp.bfloat16)
        out.append(piece)
        value = value - piece.astype(jnp.float32)
    return out


def spread(value, axis):
    high, mid = split(value, 2)
    return jnp.concatenate([high, high, high, mid], axis=axis)


def fill_columns(col_ref, taps):
    shape = (LANES, LANES)
    lag = lax.broadcasted_iota(jnp.int32, shape, 0) - lax.broadcasted_iota(jnp.int32, shape, 1)
    near = split(pick_taps(lag + RADIUS, taps), 3)
    far = pick_taps(jnp.where(lag > 0, lag + RADIUS - LANES, lag + RADIUS + LANES), taps)
    above = split(jnp.where(lag > 0, far, 0.0), 3)
    below = split(jnp.where(lag > 0, 0.0, far), 3)
    for n, piece in enumerate((0, 1, 2, 0)):
        at = n * 3 * LANES
        for i, pair in enumerate(((near, above), (below, near), (above, below))):
            for j, block in enumerate(pair):
                col_ref[at + i * LANES:at + (i + 1) * LANES, j * LANES:(j + 1) * LANES] = block[piece]


def row_band(out_rows, in_rows, taps):
    shape = (out_rows, 4 * in_rows)
    lane = lax.broadcasted_iota(jnp.int32, shape, 1)
    row = lax.broadcasted_iota(jnp.int32, shape, 0)
    part = jnp.zeros(shape, jnp.int32)
    for n in range(1, 4):
        part = jnp.where(lane >= n * in_rows, n, part)
    return lane - part * in_rows, row, part


def pieces_of(values, part):
    high, mid, low = [p.astype(jnp.float32) for p in split(values, 3)]
    return jnp.where(part == 1, mid, jnp.where(part == 2, low, high)).astype(jnp.bfloat16)


def filter_columns(mid, rim, col):
    rows = mid.shape[0]
    window = jnp.concatenate([mid, rim], axis=1)
    return jnp.dot(spread(window, 1), col, preferred_element_type=jnp.float32)


def rim_tile(left, right, block, parts):
    lane = lax.broadcasted_iota(jnp.int32, left.shape, len(left.shape) - 1)
    first = lane < LANES // 2
    keep = (first & (block < parts - 1)) | (~first & (block > 0))
    return jnp.where(keep, jnp.where(first, right, left), 0.0)


def interior_kernel(offsets, parts, group, alone, place, taps, stack, *rest):
    count = len(offsets)
    outs, brims, rest = rest[:count], rest[count:2 * count], rest[2 * count:]
    if alone:
        halos, rest = rest[:2], rest[2:]
        mid_ref, left_ref, right_ref, halo_sem = rest[:4]
        rest = rest[4:]
    else:
        x_ref, rest = rest[0], rest[1:]
    out_ref, brim_ref, col_ref, row_ref, in_sem, out_sem = rest
    _, dates, inner, width = out_ref.shape
    rows = inner + 2 * EDGE
    cols = width * parts

    def bounds(offset):
        start = (place[0] ^ offset) * width
        places = start, jnp.maximum(start - LANES, 0), jnp.minimum(start + width, cols - LANES)
        return [pl.multiple_of(first, LANES) for first in places]

    def load(g):
        at = pl.ds(g * group, group)
        if not alone:
            return [pltpu.make_async_copy(stack.at[at], x_ref.at[at], in_sem.at[0, g])]
        return [
            pltpu.make_async_copy(stack.at[at, :, pl.ds(first, ref.shape[2])], ref.at[at], in_sem.at[n, g])
            for n, (first, ref) in enumerate(zip(bounds(offsets[0]), (mid_ref, left_ref, right_ref)))
        ]

    def window(at, offset):
        if alone:
            return mid_ref[at], left_ref[at], right_ref[at]
        start, before, after = bounds(offset)
        return x_ref[at, :, pl.ds(start, width)], x_ref[at, :, pl.ds(before, LANES)], x_ref[at, :, pl.ds(after, LANES)]

    def store(g):
        at = pl.ds(g * group, group)
        return [
            pltpu.make_async_copy(ref.at[n, at], whole[n].at[at], out_sem.at[2 * n + i, g])
            for n in range(count) for i, (ref, whole) in enumerate(((out_ref, outs), (brim_ref, brims)))
        ]

    steps = dates // group
    for g in range(steps):
        for copy in load(g):
            copy.start()
    copies = []
    if alone:
        copies = [
            pltpu.make_async_copy(stack.at[:, pl.ds(rows - EDGE, EDGE), :], halos[0], halo_sem.at[0]),
            pltpu.make_async_copy(stack.at[:, pl.ds(0, EDGE), :], halos[1], halo_sem.at[1]),
        ]
        for copy in copies:
            copy.start()
    fill_columns(col_ref, taps)
    q, r, part = row_band(inner, rows, taps)
    row_ref[...] = pieces_of(pick_taps(q - r - (EDGE - RADIUS), taps), part)

    def step(g, carry):
        for copy in load(g):
            copy.wait()
        at = pl.ds(g * group, group)
        for n, offset in enumerate(offsets):
            mid, left, right = window(at, offset)
            rim = rim_tile(left, right, place[0] ^ offset, parts)
            across = filter_columns(mid.reshape(group * rows, width), rim.reshape(group * rows, LANES), col_ref[...])
            for t in range(group):
                one = across[t * rows:(t + 1) * rows]
                low = jnp.dot(row_ref[...], spread(one, 0), preferred_element_type=jnp.float32)
                out_ref[n, g * group + t] = mid[t, EDGE:rows - EDGE, :] - low
                brim_ref[n, g * group + t] = jnp.concatenate([one[:2 * EDGE], one[rows - 2 * EDGE:]], axis=0)
        for copy in store(g):
            copy.start()
        return carry

    lax.fori_loop(0, steps, step, 0)
    for copy in copies:
        copy.wait()
    for g in range(steps):
        for copy in store(g):
            copy.wait()


def interior(stack, taps, place, offsets, parts, alone):
    dates, rows, cols = stack.shape
    width = cols // parts
    group = min(4, dates)
    inner = rows - 2 * EDGE
    count = len(offsets)
    anywhere = pl.BlockSpec(memory_space=pl.ANY)
    out_shape = [jax.ShapeDtypeStruct((dates, inner, width), jnp.float32)] * count
    out_shape += [jax.ShapeDtypeStruct((dates, 4 * EDGE, width), jnp.float32)] * count
    scratch = [pltpu.VMEM((dates, rows, cols), jnp.float32)]
    if alone:
        out_shape += [jax.ShapeDtypeStruct((dates, EDGE, cols), jnp.float32)] * 2
        scratch = [pltpu.VMEM((dates, rows, span), jnp.float32) for span in (width, LANES, LANES)]
        scratch.append(pltpu.SemaphoreType.DMA((2,)))
    return pl.pallas_call(
        functools.partial(interior_kernel, offsets, parts, group, alone),
        grid_spec=pltpu.PrefetchScalarGridSpec(
            num_scalar_prefetch=2,
            grid=(),
            in_specs=[anywhere],
            out_specs=[anywhere] * len(out_shape),
            scratch_shapes=scratch + [
                pltpu.VMEM((count, dates, inner, width), jnp.float32),
                pltpu.VMEM((count, dates, 4 * EDGE, width), jnp.float32),
                pltpu.VMEM((12 * LANES, width), jnp.bfloat16),
                pltpu.VMEM((inner, 4 * rows), jnp.bfloat16),
                pltpu.SemaphoreType.DMA((3, dates // group)),
                pltpu.SemaphoreType.DMA((2 * count, dates // group)),
            ],
        ),
        out_shape=out_shape,
        compiler_params=params(60),
        cost_estimate=cost(60 * count * dates * rows * width, 3 * 4 * count * dates * rows * width),
    )(place, taps, stack)


def edge_kernel(parts, place, taps, stack, up, down, *rest):
    brims, outs = rest[:parts], rest[parts:2 * parts]
    x_ref, halo_ref, brim_ref, out_ref, col_ref, row_ref, in_sem, brim_sem, out_sem = rest[2 * parts:]
    dates, _, cols = halo_ref.shape
    rows = stack.shape[1]
    width = cols // parts
    span = 6 * EDGE
    low_half, high_half = pl.ds(0, EDGE), pl.ds(EDGE, EDGE)
    loads = [
        pltpu.make_async_copy(up, halo_ref.at[:, low_half, :], in_sem.at[0]),
        pltpu.make_async_copy(down, halo_ref.at[:, high_half, :], in_sem.at[1]),
        pltpu.make_async_copy(stack.at[:, low_half, :], x_ref.at[:, low_half, :], in_sem.at[2]),
        pltpu.make_async_copy(stack.at[:, pl.ds(rows - EDGE, EDGE), :], x_ref.at[:, high_half, :], in_sem.at[3]),
    ]
    kept = [pltpu.make_async_copy(brims[k], brim_ref.at[k], brim_sem.at[k]) for k in range(parts)]
    for copy in loads + kept:
        copy.start()
    fill_columns(col_ref, taps)
    q, r, part = row_band(2 * EDGE, span, taps)
    own = (q >= span // 2) == (r >= EDGE)
    at = jnp.where(own, (q % (span // 2)) - (r % EDGE) - (EDGE - RADIUS), -1)
    row_ref[...] = pieces_of(pick_taps(at, taps), part)
    for copy in loads:
        copy.wait()
    sends = []
    for k in range(parts):
        block = place[0] ^ k
        start = pl.multiple_of(block * width, LANES)
        before = pl.multiple_of(jnp.maximum(start - LANES, 0), LANES)
        after = pl.multiple_of(jnp.minimum(start + width, cols - LANES), LANES)
        kept[k].wait()
        mid = halo_ref[:, :, pl.ds(start, width)].reshape(dates * 2 * EDGE, width)
        rim = rim_tile(halo_ref[:, :, pl.ds(before, LANES)], halo_ref[:, :, pl.ds(after, LANES)], block, parts)
        across = filter_columns(mid, rim.reshape(dates * 2 * EDGE, LANES), col_ref[...])
        for t in range(dates):
            one = across[t * 2 * EDGE:(t + 1) * 2 * EDGE]
            one = jnp.concatenate([one[:EDGE], brim_ref[k, t], one[EDGE:]], axis=0)
            low = jnp.dot(row_ref[...], spread(one, 0), preferred_element_type=jnp.float32)
            out_ref[k, t] = x_ref[t, :, pl.ds(start, width)] - low
        sends.append(pltpu.make_async_copy(out_ref.at[k], outs[k], out_sem.at[k]))
        sends[-1].start()
    for copy in sends:
        copy.wait()


def edges(stack, up, down, brims, taps, place):
    parts = len(brims)
    dates, rows, cols = stack.shape
    width = cols // parts
    anywhere = pl.BlockSpec(memory_space=pl.ANY)
    return pl.pallas_call(
        functools.partial(edge_kernel, parts),
        grid_spec=pltpu.PrefetchScalarGridSpec(
            num_scalar_prefetch=2,
            grid=(),
            in_specs=[anywhere] * (3 + parts),
            out_specs=[anywhere] * parts,
            scratch_shapes=[
                pltpu.VMEM((dates, 2 * EDGE, cols), jnp.float32),
                pltpu.VMEM((dates, 2 * EDGE, cols), jnp.float32),
                pltpu.VMEM((parts, dates, 4 * EDGE, width), jnp.float32),
                pltpu.VMEM((parts, dates, 2 * EDGE, width), jnp.float32),
                pltpu.VMEM((12 * LANES, width), jnp.bfloat16),
                pltpu.VMEM((2 * EDGE, 24 * EDGE), jnp.bfloat16),
                pltpu.SemaphoreType.DMA((4,)),
                pltpu.SemaphoreType.DMA((parts,)),
                pltpu.SemaphoreType.DMA((parts,)),
            ],
        ),
        out_shape=[jax.ShapeDtypeStruct((dates, 2 * EDGE, width), jnp.float32)] * parts,
        compiler_params=params(60),
        cost_estimate=cost(60 * dates * 32 * cols, 4 * dates * 64 * cols),
    )(place, taps, stack, up, down, *brims)


def temporal_kernel(parts, with_base, tiles, place, taps, *rest):
    pieces = rest[:parts]
    out, z_ref, f_ref, out_ref, in_sem, out_sem = rest[parts + with_base:]
    _, total, _, width = out_ref.shape
    local = total // parts
    pad = REACH * DILATION
    step = 8
    loads = []
    for n in range(len(tiles)):
        for k in range(parts):
            into = z_ref.at[n, pl.ds(REACH + (place[0] ^ k) * local, local)]
            loads.append(pltpu.make_async_copy(pieces[k].at[:, pl.ds(n * EDGE, EDGE), :], into, in_sem.at[n, k]))
    for copy in loads:
        copy.start()
    none = jnp.zeros((REACH, EDGE, width), jnp.float32)
    for n in range(len(tiles)):
        z_ref[n, 0:REACH] = none
        z_ref[n, REACH + total:REACH + total + REACH] = none
    wide = jnp.zeros((pad, EDGE, width), jnp.float32)
    f_ref[0:pad] = wide
    f_ref[pad + total:pad + total + pad] = wide
    own = 1.0 - taps[0, REACH]
    own_wide = 1.0 - taps[1, REACH]
    others = [k for k in range(2 * REACH + 1) if k != REACH]
    sends = []
    for n, tile in enumerate(tiles):
        for k in range(parts):
            loads[n * parts + k].wait()

        def first(i, carry):
            t = i * step
            z = z_ref[n, pl.ds(t, step + 2 * REACH)]
            kept = own * z[REACH:REACH + step]
            for k in others:
                kept = kept - taps[0, k] * z[k:k + step]
            f_ref[pl.ds(pad + t, step)] = kept
            return carry

        lax.fori_loop(0, total // step, first, 0)

        def second(i, carry):
            t = i * step
            kept = own_wide * f_ref[pl.ds(pad + t, step)]
            for k in others:
                kept = kept - taps[1, k] * f_ref[pl.ds(t + k * DILATION, step)]
            out_ref[n, pl.ds(t, step)] = kept
            return carry

        lax.fori_loop(0, total // step, second, 0)
        sends.append(pltpu.make_async_copy(out_ref.at[n], out.at[:, pl.ds(tile * EDGE, EDGE), :], out_sem.at[n]))
        sends[-1].start()
    for copy in sends:
        copy.wait()


def temporal(pieces, base, taps, place, tiles, rows):
    parts = len(pieces)
    local, _, width = pieces[0].shape
    total = local * parts
    extra = [] if base is None else [base]
    count = len(tiles)
    anywhere = pl.BlockSpec(memory_space=pl.ANY)
    return pl.pallas_call(
        functools.partial(temporal_kernel, parts, len(extra), tiles),
        grid_spec=pltpu.PrefetchScalarGridSpec(
            num_scalar_prefetch=2,
            grid=(),
            in_specs=[anywhere] * (parts + len(extra)),
            out_specs=anywhere,
            scratch_shapes=[
                pltpu.VMEM((count, total + 2 * REACH, EDGE, width), jnp.float32),
                pltpu.VMEM((total + 2 * REACH * DILATION, EDGE, width), jnp.float32),
                pltpu.VMEM((count, total, EDGE, width), jnp.float32),
                pltpu.SemaphoreType.DMA((count, parts)),
                pltpu.SemaphoreType.DMA((count,)),
            ],
        ),
        out_shape=jax.ShapeDtypeStruct((total, rows, width), jnp.float32),
        input_output_aliases={} if base is None else {2 + parts: 0},
        compiler_params=params(20),
        cost_estimate=cost(20 * total * EDGE * count * width, 8 * total * EDGE * count * width),
    )(place, taps, *pieces, *extra)


def footprint_kernel(parts, feet, place, *rest):
    meta, vectors, rest = rest[:parts], rest[parts:2 * parts], rest[2 * parts:]
    inner, rim = rest[:parts], rest[parts:2 * parts]
    out_ref, x_ref, sem = rest[2 * parts:]
    per, dates, rows, _ = x_ref.shape
    per = per // parts
    owners = out_ref.shape[0]
    copies = []
    for k in range(parts):
        for h in range(per):
            lanes = pl.ds(h * LANES, LANES)
            into = x_ref.at[k * per + h]
            copies.append(pltpu.make_async_copy(
                inner[k].at[:, :, lanes], into.at[:, EDGE:rows - EDGE, :], sem.at[3 * (k * per + h)]))
            copies.append(pltpu.make_async_copy(
                rim[k].at[:, 0:EDGE, lanes], into.at[:, 0:EDGE, :], sem.at[3 * (k * per + h) + 1]))
            copies.append(pltpu.make_async_copy(
                rim[k].at[:, EDGE:2 * EDGE, lanes], into.at[:, rows - EDGE:rows, :], sem.at[3 * (k * per + h) + 2]))
    for copy in copies:
        copy.start()
    lane = lax.broadcasted_iota(jnp.int32, (dates, LANES), 1)
    both = [jnp.concatenate([ref[n:n + 1, :] for ref in vectors], axis=1) for n in range(1, 4)]
    index = lax.broadcasted_iota(jnp.int32, both[0].shape, 1)
    source = (index // feet) ^ place[0]
    named = lax.broadcasted_iota(jnp.int32, (owners, index.shape[1]), 0) == both[1]
    places = []
    for block in range(parts):
        for slot in range(PAIR_CAP):
            hit = named & (source == block) & (both[2] == slot)
            places.append(jnp.where(hit, 1.0, 0.0).astype(jnp.bfloat16))
    places = jnp.concatenate(places, axis=0)
    for copy in copies:
        copy.wait()
    flat = x_ref.reshape(parts * per * dates * rows, LANES)
    tiles = []
    for first in range(0, parts * feet, LANES):
        total = jnp.zeros((dates, LANES), jnp.float32)
        for k in range(first // feet, -(-(first + LANES) // feet)):
            base = k * per * dates * rows

            def take(f, total):
                pixels = flat[pl.ds(base + meta[k][0, f], dates, stride=rows), :]
                one = jnp.sum(jnp.where(lane < meta[k][1, f], pixels, 0.0), axis=1, keepdims=True)
                return jnp.where(lane == k * feet + f - first, one, total)

            total = lax.fori_loop(max(first - k * feet, 0), min(feet, first + LANES - k * feet), take, total, unroll=16)
        tiles.append(total)
    counts = jnp.broadcast_to(both[0].astype(jnp.float32), (dates, index.shape[1]))
    sums = jnp.concatenate([jnp.concatenate(tiles, axis=1), counts], axis=0)
    held = jnp.zeros((places.shape[0], 2 * dates), jnp.float32)
    for piece in split(sums, 3):
        held = held + lax.dot_general(places, piece, (((1,), (1,)), ((), ())), preferred_element_type=jnp.float32)
    for n in range(parts * PAIR_CAP):
        at = pl.ds(n * dates, dates)
        out_ref[:, 0, at] = held[n * owners:(n + 1) * owners, :dates]
        out_ref[:, 1, at] = held[n * owners:(n + 1) * owners, dates:]


def footprints(inner, rim, meta, place, owners):
    parts = len(inner)
    dates, inner_rows, width = inner[0].shape
    feet = meta[0].shape[1]
    rows = inner_rows + 2 * EDGE
    per = width // LANES
    message = parts * PAIR_CAP * dates
    return pl.pallas_call(
        functools.partial(footprint_kernel, parts, feet),
        grid_spec=pltpu.PrefetchScalarGridSpec(
            num_scalar_prefetch=1 + parts,
            grid=(),
            in_specs=[pl.BlockSpec(memory_space=pltpu.VMEM)] * parts + [pl.BlockSpec(memory_space=pl.ANY)] * (2 * parts),
            out_specs=pl.BlockSpec(memory_space=pltpu.VMEM),
            scratch_shapes=[
                pltpu.VMEM((parts * per, dates, rows, LANES), jnp.float32),
                pltpu.SemaphoreType.DMA((3 * parts * per,)),
            ],
        ),
        out_shape=jax.ShapeDtypeStruct((owners, 2, message), jnp.float32),
        compiler_params=params(60),
        cost_estimate=cost(4 * owners * message * LANES, 8 * dates * rows * width * parts),
    )(place, *meta, *meta, *inner, *rim)


def owner_kernel(parts, strips, taps, got_ref, anomaly_ref, series_ref):
    owners = parts * strips
    slots = owners * PAIR_CAP
    dates = got_ref.shape[2] // PAIR_CAP
    local = dates // parts
    sums, held = got_ref[:, 0, :], got_ref[:, 1, :]
    rows, weights = [], []
    for block in range(parts):
        for slot in range(PAIR_CAP):
            at = (block * PAIR_CAP + slot) * local
            rows.append(jnp.concatenate(
                [sums[e * strips:(e + 1) * strips, at:at + local] for e in range(parts)], axis=1))
            weights.append(held[0:strips, at:at + 1])
    sums = jnp.concatenate(rows, axis=0)
    weight = jnp.concatenate(weights, axis=0)
    shape = (dates, dates)
    lag = lax.broadcasted_iota(jnp.int32, shape, 0) - lax.broadcasted_iota(jnp.int32, shape, 1)
    for level, spacing in ((0, 1), (1, DILATION)):
        filt = jnp.where(lag == 0, 1.0, 0.0)
        for k in range(2 * REACH + 1):
            filt = filt - jnp.where(lag == (k - REACH) * spacing, taps[level, k], 0.0)
        sums = jnp.dot(sums, filt, precision=HIGHEST, preferred_element_type=jnp.float32)
    mean = sums / jnp.where(weight > 0, weight, 1.0)
    asset = jnp.sum(weight * mean, axis=0, keepdims=True) / jnp.sum(weight, axis=0, keepdims=True)
    odd = jnp.where(weight > 0, mean - asset, 0.0)
    series_ref[...] = asset
    shape = (slots, slots)
    to = lax.broadcasted_iota(jnp.int32, shape, 0)
    source = lax.broadcasted_iota(jnp.int32, shape, 1)
    block, rest = source // (PAIR_CAP * strips), source % (PAIR_CAP * strips)
    place_of = block * (PAIR_CAP * strips) + (rest % strips) * PAIR_CAP + rest // strips
    order = jnp.where(to == place_of, 1.0, 0.0)
    anomaly_ref[0] = jnp.dot(order, odd, precision=HIGHEST, preferred_element_type=jnp.float32)


def owner_series(got, taps, parts, strips):
    owners = parts * strips
    dates = got.shape[2] // PAIR_CAP
    slots = owners * PAIR_CAP
    return pl.pallas_call(
        functools.partial(owner_kernel, parts, strips),
        grid_spec=pltpu.PrefetchScalarGridSpec(
            num_scalar_prefetch=1,
            grid=(),
            in_specs=[pl.BlockSpec(memory_space=pltpu.VMEM)],
            out_specs=[pl.BlockSpec(memory_space=pltpu.VMEM)] * 2,
        ),
        out_shape=[
            jax.ShapeDtypeStruct((1, slots, dates), jnp.float32),
            jax.ShapeDtypeStruct((1, dates), jnp.float32),
        ],
        compiler_params=params(20),
        cost_estimate=cost(4 * slots * dates * dates, 16 * slots * dates),
    )(taps, got)


def shards(stack, spatial_taps, temporal_taps, foot_tile, foot_row, foot_count, foot_owner):
    parts, strips = lax.axis_size("date"), lax.axis_size("strip")
    place = lax.axis_index("date").astype(jnp.int32)[None]
    dates, rows, cols = stack.shape
    feet = foot_row.shape[0]
    owner = foot_owner[:, 0]
    position = jnp.arange(feet, dtype=jnp.int32)
    earlier = (owner[:, None] == owner[None, :]) & (position[None, :] < position[:, None])
    slot = jnp.sum(earlier.astype(jnp.int32), axis=1)
    own = jnp.stack([foot_tile * (dates * rows) + foot_row, foot_count, owner, slot])

    def swap(value, offset):
        return lax.ppermute(value, "date", [(i, i ^ offset) for i in range(parts)])

    far = list(range(2, parts)) if parts > 2 else [1]
    first, rest = far[0], far[1:] + ([1, 0] if parts > 2 else [0])
    order = [first] + [k for k in rest if k]
    inner, brim, far_inner = {}, {}, {}
    inner[first], brim[first], last_rows, first_rows = interior(stack, spatial_taps, place, (first,), parts, True)
    far_inner[first] = swap(inner[first], first)
    up = lax.ppermute(last_rows, "strip", [(i, i + 1) for i in range(strips - 1)])
    down = lax.ppermute(first_rows, "strip", [(i + 1, i) for i in range(strips - 1)])
    made = interior(stack, spatial_taps, place, tuple(rest), parts, False)
    *made, own = lax.optimization_barrier((*made, own))
    for n, offset in enumerate(rest):
        inner[offset], brim[offset] = made[n], made[len(rest) + n]
    for offset in order[1:]:
        far_inner[offset] = swap(inner[offset], offset)
    meta = [own] + [swap(own, k) for k in range(1, parts)]
    rim = edges(stack, up, down, [brim[k] for k in range(parts)], spatial_taps, place)
    far_rim = {offset: swap(rim[offset], offset) for offset in order}
    sums = footprints([inner[k] for k in range(parts)], rim, meta, place, parts * strips)
    got = lax.all_to_all(sums, ("date", "strip"), split_axis=0, concat_axis=0, tiled=True)
    last = rows // EDGE - 1
    residual = temporal(
        [inner[0]] + [far_inner[k] for k in range(1, parts)], None, temporal_taps, place, tuple(range(1, last)), rows)
    got, residual = lax.optimization_barrier((got, residual))
    anomaly, series = owner_series(got, temporal_taps, parts, strips)
    residual = temporal(
        [rim[0]] + [far_rim[k] for k in range(1, parts)], residual, temporal_taps, place, (0, last), rows)
    return residual, anomaly, series


def solution(mesh):
    placed = (
        P("date", "strip", None),
        P(),
        P(),
        P(("date", "strip")),
        P(("date", "strip")),
        P(("date", "strip")),
        P(("date", "strip"), None),
    )
    return jax.shard_map(
        shards,
        mesh=mesh,
        in_specs=placed,
        out_specs=(
            P(None, "strip", "date"),
            P(("date", "strip"), None, None),
            P(("date", "strip"), None),
        ),
        check_vma=False,
    )
```

```python
import functools

import jax
import jax.numpy as jnp
from jax import lax
from jax.experimental import pallas as pl
from jax.experimental.pallas import tpu as pltpu
from jax.sharding import PartitionSpec as P

TILE = 128
RADIUS = 6
REACH = 2
DILATION = 8
PAIR_CAP = 2
LANES = 128
EDGE = 8
HIGHEST = lax.Precision.HIGHEST


def params(mebibytes):
    return pltpu.CompilerParams(vmem_limit_bytes=mebibytes * 1024 * 1024)


def cost(flops, bytes_accessed):
    return pl.CostEstimate(flops=flops, bytes_accessed=bytes_accessed, transcendentals=0)


def pick_taps(at, taps):
    count = taps.shape[0]
    total = taps[0]
    for k in range(1, count):
        total = total + taps[k]
    out = jnp.zeros(at.shape, jnp.float32)
    for k in range(count):
        out = jnp.where(at == k, taps[k], out)
    return out / jnp.full(at.shape, total, jnp.float32)


def split(value, count):
    out = []
    for _ in range(count):
        piece = value.astype(jnp.bfloat16)
        out.append(piece)
        value = value - piece.astype(jnp.float32)
    return out


def spread(value, axis):
    high, mid = split(value, 2)
    return jnp.concatenate([high, high, high, mid], axis=axis)


def fill_columns(col_ref, taps):
    shape = (LANES, LANES)
    lag = lax.broadcasted_iota(jnp.int32, shape, 0) - lax.broadcasted_iota(jnp.int32, shape, 1)
    near = split(pick_taps(lag + RADIUS, taps), 3)
    far = pick_taps(jnp.where(lag > 0, lag + RADIUS - LANES, lag + RADIUS + LANES), taps)
    above = split(jnp.where(lag > 0, far, 0.0), 3)
    below = split(jnp.where(lag > 0, 0.0, far), 3)
    for n, piece in enumerate((0, 1, 2, 0)):
        at = n * 3 * LANES
        for i, pair in enumerate(((near, above), (below, near), (above, below))):
            for j, block in enumerate(pair):
                col_ref[at + i * LANES:at + (i + 1) * LANES, j * LANES:(j + 1) * LANES] = block[piece]


def row_band(out_rows, in_rows, taps):
    shape = (out_rows, 4 * in_rows)
    lane = lax.broadcasted_iota(jnp.int32, shape, 1)
    row = lax.broadcasted_iota(jnp.int32, shape, 0)
    part = jnp.zeros(shape, jnp.int32)
    for n in range(1, 4):
        part = jnp.where(lane >= n * in_rows, n, part)
    return lane - part * in_rows, row, part


def pieces_of(values, part):
    high, mid, low = [p.astype(jnp.float32) for p in split(values, 3)]
    return jnp.where(part == 1, mid, jnp.where(part == 2, low, high)).astype(jnp.bfloat16)


def filter_columns(mid, rim, col):
    rows = mid.shape[0]
    window = jnp.concatenate([mid, rim], axis=1)
    return jnp.dot(spread(window, 1), col, preferred_element_type=jnp.float32)


def rim_tile(left, right, block, parts):
    lane = lax.broadcasted_iota(jnp.int32, left.shape, len(left.shape) - 1)
    first = lane < LANES // 2
    keep = (first & (block < parts - 1)) | (~first & (block > 0))
    return jnp.where(keep, jnp.where(first, right, left), 0.0)


def interior_kernel(offsets, parts, group, alone, place, taps, stack, *rest):
    count = len(offsets)
    outs, brims, rest = rest[:count], rest[count:2 * count], rest[2 * count:]
    if alone:
        halos, rest = rest[:2], rest[2:]
        mid_ref, left_ref, right_ref, halo_sem = rest[:4]
        rest = rest[4:]
    else:
        x_ref, rest = rest[0], rest[1:]
    col_ref, row_ref, in_sem = rest
    per, dates, inner, _ = outs[0].shape
    width = per * LANES
    rows = inner + 2 * EDGE
    cols = width * parts

    def bounds(offset):
        start = (place[0] ^ offset) * width
        places = start, jnp.maximum(start - LANES, 0), jnp.minimum(start + width, cols - LANES)
        return [pl.multiple_of(first, LANES) for first in places]

    def load(g):
        at = pl.ds(g * group, group)
        if not alone:
            return [pltpu.make_async_copy(stack.at[at], x_ref.at[at], in_sem.at[0, g])]
        return [
            pltpu.make_async_copy(stack.at[at, :, pl.ds(first, ref.shape[2])], ref.at[at], in_sem.at[n, g])
            for n, (first, ref) in enumerate(zip(bounds(offsets[0]), (mid_ref, left_ref, right_ref)))
        ]

    def window(at, offset):
        if alone:
            return mid_ref[at], left_ref[at], right_ref[at]
        start, before, after = bounds(offset)
        return x_ref[at, :, pl.ds(start, width)], x_ref[at, :, pl.ds(before, LANES)], x_ref[at, :, pl.ds(after, LANES)]

    steps = dates // group
    for g in range(steps):
        for copy in load(g):
            copy.start()
    copies = []
    if alone:
        copies = [
            pltpu.make_async_copy(stack.at[:, pl.ds(rows - EDGE, EDGE), :], halos[0], halo_sem.at[0]),
            pltpu.make_async_copy(stack.at[:, pl.ds(0, EDGE), :], halos[1], halo_sem.at[1]),
        ]
        for copy in copies:
            copy.start()
    fill_columns(col_ref, taps)
    q, r, part = row_band(inner, rows, taps)
    row_ref[...] = pieces_of(pick_taps(q - r - (EDGE - RADIUS), taps), part)

    def step(g, carry):
        for copy in load(g):
            copy.wait()
        at = pl.ds(g * group, group)
        for n, offset in enumerate(offsets):
            mid, left, right = window(at, offset)
            rim = rim_tile(left, right, place[0] ^ offset, parts)
            across = filter_columns(mid.reshape(group * rows, width), rim.reshape(group * rows, LANES), col_ref[...])
            for t in range(group):
                one = across[t * rows:(t + 1) * rows]
                low = jnp.dot(row_ref[...], spread(one, 0), preferred_element_type=jnp.float32)
                done = mid[t, EDGE:rows - EDGE, :] - low
                for h in range(per):
                    outs[n][h, g * group + t] = done[:, h * LANES:(h + 1) * LANES]
                brims[n][g * group + t] = jnp.concatenate([one[:2 * EDGE], one[rows - 2 * EDGE:]], axis=0)
        return carry

    lax.fori_loop(0, steps, step, 0)
    for copy in copies:
        copy.wait()


def interior(stack, taps, place, offsets, parts, alone):
    dates, rows, cols = stack.shape
    width = cols // parts
    group = min(4, dates)
    inner = rows - 2 * EDGE
    count = len(offsets)
    out_shape = [jax.ShapeDtypeStruct((width // LANES, dates, inner, LANES), jnp.float32)] * count
    out_shape += [jax.ShapeDtypeStruct((dates, 4 * EDGE, width), jnp.float32)] * count
    scratch = [pltpu.VMEM((dates, rows, cols), jnp.float32)]
    if alone:
        out_shape += [jax.ShapeDtypeStruct((dates, EDGE, cols), jnp.float32)] * 2
        scratch = [pltpu.VMEM((dates, rows, span), jnp.float32) for span in (width, LANES, LANES)]
        scratch.append(pltpu.SemaphoreType.DMA((2,)))
    return pl.pallas_call(
        functools.partial(interior_kernel, offsets, parts, group, alone),
        grid_spec=pltpu.PrefetchScalarGridSpec(
            num_scalar_prefetch=2,
            grid=(),
            in_specs=[pl.BlockSpec(memory_space=pltpu.HBM)],
            out_specs=[pl.BlockSpec(memory_space=pltpu.VMEM)] * len(out_shape),
            scratch_shapes=scratch + [
                pltpu.VMEM((12 * LANES, width), jnp.bfloat16),
                pltpu.VMEM((inner, 4 * rows), jnp.bfloat16),
                pltpu.SemaphoreType.DMA((3, dates // group)),
            ],
        ),
        out_shape=out_shape,
        compiler_params=params(60 if alone else 56),
        cost_estimate=cost(60 * count * dates * rows * width, 3 * 4 * count * dates * rows * width),
    )(place, taps, stack)


def edge_kernel(parts, place, taps, stack, up_ref, down_ref, *rest):
    brims, outs = rest[:parts], rest[parts:2 * parts]
    x_ref, col_ref, row_ref, in_sem = rest[2 * parts:]
    dates, _, cols = up_ref.shape
    rows = stack.shape[1]
    width = cols // parts
    span = 6 * EDGE
    loads = [
        pltpu.make_async_copy(stack.at[:, pl.ds(0, EDGE), :], x_ref.at[:, pl.ds(0, EDGE), :], in_sem.at[0]),
        pltpu.make_async_copy(stack.at[:, pl.ds(rows - EDGE, EDGE), :], x_ref.at[:, pl.ds(EDGE, EDGE), :], in_sem.at[1]),
    ]
    for copy in loads:
        copy.start()
    fill_columns(col_ref, taps)
    q, r, part = row_band(2 * EDGE, span, taps)
    own = (q >= span // 2) == (r >= EDGE)
    at = jnp.where(own, (q % (span // 2)) - (r % EDGE) - (EDGE - RADIUS), -1)
    row_ref[...] = pieces_of(pick_taps(at, taps), part)
    for copy in loads:
        copy.wait()
    for k in range(parts):
        block = place[0] ^ k
        start = pl.multiple_of(block * width, LANES)
        before = pl.multiple_of(jnp.maximum(start - LANES, 0), LANES)
        after = pl.multiple_of(jnp.minimum(start + width, cols - LANES), LANES)

        def both(first, span):
            at = pl.ds(first, span)
            return jnp.concatenate([up_ref[:, :, at], down_ref[:, :, at]], axis=1).reshape(dates * 2 * EDGE, span)

        rim = rim_tile(both(before, LANES), both(after, LANES), block, parts)
        across = filter_columns(both(start, width), rim, col_ref[...])
        for t in range(dates):
            one = across[t * 2 * EDGE:(t + 1) * 2 * EDGE]
            one = jnp.concatenate([one[:EDGE], brims[k][t], one[EDGE:]], axis=0)
            low = jnp.dot(row_ref[...], spread(one, 0), preferred_element_type=jnp.float32)
            done = x_ref[t, :, pl.ds(start, width)] - low
            for h in range(width // LANES):
                outs[k][h, t] = done[:, h * LANES:(h + 1) * LANES]


def edges(stack, up, down, brims, taps, place):
    parts = len(brims)
    dates, rows, cols = stack.shape
    width = cols // parts
    resident = pl.BlockSpec(memory_space=pltpu.VMEM)
    return pl.pallas_call(
        functools.partial(edge_kernel, parts),
        grid_spec=pltpu.PrefetchScalarGridSpec(
            num_scalar_prefetch=2,
            grid=(),
            in_specs=[pl.BlockSpec(memory_space=pltpu.HBM)] + [resident] * (2 + parts),
            out_specs=[resident] * parts,
            scratch_shapes=[
                pltpu.VMEM((dates, 2 * EDGE, cols), jnp.float32),
                pltpu.VMEM((12 * LANES, width), jnp.bfloat16),
                pltpu.VMEM((2 * EDGE, 24 * EDGE), jnp.bfloat16),
                pltpu.SemaphoreType.DMA((2,)),
            ],
        ),
        out_shape=[jax.ShapeDtypeStruct((width // LANES, dates, 2 * EDGE, LANES), jnp.float32)] * parts,
        compiler_params=params(52),
        cost_estimate=cost(60 * dates * 32 * cols, 4 * dates * 64 * cols),
    )(place, taps, stack, up, down, *brims)


def temporal_kernel(parts, with_base, first_tile, tile_step, place, taps, *rest):
    pieces = rest[:parts]
    out, z_ref, f_ref, out_ref, out_sem = rest[parts + with_base:]
    count, total, _, _ = out_ref.shape
    per = pieces[0].shape[0]
    local = total // parts
    pad = REACH * DILATION
    step = 8
    none = jnp.zeros((REACH, EDGE, LANES), jnp.float32)
    wide = jnp.zeros((pad, EDGE, LANES), jnp.float32)
    for h in range(per):
        z_ref[h, 0:REACH] = none
        z_ref[h, REACH + total:REACH + total + REACH] = none
        f_ref[h, 0:pad] = wide
        f_ref[h, pad + total:pad + total + pad] = wide
    own = 1.0 - taps[0, REACH]
    own_wide = 1.0 - taps[1, REACH]
    others = [k for k in range(2 * REACH + 1) if k != REACH]

    def store(n):
        tile = first_tile + n * tile_step
        rows = pl.ds(pl.multiple_of(tile * EDGE, EDGE), EDGE)
        return pltpu.make_async_copy(out_ref.at[n], out.at[:, rows, :], out_sem.at[n])

    def one(n, carry):
        rows = pl.ds(pl.multiple_of(n * EDGE, EDGE), EDGE)
        for h in range(per):
            for k in range(parts):
                z_ref[h, pl.ds(REACH + (place[0] ^ k) * local, local)] = pieces[k][h, :, rows, :]
            for t in range(0, total, step):
                z = z_ref[h, t:t + step + 2 * REACH]
                kept = own * z[REACH:REACH + step]
                for k in others:
                    kept = kept - taps[0, k] * z[k:k + step]
                f_ref[h, pad + t:pad + t + step] = kept
            for t in range(0, total, step):
                kept = own_wide * f_ref[h, pad + t:pad + t + step]
                for k in others:
                    kept = kept - taps[1, k] * f_ref[h, t + k * DILATION:t + k * DILATION + step]
                out_ref[n, t:t + step, :, h * LANES:(h + 1) * LANES] = kept
        store(n).start()
        return carry

    lax.fori_loop(0, count, one, 0)
    for n in range(count):
        store(n).wait()


def temporal(pieces, base, taps, place, first_tile, tile_step, rows):
    parts = len(pieces)
    per, local, here, _ = pieces[0].shape
    total = local * parts
    extra = [] if base is None else [base]
    count = here // EDGE
    width = per * LANES
    return pl.pallas_call(
        functools.partial(temporal_kernel, parts, len(extra), first_tile, tile_step),
        grid_spec=pltpu.PrefetchScalarGridSpec(
            num_scalar_prefetch=2,
            grid=(),
            in_specs=[pl.BlockSpec(memory_space=pltpu.VMEM)] * parts + [pl.BlockSpec(memory_space=pltpu.HBM)] * len(extra),
            out_specs=pl.BlockSpec(memory_space=pltpu.HBM),
            scratch_shapes=[
                pltpu.VMEM((per, total + 2 * REACH, EDGE, LANES), jnp.float32),
                pltpu.VMEM((per, total + 2 * REACH * DILATION, EDGE, LANES), jnp.float32),
                pltpu.VMEM((count, total, EDGE, width), jnp.float32),
                pltpu.SemaphoreType.DMA((count,)),
            ],
        ),
        out_shape=jax.ShapeDtypeStruct((total, rows, width), jnp.float32),
        input_output_aliases={} if base is None else {2 + parts: 0},
        compiler_params=params(24),
        cost_estimate=cost(20 * total * EDGE * count * width, 8 * total * EDGE * count * width),
    )(place, taps, *pieces, *extra)


def footprint_kernel(parts, feet, place, *rest):
    meta, vectors, rest = rest[:parts], rest[parts:2 * parts], rest[2 * parts:]
    inner, rim = rest[:parts], rest[parts:2 * parts]
    out_ref = rest[2 * parts]
    per, dates, rows, _ = inner[0].shape
    owners = out_ref.shape[0]
    lane = lax.broadcasted_iota(jnp.int32, (dates, LANES), 1)
    both = [jnp.concatenate([ref[n:n + 1, :] for ref in vectors], axis=1) for n in range(1, 4)]
    index = lax.broadcasted_iota(jnp.int32, both[0].shape, 1)
    source = (index // feet) ^ place[0]
    named = lax.broadcasted_iota(jnp.int32, (owners, index.shape[1]), 0) == both[1]
    places = []
    for block in range(parts):
        for slot in range(PAIR_CAP):
            hit = named & (source == block) & (both[2] == slot)
            places.append(jnp.where(hit, 1.0, 0.0).astype(jnp.bfloat16))
    places = jnp.concatenate(places, axis=0)
    tiles = []
    for first in range(0, parts * feet, LANES):
        total = jnp.zeros((dates, LANES), jnp.float32)
        for k in range(first // feet, -(-(first + LANES) // feet)):
            middle, ends = [ref.reshape(per * dates * ref.shape[2], LANES) for ref in (inner[k], rim[k])]

            def take(f, total):
                row, tile = meta[k][0, f] & 0xFFFF, meta[k][0, f] >> 16
                in_middle = (row >= EDGE) & (row < EDGE + rows)
                end_row = jnp.where(row < EDGE, row, jnp.clip(row - rows, 0, 2 * EDGE - 1))
                pixels = jnp.where(
                    in_middle,
                    middle[pl.ds(tile * dates * rows + jnp.clip(row - EDGE, 0, rows - 1), dates, stride=rows), :],
                    ends[pl.ds(tile * dates * 2 * EDGE + end_row, dates, stride=2 * EDGE), :])
                one = jnp.sum(jnp.where(lane < meta[k][1, f], pixels, 0.0), axis=1, keepdims=True)
                return jnp.where(lane == k * feet + f - first, one, total)

            total = lax.fori_loop(max(first - k * feet, 0), min(feet, first + LANES - k * feet), take, total, unroll=16)
        tiles.append(total)
    counts = jnp.broadcast_to(both[0].astype(jnp.float32), (dates, index.shape[1]))
    sums = jnp.concatenate([jnp.concatenate(tiles, axis=1), counts], axis=0)
    held = jnp.zeros((places.shape[0], 2 * dates), jnp.float32)
    for piece in split(sums, 3):
        held = held + lax.dot_general(places, piece, (((1,), (1,)), ((), ())), preferred_element_type=jnp.float32)
    for n in range(parts * PAIR_CAP):
        at = pl.ds(n * dates, dates)
        out_ref[:, 0, at] = held[n * owners:(n + 1) * owners, :dates]
        out_ref[:, 1, at] = held[n * owners:(n + 1) * owners, dates:]


def footprints(inner, rim, meta, place, owners):
    parts = len(inner)
    per, dates, inner_rows, _ = inner[0].shape
    feet = meta[0].shape[1]
    message = parts * PAIR_CAP * dates
    return pl.pallas_call(
        functools.partial(footprint_kernel, parts, feet),
        grid_spec=pltpu.PrefetchScalarGridSpec(
            num_scalar_prefetch=1 + parts,
            grid=(),
            in_specs=[pl.BlockSpec(memory_space=pltpu.VMEM)] * (3 * parts),
            out_specs=pl.BlockSpec(memory_space=pltpu.VMEM),
        ),
        out_shape=jax.ShapeDtypeStruct((owners, 2, message), jnp.float32),
        compiler_params=params(24),
        cost_estimate=cost(4 * owners * message * LANES, 8 * dates * inner_rows * per * LANES * parts),
    )(place, *meta, *meta, *inner, *rim)


def owner_kernel(parts, strips, taps, got_ref, anomaly_ref, series_ref):
    owners = parts * strips
    slots = owners * PAIR_CAP
    dates = got_ref.shape[2] // PAIR_CAP
    local = dates // parts
    sums, held = got_ref[:, 0, :], got_ref[:, 1, :]
    rows, weights = [], []
    for block in range(parts):
        for slot in range(PAIR_CAP):
            at = (block * PAIR_CAP + slot) * local
            rows.append(jnp.concatenate(
                [sums[e * strips:(e + 1) * strips, at:at + local] for e in range(parts)], axis=1))
            weights.append(held[0:strips, at:at + 1])
    sums = jnp.concatenate(rows, axis=0)
    weight = jnp.concatenate(weights, axis=0)
    shape = (dates, dates)
    lag = lax.broadcasted_iota(jnp.int32, shape, 0) - lax.broadcasted_iota(jnp.int32, shape, 1)
    for level, spacing in ((0, 1), (1, DILATION)):
        filt = jnp.where(lag == 0, 1.0, 0.0)
        for k in range(2 * REACH + 1):
            filt = filt - jnp.where(lag == (k - REACH) * spacing, taps[level, k], 0.0)
        sums = jnp.dot(sums, filt, precision=HIGHEST, preferred_element_type=jnp.float32)
    mean = sums / jnp.where(weight > 0, weight, 1.0)
    asset = jnp.sum(weight * mean, axis=0, keepdims=True) / jnp.sum(weight, axis=0, keepdims=True)
    odd = jnp.where(weight > 0, mean - asset, 0.0)
    series_ref[...] = asset
    shape = (slots, slots)
    to = lax.broadcasted_iota(jnp.int32, shape, 0)
    source = lax.broadcasted_iota(jnp.int32, shape, 1)
    block, rest = source // (PAIR_CAP * strips), source % (PAIR_CAP * strips)
    place_of = block * (PAIR_CAP * strips) + (rest % strips) * PAIR_CAP + rest // strips
    order = jnp.where(to == place_of, 1.0, 0.0)
    anomaly_ref[0] = jnp.dot(order, odd, precision=HIGHEST, preferred_element_type=jnp.float32)


def owner_series(got, taps, parts, strips):
    owners = parts * strips
    dates = got.shape[2] // PAIR_CAP
    slots = owners * PAIR_CAP
    return pl.pallas_call(
        functools.partial(owner_kernel, parts, strips),
        grid_spec=pltpu.PrefetchScalarGridSpec(
            num_scalar_prefetch=1,
            grid=(),
            in_specs=[pl.BlockSpec(memory_space=pltpu.VMEM)],
            out_specs=[pl.BlockSpec(memory_space=pltpu.VMEM)] * 2,
        ),
        out_shape=[
            jax.ShapeDtypeStruct((1, slots, dates), jnp.float32),
            jax.ShapeDtypeStruct((1, dates), jnp.float32),
        ],
        compiler_params=params(24),
        cost_estimate=cost(4 * slots * dates * dates, 16 * slots * dates),
    )(taps, got)


def spread_meta(meta, offset, swap):
    known = sorted(meta)
    got = swap(jnp.concatenate([meta[k] for k in known], axis=1), offset)
    width = meta[0].shape[1]
    return meta | {k ^ offset: got[:, n * width:(n + 1) * width] for n, k in enumerate(known)}


def shards(stack, spatial_taps, temporal_taps, foot_tile, foot_row, foot_count, foot_owner):
    parts, strips = lax.axis_size("date"), lax.axis_size("strip")
    place = lax.axis_index("date").astype(jnp.int32)[None]
    dates, rows, cols = stack.shape
    feet = foot_row.shape[0]
    owner = foot_owner[:, 0]
    position = jnp.arange(feet, dtype=jnp.int32)
    earlier = (owner[:, None] == owner[None, :]) & (position[None, :] < position[:, None])
    slot = jnp.sum(earlier.astype(jnp.int32), axis=1)
    own = jnp.stack([(foot_tile << 16) + foot_row, foot_count, owner, slot])

    def swap(value, offset):
        return lax.ppermute(value, "date", [(i, i ^ offset) for i in range(parts)])

    far = list(range(2, parts)) if parts > 2 else [1]
    first, rest = far[0], far[1:] + ([1, 0] if parts > 2 else [0])
    order = [first] + [k for k in rest if k]
    inner, brim, far_inner = {}, {}, {}
    inner[first], brim[first], last_rows, first_rows = interior(stack, spatial_taps, place, (first,), parts, True)
    far_inner[first] = swap(inner[first], first)
    up = lax.ppermute(last_rows, "strip", [(i, i + 1) for i in range(strips - 1)])
    down = lax.ppermute(first_rows, "strip", [(i + 1, i) for i in range(strips - 1)])
    meta = {0: own}
    for bit in [b for b in range(parts.bit_length() - 2, 0, -1)]:
        meta = spread_meta(meta, 1 << bit, swap)
    made = interior(stack, spatial_taps, place, tuple(rest), parts, False)
    for n, offset in enumerate(rest):
        inner[offset], brim[offset] = made[n], made[len(rest) + n]
    for offset in order[1:-1]:
        far_inner[offset] = swap(inner[offset], offset)
    known = sorted(meta)
    *held, inner[1] = lax.optimization_barrier((*[meta[k] for k in known], inner[1]))
    meta = spread_meta(dict(zip(known, held)), 1, swap)
    far_inner[1] = swap(inner[1], 1)
    meta = [meta[k] for k in range(parts)]
    rim = edges(stack, up, down, [brim[k] for k in range(parts)], spatial_taps, place)
    far_rim = {offset: swap(rim[offset], offset) for offset in order}
    sums = footprints([inner[k] for k in range(parts)], rim, meta, place, parts * strips)
    got = lax.all_to_all(sums, ("date", "strip"), split_axis=0, concat_axis=0, tiled=True)
    last = rows // EDGE - 1
    residual = temporal(
        [inner[0]] + [far_inner[k] for k in range(1, parts)], None, temporal_taps, place, 1, 1, rows)
    got, residual = lax.optimization_barrier((got, residual))
    anomaly, series = owner_series(got, temporal_taps, parts, strips)
    residual = temporal(
        [rim[0]] + [far_rim[k] for k in range(1, parts)], residual, temporal_taps, place, 0, last, rows)
    return residual, anomaly, series


def solution(mesh):
    placed = (
        P("date", "strip", None),
        P(),
        P(),
        P(("date", "strip")),
        P(("date", "strip")),
        P(("date", "strip")),
        P(("date", "strip"), None),
    )
    return jax.shard_map(
        shards,
        mesh=mesh,
        in_specs=placed,
        out_specs=(
            P(None, "strip", "date"),
            P(("date", "strip"), None, None),
            P(("date", "strip"), None),
        ),
        check_vma=False,
    )
```

```python
import functools

import jax
import jax.numpy as jnp
from jax import lax
from jax.experimental import pallas as pl
from jax.experimental.pallas import tpu as pltpu
from jax.sharding import PartitionSpec as P

TILE = 128
RADIUS = 6
REACH = 2
DILATION = 8
PAIR_CAP = 2
LANES = 128
EDGE = 8
HIGHEST = lax.Precision.HIGHEST


def params(mebibytes):
    return pltpu.CompilerParams(vmem_limit_bytes=mebibytes * 1024 * 1024)


def cost(flops, bytes_accessed):
    return pl.CostEstimate(flops=flops, bytes_accessed=bytes_accessed, transcendentals=0)


def pick_taps(at, taps):
    count = taps.shape[0]
    total = taps[0]
    for k in range(1, count):
        total = total + taps[k]
    out = jnp.zeros(at.shape, jnp.float32)
    for k in range(count):
        out = jnp.where(at == k, taps[k], out)
    return out / jnp.full(at.shape, total, jnp.float32)


def split(value, count):
    out = []
    for _ in range(count):
        piece = value.astype(jnp.bfloat16)
        out.append(piece)
        value = value - piece.astype(jnp.float32)
    return out


def spread(value, axis):
    high, mid = split(value, 2)
    return jnp.concatenate([high, high, high, mid], axis=axis)


def fill_columns(col_ref, taps):
    shape = (LANES, LANES)
    lag = lax.broadcasted_iota(jnp.int32, shape, 0) - lax.broadcasted_iota(jnp.int32, shape, 1)
    near = split(pick_taps(lag + RADIUS, taps), 3)
    far = pick_taps(jnp.where(lag > 0, lag + RADIUS - LANES, lag + RADIUS + LANES), taps)
    above = split(jnp.where(lag > 0, far, 0.0), 3)
    below = split(jnp.where(lag > 0, 0.0, far), 3)
    for n, piece in enumerate((0, 1, 2, 0)):
        at = n * 3 * LANES
        for i, pair in enumerate(((near, above), (below, near), (above, below))):
            for j, block in enumerate(pair):
                col_ref[at + i * LANES:at + (i + 1) * LANES, j * LANES:(j + 1) * LANES] = block[piece]


def row_band(out_rows, in_rows, taps):
    shape = (out_rows, 4 * in_rows)
    lane = lax.broadcasted_iota(jnp.int32, shape, 1)
    row = lax.broadcasted_iota(jnp.int32, shape, 0)
    part = jnp.zeros(shape, jnp.int32)
    for n in range(1, 4):
        part = jnp.where(lane >= n * in_rows, n, part)
    return lane - part * in_rows, row, part


def pieces_of(values, part):
    high, mid, low = [p.astype(jnp.float32) for p in split(values, 3)]
    return jnp.where(part == 1, mid, jnp.where(part == 2, low, high)).astype(jnp.bfloat16)


def filter_columns(mid, rim, col):
    rows = mid.shape[0]
    window = jnp.concatenate([mid, rim], axis=1)
    return jnp.dot(spread(window, 1), col, preferred_element_type=jnp.float32)


def rim_tile(left, right, block, parts):
    lane = lax.broadcasted_iota(jnp.int32, left.shape, len(left.shape) - 1)
    first = lane < LANES // 2
    keep = (first & (block < parts - 1)) | (~first & (block > 0))
    return jnp.where(keep, jnp.where(first, right, left), 0.0)


def interior_kernel(offsets, parts, group, alone, place, taps, stack, *rest):
    count = len(offsets)
    outs, brims, rest = rest[:count], rest[count:2 * count], rest[2 * count:]
    if alone:
        halos, rest = rest[:2], rest[2:]
        mid_ref, left_ref, right_ref, halo_sem = rest[:4]
        rest = rest[4:]
    else:
        x_ref, rest = rest[0], rest[1:]
    col_ref, row_ref, in_sem = rest
    per, dates, inner, _ = outs[0].shape
    width = per * LANES
    rows = inner + 2 * EDGE
    cols = width * parts

    def bounds(offset):
        start = (place[0] ^ offset) * width
        places = start, jnp.maximum(start - LANES, 0), jnp.minimum(start + width, cols - LANES)
        return [pl.multiple_of(first, LANES) for first in places]

    def load(g):
        at = pl.ds(g * group, group)
        if not alone:
            return [pltpu.make_async_copy(stack.at[at], x_ref.at[at], in_sem.at[0, g])]
        return [
            pltpu.make_async_copy(stack.at[at, :, pl.ds(first, ref.shape[2])], ref.at[at], in_sem.at[n, g])
            for n, (first, ref) in enumerate(zip(bounds(offsets[0]), (mid_ref, left_ref, right_ref)))
        ]

    def window(at, offset):
        if alone:
            return mid_ref[at], left_ref[at], right_ref[at]
        start, before, after = bounds(offset)
        return x_ref[at, :, pl.ds(start, width)], x_ref[at, :, pl.ds(before, LANES)], x_ref[at, :, pl.ds(after, LANES)]

    steps = dates // group
    for g in range(steps):
        for copy in load(g):
            copy.start()
    copies = []
    if alone:
        copies = [
            pltpu.make_async_copy(stack.at[:, pl.ds(rows - EDGE, EDGE), :], halos[0], halo_sem.at[0]),
            pltpu.make_async_copy(stack.at[:, pl.ds(0, EDGE), :], halos[1], halo_sem.at[1]),
        ]
        for copy in copies:
            copy.start()
    fill_columns(col_ref, taps)
    q, r, part = row_band(inner, rows, taps)
    row_ref[...] = pieces_of(pick_taps(q - r - (EDGE - RADIUS), taps), part)

    def step(g, carry):
        for copy in load(g):
            copy.wait()
        at = pl.ds(g * group, group)
        for n, offset in enumerate(offsets):
            mid, left, right = window(at, offset)
            rim = rim_tile(left, right, place[0] ^ offset, parts)
            across = filter_columns(mid.reshape(group * rows, width), rim.reshape(group * rows, LANES), col_ref[...])
            for t in range(group):
                one = across[t * rows:(t + 1) * rows]
                low = jnp.dot(row_ref[...], spread(one, 0), preferred_element_type=jnp.float32)
                done = mid[t, EDGE:rows - EDGE, :] - low
                for h in range(per):
                    outs[n][h, g * group + t] = done[:, h * LANES:(h + 1) * LANES]
                brims[n][g * group + t] = jnp.concatenate([one[:2 * EDGE], one[rows - 2 * EDGE:]], axis=0)
        return carry

    lax.fori_loop(0, steps, step, 0)
    for copy in copies:
        copy.wait()


def interior(stack, taps, place, offsets, parts, alone):
    dates, rows, cols = stack.shape
    width = cols // parts
    group = min(8, dates)
    inner = rows - 2 * EDGE
    count = len(offsets)
    out_shape = [jax.ShapeDtypeStruct((width // LANES, dates, inner, LANES), jnp.float32)] * count
    out_shape += [jax.ShapeDtypeStruct((dates, 4 * EDGE, width), jnp.float32)] * count
    scratch = [pltpu.VMEM((dates, rows, cols), jnp.float32)]
    if alone:
        out_shape += [jax.ShapeDtypeStruct((dates, EDGE, cols), jnp.float32)] * 2
        scratch = [pltpu.VMEM((dates, rows, span), jnp.float32) for span in (width, LANES, LANES)]
        scratch.append(pltpu.SemaphoreType.DMA((2,)))
    return pl.pallas_call(
        functools.partial(interior_kernel, offsets, parts, group, alone),
        grid_spec=pltpu.PrefetchScalarGridSpec(
            num_scalar_prefetch=2,
            grid=(),
            in_specs=[pl.BlockSpec(memory_space=pltpu.HBM)],
            out_specs=[pl.BlockSpec(memory_space=pltpu.VMEM)] * len(out_shape),
            scratch_shapes=scratch + [
                pltpu.VMEM((12 * LANES, width), jnp.bfloat16),
                pltpu.VMEM((inner, 4 * rows), jnp.bfloat16),
                pltpu.SemaphoreType.DMA((3, dates // group)),
            ],
        ),
        out_shape=out_shape,
        compiler_params=params(60 if alone else 56),
        cost_estimate=cost(60 * count * dates * rows * width, 3 * 4 * count * dates * rows * width),
    )(place, taps, stack)


def edge_kernel(parts, place, taps, stack, up_ref, down_ref, *rest):
    brims, outs = rest[:parts], rest[parts:2 * parts]
    x_ref, col_ref, row_ref, in_sem = rest[2 * parts:]
    dates, _, cols = up_ref.shape
    rows = stack.shape[1]
    width = cols // parts
    span = 6 * EDGE
    loads = [
        pltpu.make_async_copy(stack.at[:, pl.ds(0, EDGE), :], x_ref.at[:, pl.ds(0, EDGE), :], in_sem.at[0]),
        pltpu.make_async_copy(stack.at[:, pl.ds(rows - EDGE, EDGE), :], x_ref.at[:, pl.ds(EDGE, EDGE), :], in_sem.at[1]),
    ]
    for copy in loads:
        copy.start()
    fill_columns(col_ref, taps)
    q, r, part = row_band(2 * EDGE, span, taps)
    own = (q >= span // 2) == (r >= EDGE)
    at = jnp.where(own, (q % (span // 2)) - (r % EDGE) - (EDGE - RADIUS), -1)
    row_ref[...] = pieces_of(pick_taps(at, taps), part)
    for copy in loads:
        copy.wait()
    for k in range(parts):
        block = place[0] ^ k
        start = pl.multiple_of(block * width, LANES)
        before = pl.multiple_of(jnp.maximum(start - LANES, 0), LANES)
        after = pl.multiple_of(jnp.minimum(start + width, cols - LANES), LANES)

        def both(first, span):
            at = pl.ds(first, span)
            return jnp.concatenate([up_ref[:, :, at], down_ref[:, :, at]], axis=1).reshape(dates * 2 * EDGE, span)

        rim = rim_tile(both(before, LANES), both(after, LANES), block, parts)
        across = filter_columns(both(start, width), rim, col_ref[...])
        for t in range(dates):
            one = across[t * 2 * EDGE:(t + 1) * 2 * EDGE]
            one = jnp.concatenate([one[:EDGE], brims[k][t], one[EDGE:]], axis=0)
            low = jnp.dot(row_ref[...], spread(one, 0), preferred_element_type=jnp.float32)
            done = x_ref[t, :, pl.ds(start, width)] - low
            for h in range(width // LANES):
                outs[k][h, t] = done[:, h * LANES:(h + 1) * LANES]


def edges(stack, up, down, brims, taps, place):
    parts = len(brims)
    dates, rows, cols = stack.shape
    width = cols // parts
    resident = pl.BlockSpec(memory_space=pltpu.VMEM)
    return pl.pallas_call(
        functools.partial(edge_kernel, parts),
        grid_spec=pltpu.PrefetchScalarGridSpec(
            num_scalar_prefetch=2,
            grid=(),
            in_specs=[pl.BlockSpec(memory_space=pltpu.HBM)] + [resident] * (2 + parts),
            out_specs=[resident] * parts,
            scratch_shapes=[
                pltpu.VMEM((dates, 2 * EDGE, cols), jnp.float32),
                pltpu.VMEM((12 * LANES, width), jnp.bfloat16),
                pltpu.VMEM((2 * EDGE, 24 * EDGE), jnp.bfloat16),
                pltpu.SemaphoreType.DMA((2,)),
            ],
        ),
        out_shape=[jax.ShapeDtypeStruct((width // LANES, dates, 2 * EDGE, LANES), jnp.float32)] * parts,
        compiler_params=params(52),
        cost_estimate=cost(60 * dates * 32 * cols, 4 * dates * 64 * cols),
    )(place, taps, stack, up, down, *brims)


def temporal_kernel(parts, with_base, first_tile, tile_step, place, taps, *rest):
    pieces = rest[:parts]
    out, z_ref, f_ref, out_ref, out_sem = rest[parts + with_base:]
    count, total, _, _ = out_ref.shape
    per = pieces[0].shape[0]
    local = total // parts
    pad = REACH * DILATION
    step = 8
    none = jnp.zeros((REACH, EDGE, LANES), jnp.float32)
    wide = jnp.zeros((pad, EDGE, LANES), jnp.float32)
    for h in range(per):
        z_ref[h, 0:REACH] = none
        z_ref[h, REACH + total:REACH + total + REACH] = none
        f_ref[h, 0:pad] = wide
        f_ref[h, pad + total:pad + total + pad] = wide
    own = 1.0 - taps[0, REACH]
    own_wide = 1.0 - taps[1, REACH]
    others = [k for k in range(2 * REACH + 1) if k != REACH]

    def store(n):
        tile = first_tile + n * tile_step
        rows = pl.ds(pl.multiple_of(tile * EDGE, EDGE), EDGE)
        return pltpu.make_async_copy(out_ref.at[n], out.at[:, rows, :], out_sem.at[n])

    def one(n, carry):
        rows = pl.ds(pl.multiple_of(n * EDGE, EDGE), EDGE)
        for h in range(per):
            for k in range(parts):
                z_ref[h, pl.ds(REACH + (place[0] ^ k) * local, local)] = pieces[k][h, :, rows, :]
            for t in range(0, total, step):
                z = z_ref[h, t:t + step + 2 * REACH]
                kept = own * z[REACH:REACH + step]
                for k in others:
                    kept = kept - taps[0, k] * z[k:k + step]
                f_ref[h, pad + t:pad + t + step] = kept
            for t in range(0, total, step):
                kept = own_wide * f_ref[h, pad + t:pad + t + step]
                for k in others:
                    kept = kept - taps[1, k] * f_ref[h, t + k * DILATION:t + k * DILATION + step]
                out_ref[n, t:t + step, :, h * LANES:(h + 1) * LANES] = kept
        store(n).start()
        return carry

    lax.fori_loop(0, count, one, 0)
    for n in range(count):
        store(n).wait()


def temporal(pieces, base, taps, place, first_tile, tile_step, rows):
    parts = len(pieces)
    per, local, here, _ = pieces[0].shape
    total = local * parts
    extra = [] if base is None else [base]
    count = here // EDGE
    width = per * LANES
    return pl.pallas_call(
        functools.partial(temporal_kernel, parts, len(extra), first_tile, tile_step),
        grid_spec=pltpu.PrefetchScalarGridSpec(
            num_scalar_prefetch=2,
            grid=(),
            in_specs=[pl.BlockSpec(memory_space=pltpu.VMEM)] * parts + [pl.BlockSpec(memory_space=pltpu.HBM)] * len(extra),
            out_specs=pl.BlockSpec(memory_space=pltpu.HBM),
            scratch_shapes=[
                pltpu.VMEM((per, total + 2 * REACH, EDGE, LANES), jnp.float32),
                pltpu.VMEM((per, total + 2 * REACH * DILATION, EDGE, LANES), jnp.float32),
                pltpu.VMEM((count, total, EDGE, width), jnp.float32),
                pltpu.SemaphoreType.DMA((count,)),
            ],
        ),
        out_shape=jax.ShapeDtypeStruct((total, rows, width), jnp.float32),
        input_output_aliases={} if base is None else {2 + parts: 0},
        compiler_params=params(24),
        cost_estimate=cost(20 * total * EDGE * count * width, 8 * total * EDGE * count * width),
    )(place, taps, *pieces, *extra)


def footprint_kernel(parts, feet, place, *rest):
    meta, vectors, rest = rest[:parts], rest[parts:2 * parts], rest[2 * parts:]
    inner, rim = rest[:parts], rest[parts:2 * parts]
    out_ref = rest[2 * parts]
    per, dates, rows, _ = inner[0].shape
    owners = out_ref.shape[0]
    lane = lax.broadcasted_iota(jnp.int32, (dates, LANES), 1)
    both = [jnp.concatenate([ref[n:n + 1, :] for ref in vectors], axis=1) for n in range(1, 4)]
    index = lax.broadcasted_iota(jnp.int32, both[0].shape, 1)
    source = (index // feet) ^ place[0]
    named = lax.broadcasted_iota(jnp.int32, (owners, index.shape[1]), 0) == both[1]
    places = []
    for block in range(parts):
        for slot in range(PAIR_CAP):
            hit = named & (source == block) & (both[2] == slot)
            places.append(jnp.where(hit, 1.0, 0.0).astype(jnp.bfloat16))
    places = jnp.concatenate(places, axis=0)
    tiles = []
    for first in range(0, parts * feet, LANES):
        total = jnp.zeros((dates, LANES), jnp.float32)
        for k in range(first // feet, -(-(first + LANES) // feet)):
            middle, ends = [ref.reshape(per * dates * ref.shape[2], LANES) for ref in (inner[k], rim[k])]

            def take(f, total):
                row, tile = meta[k][0, f] & 0xFFFF, meta[k][0, f] >> 16
                in_middle = (row >= EDGE) & (row < EDGE + rows)
                end_row = jnp.where(row < EDGE, row, jnp.clip(row - rows, 0, 2 * EDGE - 1))
                pixels = jnp.where(
                    in_middle,
                    middle[pl.ds(tile * dates * rows + jnp.clip(row - EDGE, 0, rows - 1), dates, stride=rows), :],
                    ends[pl.ds(tile * dates * 2 * EDGE + end_row, dates, stride=2 * EDGE), :])
                one = jnp.sum(jnp.where(lane < meta[k][1, f], pixels, 0.0), axis=1, keepdims=True)
                return jnp.where(lane == k * feet + f - first, one, total)

            total = lax.fori_loop(max(first - k * feet, 0), min(feet, first + LANES - k * feet), take, total, unroll=16)
        tiles.append(total)
    counts = jnp.broadcast_to(both[0].astype(jnp.float32), (dates, index.shape[1]))
    sums = jnp.concatenate([jnp.concatenate(tiles, axis=1), counts], axis=0)
    held = jnp.zeros((places.shape[0], 2 * dates), jnp.float32)
    for piece in split(sums, 3):
        held = held + lax.dot_general(places, piece, (((1,), (1,)), ((), ())), preferred_element_type=jnp.float32)
    for n in range(parts * PAIR_CAP):
        at = pl.ds(n * dates, dates)
        out_ref[:, 0, at] = held[n * owners:(n + 1) * owners, :dates]
        out_ref[:, 1, at] = held[n * owners:(n + 1) * owners, dates:]


def footprints(inner, rim, meta, place, owners):
    parts = len(inner)
    per, dates, inner_rows, _ = inner[0].shape
    feet = meta[0].shape[1]
    message = parts * PAIR_CAP * dates
    return pl.pallas_call(
        functools.partial(footprint_kernel, parts, feet),
        grid_spec=pltpu.PrefetchScalarGridSpec(
            num_scalar_prefetch=1 + parts,
            grid=(),
            in_specs=[pl.BlockSpec(memory_space=pltpu.VMEM)] * (3 * parts),
            out_specs=pl.BlockSpec(memory_space=pltpu.VMEM),
        ),
        out_shape=jax.ShapeDtypeStruct((owners, 2, message), jnp.float32),
        compiler_params=params(24),
        cost_estimate=cost(4 * owners * message * LANES, 8 * dates * inner_rows * per * LANES * parts),
    )(place, *meta, *meta, *inner, *rim)


def owner_kernel(parts, strips, taps, got_ref, anomaly_ref, series_ref):
    owners = parts * strips
    slots = owners * PAIR_CAP
    dates = got_ref.shape[2] // PAIR_CAP
    local = dates // parts
    sums, held = got_ref[:, 0, :], got_ref[:, 1, :]
    rows, weights = [], []
    for block in range(parts):
        for slot in range(PAIR_CAP):
            at = (block * PAIR_CAP + slot) * local
            rows.append(jnp.concatenate(
                [sums[e * strips:(e + 1) * strips, at:at + local] for e in range(parts)], axis=1))
            weights.append(held[0:strips, at:at + 1])
    sums = jnp.concatenate(rows, axis=0)
    weight = jnp.concatenate(weights, axis=0)
    shape = (dates, dates)
    lag = lax.broadcasted_iota(jnp.int32, shape, 0) - lax.broadcasted_iota(jnp.int32, shape, 1)
    for level, spacing in ((0, 1), (1, DILATION)):
        filt = jnp.where(lag == 0, 1.0, 0.0)
        for k in range(2 * REACH + 1):
            filt = filt - jnp.where(lag == (k - REACH) * spacing, taps[level, k], 0.0)
        sums = jnp.dot(sums, filt, precision=HIGHEST, preferred_element_type=jnp.float32)
    mean = sums / jnp.where(weight > 0, weight, 1.0)
    asset = jnp.sum(weight * mean, axis=0, keepdims=True) / jnp.sum(weight, axis=0, keepdims=True)
    odd = jnp.where(weight > 0, mean - asset, 0.0)
    series_ref[...] = asset
    shape = (slots, slots)
    to = lax.broadcasted_iota(jnp.int32, shape, 0)
    source = lax.broadcasted_iota(jnp.int32, shape, 1)
    block, rest = source // (PAIR_CAP * strips), source % (PAIR_CAP * strips)
    place_of = block * (PAIR_CAP * strips) + (rest % strips) * PAIR_CAP + rest // strips
    order = jnp.where(to == place_of, 1.0, 0.0)
    anomaly_ref[0] = jnp.dot(order, odd, precision=HIGHEST, preferred_element_type=jnp.float32)


def owner_series(got, taps, parts, strips):
    owners = parts * strips
    dates = got.shape[2] // PAIR_CAP
    slots = owners * PAIR_CAP
    return pl.pallas_call(
        functools.partial(owner_kernel, parts, strips),
        grid_spec=pltpu.PrefetchScalarGridSpec(
            num_scalar_prefetch=1,
            grid=(),
            in_specs=[pl.BlockSpec(memory_space=pltpu.VMEM)],
            out_specs=[pl.BlockSpec(memory_space=pltpu.VMEM)] * 2,
        ),
        out_shape=[
            jax.ShapeDtypeStruct((1, slots, dates), jnp.float32),
            jax.ShapeDtypeStruct((1, dates), jnp.float32),
        ],
        compiler_params=params(24),
        cost_estimate=cost(4 * slots * dates * dates, 16 * slots * dates),
    )(taps, got)


def spread_meta(meta, offset, swap):
    known = sorted(meta)
    got = swap(jnp.concatenate([meta[k] for k in known], axis=1), offset)
    width = meta[0].shape[1]
    return meta | {k ^ offset: got[:, n * width:(n + 1) * width] for n, k in enumerate(known)}


def shards(stack, spatial_taps, temporal_taps, foot_tile, foot_row, foot_count, foot_owner):
    parts, strips = lax.axis_size("date"), lax.axis_size("strip")
    place = lax.axis_index("date").astype(jnp.int32)[None]
    dates, rows, cols = stack.shape
    feet = foot_row.shape[0]
    owner = foot_owner[:, 0]
    position = jnp.arange(feet, dtype=jnp.int32)
    earlier = (owner[:, None] == owner[None, :]) & (position[None, :] < position[:, None])
    slot = jnp.sum(earlier.astype(jnp.int32), axis=1)
    own = jnp.stack([(foot_tile << 16) + foot_row, foot_count, owner, slot])

    def swap(value, offset):
        return lax.ppermute(value, "date", [(i, i ^ offset) for i in range(parts)])

    far = list(range(2, parts)) if parts > 2 else [1]
    first, rest = far[0], far[1:] + ([1, 0] if parts > 2 else [0])
    order = [first] + [k for k in rest if k]
    inner, brim, far_inner = {}, {}, {}
    inner[first], brim[first], last_rows, first_rows = interior(stack, spatial_taps, place, (first,), parts, True)
    far_inner[first] = swap(inner[first], first)
    up = lax.ppermute(last_rows, "strip", [(i, i + 1) for i in range(strips - 1)])
    down = lax.ppermute(first_rows, "strip", [(i + 1, i) for i in range(strips - 1)])
    meta = {0: own}
    for bit in [b for b in range(parts.bit_length() - 2, 0, -1)]:
        meta = spread_meta(meta, 1 << bit, swap)
    made = interior(stack, spatial_taps, place, tuple(rest), parts, False)
    for n, offset in enumerate(rest):
        inner[offset], brim[offset] = made[n], made[len(rest) + n]
    for offset in order[1:-1]:
        far_inner[offset] = swap(inner[offset], offset)
    known = sorted(meta)
    *held, inner[1] = lax.optimization_barrier((*[meta[k] for k in known], inner[1]))
    meta = spread_meta(dict(zip(known, held)), 1, swap)
    far_inner[1] = swap(inner[1], 1)
    meta = [meta[k] for k in range(parts)]
    far_inner[first], brim[first] = lax.optimization_barrier((far_inner[first], brim[first]))
    rim = edges(stack, up, down, [brim[k] for k in range(parts)], spatial_taps, place)
    far_rim = {offset: swap(rim[offset], offset) for offset in order}
    sums = footprints([inner[k] for k in range(parts)], rim, meta, place, parts * strips)
    got = lax.all_to_all(sums, ("date", "strip"), split_axis=0, concat_axis=0, tiled=True)
    last = rows // EDGE - 1
    residual = temporal(
        [inner[0]] + [far_inner[k] for k in range(1, parts)], None, temporal_taps, place, 1, 1, rows)
    got, residual = lax.optimization_barrier((got, residual))
    anomaly, series = owner_series(got, temporal_taps, parts, strips)
    residual = temporal(
        [rim[0]] + [far_rim[k] for k in range(1, parts)], residual, temporal_taps, place, 0, last, rows)
    return residual, anomaly, series


def solution(mesh):
    placed = (
        P("date", "strip", None),
        P(),
        P(),
        P(("date", "strip")),
        P(("date", "strip")),
        P(("date", "strip")),
        P(("date", "strip"), None),
    )
    return jax.shard_map(
        shards,
        mesh=mesh,
        in_specs=placed,
        out_specs=(
            P(None, "strip", "date"),
            P(("date", "strip"), None, None),
            P(("date", "strip"), None),
        ),
        check_vma=False,
    )
```

```python
import functools

import jax
import jax.numpy as jnp
from jax import lax
from jax.experimental import pallas as pl
from jax.experimental.pallas import tpu as pltpu
from jax.sharding import PartitionSpec as P

TILE = 128
RADIUS = 6
REACH = 2
DILATION = 8
PAIR_CAP = 2
LANES = 128
EDGE = 8
HIGHEST = lax.Precision.HIGHEST


def params(mebibytes):
    return pltpu.CompilerParams(vmem_limit_bytes=mebibytes * 1024 * 1024)


def cost(micros):
    return pl.CostEstimate(flops=0, bytes_accessed=int(micros * 3.69e6), transcendentals=0)


def pick_taps(at, taps):
    count = taps.shape[0]
    total = taps[0]
    for k in range(1, count):
        total = total + taps[k]
    out = jnp.zeros(at.shape, jnp.float32)
    for k in range(count):
        out = jnp.where(at == k, taps[k], out)
    return out / jnp.full(at.shape, total, jnp.float32)


def split(value, count):
    out = []
    for _ in range(count):
        piece = value.astype(jnp.bfloat16)
        out.append(piece)
        value = value - piece.astype(jnp.float32)
    return out


def spread(value, axis):
    high, mid = split(value, 2)
    return jnp.concatenate([high, high, high, mid], axis=axis)


def fill_columns(col_ref, taps):
    shape = (LANES, LANES)
    lag = lax.broadcasted_iota(jnp.int32, shape, 0) - lax.broadcasted_iota(jnp.int32, shape, 1)
    near = split(pick_taps(lag + RADIUS, taps), 3)
    far = pick_taps(jnp.where(lag > 0, lag + RADIUS - LANES, lag + RADIUS + LANES), taps)
    above = split(jnp.where(lag > 0, far, 0.0), 3)
    below = split(jnp.where(lag > 0, 0.0, far), 3)
    for n, piece in enumerate((0, 1, 2, 0)):
        at = n * 3 * LANES
        for i, pair in enumerate(((near, above), (below, near), (above, below))):
            for j, block in enumerate(pair):
                col_ref[at + i * LANES:at + (i + 1) * LANES, j * LANES:(j + 1) * LANES] = block[piece]


def row_band(out_rows, in_rows, taps):
    shape = (out_rows, 4 * in_rows)
    lane = lax.broadcasted_iota(jnp.int32, shape, 1)
    row = lax.broadcasted_iota(jnp.int32, shape, 0)
    part = jnp.zeros(shape, jnp.int32)
    for n in range(1, 4):
        part = jnp.where(lane >= n * in_rows, n, part)
    return lane - part * in_rows, row, part


def pieces_of(values, part):
    high, mid, low = [p.astype(jnp.float32) for p in split(values, 3)]
    return jnp.where(part == 1, mid, jnp.where(part == 2, low, high)).astype(jnp.bfloat16)


def filter_columns(mid, rim, col):
    rows = mid.shape[0]
    window = jnp.concatenate([mid, rim], axis=1)
    return jnp.dot(spread(window, 1), col, preferred_element_type=jnp.float32)


def rim_tile(left, right, block, parts):
    lane = lax.broadcasted_iota(jnp.int32, left.shape, len(left.shape) - 1)
    first = lane < LANES // 2
    keep = (first & (block < parts - 1)) | (~first & (block > 0))
    return jnp.where(keep, jnp.where(first, right, left), 0.0)


def interior_kernel(offsets, parts, group, alone, halo, place, taps, stack, *rest):
    count = len(offsets)
    outs, brims, rest = rest[:count], rest[count:2 * count], rest[2 * count:]
    if halo:
        halos, rest = rest[:2], rest[2:]
    if alone:
        mid_ref, left_ref, right_ref, *rest = rest
    else:
        x_ref, *rest = rest
    if halo:
        halo_ref, halo_sem, *rest = rest
    col_ref, row_ref, in_sem = rest
    per, dates, inner, _ = outs[0].shape
    width = per * LANES
    rows = inner + 2 * EDGE
    cols = width * parts

    def bounds(offset):
        start = (place[0] ^ offset) * width
        places = start, jnp.maximum(start - LANES, 0), jnp.minimum(start + width, cols - LANES)
        return [pl.multiple_of(first, LANES) for first in places]

    def load(g):
        at = pl.ds(g * group, group)
        if not alone:
            return [pltpu.make_async_copy(stack.at[at], x_ref.at[at], in_sem.at[0, g])]
        return [
            pltpu.make_async_copy(stack.at[at, :, pl.ds(first, ref.shape[2])], ref.at[at], in_sem.at[n, g])
            for n, (first, ref) in enumerate(zip(bounds(offsets[0]), (mid_ref, left_ref, right_ref)))
        ]

    def window(at, offset):
        if alone:
            return mid_ref[at], left_ref[at], right_ref[at]
        start, before, after = bounds(offset)
        return x_ref[at, :, pl.ds(start, width)], x_ref[at, :, pl.ds(before, LANES)], x_ref[at, :, pl.ds(after, LANES)]

    steps = dates // group
    for g in range(steps):
        for copy in load(g):
            copy.start()
    copies = []
    if halo:
        copies = [
            pltpu.make_async_copy(
                stack.at[:, pl.ds(side * (rows - EDGE), EDGE), pl.ds(c * LANES, LANES)],
                halo_ref.at[side, c], halo_sem.at[side, c])
            for side in range(2) for c in range(cols // LANES)
        ]
        for copy in copies:
            copy.start()
    fill_columns(col_ref, taps)
    q, r, part = row_band(inner, rows, taps)
    row_ref[...] = pieces_of(pick_taps(q - r - (EDGE - RADIUS), taps), part)

    def step(g, carry):
        for copy in load(g):
            copy.wait()
        at = pl.ds(g * group, group)
        for n, offset in enumerate(offsets):
            mid, left, right = window(at, offset)
            rim = rim_tile(left, right, place[0] ^ offset, parts)
            across = filter_columns(mid.reshape(group * rows, width), rim.reshape(group * rows, LANES), col_ref[...])
            for t in range(group):
                one = across[t * rows:(t + 1) * rows]
                low = jnp.dot(row_ref[...], spread(one, 0), preferred_element_type=jnp.float32)
                done = mid[t, EDGE:rows - EDGE, :] - low
                for h in range(per):
                    outs[n][h, g * group + t] = done[:, h * LANES:(h + 1) * LANES]
                for h in range(per):
                    for side in range(2):
                        ends = one[side * (rows - 2 * EDGE):side * (rows - 2 * EDGE) + 2 * EDGE, h * LANES:(h + 1) * LANES]
                        brims[n][h, pl.ds(side * 2 * EDGE * dates + g * group + t, 2 * EDGE, stride=dates), :] = ends
        return carry

    lax.fori_loop(0, steps, step, 0)
    for copy in copies:
        copy.wait()
    if halo:
        for c in range(cols // LANES):
            at = slice(c * LANES, (c + 1) * LANES)
            first, last = [halo_ref.at[side, c].reshape(dates * EDGE, LANES) for side in range(2)]
            for r in range(RADIUS):
                halos[0][r, :, at] = last[pl.ds(EDGE - RADIUS + r, dates, stride=EDGE), :]
                halos[1][r, :, at] = first[pl.ds(r, dates, stride=EDGE), :]


def interior(stack, taps, place, offsets, parts, halo=False):
    dates, rows, cols = stack.shape
    width = cols // parts
    group = min(8, dates)
    inner = rows - 2 * EDGE
    count = len(offsets)
    alone = count == 1
    out_shape = [jax.ShapeDtypeStruct((width // LANES, dates, inner, LANES), jnp.float32)] * count
    out_shape += [jax.ShapeDtypeStruct((width // LANES, 4 * EDGE * dates, LANES), jnp.float32)] * count
    scratch = [pltpu.VMEM((dates, rows, span), jnp.float32) for span in ((width, LANES, LANES) if alone else (cols,))]
    if halo:
        out_shape += [jax.ShapeDtypeStruct((RADIUS, dates, cols), jnp.float32)] * 2
        scratch.append(pltpu.VMEM((2, cols // LANES, dates, EDGE, LANES), jnp.float32))
        scratch.append(pltpu.SemaphoreType.DMA((2, cols // LANES)))
    return pl.pallas_call(
        functools.partial(interior_kernel, offsets, parts, group, alone, halo),
        grid_spec=pltpu.PrefetchScalarGridSpec(
            num_scalar_prefetch=2,
            grid=(),
            in_specs=[pl.BlockSpec(memory_space=pltpu.HBM)],
            out_specs=[pl.BlockSpec(memory_space=pltpu.VMEM)] * len(out_shape),
            scratch_shapes=scratch + [
                pltpu.VMEM((12 * LANES, width), jnp.bfloat16),
                pltpu.VMEM((inner, 4 * rows), jnp.bfloat16),
                pltpu.SemaphoreType.DMA((3, dates // group)),
            ],
        ),
        out_shape=out_shape,
        compiler_params=params(58 if alone else 56),
        cost_estimate=cost(2.5 + 2.5 * count),
    )(place, taps, stack)


def edge_kernel(parts, place, taps, stack, up_ref, down_ref, *rest):
    brims, outs = rest[:parts], rest[parts:2 * parts]
    x_ref, across_ref, col_ref, in_sem = rest[2 * parts:]
    _, dates, cols = up_ref.shape
    rows = stack.shape[1]
    width = cols // parts
    per = width // LANES
    loads = [
        pltpu.make_async_copy(
            stack.at[:, pl.ds(side * (rows - EDGE), EDGE), pl.ds(c * LANES, LANES)],
            x_ref.at[c, :, pl.ds(side * EDGE, EDGE), :], in_sem.at[side, c])
        for side in range(2) for c in range(cols // LANES)
    ]
    for copy in loads:
        copy.start()
    fill_columns(col_ref, taps)
    total = taps[0]
    for k in range(1, 2 * RADIUS + 1):
        total = total + taps[k]
    scale = 1.0 / jnp.full((dates, LANES), total, jnp.float32)
    for k in range(parts):
        block = place[0] ^ k
        start = pl.multiple_of(block * width, LANES)
        before = pl.multiple_of(jnp.maximum(start - LANES, 0), LANES)
        after = pl.multiple_of(jnp.minimum(start + width, cols - LANES), LANES)

        def both(first, span):
            at = pl.ds(first, span)
            return jnp.concatenate([up_ref[:, :, at], down_ref[:, :, at]], axis=0).reshape(2 * RADIUS * dates, span)

        rim = rim_tile(both(before, LANES), both(after, LANES), block, parts)
        across = filter_columns(both(start, width), rim, col_ref[...])
        for h in range(per):
            across_ref[k, h] = across[:, h * LANES:(h + 1) * LANES]
    for copy in loads:
        copy.wait()
    flat = x_ref.reshape(cols // LANES, dates * 2 * EDGE, LANES)
    for k in range(parts):
        for h in range(per):
            tile = (place[0] ^ k) * per + h
            out = outs[k].reshape(per, dates * 2 * EDGE, LANES)

            def row(side, r):
                if side == 0 and r < 0:
                    return across_ref[k, h, (r + RADIUS) * dates:(r + RADIUS + 1) * dates, :]
                if side == 1 and r >= 2 * EDGE:
                    at = (RADIUS + r - 2 * EDGE) * dates
                    return across_ref[k, h, at:at + dates, :]
                at = (side * 2 * EDGE + r) * dates
                return brims[k][h, at:at + dates, :]

            for side in range(2):
                held = {}
                for r in range(EDGE):
                    centre = side * EDGE + r
                    for q in range(centre - RADIUS, centre + RADIUS + 1):
                        if q not in held:
                            held[q] = row(side, q)
                    low = taps[0] * held[centre - RADIUS]
                    for j in range(1, 2 * RADIUS + 1):
                        low = low + taps[j] * held[centre - RADIUS + j]
                    at = pl.ds(centre, dates, stride=2 * EDGE)
                    out[h, at, :] = flat[tile, at, :] - scale * low
                    del held[centre - RADIUS]


def edges(stack, up, down, brims, taps, place):
    parts = len(brims)
    dates, rows, cols = stack.shape
    width = cols // parts
    resident = pl.BlockSpec(memory_space=pltpu.VMEM)
    return pl.pallas_call(
        functools.partial(edge_kernel, parts),
        grid_spec=pltpu.PrefetchScalarGridSpec(
            num_scalar_prefetch=2,
            grid=(),
            in_specs=[pl.BlockSpec(memory_space=pltpu.HBM)] + [resident] * (2 + parts),
            out_specs=[resident] * parts,
            scratch_shapes=[
                pltpu.VMEM((cols // LANES, dates, 2 * EDGE, LANES), jnp.float32),
                pltpu.VMEM((parts, width // LANES, 2 * RADIUS * dates, LANES), jnp.float32),
                pltpu.VMEM((12 * LANES, width), jnp.bfloat16),
                pltpu.SemaphoreType.DMA((2, cols // LANES)),
            ],
        ),
        out_shape=[jax.ShapeDtypeStruct((width // LANES, dates, 2 * EDGE, LANES), jnp.float32)] * parts,
        compiler_params=params(52),
        cost_estimate=cost(4),
    )(place, taps, stack, up, down, *brims)


def temporal_kernel(parts, with_base, first_tile, tile_step, place, taps, *rest):
    pieces = rest[:parts]
    out, z_ref, f_ref, out_ref, out_sem = rest[parts + with_base:]
    count, total, _, _ = out_ref.shape
    per = pieces[0].shape[0]
    local = total // parts
    pad = REACH * DILATION
    step = 8
    none = jnp.zeros((REACH, EDGE, LANES), jnp.float32)
    wide = jnp.zeros((pad, EDGE, LANES), jnp.float32)
    for h in range(per):
        z_ref[h, 0:REACH] = none
        z_ref[h, REACH + total:REACH + total + REACH] = none
        f_ref[h, 0:pad] = wide
        f_ref[h, pad + total:pad + total + pad] = wide
    own = 1.0 - taps[0, REACH]
    own_wide = 1.0 - taps[1, REACH]
    others = [k for k in range(2 * REACH + 1) if k != REACH]

    def store(n):
        tile = first_tile + n * tile_step
        rows = pl.ds(pl.multiple_of(tile * EDGE, EDGE), EDGE)
        return pltpu.make_async_copy(out_ref.at[n], out.at[:, rows, :], out_sem.at[n])

    def one(n, carry):
        rows = pl.ds(pl.multiple_of(n * EDGE, EDGE), EDGE)
        for h in range(per):
            for k in range(parts):
                z_ref[h, pl.ds(REACH + (place[0] ^ k) * local, local)] = pieces[k][h, :, rows, :]
            for t in range(0, total, step):
                z = z_ref[h, t:t + step + 2 * REACH]
                kept = own * z[REACH:REACH + step]
                for k in others:
                    kept = kept - taps[0, k] * z[k:k + step]
                f_ref[h, pad + t:pad + t + step] = kept
            for t in range(0, total, step):
                kept = own_wide * f_ref[h, pad + t:pad + t + step]
                for k in others:
                    kept = kept - taps[1, k] * f_ref[h, t + k * DILATION:t + k * DILATION + step]
                out_ref[n, t:t + step, :, h * LANES:(h + 1) * LANES] = kept
        store(n).start()
        return carry

    lax.fori_loop(0, count, one, 0)
    for n in range(count):
        store(n).wait()


def temporal(pieces, base, taps, place, first_tile, tile_step, rows):
    parts = len(pieces)
    per, local, here, _ = pieces[0].shape
    total = local * parts
    extra = [] if base is None else [base]
    count = here // EDGE
    width = per * LANES
    return pl.pallas_call(
        functools.partial(temporal_kernel, parts, len(extra), first_tile, tile_step),
        grid_spec=pltpu.PrefetchScalarGridSpec(
            num_scalar_prefetch=2,
            grid=(),
            in_specs=[pl.BlockSpec(memory_space=pltpu.VMEM)] * parts + [pl.BlockSpec(memory_space=pltpu.HBM)] * len(extra),
            out_specs=pl.BlockSpec(memory_space=pltpu.HBM),
            scratch_shapes=[
                pltpu.VMEM((per, total + 2 * REACH, EDGE, LANES), jnp.float32),
                pltpu.VMEM((per, total + 2 * REACH * DILATION, EDGE, LANES), jnp.float32),
                pltpu.VMEM((count, total, EDGE, width), jnp.float32),
                pltpu.SemaphoreType.DMA((count,)),
            ],
        ),
        out_shape=jax.ShapeDtypeStruct((total, rows, width), jnp.float32),
        input_output_aliases={} if base is None else {2 + parts: 0},
        compiler_params=params(24),
        cost_estimate=cost(2.5 + 0.4 * count),
    )(place, taps, *pieces, *extra)


def footprint_kernel(parts, feet, place, *rest):
    meta, vectors, rest = rest[:parts], rest[parts:2 * parts], rest[2 * parts:]
    inner, rim = rest[:parts], rest[parts:2 * parts]
    out_ref = rest[2 * parts]
    per, dates, rows, _ = inner[0].shape
    owners = out_ref.shape[0]
    lane = lax.broadcasted_iota(jnp.int32, (dates, LANES), 1)
    both = [jnp.concatenate([ref[n:n + 1, :] for ref in vectors], axis=1) for n in range(1, 4)]
    index = lax.broadcasted_iota(jnp.int32, both[0].shape, 1)
    source = (index // feet) ^ place[0]
    named = lax.broadcasted_iota(jnp.int32, (owners, index.shape[1]), 0) == both[1]
    places = []
    for block in range(parts):
        for slot in range(PAIR_CAP):
            hit = named & (source == block) & (both[2] == slot)
            places.append(jnp.where(hit, 1.0, 0.0).astype(jnp.bfloat16))
    places = jnp.concatenate(places, axis=0)
    tiles = []
    for first in range(0, parts * feet, LANES):
        total = jnp.zeros((dates, LANES), jnp.float32)
        for k in range(first // feet, -(-(first + LANES) // feet)):
            middle, ends = [ref.reshape(per * dates * ref.shape[2], LANES) for ref in (inner[k], rim[k])]

            def take(f, total):
                row, tile = meta[k][0, f] & 0xFFFF, meta[k][0, f] >> 16
                in_middle = (row >= EDGE) & (row < EDGE + rows)
                end_row = jnp.where(row < EDGE, row, jnp.clip(row - rows, 0, 2 * EDGE - 1))
                pixels = jnp.where(
                    in_middle,
                    middle[pl.ds(tile * dates * rows + jnp.clip(row - EDGE, 0, rows - 1), dates, stride=rows), :],
                    ends[pl.ds(tile * dates * 2 * EDGE + end_row, dates, stride=2 * EDGE), :])
                one = jnp.sum(jnp.where(lane < meta[k][1, f], pixels, 0.0), axis=1, keepdims=True)
                return jnp.where(lane == k * feet + f - first, one, total)

            total = lax.fori_loop(max(first - k * feet, 0), min(feet, first + LANES - k * feet), take, total, unroll=16)
        tiles.append(total)
    counts = jnp.broadcast_to(both[0].astype(jnp.float32), (dates, index.shape[1]))
    sums = jnp.concatenate([jnp.concatenate(tiles, axis=1), counts], axis=0)
    held = jnp.zeros((places.shape[0], 2 * dates), jnp.float32)
    for piece in split(sums, 3):
        held = held + lax.dot_general(places, piece, (((1,), (1,)), ((), ())), preferred_element_type=jnp.float32)
    for n in range(parts * PAIR_CAP):
        at = pl.ds(n * dates, dates)
        out_ref[:, 0, at] = held[n * owners:(n + 1) * owners, :dates]
        out_ref[:, 1, at] = held[n * owners:(n + 1) * owners, dates:]


def footprints(inner, rim, meta, place, owners):
    parts = len(inner)
    per, dates, inner_rows, _ = inner[0].shape
    feet = meta[0].shape[1]
    message = parts * PAIR_CAP * dates
    return pl.pallas_call(
        functools.partial(footprint_kernel, parts, feet),
        grid_spec=pltpu.PrefetchScalarGridSpec(
            num_scalar_prefetch=1 + parts,
            grid=(),
            in_specs=[pl.BlockSpec(memory_space=pltpu.VMEM)] * (3 * parts),
            out_specs=pl.BlockSpec(memory_space=pltpu.VMEM),
        ),
        out_shape=jax.ShapeDtypeStruct((owners, 2, message), jnp.float32),
        compiler_params=params(24),
        cost_estimate=cost(5),
    )(place, *meta, *meta, *inner, *rim)


def owner_kernel(parts, strips, taps, got_ref, anomaly_ref, series_ref):
    owners = parts * strips
    slots = owners * PAIR_CAP
    dates = got_ref.shape[2] // PAIR_CAP
    local = dates // parts
    sums, held = got_ref[:, 0, :], got_ref[:, 1, :]
    rows, weights = [], []
    for block in range(parts):
        for slot in range(PAIR_CAP):
            at = (block * PAIR_CAP + slot) * local
            rows.append(jnp.concatenate(
                [sums[e * strips:(e + 1) * strips, at:at + local] for e in range(parts)], axis=1))
            weights.append(held[0:strips, at:at + 1])
    sums = jnp.concatenate(rows, axis=0)
    weight = jnp.concatenate(weights, axis=0)
    shape = (dates, dates)
    lag = lax.broadcasted_iota(jnp.int32, shape, 0) - lax.broadcasted_iota(jnp.int32, shape, 1)
    for level, spacing in ((0, 1), (1, DILATION)):
        filt = jnp.where(lag == 0, 1.0, 0.0)
        for k in range(2 * REACH + 1):
            filt = filt - jnp.where(lag == (k - REACH) * spacing, taps[level, k], 0.0)
        sums = jnp.dot(sums, filt, precision=HIGHEST, preferred_element_type=jnp.float32)
    mean = sums / jnp.where(weight > 0, weight, 1.0)
    asset = jnp.sum(weight * mean, axis=0, keepdims=True) / jnp.sum(weight, axis=0, keepdims=True)
    odd = jnp.where(weight > 0, mean - asset, 0.0)
    series_ref[...] = asset
    shape = (slots, slots)
    to = lax.broadcasted_iota(jnp.int32, shape, 0)
    source = lax.broadcasted_iota(jnp.int32, shape, 1)
    block, rest = source // (PAIR_CAP * strips), source % (PAIR_CAP * strips)
    place_of = block * (PAIR_CAP * strips) + (rest % strips) * PAIR_CAP + rest // strips
    order = jnp.where(to == place_of, 1.0, 0.0)
    anomaly_ref[0] = jnp.dot(order, odd, precision=HIGHEST, preferred_element_type=jnp.float32)


def owner_series(got, taps, parts, strips):
    owners = parts * strips
    dates = got.shape[2] // PAIR_CAP
    slots = owners * PAIR_CAP
    return pl.pallas_call(
        functools.partial(owner_kernel, parts, strips),
        grid_spec=pltpu.PrefetchScalarGridSpec(
            num_scalar_prefetch=1,
            grid=(),
            in_specs=[pl.BlockSpec(memory_space=pltpu.VMEM)],
            out_specs=[pl.BlockSpec(memory_space=pltpu.VMEM)] * 2,
        ),
        out_shape=[
            jax.ShapeDtypeStruct((1, slots, dates), jnp.float32),
            jax.ShapeDtypeStruct((1, dates), jnp.float32),
        ],
        compiler_params=params(24),
        cost_estimate=cost(1.8),
    )(taps, got)


def spread_meta(meta, offset, swap):
    known = sorted(meta)
    got = swap(jnp.concatenate([meta[k] for k in known], axis=1), offset)
    width = meta[0].shape[1]
    return meta | {k ^ offset: got[:, n * width:(n + 1) * width] for n, k in enumerate(known)}


def shards(stack, spatial_taps, temporal_taps, foot_tile, foot_row, foot_count, foot_owner):
    parts, strips = lax.axis_size("date"), lax.axis_size("strip")
    place = lax.axis_index("date").astype(jnp.int32)[None]
    dates, rows, cols = stack.shape
    feet = foot_row.shape[0]
    owner = foot_owner[:, 0]
    position = jnp.arange(feet, dtype=jnp.int32)
    earlier = (owner[:, None] == owner[None, :]) & (position[None, :] < position[:, None])
    slot = jnp.sum(earlier.astype(jnp.int32), axis=1)
    own = jnp.stack([(foot_tile << 16) + foot_row, foot_count, owner, slot])

    def swap(value, offset):
        return lax.ppermute(value, "date", [(i, i ^ offset) for i in range(parts)])

    far = list(range(2, parts)) + [1, 0]
    inner, brim, far_inner = {}, {}, {}
    meta = {0: own}
    for bit in range(parts.bit_length() - 2, 0, -1):
        meta = spread_meta(meta, 1 << bit, swap)
    k = far[0]
    inner[k], brim[k] = interior(stack, spatial_taps, place, (k,), parts)
    known = sorted(meta)
    *held, inner[k], later = lax.optimization_barrier((*[meta[n] for n in known], inner[k], place))
    far_inner[k] = swap(inner[k], k)
    meta = spread_meta(dict(zip(known, held)), 1, swap)
    k = far[1]
    inner[k], brim[k], last_rows, first_rows = interior(stack, spatial_taps, later, (k,), parts, True)
    up = lax.ppermute(last_rows, "strip", [(i, i + 1) for i in range(strips - 1)])
    down = lax.ppermute(first_rows, "strip", [(i + 1, i) for i in range(strips - 1)])
    far_inner[k] = swap(inner[k], k)
    *meta, brim[k], later = lax.optimization_barrier((*[meta[n] for n in range(parts)], brim[k], later))
    for n in far[2:-1]:
        inner[n], brim[n] = interior(stack, spatial_taps, later, (n,), parts)
        if n > 1:
            far_inner[n] = swap(inner[n], n)
    far_inner[far[0]], later = lax.optimization_barrier((far_inner[far[0]], later))
    inner[0], brim[0] = interior(stack, spatial_taps, later, (0,), parts)
    order = far[:-1]
    rim = list(edges(stack, up, down, [brim[k] for k in range(parts)], spatial_taps, place))
    inner[1], rim[0] = lax.optimization_barrier((inner[1], rim[0]))
    far_inner[1] = swap(inner[1], 1)
    far_rim = {offset: swap(rim[offset], offset) for offset in order}
    sums = footprints([inner[k] for k in range(parts)], rim, meta, place, parts * strips)
    got = lax.all_to_all(sums, ("date", "strip"), split_axis=0, concat_axis=0, tiled=True)
    last = rows // EDGE - 1
    residual = temporal(
        [inner[0]] + [far_inner[k] for k in range(1, parts)], None, temporal_taps, place, 1, 1, rows)
    got, residual = lax.optimization_barrier((got, residual))
    anomaly, series = owner_series(got, temporal_taps, parts, strips)
    residual = temporal(
        [rim[0]] + [far_rim[k] for k in range(1, parts)], residual, temporal_taps, place, 0, last, rows)
    return residual, anomaly, series


def solution(mesh):
    placed = (
        P("date", "strip", None),
        P(),
        P(),
        P(("date", "strip")),
        P(("date", "strip")),
        P(("date", "strip")),
        P(("date", "strip"), None),
    )
    return jax.shard_map(
        shards,
        mesh=mesh,
        in_specs=placed,
        out_specs=(
            P(None, "strip", "date"),
            P(("date", "strip"), None, None),
            P(("date", "strip"), None),
        ),
        check_vma=False,
    )
```

```python
import functools

import jax
import jax.numpy as jnp
from jax import lax
from jax.experimental import pallas as pl
from jax.experimental.pallas import tpu as pltpu
from jax.sharding import PartitionSpec as P

TILE = 128
RADIUS = 6
REACH = 2
DILATION = 8
PAIR_CAP = 2
LANES = 128
EDGE = 8
HIGHEST = lax.Precision.HIGHEST


def params(mebibytes):
    return pltpu.CompilerParams(vmem_limit_bytes=mebibytes * 1024 * 1024)


def cost(micros):
    return pl.CostEstimate(flops=0, bytes_accessed=int(micros * 3.69e6), transcendentals=0)


def pick_taps(at, taps):
    count = taps.shape[0]
    total = taps[0]
    for k in range(1, count):
        total = total + taps[k]
    out = jnp.zeros(at.shape, jnp.float32)
    for k in range(count):
        out = jnp.where(at == k, taps[k], out)
    return out / jnp.full(at.shape, total, jnp.float32)


def split(value, count):
    out = []
    for _ in range(count):
        piece = value.astype(jnp.bfloat16)
        out.append(piece)
        value = value - piece.astype(jnp.float32)
    return out


def spread(value, axis):
    high, mid = split(value, 2)
    return jnp.concatenate([high, high, high, mid], axis=axis)


def fill_columns(col_ref, taps):
    shape = (LANES, LANES)
    lag = lax.broadcasted_iota(jnp.int32, shape, 0) - lax.broadcasted_iota(jnp.int32, shape, 1)
    near = split(pick_taps(lag + RADIUS, taps), 3)
    far = pick_taps(jnp.where(lag > 0, lag + RADIUS - LANES, lag + RADIUS + LANES), taps)
    above = split(jnp.where(lag > 0, far, 0.0), 3)
    below = split(jnp.where(lag > 0, 0.0, far), 3)
    for n, piece in enumerate((0, 1, 2, 0)):
        at = n * 3 * LANES
        for i, pair in enumerate(((near, above), (below, near), (above, below))):
            for j, block in enumerate(pair):
                col_ref[at + i * LANES:at + (i + 1) * LANES, j * LANES:(j + 1) * LANES] = block[piece]


def row_band(out_rows, in_rows, taps):
    shape = (out_rows, 4 * in_rows)
    lane = lax.broadcasted_iota(jnp.int32, shape, 1)
    row = lax.broadcasted_iota(jnp.int32, shape, 0)
    part = jnp.zeros(shape, jnp.int32)
    for n in range(1, 4):
        part = jnp.where(lane >= n * in_rows, n, part)
    return lane - part * in_rows, row, part


def pieces_of(values, part):
    high, mid, low = [p.astype(jnp.float32) for p in split(values, 3)]
    return jnp.where(part == 1, mid, jnp.where(part == 2, low, high)).astype(jnp.bfloat16)


def filter_columns(mid, rim, col):
    rows = mid.shape[0]
    window = jnp.concatenate([mid, rim], axis=1)
    return jnp.dot(spread(window, 1), col, preferred_element_type=jnp.float32)


def rim_tile(left, right, block, parts):
    lane = lax.broadcasted_iota(jnp.int32, left.shape, len(left.shape) - 1)
    first = lane < LANES // 2
    keep = (first & (block < parts - 1)) | (~first & (block > 0))
    return jnp.where(keep, jnp.where(first, right, left), 0.0)


def chosen(n, values):
    out = values[0]
    for m in range(1, len(values)):
        out = jnp.where(n == m, values[m], out)
    return out


def interior_kernel(offsets, slot, parts, group, place, taps, stack, *rest):
    count = len(offsets)
    first = slot == 0
    if not first:
        rest = rest[1:]
    outs, brim, rest = rest[:count], rest[count], rest[count + 1:]
    if first:
        up, down, ends, mid_ref, left_ref, right_ref, halo_ref, up_ref, down_ref, halo_sem, halo_out_sem, *rest = rest
    else:
        x_ref, *rest = rest
    out_ref, brim_ref, col_ref, row_ref, in_sem, out_sem, brim_sem = rest
    _, per, dates, inner, _ = out_ref.shape
    width = per * LANES
    rows = inner + 2 * EDGE
    cols = width * parts
    steps = dates // group

    def bounds(block):
        start = block * width
        places = start, jnp.maximum(start - LANES, 0), jnp.minimum(start + width, cols - LANES)
        return [pl.multiple_of(at, LANES) for at in places]

    def load(g):
        at = pl.ds(g * group, group)
        if not first:
            return [pltpu.make_async_copy(stack.at[at], x_ref.at[at], in_sem.at[0, g])]
        return [
            pltpu.make_async_copy(stack.at[at, :, pl.ds(start, ref.shape[2])], ref.at[at], in_sem.at[n, g])
            for n, (start, ref) in enumerate(zip(bounds(place[0] ^ offsets[0]), (mid_ref, left_ref, right_ref)))
        ]

    def store(m, g):
        at = pl.ds(g * group, group)
        return pltpu.make_async_copy(out_ref.at[m, :, at], outs[m].at[:, at], out_sem.at[m, g])

    def store_brim(n):
        return pltpu.make_async_copy(brim_ref.at[n], brim.at[slot + n], brim_sem.at[n])

    for g in range(steps):
        for copy in load(g):
            copy.start()
    halo_loads, halo_stores = [], []
    if first:
        halo_loads = [
            pltpu.make_async_copy(
                stack.at[:, pl.ds(side * (rows - EDGE), EDGE), pl.ds(c * LANES, LANES)],
                halo_ref.at[c, :, pl.ds(side * EDGE, EDGE), :], halo_sem.at[side, c])
            for side in range(2) for c in range(cols // LANES)
        ]
        halo_stores = [
            pltpu.make_async_copy(halo_ref, ends, halo_out_sem.at[0]),
            pltpu.make_async_copy(up_ref, up, halo_out_sem.at[1]),
            pltpu.make_async_copy(down_ref, down, halo_out_sem.at[2]),
        ]
        for copy in halo_loads:
            copy.start()
    fill_columns(col_ref, taps)
    q, r, part = row_band(inner, rows, taps)
    row_ref[...] = pieces_of(pick_taps(q - r - (EDGE - RADIUS), taps), part)
    if first:
        for copy in halo_loads:
            copy.wait()

        def pack(c, carry):
            at = pl.ds(pl.multiple_of(c * LANES, LANES), LANES)
            rows_of = halo_ref.at[c].reshape(dates * 2 * EDGE, LANES)
            for r in range(RADIUS):
                up_ref[r, :, at] = rows_of[pl.ds(2 * EDGE - RADIUS + r, dates, stride=2 * EDGE), :]
                down_ref[r, :, at] = rows_of[pl.ds(r, dates, stride=2 * EDGE), :]
            return carry

        lax.fori_loop(0, cols // LANES, pack, 0)
        for copy in halo_stores:
            copy.start()

    def step(i, carry):
        n, g = i // steps, i % steps
        block = place[0] ^ chosen(n, offsets)
        at = pl.ds(g * group, group)

        @pl.when(n == 0)
        def _():
            for copy in load(g):
                copy.wait()

        if first:
            mid, left, right = mid_ref[at], left_ref[at], right_ref[at]
        else:
            start, before, after = bounds(block)
            mid, left, right = [x_ref[at, :, pl.ds(f, w)] for f, w in ((start, width), (before, LANES), (after, LANES))]
        rim = rim_tile(left, right, block, parts)
        across = filter_columns(mid.reshape(group * rows, width), rim.reshape(group * rows, LANES), col_ref[...])
        for t in range(group):
            one = across[t * rows:(t + 1) * rows]
            low = jnp.dot(row_ref[...], spread(one, 0), preferred_element_type=jnp.float32)
            done = mid[t, EDGE:rows - EDGE, :] - low
            for h in range(per):
                out_ref[n, h, g * group + t] = done[:, h * LANES:(h + 1) * LANES]
                for side in range(2):
                    lines = one[side * (rows - 2 * EDGE):side * (rows - 2 * EDGE) + 2 * EDGE, h * LANES:(h + 1) * LANES]
                    brim_ref[n, h, pl.ds(side * 2 * EDGE * dates + g * group + t, 2 * EDGE, stride=dates), :] = lines
        for m in range(count):
            @pl.when(n == m)
            def _():
                store(m, g).start()

        @pl.when(g == steps - 1)
        def _():
            store_brim(n).start()

        return carry

    lax.fori_loop(0, count * steps, step, 0)
    for copy in halo_stores:
        copy.wait()
    for m in range(count):
        for g in range(steps):
            store(m, g).wait()
        store_brim(m).wait()


def interior(stack, brim, taps, place, offsets, slot, parts):
    dates, rows, cols = stack.shape
    width = cols // parts
    per = width // LANES
    group = min(8, dates)
    inner = rows - 2 * EDGE
    count = len(offsets)
    first = slot == 0
    here = pl.BlockSpec(memory_space=pltpu.HBM)
    out_shape = [jax.ShapeDtypeStruct((per, dates, inner, LANES), jnp.float32)] * count
    out_shape += [jax.ShapeDtypeStruct((parts, per, 4 * EDGE * dates, LANES), jnp.float32)]
    if first:
        out_shape += [jax.ShapeDtypeStruct((RADIUS, dates, cols), jnp.float32)] * 2
        out_shape += [jax.ShapeDtypeStruct((cols // LANES, dates, 2 * EDGE, LANES), jnp.float32)]
        scratch = [pltpu.VMEM((dates, rows, span), jnp.float32) for span in (width, LANES, LANES)] + [
            pltpu.VMEM((cols // LANES, dates, 2 * EDGE, LANES), jnp.float32),
            pltpu.VMEM((RADIUS, dates, cols), jnp.float32),
            pltpu.VMEM((RADIUS, dates, cols), jnp.float32),
            pltpu.SemaphoreType.DMA((2, cols // LANES)),
            pltpu.SemaphoreType.DMA((3,)),
        ]
    else:
        scratch = [pltpu.VMEM((dates, rows, cols), jnp.float32)]
    return pl.pallas_call(
        functools.partial(interior_kernel, offsets, slot, parts, group),
        grid_spec=pltpu.PrefetchScalarGridSpec(
            num_scalar_prefetch=2,
            grid=(),
            in_specs=[here] * (1 if first else 2),
            out_specs=[here] * len(out_shape),
            scratch_shapes=scratch + [
                pltpu.VMEM((count, per, dates, inner, LANES), jnp.float32),
                pltpu.VMEM((count, per, 4 * EDGE * dates, LANES), jnp.float32),
                pltpu.VMEM((12 * LANES, width), jnp.bfloat16),
                pltpu.VMEM((inner, 4 * rows), jnp.bfloat16),
                pltpu.SemaphoreType.DMA((3, dates // group)),
                pltpu.SemaphoreType.DMA((count, dates // group)),
                pltpu.SemaphoreType.DMA((count,)),
            ],
        ),
        out_shape=out_shape,
        input_output_aliases={} if first else {3: count},
        compiler_params=params(60),
        cost_estimate=cost(2.5 + 2.5 * count),
    )(place, taps, stack, *([] if first else [brim]))


def edge_kernel(order, place, taps, ends_ref, up_ref, down_ref, brim_ref, *rest):
    parts = len(order)
    outs = rest[:parts]
    out_ref, across_ref, col_ref, out_sem = rest[parts:]
    _, dates, cols = up_ref.shape
    width = cols // parts
    per = width // LANES
    fill_columns(col_ref, taps)
    total = taps[0]
    for k in range(1, 2 * RADIUS + 1):
        total = total + taps[k]
    scale = 1.0 / jnp.full((dates, LANES), total, jnp.float32)
    flat = ends_ref.reshape(cols // LANES, dates * 2 * EDGE, LANES)

    def store(n):
        return pltpu.make_async_copy(out_ref.at[n], outs[n], out_sem.at[n])

    def one(n, carry):
        block = place[0] ^ chosen(n, order)
        start = pl.multiple_of(block * width, LANES)
        before = pl.multiple_of(jnp.maximum(start - LANES, 0), LANES)
        after = pl.multiple_of(jnp.minimum(start + width, cols - LANES), LANES)

        def both(first, span):
            at = pl.ds(first, span)
            return jnp.concatenate([up_ref[:, :, at], down_ref[:, :, at]], axis=0).reshape(2 * RADIUS * dates, span)

        rim = rim_tile(both(before, LANES), both(after, LANES), block, parts)
        across = filter_columns(both(start, width), rim, col_ref[...])
        for h in range(per):
            across_ref[h] = across[:, h * LANES:(h + 1) * LANES]
        lines = out_ref.at[n].reshape(per, dates * 2 * EDGE, LANES)

        def half(h, carry):
            for side in range(2):
                held = []
                for q in range(2 * RADIUS + EDGE):
                    halo = q < RADIUS if side == 0 else q >= RADIUS + EDGE
                    if halo:
                        at = q if side == 0 else q - EDGE
                        held.append(across_ref[h, at * dates:(at + 1) * dates, :])
                    else:
                        at = q - RADIUS if side == 0 else 3 * EDGE - RADIUS + q
                        held.append(brim_ref[n, h, at * dates:(at + 1) * dates, :])
                for r in range(EDGE):
                    low = taps[0] * held[r]
                    for j in range(1, 2 * RADIUS + 1):
                        low = low + taps[j] * held[r + j]
                    at = pl.ds(side * EDGE + r, dates, stride=2 * EDGE)
                    lines[h, at, :] = flat[block * per + h, at, :] - scale * low
            return carry

        lax.fori_loop(0, per, half, 0)
        for m in range(parts):
            @pl.when(n == m)
            def _():
                store(m).start()
        return carry

    lax.fori_loop(0, parts, one, 0)
    for m in range(parts):
        store(m).wait()


def edges(ends, up, down, brim, taps, place, order):
    parts = len(order)
    tiles, dates, _, _ = ends.shape
    per = tiles // parts
    resident = pl.BlockSpec(memory_space=pltpu.VMEM)
    return pl.pallas_call(
        functools.partial(edge_kernel, order),
        grid_spec=pltpu.PrefetchScalarGridSpec(
            num_scalar_prefetch=2,
            grid=(),
            in_specs=[resident] * 4,
            out_specs=[pl.BlockSpec(memory_space=pltpu.HBM)] * parts,
            scratch_shapes=[
                pltpu.VMEM((parts, per, dates, 2 * EDGE, LANES), jnp.float32),
                pltpu.VMEM((per, 2 * RADIUS * dates, LANES), jnp.float32),
                pltpu.VMEM((12 * LANES, per * LANES), jnp.bfloat16),
                pltpu.SemaphoreType.DMA((parts,)),
            ],
        ),
        out_shape=[jax.ShapeDtypeStruct((per, dates, 2 * EDGE, LANES), jnp.float32)] * parts,
        compiler_params=params(24),
        cost_estimate=cost(4),
    )(place, taps, ends, up, down, brim)


def temporal_kernel(parts, with_base, first_tile, tile_step, place, taps, *rest):
    pieces = rest[:parts]
    out, z_ref, f_ref, out_ref, out_sem = rest[parts + with_base:]
    count, total, _, _ = out_ref.shape
    per = pieces[0].shape[0]
    local = total // parts
    pad = REACH * DILATION
    step = 8
    none = jnp.zeros((REACH, EDGE, LANES), jnp.float32)
    wide = jnp.zeros((pad, EDGE, LANES), jnp.float32)
    for h in range(per):
        z_ref[h, 0:REACH] = none
        z_ref[h, REACH + total:REACH + total + REACH] = none
        f_ref[h, 0:pad] = wide
        f_ref[h, pad + total:pad + total + pad] = wide
    own = 1.0 - taps[0, REACH]
    own_wide = 1.0 - taps[1, REACH]
    others = [k for k in range(2 * REACH + 1) if k != REACH]

    def store(n):
        tile = first_tile + n * tile_step
        rows = pl.ds(pl.multiple_of(tile * EDGE, EDGE), EDGE)
        return pltpu.make_async_copy(out_ref.at[n], out.at[:, rows, :], out_sem.at[n])

    def one(n, carry):
        rows = pl.ds(pl.multiple_of(n * EDGE, EDGE), EDGE)
        for h in range(per):
            for k in range(parts):
                z_ref[h, pl.ds(REACH + (place[0] ^ k) * local, local)] = pieces[k][h, :, rows, :]

        def smooth(i, carry):
            t = i * step
            for h in range(per):
                z = z_ref[h, pl.ds(t, step + 2 * REACH)]
                kept = own * z[REACH:REACH + step]
                for k in others:
                    kept = kept - taps[0, k] * z[k:k + step]
                f_ref[h, pl.ds(pad + t, step)] = kept
            return carry

        def smooth_wide(i, carry):
            t = i * step
            for h in range(per):
                kept = own_wide * f_ref[h, pl.ds(pad + t, step)]
                for k in others:
                    kept = kept - taps[1, k] * f_ref[h, pl.ds(t + k * DILATION, step)]
                out_ref[n, pl.ds(t, step), :, h * LANES:(h + 1) * LANES] = kept
            return carry

        lax.fori_loop(0, total // step, smooth, 0)
        lax.fori_loop(0, total // step, smooth_wide, 0)
        store(n).start()
        return carry

    lax.fori_loop(0, count, one, 0)
    for n in range(count):
        store(n).wait()


def temporal(pieces, base, taps, place, first_tile, tile_step, rows):
    parts = len(pieces)
    per, local, here, _ = pieces[0].shape
    total = local * parts
    extra = [] if base is None else [base]
    count = here // EDGE
    width = per * LANES
    return pl.pallas_call(
        functools.partial(temporal_kernel, parts, len(extra), first_tile, tile_step),
        grid_spec=pltpu.PrefetchScalarGridSpec(
            num_scalar_prefetch=2,
            grid=(),
            in_specs=[pl.BlockSpec(memory_space=pltpu.VMEM)] * parts + [pl.BlockSpec(memory_space=pltpu.HBM)] * len(extra),
            out_specs=pl.BlockSpec(memory_space=pltpu.HBM),
            scratch_shapes=[
                pltpu.VMEM((per, total + 2 * REACH, EDGE, LANES), jnp.float32),
                pltpu.VMEM((per, total + 2 * REACH * DILATION, EDGE, LANES), jnp.float32),
                pltpu.VMEM((count, total, EDGE, width), jnp.float32),
                pltpu.SemaphoreType.DMA((count,)),
            ],
        ),
        out_shape=jax.ShapeDtypeStruct((total, rows, width), jnp.float32),
        input_output_aliases={} if base is None else {2 + parts: 0},
        compiler_params=params(24),
        cost_estimate=cost(2.5 + 0.4 * count),
    )(place, taps, *pieces, *extra)


def footprint_kernel(parts, feet, place, *rest):
    meta, vectors, rest = rest[:parts], rest[parts:2 * parts], rest[2 * parts:]
    inner, rim = rest[:parts], rest[parts:2 * parts]
    out_ref = rest[2 * parts]
    per, dates, rows, _ = inner[0].shape
    owners = out_ref.shape[0]
    lane = lax.broadcasted_iota(jnp.int32, (dates, LANES), 1)
    both = [jnp.concatenate([ref[n:n + 1, :] for ref in vectors], axis=1) for n in range(1, 4)]
    index = lax.broadcasted_iota(jnp.int32, both[0].shape, 1)
    source = (index // feet) ^ place[0]
    named = lax.broadcasted_iota(jnp.int32, (owners, index.shape[1]), 0) == both[1]
    places = []
    for block in range(parts):
        for slot in range(PAIR_CAP):
            hit = named & (source == block) & (both[2] == slot)
            places.append(jnp.where(hit, 1.0, 0.0).astype(jnp.bfloat16))
    places = jnp.concatenate(places, axis=0)
    tiles = []
    for first in range(0, parts * feet, LANES):
        total = jnp.zeros((dates, LANES), jnp.float32)
        for k in range(first // feet, -(-(first + LANES) // feet)):
            middle, ends = [ref.reshape(per * dates * ref.shape[2], LANES) for ref in (inner[k], rim[k])]

            def take(f, total):
                row, tile = meta[k][0, f] & 0xFFFF, meta[k][0, f] >> 16
                in_middle = (row >= EDGE) & (row < EDGE + rows)
                end_row = jnp.where(row < EDGE, row, jnp.clip(row - rows, 0, 2 * EDGE - 1))
                pixels = jnp.where(
                    in_middle,
                    middle[pl.ds(tile * dates * rows + jnp.clip(row - EDGE, 0, rows - 1), dates, stride=rows), :],
                    ends[pl.ds(tile * dates * 2 * EDGE + end_row, dates, stride=2 * EDGE), :])
                one = jnp.sum(jnp.where(lane < meta[k][1, f], pixels, 0.0), axis=1, keepdims=True)
                return jnp.where(lane == k * feet + f - first, one, total)

            total = lax.fori_loop(max(first - k * feet, 0), min(feet, first + LANES - k * feet), take, total, unroll=4)
        tiles.append(total)
    counts = jnp.broadcast_to(both[0].astype(jnp.float32), (dates, index.shape[1]))
    sums = jnp.concatenate([jnp.concatenate(tiles, axis=1), counts], axis=0)
    held = jnp.zeros((places.shape[0], 2 * dates), jnp.float32)
    for piece in split(sums, 3):
        held = held + lax.dot_general(places, piece, (((1,), (1,)), ((), ())), preferred_element_type=jnp.float32)
    for n in range(parts * PAIR_CAP):
        at = pl.ds(n * dates, dates)
        out_ref[:, 0, at] = held[n * owners:(n + 1) * owners, :dates]
        out_ref[:, 1, at] = held[n * owners:(n + 1) * owners, dates:]


def footprints(inner, rim, meta, place, owners):
    parts = len(inner)
    per, dates, inner_rows, _ = inner[0].shape
    feet = meta[0].shape[1]
    message = parts * PAIR_CAP * dates
    return pl.pallas_call(
        functools.partial(footprint_kernel, parts, feet),
        grid_spec=pltpu.PrefetchScalarGridSpec(
            num_scalar_prefetch=1 + parts,
            grid=(),
            in_specs=[pl.BlockSpec(memory_space=pltpu.VMEM)] * (3 * parts),
            out_specs=pl.BlockSpec(memory_space=pltpu.VMEM),
        ),
        out_shape=jax.ShapeDtypeStruct((owners, 2, message), jnp.float32),
        compiler_params=params(24),
        cost_estimate=cost(5),
    )(place, *meta, *meta, *inner, *rim)


def owner_kernel(parts, strips, taps, got_ref, anomaly_ref, series_ref):
    owners = parts * strips
    slots = owners * PAIR_CAP
    dates = got_ref.shape[2] // PAIR_CAP
    local = dates // parts
    sums, held = got_ref[:, 0, :], got_ref[:, 1, :]
    rows, weights = [], []
    for block in range(parts):
        for slot in range(PAIR_CAP):
            at = (block * PAIR_CAP + slot) * local
            rows.append(jnp.concatenate(
                [sums[e * strips:(e + 1) * strips, at:at + local] for e in range(parts)], axis=1))
            weights.append(held[0:strips, at:at + 1])
    sums = jnp.concatenate(rows, axis=0)
    weight = jnp.concatenate(weights, axis=0)
    shape = (dates, dates)
    lag = lax.broadcasted_iota(jnp.int32, shape, 0) - lax.broadcasted_iota(jnp.int32, shape, 1)
    for level, spacing in ((0, 1), (1, DILATION)):
        filt = jnp.where(lag == 0, 1.0, 0.0)
        for k in range(2 * REACH + 1):
            filt = filt - jnp.where(lag == (k - REACH) * spacing, taps[level, k], 0.0)
        sums = jnp.dot(sums, filt, precision=HIGHEST, preferred_element_type=jnp.float32)
    mean = sums / jnp.where(weight > 0, weight, 1.0)
    asset = jnp.sum(weight * mean, axis=0, keepdims=True) / jnp.sum(weight, axis=0, keepdims=True)
    odd = jnp.where(weight > 0, mean - asset, 0.0)
    series_ref[...] = asset
    shape = (slots, slots)
    to = lax.broadcasted_iota(jnp.int32, shape, 0)
    source = lax.broadcasted_iota(jnp.int32, shape, 1)
    block, rest = source // (PAIR_CAP * strips), source % (PAIR_CAP * strips)
    place_of = block * (PAIR_CAP * strips) + (rest % strips) * PAIR_CAP + rest // strips
    order = jnp.where(to == place_of, 1.0, 0.0)
    anomaly_ref[0] = jnp.dot(order, odd, precision=HIGHEST, preferred_element_type=jnp.float32)


def owner_series(got, taps, parts, strips):
    owners = parts * strips
    dates = got.shape[2] // PAIR_CAP
    slots = owners * PAIR_CAP
    return pl.pallas_call(
        functools.partial(owner_kernel, parts, strips),
        grid_spec=pltpu.PrefetchScalarGridSpec(
            num_scalar_prefetch=1,
            grid=(),
            in_specs=[pl.BlockSpec(memory_space=pltpu.VMEM)],
            out_specs=[pl.BlockSpec(memory_space=pltpu.VMEM)] * 2,
        ),
        out_shape=[
            jax.ShapeDtypeStruct((1, slots, dates), jnp.float32),
            jax.ShapeDtypeStruct((1, dates), jnp.float32),
        ],
        compiler_params=params(24),
        cost_estimate=cost(1.8),
    )(taps, got)


def spread_meta(meta, offset, swap):
    known = sorted(meta)
    got = swap(jnp.concatenate([meta[k] for k in known], axis=1), offset)
    width = meta[0].shape[1]
    return meta | {k ^ offset: got[:, n * width:(n + 1) * width] for n, k in enumerate(known)}


def shards(stack, spatial_taps, temporal_taps, foot_tile, foot_row, foot_count, foot_owner):
    parts, strips = lax.axis_size("date"), lax.axis_size("strip")
    place = lax.axis_index("date").astype(jnp.int32)[None]
    dates, rows, cols = stack.shape
    feet = foot_row.shape[0]
    owner = foot_owner[:, 0]
    position = jnp.arange(feet, dtype=jnp.int32)
    earlier = (owner[:, None] == owner[None, :]) & (position[None, :] < position[:, None])
    slot = jnp.sum(earlier.astype(jnp.int32), axis=1)
    own = jnp.stack([(foot_tile << 16) + foot_row, foot_count, owner, slot])

    def swap(value, offset):
        return lax.ppermute(value, "date", [(i, i ^ offset) for i in range(parts)])

    order = (*range(2, parts), 1, 0)
    inner, far_inner = {}, {}
    lead = order[0]
    inner[lead], brim, last_rows, first_rows, ends = interior(stack, None, spatial_taps, place, (lead,), 0, parts)
    far_inner[lead] = swap(inner[lead], lead)
    up = lax.ppermute(last_rows, "strip", [(i, i + 1) for i in range(strips - 1)])
    down = lax.ppermute(first_rows, "strip", [(i + 1, i) for i in range(strips - 1)])
    own, brim = lax.optimization_barrier((own, brim))
    meta = {0: own}
    for bit in range(parts.bit_length() - 2, 0, -1):
        meta = spread_meta(meta, 1 << bit, swap)
    *made, brim = interior(stack, brim, spatial_taps, place, order[1:], 1, parts)
    for n, offset in enumerate(order[1:]):
        inner[offset] = made[n]
        if offset > 1:
            far_inner[offset] = swap(inner[offset], offset)
    made = edges(ends, up, down, brim, spatial_taps, place, order)
    rim = dict(zip(order, made))
    known = sorted(meta)
    *held, inner[1], rim[0] = lax.optimization_barrier((*[meta[k] for k in known], inner[1], rim[0]))
    meta = spread_meta(dict(zip(known, held)), 1, swap)
    meta = [meta[k] for k in range(parts)]
    far_rim = {k: swap(rim[k], k) for k in order[:-1]}
    far_inner[1] = swap(inner[1], 1)
    rim = [rim[k] for k in range(parts)]
    sums = footprints([inner[k] for k in range(parts)], rim, meta, place, parts * strips)
    got = lax.all_to_all(sums, ("date", "strip"), split_axis=0, concat_axis=0, tiled=True)
    last = rows // EDGE - 1
    residual = temporal(
        [inner[0]] + [far_inner[k] for k in range(1, parts)], None, temporal_taps, place, 1, 1, rows)
    got, residual = lax.optimization_barrier((got, residual))
    anomaly, series = owner_series(got, temporal_taps, parts, strips)
    residual = temporal(
        [rim[0]] + [far_rim[k] for k in range(1, parts)], residual, temporal_taps, place, 0, last, rows)
    return residual, anomaly, series


def solution(mesh):
    placed = (
        P("date", "strip", None),
        P(),
        P(),
        P(("date", "strip")),
        P(("date", "strip")),
        P(("date", "strip")),
        P(("date", "strip"), None),
    )
    return jax.shard_map(
        shards,
        mesh=mesh,
        in_specs=placed,
        out_specs=(
            P(None, "strip", "date"),
            P(("date", "strip"), None, None),
            P(("date", "strip"), None),
        ),
        check_vma=False,
    )
```

```python
import functools

import jax
import jax.numpy as jnp
from jax import lax
from jax.experimental import pallas as pl
from jax.experimental.pallas import tpu as pltpu
from jax.sharding import PartitionSpec as P

TILE = 128
RADIUS = 6
REACH = 2
DILATION = 8
PAIR_CAP = 2
LANES = 128
EDGE = 8
HIGHEST = lax.Precision.HIGHEST


def params(mebibytes):
    return pltpu.CompilerParams(vmem_limit_bytes=mebibytes * 1024 * 1024)


def cost(micros):
    return pl.CostEstimate(flops=0, bytes_accessed=int(micros * 3.69e6), transcendentals=0)


def pick_taps(at, taps):
    count = taps.shape[0]
    total = taps[0]
    for k in range(1, count):
        total = total + taps[k]
    out = jnp.zeros(at.shape, jnp.float32)
    for k in range(count):
        out = jnp.where(at == k, taps[k], out)
    return out / jnp.full(at.shape, total, jnp.float32)


def split(value, count):
    out = []
    for _ in range(count):
        piece = value.astype(jnp.bfloat16)
        out.append(piece)
        value = value - piece.astype(jnp.float32)
    return out


def spread(value, axis):
    high, mid = split(value, 2)
    return jnp.concatenate([high, high, high, mid], axis=axis)


def fill_columns(col_ref, taps):
    shape = (LANES, LANES)
    lag = lax.broadcasted_iota(jnp.int32, shape, 0) - lax.broadcasted_iota(jnp.int32, shape, 1)
    near = split(pick_taps(lag + RADIUS, taps), 3)
    far = pick_taps(jnp.where(lag > 0, lag + RADIUS - LANES, lag + RADIUS + LANES), taps)
    above = split(jnp.where(lag > 0, far, 0.0), 3)
    below = split(jnp.where(lag > 0, 0.0, far), 3)
    for n, piece in enumerate((0, 1, 2, 0)):
        at = n * 3 * LANES
        for i, pair in enumerate(((near, above), (below, near), (above, below))):
            for j, block in enumerate(pair):
                col_ref[at + i * LANES:at + (i + 1) * LANES, j * LANES:(j + 1) * LANES] = block[piece]


def row_band(out_rows, in_rows, taps):
    shape = (out_rows, 4 * in_rows)
    lane = lax.broadcasted_iota(jnp.int32, shape, 1)
    row = lax.broadcasted_iota(jnp.int32, shape, 0)
    part = jnp.zeros(shape, jnp.int32)
    for n in range(1, 4):
        part = jnp.where(lane >= n * in_rows, n, part)
    return lane - part * in_rows, row, part


def pieces_of(values, part):
    high, mid, low = [p.astype(jnp.float32) for p in split(values, 3)]
    return jnp.where(part == 1, mid, jnp.where(part == 2, low, high)).astype(jnp.bfloat16)


def filter_columns(mid, rim, col):
    rows = mid.shape[0]
    window = jnp.concatenate([mid, rim], axis=1)
    return jnp.dot(spread(window, 1), col, preferred_element_type=jnp.float32)


def rim_tile(left, right, block, parts):
    lane = lax.broadcasted_iota(jnp.int32, left.shape, len(left.shape) - 1)
    first = lane < LANES // 2
    keep = (first & (block < parts - 1)) | (~first & (block > 0))
    return jnp.where(keep, jnp.where(first, right, left), 0.0)


def chosen(n, values):
    out = values[0]
    for m in range(1, len(values)):
        out = jnp.where(n == m, values[m], out)
    return out


def interior_kernel(offsets, slot, parts, group, place, taps, stack, *rest):
    count = len(offsets)
    first = slot == 0
    if not first:
        rest = rest[1:]
    outs, brim, rest = rest[:count], rest[count], rest[count + 1:]
    if first:
        up, down, ends, mid_ref, left_ref, right_ref, halo_ref, up_ref, down_ref, halo_sem, halo_out_sem, *rest = rest
    else:
        x_ref, *rest = rest
    out_ref, brim_ref, col_ref, row_ref, in_sem, out_sem, brim_sem = rest
    _, per, dates, inner, _ = out_ref.shape
    width = per * LANES
    rows = inner + 2 * EDGE
    cols = width * parts
    steps = dates // group

    def bounds(block):
        start = block * width
        places = start, jnp.maximum(start - LANES, 0), jnp.minimum(start + width, cols - LANES)
        return [pl.multiple_of(at, LANES) for at in places]

    def load(g):
        at = pl.ds(g * group, group)
        if not first:
            return [pltpu.make_async_copy(stack.at[at], x_ref.at[at], in_sem.at[0, g])]
        return [
            pltpu.make_async_copy(stack.at[at, :, pl.ds(start, ref.shape[2])], ref.at[at], in_sem.at[n, g])
            for n, (start, ref) in enumerate(zip(bounds(place[0] ^ offsets[0]), (mid_ref, left_ref, right_ref)))
        ]

    def store(m, g):
        at = pl.ds(g * group, group)
        return pltpu.make_async_copy(out_ref.at[m, :, at], outs[m].at[:, at], out_sem.at[m, g])

    def store_brim(n):
        return pltpu.make_async_copy(brim_ref.at[n], brim.at[slot + n], brim_sem.at[n])

    for g in range(steps):
        for copy in load(g):
            copy.start()
    halo_loads, halo_stores = [], []
    if first:
        halo_loads = [
            pltpu.make_async_copy(
                stack.at[:, pl.ds(side * (rows - EDGE), EDGE), pl.ds(c * LANES, LANES)],
                halo_ref.at[c, :, pl.ds(side * EDGE, EDGE), :], halo_sem.at[side, c])
            for side in range(2) for c in range(cols // LANES)
        ]
        halo_stores = [
            pltpu.make_async_copy(halo_ref, ends, halo_out_sem.at[0]),
            pltpu.make_async_copy(up_ref, up, halo_out_sem.at[1]),
            pltpu.make_async_copy(down_ref, down, halo_out_sem.at[2]),
        ]
        for copy in halo_loads:
            copy.start()
    fill_columns(col_ref, taps)
    q, r, part = row_band(inner, rows, taps)
    row_ref[...] = pieces_of(pick_taps(q - r - (EDGE - RADIUS), taps), part)

    def pack(c, carry):
        at = pl.ds(pl.multiple_of(c * LANES, LANES), LANES)
        rows_of = halo_ref.at[c].reshape(dates * 2 * EDGE, LANES)
        for r in range(RADIUS):
            up_ref[r, :, at] = rows_of[pl.ds(2 * EDGE - RADIUS + r, dates, stride=2 * EDGE), :]
            down_ref[r, :, at] = rows_of[pl.ds(r, dates, stride=2 * EDGE), :]
        return carry

    def step(i, carry):
        n, g = i // steps, i % steps
        block = place[0] ^ chosen(n, offsets)
        at = pl.ds(g * group, group)

        @pl.when(n == 0)
        def _():
            for copy in load(g):
                copy.wait()

        if first:
            @pl.when(i == steps - 1)
            def _():
                for copy in halo_loads:
                    copy.wait()
                lax.fori_loop(0, cols // LANES, pack, 0)
                for copy in halo_stores:
                    copy.start()

            mid, left, right = mid_ref[at], left_ref[at], right_ref[at]
        else:
            start, before, after = bounds(block)
            mid, left, right = [x_ref[at, :, pl.ds(f, w)] for f, w in ((start, width), (before, LANES), (after, LANES))]
        rim = rim_tile(left, right, block, parts)
        across = filter_columns(mid.reshape(group * rows, width), rim.reshape(group * rows, LANES), col_ref[...])
        for t in range(group):
            one = across[t * rows:(t + 1) * rows]
            low = jnp.dot(row_ref[...], spread(one, 0), preferred_element_type=jnp.float32)
            done = mid[t, EDGE:rows - EDGE, :] - low
            for h in range(per):
                out_ref[n, h, g * group + t] = done[:, h * LANES:(h + 1) * LANES]
                for side in range(2):
                    lines = one[side * (rows - 2 * EDGE):side * (rows - 2 * EDGE) + 2 * EDGE, h * LANES:(h + 1) * LANES]
                    brim_ref[n, h, pl.ds(side * 2 * EDGE * dates + g * group + t, 2 * EDGE, stride=dates), :] = lines
        for m in range(count):
            @pl.when(n == m)
            def _():
                store(m, g).start()

        @pl.when(g == steps - 1)
        def _():
            store_brim(n).start()

        return carry

    lax.fori_loop(0, count * steps, step, 0)
    for copy in halo_stores:
        copy.wait()
    for m in range(count):
        for g in range(steps):
            store(m, g).wait()
        store_brim(m).wait()


def interior(stack, brim, taps, place, offsets, slot, parts):
    dates, rows, cols = stack.shape
    width = cols // parts
    per = width // LANES
    group = min(8, dates)
    inner = rows - 2 * EDGE
    count = len(offsets)
    first = slot == 0
    here = pl.BlockSpec(memory_space=pltpu.HBM)
    out_shape = [jax.ShapeDtypeStruct((per, dates, inner, LANES), jnp.float32)] * count
    out_shape += [jax.ShapeDtypeStruct((parts, per, 4 * EDGE * dates, LANES), jnp.float32)]
    if first:
        out_shape += [jax.ShapeDtypeStruct((RADIUS, dates, cols), jnp.float32)] * 2
        out_shape += [jax.ShapeDtypeStruct((cols // LANES, dates, 2 * EDGE, LANES), jnp.float32)]
        scratch = [pltpu.VMEM((dates, rows, span), jnp.float32) for span in (width, LANES, LANES)] + [
            pltpu.VMEM((cols // LANES, dates, 2 * EDGE, LANES), jnp.float32),
            pltpu.VMEM((RADIUS, dates, cols), jnp.float32),
            pltpu.VMEM((RADIUS, dates, cols), jnp.float32),
            pltpu.SemaphoreType.DMA((2, cols // LANES)),
            pltpu.SemaphoreType.DMA((3,)),
        ]
    else:
        scratch = [pltpu.VMEM((dates, rows, cols), jnp.float32)]
    return pl.pallas_call(
        functools.partial(interior_kernel, offsets, slot, parts, group),
        grid_spec=pltpu.PrefetchScalarGridSpec(
            num_scalar_prefetch=2,
            grid=(),
            in_specs=[here] * (1 if first else 2),
            out_specs=[here] * len(out_shape),
            scratch_shapes=scratch + [
                pltpu.VMEM((count, per, dates, inner, LANES), jnp.float32),
                pltpu.VMEM((count, per, 4 * EDGE * dates, LANES), jnp.float32),
                pltpu.VMEM((12 * LANES, width), jnp.bfloat16),
                pltpu.VMEM((inner, 4 * rows), jnp.bfloat16),
                pltpu.SemaphoreType.DMA((3, dates // group)),
                pltpu.SemaphoreType.DMA((count, dates // group)),
                pltpu.SemaphoreType.DMA((count,)),
            ],
        ),
        out_shape=out_shape,
        input_output_aliases={} if first else {3: count},
        compiler_params=params(60),
        cost_estimate=cost(2.5 + 2.5 * count),
    )(place, taps, stack, *([] if first else [brim]))


def edge_kernel(order, place, taps, ends_ref, up_ref, down_ref, brim, *rest):
    parts = len(order)
    outs = rest[:parts]
    out_ref, across_ref, brim_ref, col_ref, brim_sem, out_sem = rest[parts:]
    _, dates, cols = up_ref.shape
    width = cols // parts
    per = width // LANES
    for n in range(parts):
        pltpu.make_async_copy(brim.at[n], brim_ref.at[n], brim_sem.at[n]).start()
    fill_columns(col_ref, taps)
    total = taps[0]
    for k in range(1, 2 * RADIUS + 1):
        total = total + taps[k]
    scale = 1.0 / jnp.full((dates, LANES), total, jnp.float32)
    flat = ends_ref.reshape(cols // LANES, dates * 2 * EDGE, LANES)

    def store(n):
        return pltpu.make_async_copy(out_ref.at[n], outs[n], out_sem.at[n])

    def one(n, carry):
        block = place[0] ^ chosen(n, order)
        start = pl.multiple_of(block * width, LANES)
        before = pl.multiple_of(jnp.maximum(start - LANES, 0), LANES)
        after = pl.multiple_of(jnp.minimum(start + width, cols - LANES), LANES)

        def both(first, span):
            at = pl.ds(first, span)
            return jnp.concatenate([up_ref[:, :, at], down_ref[:, :, at]], axis=0).reshape(2 * RADIUS * dates, span)

        rim = rim_tile(both(before, LANES), both(after, LANES), block, parts)
        across = filter_columns(both(start, width), rim, col_ref[...])
        for h in range(per):
            across_ref[h] = across[:, h * LANES:(h + 1) * LANES]
        lines = out_ref.at[n].reshape(per, dates * 2 * EDGE, LANES)
        pltpu.make_async_copy(brim.at[n], brim_ref.at[n], brim_sem.at[n]).wait()

        def half(h, carry):
            for side in range(2):
                held = []
                for q in range(2 * RADIUS + EDGE):
                    halo = q < RADIUS if side == 0 else q >= RADIUS + EDGE
                    if halo:
                        at = q if side == 0 else q - EDGE
                        held.append(across_ref[h, at * dates:(at + 1) * dates, :])
                    else:
                        at = q - RADIUS if side == 0 else 3 * EDGE - RADIUS + q
                        held.append(brim_ref[n, h, at * dates:(at + 1) * dates, :])
                for r in range(EDGE):
                    low = taps[0] * held[r]
                    for j in range(1, 2 * RADIUS + 1):
                        low = low + taps[j] * held[r + j]
                    at = pl.ds(side * EDGE + r, dates, stride=2 * EDGE)
                    lines[h, at, :] = flat[block * per + h, at, :] - scale * low
            return carry

        lax.fori_loop(0, per, half, 0)
        for m in range(parts):
            @pl.when(n == m)
            def _():
                store(m).start()
        return carry

    lax.fori_loop(0, parts, one, 0)
    for m in range(parts):
        store(m).wait()


def edges(ends, up, down, brim, taps, place, order):
    parts = len(order)
    tiles, dates, _, _ = ends.shape
    per = tiles // parts
    resident = pl.BlockSpec(memory_space=pltpu.VMEM)
    return pl.pallas_call(
        functools.partial(edge_kernel, order),
        grid_spec=pltpu.PrefetchScalarGridSpec(
            num_scalar_prefetch=2,
            grid=(),
            in_specs=[resident] * 3 + [pl.BlockSpec(memory_space=pltpu.HBM)],
            out_specs=[pl.BlockSpec(memory_space=pltpu.HBM)] * parts,
            scratch_shapes=[
                pltpu.VMEM((parts, per, dates, 2 * EDGE, LANES), jnp.float32),
                pltpu.VMEM((per, 2 * RADIUS * dates, LANES), jnp.float32),
                pltpu.VMEM((parts, per, 4 * EDGE * dates, LANES), jnp.float32),
                pltpu.VMEM((12 * LANES, per * LANES), jnp.bfloat16),
                pltpu.SemaphoreType.DMA((parts,)),
                pltpu.SemaphoreType.DMA((parts,)),
            ],
        ),
        out_shape=[jax.ShapeDtypeStruct((per, dates, 2 * EDGE, LANES), jnp.float32)] * parts,
        compiler_params=params(24),
        cost_estimate=cost(4),
    )(place, taps, ends, up, down, brim)


def temporal_kernel(parts, with_base, first_tile, tile_step, place, taps, *rest):
    pieces = rest[:parts]
    out, z_ref, f_ref, out_ref, out_sem = rest[parts + with_base:]
    count, total, _, _ = out_ref.shape
    per = pieces[0].shape[0]
    local = total // parts
    pad = REACH * DILATION
    step = 8
    none = jnp.zeros((REACH, EDGE, LANES), jnp.float32)
    wide = jnp.zeros((pad, EDGE, LANES), jnp.float32)
    for h in range(per):
        z_ref[h, 0:REACH] = none
        z_ref[h, REACH + total:REACH + total + REACH] = none
        f_ref[h, 0:pad] = wide
        f_ref[h, pad + total:pad + total + pad] = wide
    own = 1.0 - taps[0, REACH]
    own_wide = 1.0 - taps[1, REACH]
    others = [k for k in range(2 * REACH + 1) if k != REACH]

    def store(n):
        tile = first_tile + n * tile_step
        rows = pl.ds(pl.multiple_of(tile * EDGE, EDGE), EDGE)
        return pltpu.make_async_copy(out_ref.at[n], out.at[:, rows, :], out_sem.at[n])

    def one(n, carry):
        rows = pl.ds(pl.multiple_of(n * EDGE, EDGE), EDGE)
        for h in range(per):
            for k in range(parts):
                z_ref[h, pl.ds(REACH + (place[0] ^ k) * local, local)] = pieces[k][h, :, rows, :]

        for h in range(per):
            for t in range(0, total, step):
                z = z_ref[h, t:t + step + 2 * REACH]
                kept = own * z[REACH:REACH + step]
                for k in others:
                    kept = kept - taps[0, k] * z[k:k + step]
                f_ref[h, pad + t:pad + t + step] = kept
            for t in range(0, total, step):
                kept = own_wide * f_ref[h, pad + t:pad + t + step]
                for k in others:
                    kept = kept - taps[1, k] * f_ref[h, t + k * DILATION:t + k * DILATION + step]
                out_ref[n, t:t + step, :, h * LANES:(h + 1) * LANES] = kept
        store(n).start()
        return carry

    lax.fori_loop(0, count, one, 0)
    for n in range(count):
        store(n).wait()


def temporal(pieces, base, taps, place, first_tile, tile_step, rows):
    parts = len(pieces)
    per, local, here, _ = pieces[0].shape
    total = local * parts
    extra = [] if base is None else [base]
    count = here // EDGE
    width = per * LANES
    return pl.pallas_call(
        functools.partial(temporal_kernel, parts, len(extra), first_tile, tile_step),
        grid_spec=pltpu.PrefetchScalarGridSpec(
            num_scalar_prefetch=2,
            grid=(),
            in_specs=[pl.BlockSpec(memory_space=pltpu.VMEM)] * parts + [pl.BlockSpec(memory_space=pltpu.HBM)] * len(extra),
            out_specs=pl.BlockSpec(memory_space=pltpu.HBM),
            scratch_shapes=[
                pltpu.VMEM((per, total + 2 * REACH, EDGE, LANES), jnp.float32),
                pltpu.VMEM((per, total + 2 * REACH * DILATION, EDGE, LANES), jnp.float32),
                pltpu.VMEM((count, total, EDGE, width), jnp.float32),
                pltpu.SemaphoreType.DMA((count,)),
            ],
        ),
        out_shape=jax.ShapeDtypeStruct((total, rows, width), jnp.float32),
        input_output_aliases={} if base is None else {2 + parts: 0},
        compiler_params=params(24),
        cost_estimate=cost(2.5 + 0.4 * count),
    )(place, taps, *pieces, *extra)


def footprint_kernel(parts, feet, place, *rest):
    meta, vectors, rest = rest[:parts], rest[parts:2 * parts], rest[2 * parts:]
    inner, rim = rest[:parts], rest[parts:2 * parts]
    out_ref, v_ref = rest[2 * parts:]
    per, dates, rows, _ = inner[0].shape
    owners = out_ref.shape[0]
    lane = lax.broadcasted_iota(jnp.int32, (dates, LANES), 1)
    both = [jnp.concatenate([ref[n:n + 1, :] for ref in vectors], axis=1) for n in range(1, 4)]
    index = lax.broadcasted_iota(jnp.int32, both[0].shape, 1)
    source = (index // feet) ^ place[0]
    named = lax.broadcasted_iota(jnp.int32, (owners, index.shape[1]), 0) == both[1]
    places = []
    for block in range(parts):
        for slot in range(PAIR_CAP):
            hit = named & (source == block) & (both[2] == slot)
            places.append(jnp.where(hit, 1.0, 0.0).astype(jnp.bfloat16))
    places = jnp.concatenate(places, axis=0)
    for k in range(parts):
        middle, ends = [ref.reshape(per * dates * ref.shape[2], LANES) for ref in (inner[k], rim[k])]

        def take(f, carry):
            row, tile = meta[k][0, f] & 0xFFFF, meta[k][0, f] >> 16
            in_middle = (row >= EDGE) & (row < EDGE + rows)
            end_row = jnp.where(row < EDGE, row, jnp.clip(row - rows, 0, 2 * EDGE - 1))
            pixels = jnp.where(
                in_middle,
                middle[pl.ds(tile * dates * rows + jnp.clip(row - EDGE, 0, rows - 1), dates, stride=rows), :],
                ends[pl.ds(tile * dates * 2 * EDGE + end_row, dates, stride=2 * EDGE), :])
            v_ref[k * feet + f] = jnp.where(lane < meta[k][1, f], pixels, 0.0)
            return carry

        lax.fori_loop(0, feet, take, 0, unroll=8)
    tiles = []
    for first in range(0, parts * feet, LANES):

        def add(f, total):
            one = jnp.sum(v_ref[first + f], axis=1, keepdims=True)
            return jnp.where(lane == f, one, total)

        tiles.append(lax.fori_loop(0, LANES, add, jnp.zeros((dates, LANES), jnp.float32), unroll=32))
    counts = jnp.broadcast_to(both[0].astype(jnp.float32), (dates, index.shape[1]))
    sums = jnp.concatenate([jnp.concatenate(tiles, axis=1), counts], axis=0)
    held = jnp.zeros((places.shape[0], 2 * dates), jnp.float32)
    for piece in split(sums, 3):
        held = held + lax.dot_general(places, piece, (((1,), (1,)), ((), ())), preferred_element_type=jnp.float32)
    for n in range(parts * PAIR_CAP):
        at = pl.ds(n * dates, dates)
        out_ref[:, 0, at] = held[n * owners:(n + 1) * owners, :dates]
        out_ref[:, 1, at] = held[n * owners:(n + 1) * owners, dates:]


def footprints(inner, rim, meta, place, owners):
    parts = len(inner)
    per, dates, inner_rows, _ = inner[0].shape
    feet = meta[0].shape[1]
    message = parts * PAIR_CAP * dates
    return pl.pallas_call(
        functools.partial(footprint_kernel, parts, feet),
        grid_spec=pltpu.PrefetchScalarGridSpec(
            num_scalar_prefetch=1 + parts,
            grid=(),
            in_specs=[pl.BlockSpec(memory_space=pltpu.VMEM)] * (3 * parts),
            out_specs=pl.BlockSpec(memory_space=pltpu.VMEM),
            scratch_shapes=[pltpu.VMEM((parts * feet, dates, LANES), jnp.float32)],
        ),
        out_shape=jax.ShapeDtypeStruct((owners, 2, message), jnp.float32),
        compiler_params=params(24),
        cost_estimate=cost(5),
    )(place, *meta, *meta, *inner, *rim)


def owner_kernel(parts, strips, taps, got_ref, anomaly_ref, series_ref):
    owners = parts * strips
    slots = owners * PAIR_CAP
    dates = got_ref.shape[2] // PAIR_CAP
    local = dates // parts
    sums, held = got_ref[:, 0, :], got_ref[:, 1, :]
    rows, weights = [], []
    for block in range(parts):
        for slot in range(PAIR_CAP):
            at = (block * PAIR_CAP + slot) * local
            rows.append(jnp.concatenate(
                [sums[e * strips:(e + 1) * strips, at:at + local] for e in range(parts)], axis=1))
            weights.append(held[0:strips, at:at + 1])
    sums = jnp.concatenate(rows, axis=0)
    weight = jnp.concatenate(weights, axis=0)
    shape = (dates, dates)
    lag = lax.broadcasted_iota(jnp.int32, shape, 0) - lax.broadcasted_iota(jnp.int32, shape, 1)
    for level, spacing in ((0, 1), (1, DILATION)):
        filt = jnp.where(lag == 0, 1.0, 0.0)
        for k in range(2 * REACH + 1):
            filt = filt - jnp.where(lag == (k - REACH) * spacing, taps[level, k], 0.0)
        sums = jnp.dot(sums, filt, precision=HIGHEST, preferred_element_type=jnp.float32)
    mean = sums / jnp.where(weight > 0, weight, 1.0)
    asset = jnp.sum(weight * mean, axis=0, keepdims=True) / jnp.sum(weight, axis=0, keepdims=True)
    odd = jnp.where(weight > 0, mean - asset, 0.0)
    series_ref[...] = asset
    shape = (slots, slots)
    to = lax.broadcasted_iota(jnp.int32, shape, 0)
    source = lax.broadcasted_iota(jnp.int32, shape, 1)
    block, rest = source // (PAIR_CAP * strips), source % (PAIR_CAP * strips)
    place_of = block * (PAIR_CAP * strips) + (rest % strips) * PAIR_CAP + rest // strips
    order = jnp.where(to == place_of, 1.0, 0.0)
    anomaly_ref[0] = jnp.dot(order, odd, precision=HIGHEST, preferred_element_type=jnp.float32)


def owner_series(got, taps, parts, strips):
    owners = parts * strips
    dates = got.shape[2] // PAIR_CAP
    slots = owners * PAIR_CAP
    return pl.pallas_call(
        functools.partial(owner_kernel, parts, strips),
        grid_spec=pltpu.PrefetchScalarGridSpec(
            num_scalar_prefetch=1,
            grid=(),
            in_specs=[pl.BlockSpec(memory_space=pltpu.VMEM)],
            out_specs=[pl.BlockSpec(memory_space=pltpu.VMEM)] * 2,
        ),
        out_shape=[
            jax.ShapeDtypeStruct((1, slots, dates), jnp.float32),
            jax.ShapeDtypeStruct((1, dates), jnp.float32),
        ],
        compiler_params=params(24),
        cost_estimate=cost(1.8),
    )(taps, got)


def spread_meta(meta, offset, swap):
    known = sorted(meta)
    got = swap(jnp.concatenate([meta[k] for k in known], axis=1), offset)
    width = meta[0].shape[1]
    return meta | {k ^ offset: got[:, n * width:(n + 1) * width] for n, k in enumerate(known)}


def shards(stack, spatial_taps, temporal_taps, foot_tile, foot_row, foot_count, foot_owner):
    parts, strips = lax.axis_size("date"), lax.axis_size("strip")
    place = lax.axis_index("date").astype(jnp.int32)[None]
    dates, rows, cols = stack.shape
    feet = foot_row.shape[0]
    owner = foot_owner[:, 0]
    position = jnp.arange(feet, dtype=jnp.int32)
    earlier = (owner[:, None] == owner[None, :]) & (position[None, :] < position[:, None])
    slot = jnp.sum(earlier.astype(jnp.int32), axis=1)
    own = jnp.stack([(foot_tile << 16) + foot_row, foot_count, owner, slot])

    def swap(value, offset):
        return lax.ppermute(value, "date", [(i, i ^ offset) for i in range(parts)])

    order = (*range(2, parts), 1, 0)
    inner, far_inner = {}, {}
    lead = order[0]
    inner[lead], brim, last_rows, first_rows, ends = interior(stack, None, spatial_taps, place, (lead,), 0, parts)
    far_inner[lead] = swap(inner[lead], lead)
    up = lax.ppermute(last_rows, "strip", [(i, i + 1) for i in range(strips - 1)])
    down = lax.ppermute(first_rows, "strip", [(i + 1, i) for i in range(strips - 1)])
    own, brim = lax.optimization_barrier((own, brim))
    meta = {0: own}
    for bit in range(parts.bit_length() - 2, 0, -1):
        meta = spread_meta(meta, 1 << bit, swap)
    *made, brim = interior(stack, brim, spatial_taps, place, order[1:], 1, parts)
    for n, offset in enumerate(order[1:]):
        inner[offset] = made[n]
        if offset > 1:
            far_inner[offset] = swap(inner[offset], offset)
    known = sorted(meta)
    *held, far_inner[lead], ends = lax.optimization_barrier((*[meta[k] for k in known], far_inner[lead], ends))
    meta = spread_meta(dict(zip(known, held)), 1, swap)
    made = edges(ends, up, down, brim, spatial_taps, place, order)
    rim = dict(zip(order, made))
    inner[1], rim[0] = lax.optimization_barrier((inner[1], rim[0]))
    meta = [meta[k] for k in range(parts)]
    far_rim = {k: swap(rim[k], k) for k in order[:-1]}
    far_inner[1] = swap(inner[1], 1)
    rim = [rim[k] for k in range(parts)]
    sums = footprints([inner[k] for k in range(parts)], rim, meta, place, parts * strips)
    got = lax.all_to_all(sums, ("date", "strip"), split_axis=0, concat_axis=0, tiled=True)
    last = rows // EDGE - 1
    residual = temporal(
        [inner[0]] + [far_inner[k] for k in range(1, parts)], None, temporal_taps, place, 1, 1, rows)
    got, residual = lax.optimization_barrier((got, residual))
    anomaly, series = owner_series(got, temporal_taps, parts, strips)
    residual = temporal(
        [rim[0]] + [far_rim[k] for k in range(1, parts)], residual, temporal_taps, place, 0, last, rows)
    return residual, anomaly, series


def solution(mesh):
    placed = (
        P("date", "strip", None),
        P(),
        P(),
        P(("date", "strip")),
        P(("date", "strip")),
        P(("date", "strip")),
        P(("date", "strip"), None),
    )
    return jax.shard_map(
        shards,
        mesh=mesh,
        in_specs=placed,
        out_specs=(
            P(None, "strip", "date"),
            P(("date", "strip"), None, None),
            P(("date", "strip"), None),
        ),
        check_vma=False,
    )
```

```python
import functools

import jax
import jax.numpy as jnp
from jax import lax
from jax.experimental import pallas as pl
from jax.experimental.pallas import tpu as pltpu
from jax.sharding import PartitionSpec as P

TILE = 128
RADIUS = 6
REACH = 2
DILATION = 8
PAIR_CAP = 2
LANES = 128
EDGE = 8
HIGHEST = lax.Precision.HIGHEST


def params(mebibytes):
    return pltpu.CompilerParams(vmem_limit_bytes=mebibytes * 1024 * 1024)


def cost(micros):
    return pl.CostEstimate(flops=0, bytes_accessed=int(micros * 3.69e6), transcendentals=0)


def pick_taps(at, taps):
    count = taps.shape[0]
    total = taps[0]
    for k in range(1, count):
        total = total + taps[k]
    out = jnp.zeros(at.shape, jnp.float32)
    for k in range(count):
        out = jnp.where(at == k, taps[k], out)
    return out / jnp.full(at.shape, total, jnp.float32)


def split(value, count):
    out = []
    for _ in range(count):
        piece = value.astype(jnp.bfloat16)
        out.append(piece)
        value = value - piece.astype(jnp.float32)
    return out


def spread(value, axis):
    high, mid = split(value, 2)
    return jnp.concatenate([high, high, high, mid], axis=axis)


def fill_columns(col_ref, taps):
    shape = (LANES, LANES)
    lag = lax.broadcasted_iota(jnp.int32, shape, 0) - lax.broadcasted_iota(jnp.int32, shape, 1)
    near = split(pick_taps(lag + RADIUS, taps), 3)
    far = pick_taps(jnp.where(lag > 0, lag + RADIUS - LANES, lag + RADIUS + LANES), taps)
    above = split(jnp.where(lag > 0, far, 0.0), 3)
    below = split(jnp.where(lag > 0, 0.0, far), 3)
    for n, piece in enumerate((0, 1, 2, 0)):
        at = n * 3 * LANES
        for i, pair in enumerate(((near, above), (below, near), (above, below))):
            for j, block in enumerate(pair):
                col_ref[at + i * LANES:at + (i + 1) * LANES, j * LANES:(j + 1) * LANES] = block[piece]


def row_band(out_rows, in_rows, taps):
    shape = (out_rows, 4 * in_rows)
    lane = lax.broadcasted_iota(jnp.int32, shape, 1)
    row = lax.broadcasted_iota(jnp.int32, shape, 0)
    part = jnp.zeros(shape, jnp.int32)
    for n in range(1, 4):
        part = jnp.where(lane >= n * in_rows, n, part)
    return lane - part * in_rows, row, part


def pieces_of(values, part):
    high, mid, low = [p.astype(jnp.float32) for p in split(values, 3)]
    return jnp.where(part == 1, mid, jnp.where(part == 2, low, high)).astype(jnp.bfloat16)


def filter_columns(mid, rim, col):
    rows = mid.shape[0]
    window = jnp.concatenate([mid, rim], axis=1)
    return jnp.dot(spread(window, 1), col, preferred_element_type=jnp.float32)


def rim_tile(left, right, block, parts):
    lane = lax.broadcasted_iota(jnp.int32, left.shape, len(left.shape) - 1)
    first = lane < LANES // 2
    keep = (first & (block < parts - 1)) | (~first & (block > 0))
    return jnp.where(keep, jnp.where(first, right, left), 0.0)


def chosen(n, values):
    out = values[0]
    for m in range(1, len(values)):
        out = jnp.where(n == m, values[m], out)
    return out


def interior_kernel(offsets, slot, parts, group, place, taps, stack, *rest):
    count = len(offsets)
    first = slot == 0
    if not first:
        rest = rest[1:]
    outs, brim, rest = rest[:count], rest[count], rest[count + 1:]
    if first:
        up, down, ends, mid_ref, left_ref, right_ref, halo_ref, up_ref, down_ref, halo_sem, halo_out_sem, *rest = rest
    else:
        x_ref, *rest = rest
    out_ref, brim_ref, col_ref, row_ref, in_sem, out_sem, brim_sem = rest
    _, per, dates, inner, _ = out_ref.shape
    width = per * LANES
    rows = inner + 2 * EDGE
    cols = width * parts
    steps = dates // group

    def bounds(block):
        start = block * width
        places = start, jnp.maximum(start - LANES, 0), jnp.minimum(start + width, cols - LANES)
        return [pl.multiple_of(at, LANES) for at in places]

    def load(g):
        at = pl.ds(g * group, group)
        if not first:
            return [pltpu.make_async_copy(stack.at[at], x_ref.at[at], in_sem.at[0, g])]
        return [
            pltpu.make_async_copy(stack.at[at, :, pl.ds(start, ref.shape[2])], ref.at[at], in_sem.at[n, g])
            for n, (start, ref) in enumerate(zip(bounds(place[0] ^ offsets[0]), (mid_ref, left_ref, right_ref)))
        ]

    def store(m, g):
        at = pl.ds(g * group, group)
        return pltpu.make_async_copy(out_ref.at[m, :, at], outs[m].at[:, at], out_sem.at[m, g])

    def store_brim(n):
        return pltpu.make_async_copy(brim_ref.at[n], brim.at[slot + n], brim_sem.at[n])

    for g in range(steps):
        for copy in load(g):
            copy.start()
    halo_loads, halo_stores = [], []
    if first:
        halo_loads = [
            pltpu.make_async_copy(
                stack.at[:, pl.ds(side * (rows - EDGE), EDGE), pl.ds(c * LANES, LANES)],
                halo_ref.at[c, :, pl.ds(side * EDGE, EDGE), :], halo_sem.at[side, c])
            for side in range(2) for c in range(cols // LANES)
        ]
        halo_stores = [
            pltpu.make_async_copy(halo_ref, ends, halo_out_sem.at[0]),
            pltpu.make_async_copy(up_ref, up, halo_out_sem.at[1]),
            pltpu.make_async_copy(down_ref, down, halo_out_sem.at[2]),
        ]
        for copy in halo_loads:
            copy.start()
    fill_columns(col_ref, taps)
    q, r, part = row_band(inner, rows, taps)
    row_ref[...] = pieces_of(pick_taps(q - r - (EDGE - RADIUS), taps), part)

    def pack(c, carry):
        at = pl.ds(pl.multiple_of(c * LANES, LANES), LANES)
        rows_of = halo_ref.at[c].reshape(dates * 2 * EDGE, LANES)
        for r in range(RADIUS):
            up_ref[r, :, at] = rows_of[pl.ds(2 * EDGE - RADIUS + r, dates, stride=2 * EDGE), :]
            down_ref[r, :, at] = rows_of[pl.ds(r, dates, stride=2 * EDGE), :]
        return carry

    def step(i, carry):
        n, g = i // steps, i % steps
        block = place[0] ^ chosen(n, offsets)
        at = pl.ds(g * group, group)

        @pl.when(n == 0)
        def _():
            for copy in load(g):
                copy.wait()

        if first:
            @pl.when(i == steps - 1)
            def _():
                for copy in halo_loads:
                    copy.wait()
                lax.fori_loop(0, cols // LANES, pack, 0)
                for copy in halo_stores:
                    copy.start()

            mid, left, right = mid_ref[at], left_ref[at], right_ref[at]
        else:
            start, before, after = bounds(block)
            mid, left, right = [x_ref[at, :, pl.ds(f, w)] for f, w in ((start, width), (before, LANES), (after, LANES))]
        rim = rim_tile(left, right, block, parts)
        across = filter_columns(mid.reshape(group * rows, width), rim.reshape(group * rows, LANES), col_ref[...])
        for t in range(group):
            one = across[t * rows:(t + 1) * rows]
            low = jnp.dot(row_ref[...], spread(one, 0), preferred_element_type=jnp.float32)
            done = mid[t, EDGE:rows - EDGE, :] - low
            for h in range(per):
                out_ref[n, h, g * group + t] = done[:, h * LANES:(h + 1) * LANES]
                for side in range(2):
                    lines = one[side * (rows - 2 * EDGE):side * (rows - 2 * EDGE) + 2 * EDGE, h * LANES:(h + 1) * LANES]
                    brim_ref[n, h, pl.ds(side * 2 * EDGE * dates + g * group + t, 2 * EDGE, stride=dates), :] = lines
        for m in range(count):
            @pl.when(n == m)
            def _():
                store(m, g).start()

        @pl.when(g == steps - 1)
        def _():
            store_brim(n).start()

        return carry

    lax.fori_loop(0, count * steps, step, 0)
    for copy in halo_stores:
        copy.wait()
    for m in range(count):
        for g in range(steps):
            store(m, g).wait()
        store_brim(m).wait()


def interior(stack, brim, taps, place, offsets, slot, parts):
    dates, rows, cols = stack.shape
    width = cols // parts
    per = width // LANES
    group = min(8, dates)
    inner = rows - 2 * EDGE
    count = len(offsets)
    first = slot == 0
    here = pl.BlockSpec(memory_space=pltpu.HBM)
    out_shape = [jax.ShapeDtypeStruct((per, dates, inner, LANES), jnp.float32)] * count
    out_shape += [jax.ShapeDtypeStruct((parts, per, 4 * EDGE * dates, LANES), jnp.float32)]
    if first:
        out_shape += [jax.ShapeDtypeStruct((RADIUS, dates, cols), jnp.float32)] * 2
        out_shape += [jax.ShapeDtypeStruct((cols // LANES, dates, 2 * EDGE, LANES), jnp.float32)]
        scratch = [pltpu.VMEM((dates, rows, span), jnp.float32) for span in (width, LANES, LANES)] + [
            pltpu.VMEM((cols // LANES, dates, 2 * EDGE, LANES), jnp.float32),
            pltpu.VMEM((RADIUS, dates, cols), jnp.float32),
            pltpu.VMEM((RADIUS, dates, cols), jnp.float32),
            pltpu.SemaphoreType.DMA((2, cols // LANES)),
            pltpu.SemaphoreType.DMA((3,)),
        ]
    else:
        scratch = [pltpu.VMEM((dates, rows, cols), jnp.float32)]
    return pl.pallas_call(
        functools.partial(interior_kernel, offsets, slot, parts, group),
        grid_spec=pltpu.PrefetchScalarGridSpec(
            num_scalar_prefetch=2,
            grid=(),
            in_specs=[here] * (1 if first else 2),
            out_specs=[here] * len(out_shape),
            scratch_shapes=scratch + [
                pltpu.VMEM((count, per, dates, inner, LANES), jnp.float32),
                pltpu.VMEM((count, per, 4 * EDGE * dates, LANES), jnp.float32),
                pltpu.VMEM((12 * LANES, width), jnp.bfloat16),
                pltpu.VMEM((inner, 4 * rows), jnp.bfloat16),
                pltpu.SemaphoreType.DMA((3, dates // group)),
                pltpu.SemaphoreType.DMA((count, dates // group)),
                pltpu.SemaphoreType.DMA((count,)),
            ],
        ),
        out_shape=out_shape,
        input_output_aliases={} if first else {3: count},
        compiler_params=params(63),
        cost_estimate=cost(2.5 + 2.5 * count),
    )(place, taps, stack, *([] if first else [brim]))


def edge_kernel(order, place, taps, ends, up, down, brim, *rest):
    parts = len(order)
    outs = rest[:parts]
    out_ref, across_ref, brim_ref, up_ref, down_ref, ends_ref, col_ref, halo_sem, brim_sem, out_sem = rest[parts:]
    _, dates, cols = up_ref.shape
    width = cols // parts
    per = width // LANES
    halos = [
        pltpu.make_async_copy(whole, ref, halo_sem.at[n])
        for n, (whole, ref) in enumerate(((up, up_ref), (down, down_ref), (ends, ends_ref)))
    ]
    for copy in halos:
        copy.start()
    for n in range(parts):
        pltpu.make_async_copy(brim.at[n], brim_ref.at[n], brim_sem.at[n]).start()
    fill_columns(col_ref, taps)
    total = taps[0]
    for k in range(1, 2 * RADIUS + 1):
        total = total + taps[k]
    scale = 1.0 / jnp.full((dates, LANES), total, jnp.float32)
    flat = ends_ref.reshape(cols // LANES, dates * 2 * EDGE, LANES)

    def store(n):
        return pltpu.make_async_copy(out_ref.at[n], outs[n], out_sem.at[n])

    for copy in halos:
        copy.wait()

    def one(n, carry):
        block = place[0] ^ chosen(n, order)
        start = pl.multiple_of(block * width, LANES)
        before = pl.multiple_of(jnp.maximum(start - LANES, 0), LANES)
        after = pl.multiple_of(jnp.minimum(start + width, cols - LANES), LANES)

        def both(first, span):
            at = pl.ds(first, span)
            return jnp.concatenate([up_ref[:, :, at], down_ref[:, :, at]], axis=0).reshape(2 * RADIUS * dates, span)

        rim = rim_tile(both(before, LANES), both(after, LANES), block, parts)
        across = filter_columns(both(start, width), rim, col_ref[...])
        for h in range(per):
            across_ref[h] = across[:, h * LANES:(h + 1) * LANES]
        lines = out_ref.at[n].reshape(per, dates * 2 * EDGE, LANES)
        pltpu.make_async_copy(brim.at[n], brim_ref.at[n], brim_sem.at[n]).wait()

        def half(h, carry):
            for side in range(2):
                held = []
                for q in range(2 * RADIUS + EDGE):
                    halo = q < RADIUS if side == 0 else q >= RADIUS + EDGE
                    if halo:
                        at = q if side == 0 else q - EDGE
                        held.append(across_ref[h, at * dates:(at + 1) * dates, :])
                    else:
                        at = q - RADIUS if side == 0 else 3 * EDGE - RADIUS + q
                        held.append(brim_ref[n, h, at * dates:(at + 1) * dates, :])
                for r in range(EDGE):
                    low = taps[0] * held[r]
                    for j in range(1, 2 * RADIUS + 1):
                        low = low + taps[j] * held[r + j]
                    at = pl.ds(side * EDGE + r, dates, stride=2 * EDGE)
                    lines[h, at, :] = flat[block * per + h, at, :] - scale * low
            return carry

        lax.fori_loop(0, per, half, 0)
        for m in range(parts):
            @pl.when(n == m)
            def _():
                store(m).start()
        return carry

    lax.fori_loop(0, parts, one, 0)
    for m in range(parts):
        store(m).wait()


def edges(ends, up, down, brim, taps, place, order):
    parts = len(order)
    tiles, dates, _, _ = ends.shape
    per = tiles // parts
    here = pl.BlockSpec(memory_space=pltpu.HBM)
    return pl.pallas_call(
        functools.partial(edge_kernel, order),
        grid_spec=pltpu.PrefetchScalarGridSpec(
            num_scalar_prefetch=2,
            grid=(),
            in_specs=[here] * 4,
            out_specs=[here] * parts,
            scratch_shapes=[
                pltpu.VMEM((parts, per, dates, 2 * EDGE, LANES), jnp.float32),
                pltpu.VMEM((per, 2 * RADIUS * dates, LANES), jnp.float32),
                pltpu.VMEM((parts, per, 4 * EDGE * dates, LANES), jnp.float32),
                pltpu.VMEM(up.shape, jnp.float32),
                pltpu.VMEM(up.shape, jnp.float32),
                pltpu.VMEM(ends.shape, jnp.float32),
                pltpu.VMEM((12 * LANES, per * LANES), jnp.bfloat16),
                pltpu.SemaphoreType.DMA((3,)),
                pltpu.SemaphoreType.DMA((parts,)),
                pltpu.SemaphoreType.DMA((parts,)),
            ],
        ),
        out_shape=[jax.ShapeDtypeStruct((per, dates, 2 * EDGE, LANES), jnp.float32)] * parts,
        compiler_params=params(63),
        cost_estimate=cost(4),
    )(place, taps, ends, up, down, brim)


def temporal_kernel(parts, with_base, first_tile, tile_step, place, taps, *rest):
    pieces = rest[:parts]
    out, z_ref, f_ref, out_ref, out_sem = rest[parts + with_base:]
    count, total, _, _ = out_ref.shape
    per = pieces[0].shape[0]
    local = total // parts
    pad = REACH * DILATION
    step = 8
    none = jnp.zeros((REACH, EDGE, LANES), jnp.float32)
    wide = jnp.zeros((pad, EDGE, LANES), jnp.float32)
    for h in range(per):
        z_ref[h, 0:REACH] = none
        z_ref[h, REACH + total:REACH + total + REACH] = none
        f_ref[h, 0:pad] = wide
        f_ref[h, pad + total:pad + total + pad] = wide
    own = 1.0 - taps[0, REACH]
    own_wide = 1.0 - taps[1, REACH]
    others = [k for k in range(2 * REACH + 1) if k != REACH]

    def store(n):
        tile = first_tile + n * tile_step
        rows = pl.ds(pl.multiple_of(tile * EDGE, EDGE), EDGE)
        return pltpu.make_async_copy(out_ref.at[n], out.at[:, rows, :], out_sem.at[n])

    def one(n, carry):
        rows = pl.ds(pl.multiple_of(n * EDGE, EDGE), EDGE)
        for h in range(per):
            for k in range(parts):
                z_ref[h, pl.ds(REACH + (place[0] ^ k) * local, local)] = pieces[k][h, :, rows, :]

        for h in range(per):
            for t in range(0, total, step):
                z = z_ref[h, t:t + step + 2 * REACH]
                kept = own * z[REACH:REACH + step]
                for k in others:
                    kept = kept - taps[0, k] * z[k:k + step]
                f_ref[h, pad + t:pad + t + step] = kept
            for t in range(0, total, step):
                kept = own_wide * f_ref[h, pad + t:pad + t + step]
                for k in others:
                    kept = kept - taps[1, k] * f_ref[h, t + k * DILATION:t + k * DILATION + step]
                out_ref[n, t:t + step, :, h * LANES:(h + 1) * LANES] = kept
        store(n).start()
        return carry

    lax.fori_loop(0, count, one, 0)
    for n in range(count):
        store(n).wait()


def temporal(pieces, base, taps, place, first_tile, tile_step, rows):
    parts = len(pieces)
    per, local, here, _ = pieces[0].shape
    total = local * parts
    extra = [] if base is None else [base]
    count = here // EDGE
    width = per * LANES
    return pl.pallas_call(
        functools.partial(temporal_kernel, parts, len(extra), first_tile, tile_step),
        grid_spec=pltpu.PrefetchScalarGridSpec(
            num_scalar_prefetch=2,
            grid=(),
            in_specs=[pl.BlockSpec(memory_space=pltpu.VMEM)] * parts + [pl.BlockSpec(memory_space=pltpu.HBM)] * len(extra),
            out_specs=pl.BlockSpec(memory_space=pltpu.HBM),
            scratch_shapes=[
                pltpu.VMEM((per, total + 2 * REACH, EDGE, LANES), jnp.float32),
                pltpu.VMEM((per, total + 2 * REACH * DILATION, EDGE, LANES), jnp.float32),
                pltpu.VMEM((count, total, EDGE, width), jnp.float32),
                pltpu.SemaphoreType.DMA((count,)),
            ],
        ),
        out_shape=jax.ShapeDtypeStruct((total, rows, width), jnp.float32),
        input_output_aliases={} if base is None else {2 + parts: 0},
        compiler_params=params(24),
        cost_estimate=cost(2.5 + 0.4 * count),
    )(place, taps, *pieces, *extra)


def footprint_kernel(parts, feet, place, *rest):
    meta, vectors, rest = rest[:parts], rest[parts:2 * parts], rest[2 * parts:]
    inner, rim = rest[:parts], rest[parts:2 * parts]
    out_ref, v_ref, x_ref, sem = rest[2 * parts:]
    _, per, dates, rows, _ = x_ref.shape
    owners = out_ref.shape[0]
    copies = [
        [
            pltpu.make_async_copy(inner[k], x_ref.at[k, :, :, pl.ds(EDGE, rows - 2 * EDGE), :], sem.at[k, 0]),
            pltpu.make_async_copy(rim[k].at[:, :, pl.ds(0, EDGE), :], x_ref.at[k, :, :, pl.ds(0, EDGE), :], sem.at[k, 1]),
            pltpu.make_async_copy(
                rim[k].at[:, :, pl.ds(EDGE, EDGE), :], x_ref.at[k, :, :, pl.ds(rows - EDGE, EDGE), :], sem.at[k, 2]),
        ]
        for k in range(parts)
    ]
    for k in range(parts):
        for copy in copies[k]:
            copy.start()
    lane = lax.broadcasted_iota(jnp.int32, (dates, LANES), 1)
    both = [jnp.concatenate([ref[n:n + 1, :] for ref in vectors], axis=1) for n in range(1, 4)]
    index = lax.broadcasted_iota(jnp.int32, both[0].shape, 1)
    source = (index // feet) ^ place[0]
    named = lax.broadcasted_iota(jnp.int32, (owners, index.shape[1]), 0) == both[1]
    places = []
    for block in range(parts):
        for slot in range(PAIR_CAP):
            hit = named & (source == block) & (both[2] == slot)
            places.append(jnp.where(hit, 1.0, 0.0).astype(jnp.bfloat16))
    places = jnp.concatenate(places, axis=0)
    flat = x_ref.reshape(parts * per * dates * rows, LANES)
    for k in range(parts):
        for copy in copies[k]:
            copy.wait()

        def take(f, carry):
            pixels = flat[pl.ds(k * per * dates * rows + meta[k][0, f], dates, stride=rows), :]
            v_ref[k * feet + f] = jnp.where(lane < meta[k][1, f], pixels, 0.0)
            return carry

        lax.fori_loop(0, feet, take, 0, unroll=8)
    tiles = []
    for first in range(0, parts * feet, LANES):

        def add(f, total):
            one = jnp.sum(v_ref[first + f], axis=1, keepdims=True)
            return jnp.where(lane == f, one, total)

        tiles.append(lax.fori_loop(0, LANES, add, jnp.zeros((dates, LANES), jnp.float32), unroll=32))
    counts = jnp.broadcast_to(both[0].astype(jnp.float32), (dates, index.shape[1]))
    sums = jnp.concatenate([jnp.concatenate(tiles, axis=1), counts], axis=0)
    held = jnp.zeros((places.shape[0], 2 * dates), jnp.float32)
    for piece in split(sums, 3):
        held = held + lax.dot_general(places, piece, (((1,), (1,)), ((), ())), preferred_element_type=jnp.float32)
    for n in range(parts * PAIR_CAP):
        at = pl.ds(n * dates, dates)
        out_ref[:, 0, at] = held[n * owners:(n + 1) * owners, :dates]
        out_ref[:, 1, at] = held[n * owners:(n + 1) * owners, dates:]


def footprints(inner, rim, meta, place, owners):
    parts = len(inner)
    per, dates, inner_rows, _ = inner[0].shape
    feet = meta[0].shape[1]
    message = parts * PAIR_CAP * dates
    return pl.pallas_call(
        functools.partial(footprint_kernel, parts, feet),
        grid_spec=pltpu.PrefetchScalarGridSpec(
            num_scalar_prefetch=1 + parts,
            grid=(),
            in_specs=[pl.BlockSpec(memory_space=pltpu.VMEM)] * parts + [pl.BlockSpec(memory_space=pltpu.HBM)] * (2 * parts),
            out_specs=pl.BlockSpec(memory_space=pltpu.VMEM),
            scratch_shapes=[
                pltpu.VMEM((parts * feet, dates, LANES), jnp.float32),
                pltpu.VMEM((parts, per, dates, inner_rows + 2 * EDGE, LANES), jnp.float32),
                pltpu.SemaphoreType.DMA((parts, 3)),
            ],
        ),
        out_shape=jax.ShapeDtypeStruct((owners, 2, message), jnp.float32),
        compiler_params=params(62),
        cost_estimate=cost(5),
    )(place, *meta, *meta, *inner, *rim)


def owner_kernel(parts, strips, taps, got_ref, anomaly_ref, series_ref):
    owners = parts * strips
    slots = owners * PAIR_CAP
    dates = got_ref.shape[2] // PAIR_CAP
    local = dates // parts
    sums, held = got_ref[:, 0, :], got_ref[:, 1, :]
    rows, weights = [], []
    for block in range(parts):
        for slot in range(PAIR_CAP):
            at = (block * PAIR_CAP + slot) * local
            rows.append(jnp.concatenate(
                [sums[e * strips:(e + 1) * strips, at:at + local] for e in range(parts)], axis=1))
            weights.append(held[0:strips, at:at + 1])
    sums = jnp.concatenate(rows, axis=0)
    weight = jnp.concatenate(weights, axis=0)
    shape = (dates, dates)
    lag = lax.broadcasted_iota(jnp.int32, shape, 0) - lax.broadcasted_iota(jnp.int32, shape, 1)
    for level, spacing in ((0, 1), (1, DILATION)):
        filt = jnp.where(lag == 0, 1.0, 0.0)
        for k in range(2 * REACH + 1):
            filt = filt - jnp.where(lag == (k - REACH) * spacing, taps[level, k], 0.0)
        sums = jnp.dot(sums, filt, precision=HIGHEST, preferred_element_type=jnp.float32)
    mean = sums / jnp.where(weight > 0, weight, 1.0)
    asset = jnp.sum(weight * mean, axis=0, keepdims=True) / jnp.sum(weight, axis=0, keepdims=True)
    odd = jnp.where(weight > 0, mean - asset, 0.0)
    series_ref[...] = asset
    shape = (slots, slots)
    to = lax.broadcasted_iota(jnp.int32, shape, 0)
    source = lax.broadcasted_iota(jnp.int32, shape, 1)
    block, rest = source // (PAIR_CAP * strips), source % (PAIR_CAP * strips)
    place_of = block * (PAIR_CAP * strips) + (rest % strips) * PAIR_CAP + rest // strips
    order = jnp.where(to == place_of, 1.0, 0.0)
    anomaly_ref[0] = jnp.dot(order, odd, precision=HIGHEST, preferred_element_type=jnp.float32)


def owner_series(got, taps, parts, strips):
    owners = parts * strips
    dates = got.shape[2] // PAIR_CAP
    slots = owners * PAIR_CAP
    return pl.pallas_call(
        functools.partial(owner_kernel, parts, strips),
        grid_spec=pltpu.PrefetchScalarGridSpec(
            num_scalar_prefetch=1,
            grid=(),
            in_specs=[pl.BlockSpec(memory_space=pltpu.VMEM)],
            out_specs=[pl.BlockSpec(memory_space=pltpu.VMEM)] * 2,
        ),
        out_shape=[
            jax.ShapeDtypeStruct((1, slots, dates), jnp.float32),
            jax.ShapeDtypeStruct((1, dates), jnp.float32),
        ],
        compiler_params=params(24),
        cost_estimate=cost(1.8),
    )(taps, got)


def spread_meta(meta, offset, swap):
    known = sorted(meta)
    got = swap(jnp.concatenate([meta[k] for k in known], axis=1), offset)
    width = meta[0].shape[1]
    return meta | {k ^ offset: got[:, n * width:(n + 1) * width] for n, k in enumerate(known)}


def shards(stack, spatial_taps, temporal_taps, foot_tile, foot_row, foot_count, foot_owner):
    parts, strips = lax.axis_size("date"), lax.axis_size("strip")
    place = lax.axis_index("date").astype(jnp.int32)[None]
    dates, rows, cols = stack.shape
    feet = foot_row.shape[0]
    owner = foot_owner[:, 0]
    position = jnp.arange(feet, dtype=jnp.int32)
    earlier = (owner[:, None] == owner[None, :]) & (position[None, :] < position[:, None])
    slot = jnp.sum(earlier.astype(jnp.int32), axis=1)
    own = jnp.stack([foot_tile * (dates * rows) + foot_row, foot_count, owner, slot])

    def swap(value, offset):
        return lax.ppermute(value, "date", [(i, i ^ offset) for i in range(parts)])

    order = (*range(2, parts), 1, 0)
    inner, far_inner = {}, {}
    lead = order[0]
    inner[lead], brim, last_rows, first_rows, ends = interior(stack, None, spatial_taps, place, (lead,), 0, parts)
    far_inner[lead] = swap(inner[lead], lead)
    up = lax.ppermute(last_rows, "strip", [(i, i + 1) for i in range(strips - 1)])
    down = lax.ppermute(first_rows, "strip", [(i + 1, i) for i in range(strips - 1)])
    own, brim = lax.optimization_barrier((own, brim))
    meta = {0: own}
    for bit in range(parts.bit_length() - 2, 0, -1):
        meta = spread_meta(meta, 1 << bit, swap)
    *made, brim = interior(stack, brim, spatial_taps, place, order[1:], 1, parts)
    for n, offset in enumerate(order[1:]):
        inner[offset] = made[n]
        if offset > 1:
            far_inner[offset] = swap(inner[offset], offset)
    known = sorted(meta)
    *held, far_inner[lead], ends = lax.optimization_barrier((*[meta[k] for k in known], far_inner[lead], ends))
    meta = spread_meta(dict(zip(known, held)), 1, swap)
    made = edges(ends, up, down, brim, spatial_taps, place, order)
    rim = dict(zip(order, made))
    inner[1], rim[0] = lax.optimization_barrier((inner[1], rim[0]))
    meta = [meta[k] for k in range(parts)]
    far_rim = {k: swap(rim[k], k) for k in order[:-1]}
    far_inner[1] = swap(inner[1], 1)
    rim = [rim[k] for k in range(parts)]
    sums = footprints([inner[k] for k in range(parts)], rim, meta, place, parts * strips)
    got = lax.all_to_all(sums, ("date", "strip"), split_axis=0, concat_axis=0, tiled=True)
    last = rows // EDGE - 1
    residual = temporal(
        [inner[0]] + [far_inner[k] for k in range(1, parts)], None, temporal_taps, place, 1, 1, rows)
    got, residual = lax.optimization_barrier((got, residual))
    anomaly, series = owner_series(got, temporal_taps, parts, strips)
    residual = temporal(
        [rim[0]] + [far_rim[k] for k in range(1, parts)], residual, temporal_taps, place, 0, last, rows)
    return residual, anomaly, series


def solution(mesh):
    placed = (
        P("date", "strip", None),
        P(),
        P(),
        P(("date", "strip")),
        P(("date", "strip")),
        P(("date", "strip")),
        P(("date", "strip"), None),
    )
    return jax.shard_map(
        shards,
        mesh=mesh,
        in_specs=placed,
        out_specs=(
            P(None, "strip", "date"),
            P(("date", "strip"), None, None),
            P(("date", "strip"), None),
        ),
        check_vma=False,
    )
```

```python
import functools

import jax
import jax.numpy as jnp
from jax import lax
from jax.experimental import pallas as pl
from jax.experimental.pallas import tpu as pltpu
from jax.sharding import PartitionSpec as P

TILE = 128
RADIUS = 6
REACH = 2
DILATION = 8
PAIR_CAP = 2
LANES = 128
EDGE = 8
HIGHEST = lax.Precision.HIGHEST


def params(mebibytes):
    return pltpu.CompilerParams(vmem_limit_bytes=mebibytes * 1024 * 1024)


def cost(micros):
    return pl.CostEstimate(flops=0, bytes_accessed=int(micros * 3.69e6), transcendentals=0)


def pick_taps(at, taps):
    count = taps.shape[0]
    total = taps[0]
    for k in range(1, count):
        total = total + taps[k]
    out = jnp.zeros(at.shape, jnp.float32)
    for k in range(count):
        out = jnp.where(at == k, taps[k], out)
    return out / jnp.full(at.shape, total, jnp.float32)


def split(value, count):
    out = []
    for _ in range(count):
        piece = value.astype(jnp.bfloat16)
        out.append(piece)
        value = value - piece.astype(jnp.float32)
    return out


def spread(value, axis):
    high, mid = split(value, 2)
    return jnp.concatenate([high, high, high, mid], axis=axis)


def fill_columns(col_ref, taps):
    shape = (LANES, LANES)
    lag = lax.broadcasted_iota(jnp.int32, shape, 0) - lax.broadcasted_iota(jnp.int32, shape, 1)
    near = split(pick_taps(lag + RADIUS, taps), 3)
    far = pick_taps(jnp.where(lag > 0, lag + RADIUS - LANES, lag + RADIUS + LANES), taps)
    above = split(jnp.where(lag > 0, far, 0.0), 3)
    below = split(jnp.where(lag > 0, 0.0, far), 3)
    for n, piece in enumerate((0, 1, 2, 0)):
        at = n * 3 * LANES
        for i, pair in enumerate(((near, above), (below, near), (above, below))):
            for j, block in enumerate(pair):
                col_ref[at + i * LANES:at + (i + 1) * LANES, j * LANES:(j + 1) * LANES] = block[piece]


def row_band(out_rows, in_rows, taps):
    shape = (out_rows, 4 * in_rows)
    lane = lax.broadcasted_iota(jnp.int32, shape, 1)
    row = lax.broadcasted_iota(jnp.int32, shape, 0)
    part = jnp.zeros(shape, jnp.int32)
    for n in range(1, 4):
        part = jnp.where(lane >= n * in_rows, n, part)
    return lane - part * in_rows, row, part


def pieces_of(values, part):
    high, mid, low = [p.astype(jnp.float32) for p in split(values, 3)]
    return jnp.where(part == 1, mid, jnp.where(part == 2, low, high)).astype(jnp.bfloat16)


def filter_columns(mid, rim, col):
    rows = mid.shape[0]
    window = jnp.concatenate([mid, rim], axis=1)
    return jnp.dot(spread(window, 1), col, preferred_element_type=jnp.float32)


def rim_tile(left, right, block, parts):
    lane = lax.broadcasted_iota(jnp.int32, left.shape, len(left.shape) - 1)
    first = lane < LANES // 2
    keep = (first & (block < parts - 1)) | (~first & (block > 0))
    return jnp.where(keep, jnp.where(first, right, left), 0.0)


def chosen(n, values):
    out = values[0]
    for m in range(1, len(values)):
        out = jnp.where(n == m, values[m], out)
    return out


def interior_kernel(offsets, slot, parts, group, place, taps, stack, *rest):
    count = len(offsets)
    first = slot == 0
    if not first:
        rest = rest[1:]
    outs, brim, rest = rest[:count], rest[count], rest[count + 1:]
    if first:
        up, down, ends, mid_ref, left_ref, right_ref, halo_ref, up_ref, down_ref, halo_sem, halo_out_sem, *rest = rest
    else:
        x_ref, *rest = rest
    out_ref, brim_ref, col_ref, row_ref, in_sem, out_sem, brim_sem = rest
    _, per, dates, inner, _ = out_ref.shape
    width = per * LANES
    rows = inner + 2 * EDGE
    cols = width * parts
    steps = dates // group

    def bounds(block):
        start = block * width
        places = start, jnp.maximum(start - LANES, 0), jnp.minimum(start + width, cols - LANES)
        return [pl.multiple_of(at, LANES) for at in places]

    def load(g):
        at = pl.ds(g * group, group)
        if not first:
            return [pltpu.make_async_copy(stack.at[at], x_ref.at[at], in_sem.at[0, g])]
        return [
            pltpu.make_async_copy(stack.at[at, :, pl.ds(start, ref.shape[2])], ref.at[at], in_sem.at[n, g])
            for n, (start, ref) in enumerate(zip(bounds(place[0] ^ offsets[0]), (mid_ref, left_ref, right_ref)))
        ]

    def store(m, g):
        at = pl.ds(g * group, group)
        return pltpu.make_async_copy(out_ref.at[m, :, at], outs[m].at[:, at], out_sem.at[m, g])

    def store_brim(n):
        return pltpu.make_async_copy(brim_ref.at[n], brim.at[slot + n], brim_sem.at[n])

    for g in range(steps):
        for copy in load(g):
            copy.start()
    halo_loads, halo_stores = [], []
    if first:
        halo_loads = [
            pltpu.make_async_copy(
                stack.at[:, pl.ds(side * (rows - EDGE), EDGE), pl.ds(c * LANES, LANES)],
                halo_ref.at[c, :, pl.ds(side * EDGE, EDGE), :], halo_sem.at[side, c])
            for side in range(2) for c in range(cols // LANES)
        ]
        halo_stores = [
            pltpu.make_async_copy(halo_ref, ends, halo_out_sem.at[0]),
            pltpu.make_async_copy(up_ref, up, halo_out_sem.at[1]),
            pltpu.make_async_copy(down_ref, down, halo_out_sem.at[2]),
        ]
        for copy in halo_loads:
            copy.start()
    fill_columns(col_ref, taps)
    q, r, part = row_band(inner, rows, taps)
    row_ref[...] = pieces_of(pick_taps(q - r - (EDGE - RADIUS), taps), part)

    def pack(c, carry):
        at = pl.ds(pl.multiple_of(c * LANES, LANES), LANES)
        rows_of = halo_ref.at[c].reshape(dates * 2 * EDGE, LANES)
        for r in range(RADIUS):
            up_ref[r, :, at] = rows_of[pl.ds(2 * EDGE - RADIUS + r, dates, stride=2 * EDGE), :]
            down_ref[r, :, at] = rows_of[pl.ds(r, dates, stride=2 * EDGE), :]
        return carry

    def step(i, carry):
        n, g = i // steps, i % steps
        block = place[0] ^ chosen(n, offsets)
        at = pl.ds(g * group, group)

        @pl.when(n == 0)
        def _():
            for copy in load(g):
                copy.wait()

        if first:
            @pl.when(i == steps - 1)
            def _():
                for copy in halo_loads:
                    copy.wait()
                lax.fori_loop(0, cols // LANES, pack, 0)
                for copy in halo_stores:
                    copy.start()

            mid, left, right = mid_ref[at], left_ref[at], right_ref[at]
        else:
            start, before, after = bounds(block)
            mid, left, right = [x_ref[at, :, pl.ds(f, w)] for f, w in ((start, width), (before, LANES), (after, LANES))]
        rim = rim_tile(left, right, block, parts)
        across = filter_columns(mid.reshape(group * rows, width), rim.reshape(group * rows, LANES), col_ref[...])
        for t in range(group):
            one = across[t * rows:(t + 1) * rows]
            low = jnp.dot(row_ref[...], spread(one, 0), preferred_element_type=jnp.float32)
            done = mid[t, EDGE:rows - EDGE, :] - low
            for h in range(per):
                out_ref[n, h, g * group + t] = done[:, h * LANES:(h + 1) * LANES]
                for side in range(2):
                    lines = one[side * (rows - 2 * EDGE):side * (rows - 2 * EDGE) + 2 * EDGE, h * LANES:(h + 1) * LANES]
                    brim_ref[n, h, pl.ds(side * 2 * EDGE * dates + g * group + t, 2 * EDGE, stride=dates), :] = lines
        for m in range(count):
            @pl.when(n == m)
            def _():
                store(m, g).start()

        @pl.when(g == steps - 1)
        def _():
            store_brim(n).start()

        return carry

    lax.fori_loop(0, count * steps, step, 0)
    for copy in halo_stores:
        copy.wait()
    for m in range(count):
        for g in range(steps):
            store(m, g).wait()
        store_brim(m).wait()


def interior(stack, brim, taps, place, offsets, slot, parts):
    dates, rows, cols = stack.shape
    width = cols // parts
    per = width // LANES
    group = min(8, dates)
    inner = rows - 2 * EDGE
    count = len(offsets)
    first = slot == 0
    here = pl.BlockSpec(memory_space=pltpu.HBM)
    out_shape = [jax.ShapeDtypeStruct((per, dates, inner, LANES), jnp.float32)] * count
    out_shape += [jax.ShapeDtypeStruct((parts, per, 4 * EDGE * dates, LANES), jnp.float32)]
    if first:
        out_shape += [jax.ShapeDtypeStruct((RADIUS, dates, cols), jnp.float32)] * 2
        out_shape += [jax.ShapeDtypeStruct((cols // LANES, dates, 2 * EDGE, LANES), jnp.float32)]
        scratch = [pltpu.VMEM((dates, rows, span), jnp.float32) for span in (width, LANES, LANES)] + [
            pltpu.VMEM((cols // LANES, dates, 2 * EDGE, LANES), jnp.float32),
            pltpu.VMEM((RADIUS, dates, cols), jnp.float32),
            pltpu.VMEM((RADIUS, dates, cols), jnp.float32),
            pltpu.SemaphoreType.DMA((2, cols // LANES)),
            pltpu.SemaphoreType.DMA((3,)),
        ]
    else:
        scratch = [pltpu.VMEM((dates, rows, cols), jnp.float32)]
    return pl.pallas_call(
        functools.partial(interior_kernel, offsets, slot, parts, group),
        grid_spec=pltpu.PrefetchScalarGridSpec(
            num_scalar_prefetch=2,
            grid=(),
            in_specs=[here] * (1 if first else 2),
            out_specs=[here] * len(out_shape),
            scratch_shapes=scratch + [
                pltpu.VMEM((count, per, dates, inner, LANES), jnp.float32),
                pltpu.VMEM((count, per, 4 * EDGE * dates, LANES), jnp.float32),
                pltpu.VMEM((12 * LANES, width), jnp.bfloat16),
                pltpu.VMEM((inner, 4 * rows), jnp.bfloat16),
                pltpu.SemaphoreType.DMA((3, dates // group)),
                pltpu.SemaphoreType.DMA((count, dates // group)),
                pltpu.SemaphoreType.DMA((count,)),
            ],
        ),
        out_shape=out_shape,
        input_output_aliases={} if first else {3: count},
        compiler_params=params(63),
        cost_estimate=cost(2.5 + 2.5 * count),
    )(place, taps, stack, *([] if first else [brim]))


def edge_kernel(order, feet, place, taps, *rest):
    parts = len(order)
    meta, vectors, rest = rest[:parts], rest[parts:2 * parts], rest[2 * parts:]
    ends, up, down, brim, *rest = rest
    inner, outs, rest = rest[:parts], rest[parts:2 * parts], rest[2 * parts:]
    sums_ref, out_ref, across_ref, brim_ref, up_ref, down_ref, ends_ref, col_ref, x_ref, v_ref = rest[:10]
    halo_sem, brim_sem, out_sem, x_sem = rest[10:]
    _, dates, cols = up_ref.shape
    width = cols // parts
    per = width // LANES
    rows = x_ref.shape[3]
    owners = sums_ref.shape[0]
    halos = [
        pltpu.make_async_copy(whole, ref, halo_sem.at[n])
        for n, (whole, ref) in enumerate(((up, up_ref), (down, down_ref), (ends, ends_ref)))
    ]
    for copy in halos:
        copy.start()
    for n in range(parts):
        pltpu.make_async_copy(brim.at[n], brim_ref.at[n], brim_sem.at[n]).start()
    middles = [
        pltpu.make_async_copy(inner[n], x_ref.at[n, :, :, pl.ds(EDGE, rows - 2 * EDGE), :], x_sem.at[n]) for n in range(parts)
    ]
    for copy in middles:
        copy.start()
    fill_columns(col_ref, taps)
    total = taps[0]
    for k in range(1, 2 * RADIUS + 1):
        total = total + taps[k]
    scale = 1.0 / jnp.full((dates, LANES), total, jnp.float32)
    flat = ends_ref.reshape(cols // LANES, dates * 2 * EDGE, LANES)

    def store(n):
        return pltpu.make_async_copy(out_ref.at[n], outs[n], out_sem.at[n])

    for copy in halos:
        copy.wait()

    def one(n, carry):
        block = place[0] ^ chosen(n, order)
        start = pl.multiple_of(block * width, LANES)
        before = pl.multiple_of(jnp.maximum(start - LANES, 0), LANES)
        after = pl.multiple_of(jnp.minimum(start + width, cols - LANES), LANES)

        def both(first, span):
            at = pl.ds(first, span)
            return jnp.concatenate([up_ref[:, :, at], down_ref[:, :, at]], axis=0).reshape(2 * RADIUS * dates, span)

        rim = rim_tile(both(before, LANES), both(after, LANES), block, parts)
        across = filter_columns(both(start, width), rim, col_ref[...])
        for h in range(per):
            across_ref[h] = across[:, h * LANES:(h + 1) * LANES]
        lines = out_ref.at[n].reshape(per, dates * 2 * EDGE, LANES)
        every = x_ref.at[n].reshape(per, dates * rows, LANES)
        pltpu.make_async_copy(brim.at[n], brim_ref.at[n], brim_sem.at[n]).wait()

        def half(h, carry):
            for side in range(2):
                held = []
                for q in range(2 * RADIUS + EDGE):
                    halo = q < RADIUS if side == 0 else q >= RADIUS + EDGE
                    if halo:
                        at = q if side == 0 else q - EDGE
                        held.append(across_ref[h, at * dates:(at + 1) * dates, :])
                    else:
                        at = q - RADIUS if side == 0 else 3 * EDGE - RADIUS + q
                        held.append(brim_ref[n, h, at * dates:(at + 1) * dates, :])
                for r in range(EDGE):
                    low = taps[0] * held[r]
                    for j in range(1, 2 * RADIUS + 1):
                        low = low + taps[j] * held[r + j]
                    at = pl.ds(side * EDGE + r, dates, stride=2 * EDGE)
                    done = flat[block * per + h, at, :] - scale * low
                    lines[h, at, :] = done
                    every[h, pl.ds(side * (rows - EDGE) + r, dates, stride=rows), :] = done
            return carry

        lax.fori_loop(0, per, half, 0)
        for m in range(parts):
            @pl.when(n == m)
            def _():
                store(m).start()
        return carry

    lax.fori_loop(0, parts, one, 0)

    lane = lax.broadcasted_iota(jnp.int32, (dates, LANES), 1)
    both = [jnp.concatenate([ref[n:n + 1, :] for ref in vectors], axis=1) for n in range(1, 4)]
    index = lax.broadcasted_iota(jnp.int32, both[0].shape, 1)
    source = (index // feet) ^ place[0]
    named = lax.broadcasted_iota(jnp.int32, (owners, index.shape[1]), 0) == both[1]
    places = []
    for block in range(parts):
        for slot in range(PAIR_CAP):
            hit = named & (source == block) & (both[2] == slot)
            places.append(jnp.where(hit, 1.0, 0.0).astype(jnp.bfloat16))
    places = jnp.concatenate(places, axis=0)
    pixel_rows = x_ref.reshape(parts * per * dates * rows, LANES)
    for copy in middles:
        copy.wait()
    for k in range(parts):
        base = order.index(k) * per * dates * rows

        def take(f, carry):
            pixels = pixel_rows[pl.ds(base + meta[k][0, f], dates, stride=rows), :]
            v_ref[k * feet + f] = jnp.where(lane < meta[k][1, f], pixels, 0.0)
            return carry

        lax.fori_loop(0, feet, take, 0, unroll=8)
    tiles = []
    for first in range(0, parts * feet, LANES):

        def add(f, total):
            one = jnp.sum(v_ref[first + f], axis=1, keepdims=True)
            return jnp.where(lane == f, one, total)

        tiles.append(lax.fori_loop(0, LANES, add, jnp.zeros((dates, LANES), jnp.float32), unroll=32))
    counts = jnp.broadcast_to(both[0].astype(jnp.float32), (dates, index.shape[1]))
    sums = jnp.concatenate([jnp.concatenate(tiles, axis=1), counts], axis=0)
    held = jnp.zeros((places.shape[0], 2 * dates), jnp.float32)
    for piece in split(sums, 3):
        held = held + lax.dot_general(places, piece, (((1,), (1,)), ((), ())), preferred_element_type=jnp.float32)
    for n in range(parts * PAIR_CAP):
        at = pl.ds(n * dates, dates)
        sums_ref[:, 0, at] = held[n * owners:(n + 1) * owners, :dates]
        sums_ref[:, 1, at] = held[n * owners:(n + 1) * owners, dates:]
    for m in range(parts):
        store(m).wait()


def edges(ends, up, down, brim, inner, meta, taps, place, order, owners):
    parts = len(order)
    tiles, dates, _, _ = ends.shape
    per = tiles // parts
    feet = meta[0].shape[1]
    rows = inner[0].shape[2] + 2 * EDGE
    here = pl.BlockSpec(memory_space=pltpu.HBM)
    resident = pl.BlockSpec(memory_space=pltpu.VMEM)
    return pl.pallas_call(
        functools.partial(edge_kernel, order, feet),
        grid_spec=pltpu.PrefetchScalarGridSpec(
            num_scalar_prefetch=2 + parts,
            grid=(),
            in_specs=[resident] * parts + [here] * (4 + parts),
            out_specs=[here] * parts + [resident],
            scratch_shapes=[
                pltpu.VMEM((parts, per, dates, 2 * EDGE, LANES), jnp.float32),
                pltpu.VMEM((per, 2 * RADIUS * dates, LANES), jnp.float32),
                pltpu.VMEM((parts, per, 4 * EDGE * dates, LANES), jnp.float32),
                pltpu.VMEM(up.shape, jnp.float32),
                pltpu.VMEM(up.shape, jnp.float32),
                pltpu.VMEM(ends.shape, jnp.float32),
                pltpu.VMEM((12 * LANES, per * LANES), jnp.bfloat16),
                pltpu.VMEM((parts, per, dates, rows, LANES), jnp.float32),
                pltpu.VMEM((parts * feet, dates, LANES), jnp.float32),
                pltpu.SemaphoreType.DMA((3,)),
                pltpu.SemaphoreType.DMA((parts,)),
                pltpu.SemaphoreType.DMA((parts,)),
                pltpu.SemaphoreType.DMA((parts,)),
            ],
        ),
        out_shape=[jax.ShapeDtypeStruct((per, dates, 2 * EDGE, LANES), jnp.float32)] * parts
        + [jax.ShapeDtypeStruct((owners, 2, parts * PAIR_CAP * dates), jnp.float32)],
        compiler_params=params(63),
        cost_estimate=cost(8),
    )(place, taps, *meta, *meta, ends, up, down, brim, *inner)


def temporal_kernel(parts, with_base, first_tile, tile_step, place, taps, *rest):
    pieces = rest[:parts]
    out, z_ref, f_ref, out_ref, in_sem, out_sem = rest[parts + with_base:]
    count, total, _, _ = out_ref.shape
    per = pieces[0].shape[0]
    local = total // parts
    pad = REACH * DILATION
    step = 8

    def load(n):
        rows = pl.ds(pl.multiple_of(n * EDGE, EDGE), EDGE)
        return [
            pltpu.make_async_copy(
                pieces[k].at[:, :, rows, :],
                z_ref.at[n, :, pl.ds(REACH + (place[0] ^ k) * local, local)], in_sem.at[n, k])
            for k in range(parts)
        ]

    def store(n):
        tile = first_tile + n * tile_step
        rows = pl.ds(pl.multiple_of(tile * EDGE, EDGE), EDGE)
        return pltpu.make_async_copy(out_ref.at[n], out.at[:, rows, :], out_sem.at[n])

    for n in range(count):
        for copy in load(n):
            copy.start()
    none = jnp.zeros((REACH, EDGE, LANES), jnp.float32)
    wide = jnp.zeros((pad, EDGE, LANES), jnp.float32)
    for h in range(per):
        for n in range(count):
            z_ref[n, h, 0:REACH] = none
            z_ref[n, h, REACH + total:REACH + total + REACH] = none
        f_ref[h, 0:pad] = wide
        f_ref[h, pad + total:pad + total + pad] = wide
    own = 1.0 - taps[0, REACH]
    own_wide = 1.0 - taps[1, REACH]
    others = [k for k in range(2 * REACH + 1) if k != REACH]

    def one(n, carry):
        for copy in load(n):
            copy.wait()
        for h in range(per):
            for t in range(0, total, step):
                z = z_ref[n, h, t:t + step + 2 * REACH]
                kept = own * z[REACH:REACH + step]
                for k in others:
                    kept = kept - taps[0, k] * z[k:k + step]
                f_ref[h, pad + t:pad + t + step] = kept
            for t in range(0, total, step):
                kept = own_wide * f_ref[h, pad + t:pad + t + step]
                for k in others:
                    kept = kept - taps[1, k] * f_ref[h, t + k * DILATION:t + k * DILATION + step]
                out_ref[n, t:t + step, :, h * LANES:(h + 1) * LANES] = kept
        store(n).start()
        return carry

    lax.fori_loop(0, count, one, 0)
    for n in range(count):
        store(n).wait()


def temporal(pieces, base, taps, place, first_tile, tile_step, rows):
    parts = len(pieces)
    per, local, here, _ = pieces[0].shape
    total = local * parts
    extra = [] if base is None else [base]
    count = here // EDGE
    width = per * LANES
    return pl.pallas_call(
        functools.partial(temporal_kernel, parts, len(extra), first_tile, tile_step),
        grid_spec=pltpu.PrefetchScalarGridSpec(
            num_scalar_prefetch=2,
            grid=(),
            in_specs=[pl.BlockSpec(memory_space=pl.ANY)] * (parts + len(extra)),
            out_specs=pl.BlockSpec(memory_space=pltpu.HBM),
            scratch_shapes=[
                pltpu.VMEM((count, per, total + 2 * REACH, EDGE, LANES), jnp.float32),
                pltpu.VMEM((per, total + 2 * REACH * DILATION, EDGE, LANES), jnp.float32),
                pltpu.VMEM((count, total, EDGE, width), jnp.float32),
                pltpu.SemaphoreType.DMA((count, parts)),
                pltpu.SemaphoreType.DMA((count,)),
            ],
        ),
        out_shape=jax.ShapeDtypeStruct((total, rows, width), jnp.float32),
        input_output_aliases={} if base is None else {2 + parts: 0},
        compiler_params=params(24),
        cost_estimate=cost(2.5 + 0.4 * count),
    )(place, taps, *pieces, *extra)


def owner_kernel(parts, strips, taps, got_ref, anomaly_ref, series_ref):
    owners = parts * strips
    slots = owners * PAIR_CAP
    dates = got_ref.shape[2] // PAIR_CAP
    local = dates // parts
    sums, held = got_ref[:, 0, :], got_ref[:, 1, :]
    rows, weights = [], []
    for block in range(parts):
        for slot in range(PAIR_CAP):
            at = (block * PAIR_CAP + slot) * local
            rows.append(jnp.concatenate(
                [sums[e * strips:(e + 1) * strips, at:at + local] for e in range(parts)], axis=1))
            weights.append(held[0:strips, at:at + 1])
    sums = jnp.concatenate(rows, axis=0)
    weight = jnp.concatenate(weights, axis=0)
    shape = (dates, dates)
    lag = lax.broadcasted_iota(jnp.int32, shape, 0) - lax.broadcasted_iota(jnp.int32, shape, 1)
    for level, spacing in ((0, 1), (1, DILATION)):
        filt = jnp.where(lag == 0, 1.0, 0.0)
        for k in range(2 * REACH + 1):
            filt = filt - jnp.where(lag == (k - REACH) * spacing, taps[level, k], 0.0)
        sums = jnp.dot(sums, filt, precision=HIGHEST, preferred_element_type=jnp.float32)
    mean = sums / jnp.where(weight > 0, weight, 1.0)
    asset = jnp.sum(weight * mean, axis=0, keepdims=True) / jnp.sum(weight, axis=0, keepdims=True)
    odd = jnp.where(weight > 0, mean - asset, 0.0)
    series_ref[...] = asset
    shape = (slots, slots)
    to = lax.broadcasted_iota(jnp.int32, shape, 0)
    source = lax.broadcasted_iota(jnp.int32, shape, 1)
    block, rest = source // (PAIR_CAP * strips), source % (PAIR_CAP * strips)
    place_of = block * (PAIR_CAP * strips) + (rest % strips) * PAIR_CAP + rest // strips
    order = jnp.where(to == place_of, 1.0, 0.0)
    anomaly_ref[0] = jnp.dot(order, odd, precision=HIGHEST, preferred_element_type=jnp.float32)


def owner_series(got, taps, parts, strips):
    owners = parts * strips
    dates = got.shape[2] // PAIR_CAP
    slots = owners * PAIR_CAP
    return pl.pallas_call(
        functools.partial(owner_kernel, parts, strips),
        grid_spec=pltpu.PrefetchScalarGridSpec(
            num_scalar_prefetch=1,
            grid=(),
            in_specs=[pl.BlockSpec(memory_space=pltpu.VMEM)],
            out_specs=[pl.BlockSpec(memory_space=pltpu.VMEM)] * 2,
        ),
        out_shape=[
            jax.ShapeDtypeStruct((1, slots, dates), jnp.float32),
            jax.ShapeDtypeStruct((1, dates), jnp.float32),
        ],
        compiler_params=params(24),
        cost_estimate=cost(1.8),
    )(taps, got)


def spread_meta(meta, offset, swap):
    known = sorted(meta)
    got = swap(jnp.concatenate([meta[k] for k in known], axis=1), offset)
    width = meta[0].shape[1]
    return meta | {k ^ offset: got[:, n * width:(n + 1) * width] for n, k in enumerate(known)}


def shards(stack, spatial_taps, temporal_taps, foot_tile, foot_row, foot_count, foot_owner):
    parts, strips = lax.axis_size("date"), lax.axis_size("strip")
    place = lax.axis_index("date").astype(jnp.int32)[None]
    dates, rows, cols = stack.shape
    feet = foot_row.shape[0]
    owner = foot_owner[:, 0]
    position = jnp.arange(feet, dtype=jnp.int32)
    earlier = (owner[:, None] == owner[None, :]) & (position[None, :] < position[:, None])
    slot = jnp.sum(earlier.astype(jnp.int32), axis=1)
    own = jnp.stack([foot_tile * (dates * rows) + foot_row, foot_count, owner, slot])

    def swap(value, offset):
        return lax.ppermute(value, "date", [(i, i ^ offset) for i in range(parts)])

    order = (*range(2, parts), 1, 0)
    inner, far_inner = {}, {}
    lead = order[0]
    inner[lead], brim, last_rows, first_rows, ends = interior(stack, None, spatial_taps, place, (lead,), 0, parts)
    far_inner[lead] = swap(inner[lead], lead)
    up = lax.ppermute(last_rows, "strip", [(i, i + 1) for i in range(strips - 1)])
    down = lax.ppermute(first_rows, "strip", [(i + 1, i) for i in range(strips - 1)])
    own, brim = lax.optimization_barrier((own, brim))
    meta = {0: own}
    for bit in range(parts.bit_length() - 2, 0, -1):
        meta = spread_meta(meta, 1 << bit, swap)
    *made, brim = interior(stack, brim, spatial_taps, place, order[1:], 1, parts)
    for n, offset in enumerate(order[1:]):
        inner[offset] = made[n]
        if offset > 1:
            far_inner[offset] = swap(inner[offset], offset)
    known = sorted(meta)
    *held, far_inner[lead], brim = lax.optimization_barrier((*[meta[k] for k in known], far_inner[lead], brim))
    meta = spread_meta(dict(zip(known, held)), 1, swap)
    meta = [meta[k] for k in range(parts)]
    *made, sums = edges(
        ends, up, down, brim, [inner[k] for k in order], meta, spatial_taps, place, order, parts * strips)
    rim = dict(zip(order, made))
    far_inner[1] = swap(inner[1], 1)
    got = lax.all_to_all(sums, ("date", "strip"), split_axis=0, concat_axis=0, tiled=True)
    gate, *made = lax.optimization_barrier((swap(rim[1], 1), *[rim[k] for k in order[:-2]]))
    far_rim = {k: swap(made[n], k) for n, k in enumerate(order[:-2])}
    far_rim[1] = gate
    last = rows // EDGE - 1
    residual = temporal(
        [inner[0]] + [far_inner[k] for k in range(1, parts)], None, temporal_taps, place, 1, 1, rows)
    got, residual = lax.optimization_barrier((got, residual))
    anomaly, series = owner_series(got, temporal_taps, parts, strips)
    residual = temporal(
        [rim[0]] + [far_rim[k] for k in range(1, parts)], residual, temporal_taps, place, 0, last, rows)
    return residual, anomaly, series


def solution(mesh):
    placed = (
        P("date", "strip", None),
        P(),
        P(),
        P(("date", "strip")),
        P(("date", "strip")),
        P(("date", "strip")),
        P(("date", "strip"), None),
    )
    return jax.shard_map(
        shards,
        mesh=mesh,
        in_specs=placed,
        out_specs=(
            P(None, "strip", "date"),
            P(("date", "strip"), None, None),
            P(("date", "strip"), None),
        ),
        check_vma=False,
    )
```

```python
import functools

import jax
import jax.numpy as jnp
from jax import lax
from jax.experimental import pallas as pl
from jax.experimental.pallas import tpu as pltpu
from jax.sharding import PartitionSpec as P

TILE = 128
RADIUS = 6
REACH = 2
DILATION = 8
PAIR_CAP = 2
LANES = 128
EDGE = 8
HIGHEST = lax.Precision.HIGHEST


def params(mebibytes):
    return pltpu.CompilerParams(vmem_limit_bytes=mebibytes * 1024 * 1024)


def cost(micros):
    return pl.CostEstimate(flops=0, bytes_accessed=int(micros * 3.69e6), transcendentals=0)


def pick_taps(at, taps):
    count = taps.shape[0]
    total = taps[0]
    for k in range(1, count):
        total = total + taps[k]
    out = jnp.zeros(at.shape, jnp.float32)
    for k in range(count):
        out = jnp.where(at == k, taps[k], out)
    return out / jnp.full(at.shape, total, jnp.float32)


def split(value, count):
    out = []
    for _ in range(count):
        piece = value.astype(jnp.bfloat16)
        out.append(piece)
        value = value - piece.astype(jnp.float32)
    return out


def spread(value, axis):
    high, mid = split(value, 2)
    return jnp.concatenate([high, high, high, mid], axis=axis)


def fill_columns(col_ref, taps):
    shape = (LANES, LANES)
    lag = lax.broadcasted_iota(jnp.int32, shape, 0) - lax.broadcasted_iota(jnp.int32, shape, 1)
    near = split(pick_taps(lag + RADIUS, taps), 3)
    far = pick_taps(jnp.where(lag > 0, lag + RADIUS - LANES, lag + RADIUS + LANES), taps)
    above = split(jnp.where(lag > 0, far, 0.0), 3)
    below = split(jnp.where(lag > 0, 0.0, far), 3)
    for n, piece in enumerate((0, 1, 2, 0)):
        at = n * 3 * LANES
        for i, pair in enumerate(((near, above), (below, near), (above, below))):
            for j, block in enumerate(pair):
                col_ref[at + i * LANES:at + (i + 1) * LANES, j * LANES:(j + 1) * LANES] = block[piece]


def row_band(out_rows, in_rows, taps):
    shape = (out_rows, 4 * in_rows)
    lane = lax.broadcasted_iota(jnp.int32, shape, 1)
    row = lax.broadcasted_iota(jnp.int32, shape, 0)
    part = jnp.zeros(shape, jnp.int32)
    for n in range(1, 4):
        part = jnp.where(lane >= n * in_rows, n, part)
    return lane - part * in_rows, row, part


def pieces_of(values, part):
    high, mid, low = [p.astype(jnp.float32) for p in split(values, 3)]
    return jnp.where(part == 1, mid, jnp.where(part == 2, low, high)).astype(jnp.bfloat16)


def filter_columns(mid, rim, col):
    rows = mid.shape[0]
    window = jnp.concatenate([mid, rim], axis=1)
    return jnp.dot(spread(window, 1), col, preferred_element_type=jnp.float32)


def rim_tile(left, right, block, parts):
    lane = lax.broadcasted_iota(jnp.int32, left.shape, len(left.shape) - 1)
    first = lane < LANES // 2
    keep = (first & (block < parts - 1)) | (~first & (block > 0))
    return jnp.where(keep, jnp.where(first, right, left), 0.0)


def chosen(n, values):
    out = values[0]
    for m in range(1, len(values)):
        out = jnp.where(n == m, values[m], out)
    return out


def interior_kernel(offsets, slot, parts, group, place, taps, stack, *rest):
    count = len(offsets)
    first = slot == 0
    if not first:
        rest = rest[1:]
    outs, brim, rest = rest[:count], rest[count], rest[count + 1:]
    if first:
        up, down, ends, mid_ref, left_ref, right_ref, halo_ref, up_ref, down_ref, halo_sem, halo_out_sem, *rest = rest
    else:
        x_ref, *rest = rest
    out_ref, brim_ref, col_ref, row_ref, in_sem, out_sem, brim_sem = rest
    _, per, dates, inner, _ = out_ref.shape
    width = per * LANES
    rows = inner + 2 * EDGE
    cols = width * parts
    steps = dates // group

    def bounds(block):
        start = block * width
        places = start, jnp.maximum(start - LANES, 0), jnp.minimum(start + width, cols - LANES)
        return [pl.multiple_of(at, LANES) for at in places]

    def load(g):
        at = pl.ds(g * group, group)
        if not first:
            return [pltpu.make_async_copy(stack.at[at], x_ref.at[at], in_sem.at[0, g])]
        return [
            pltpu.make_async_copy(stack.at[at, :, pl.ds(start, ref.shape[2])], ref.at[at], in_sem.at[n, g])
            for n, (start, ref) in enumerate(zip(bounds(place[0] ^ offsets[0]), (mid_ref, left_ref, right_ref)))
        ]

    def store(m, g):
        at = pl.ds(g * group, group)
        return pltpu.make_async_copy(out_ref.at[m, :, at], outs[m].at[:, at], out_sem.at[m, g])

    def store_brim(n):
        return pltpu.make_async_copy(brim_ref.at[n], brim.at[slot + n], brim_sem.at[n])

    for g in range(steps):
        for copy in load(g):
            copy.start()
    halo_loads, halo_stores = [], []
    if first:
        halo_loads = [
            pltpu.make_async_copy(
                stack.at[:, pl.ds(side * (rows - EDGE), EDGE), pl.ds(c * LANES, LANES)],
                halo_ref.at[c, :, pl.ds(side * EDGE, EDGE), :], halo_sem.at[side, c])
            for side in range(2) for c in range(cols // LANES)
        ]
        halo_stores = [
            pltpu.make_async_copy(halo_ref, ends, halo_out_sem.at[0]),
            pltpu.make_async_copy(up_ref, up, halo_out_sem.at[1]),
            pltpu.make_async_copy(down_ref, down, halo_out_sem.at[2]),
        ]
        for copy in halo_loads:
            copy.start()
    fill_columns(col_ref, taps)
    q, r, part = row_band(inner, rows, taps)
    row_ref[...] = pieces_of(pick_taps(q - r - (EDGE - RADIUS), taps), part)

    def pack(c, carry):
        at = pl.ds(pl.multiple_of(c * LANES, LANES), LANES)
        rows_of = halo_ref.at[c].reshape(dates * 2 * EDGE, LANES)
        for r in range(RADIUS):
            up_ref[r, :, at] = rows_of[pl.ds(2 * EDGE - RADIUS + r, dates, stride=2 * EDGE), :]
            down_ref[r, :, at] = rows_of[pl.ds(r, dates, stride=2 * EDGE), :]
        return carry

    def step(i, carry):
        n, g = i // steps, i % steps
        block = place[0] ^ chosen(n, offsets)
        at = pl.ds(g * group, group)

        @pl.when(n == 0)
        def _():
            for copy in load(g):
                copy.wait()

        if first:
            @pl.when(i == steps - 1)
            def _():
                for copy in halo_loads:
                    copy.wait()
                lax.fori_loop(0, cols // LANES, pack, 0)
                for copy in halo_stores:
                    copy.start()

            mid, left, right = mid_ref[at], left_ref[at], right_ref[at]
        else:
            start, before, after = bounds(block)
            mid, left, right = [x_ref[at, :, pl.ds(f, w)] for f, w in ((start, width), (before, LANES), (after, LANES))]
        rim = rim_tile(left, right, block, parts)
        across = filter_columns(mid.reshape(group * rows, width), rim.reshape(group * rows, LANES), col_ref[...])
        for t in range(group):
            one = across[t * rows:(t + 1) * rows]
            low = jnp.dot(row_ref[...], spread(one, 0), preferred_element_type=jnp.float32)
            done = mid[t, EDGE:rows - EDGE, :] - low
            for h in range(per):
                out_ref[n, h, g * group + t] = done[:, h * LANES:(h + 1) * LANES]
                for side in range(2):
                    lines = one[side * (rows - 2 * EDGE):side * (rows - 2 * EDGE) + 2 * EDGE, h * LANES:(h + 1) * LANES]
                    date = g * group + t
                    at = ((date // EDGE) * 4 * EDGE + side * 2 * EDGE) * EDGE + date % EDGE
                    brim_ref[n, h, pl.ds(at, 2 * EDGE, stride=EDGE), :] = lines
        for m in range(count):
            @pl.when(n == m)
            def _():
                store(m, g).start()

        @pl.when(g == steps - 1)
        def _():
            store_brim(n).start()

        return carry

    lax.fori_loop(0, count * steps, step, 0)
    for copy in halo_stores:
        copy.wait()
    for m in range(count):
        for g in range(steps):
            store(m, g).wait()
        store_brim(m).wait()


def interior(stack, brim, taps, place, offsets, slot, parts):
    dates, rows, cols = stack.shape
    width = cols // parts
    per = width // LANES
    group = min(8, dates)
    inner = rows - 2 * EDGE
    count = len(offsets)
    first = slot == 0
    here = pl.BlockSpec(memory_space=pltpu.HBM)
    out_shape = [jax.ShapeDtypeStruct((per, dates, inner, LANES), jnp.float32)] * count
    out_shape += [jax.ShapeDtypeStruct((parts, per, 4 * EDGE * dates, LANES), jnp.float32)]
    if first:
        out_shape += [jax.ShapeDtypeStruct((RADIUS, dates, cols), jnp.float32)] * 2
        out_shape += [jax.ShapeDtypeStruct((cols // LANES, dates, 2 * EDGE, LANES), jnp.float32)]
        scratch = [pltpu.VMEM((dates, rows, span), jnp.float32) for span in (width, LANES, LANES)] + [
            pltpu.VMEM((cols // LANES, dates, 2 * EDGE, LANES), jnp.float32),
            pltpu.VMEM((RADIUS, dates, cols), jnp.float32),
            pltpu.VMEM((RADIUS, dates, cols), jnp.float32),
            pltpu.SemaphoreType.DMA((2, cols // LANES)),
            pltpu.SemaphoreType.DMA((3,)),
        ]
    else:
        scratch = [pltpu.VMEM((dates, rows, cols), jnp.float32)]
    return pl.pallas_call(
        functools.partial(interior_kernel, offsets, slot, parts, group),
        grid_spec=pltpu.PrefetchScalarGridSpec(
            num_scalar_prefetch=2,
            grid=(),
            in_specs=[here] * (1 if first else 2),
            out_specs=[here] * len(out_shape),
            scratch_shapes=scratch + [
                pltpu.VMEM((count, per, dates, inner, LANES), jnp.float32),
                pltpu.VMEM((count, per, 4 * EDGE * dates, LANES), jnp.float32),
                pltpu.VMEM((12 * LANES, width), jnp.bfloat16),
                pltpu.VMEM((inner, 4 * rows), jnp.bfloat16),
                pltpu.SemaphoreType.DMA((3, dates // group)),
                pltpu.SemaphoreType.DMA((count, dates // group)),
                pltpu.SemaphoreType.DMA((count,)),
            ],
        ),
        out_shape=out_shape,
        input_output_aliases={} if first else {3: count},
        compiler_params=params(63),
        cost_estimate=cost(2.5 + 2.5 * count),
    )(place, taps, stack, *([] if first else [brim]))


def edge_kernel(order, feet, place, taps, *rest):
    parts = len(order)
    meta, vectors, rest = rest[:parts], rest[parts:2 * parts], rest[2 * parts:]
    ends, up, down, brim, *rest = rest
    inner, outs, rest = rest[:parts], rest[parts:2 * parts], rest[2 * parts:]
    sums_ref, across_ref, brim_ref, up_ref, down_ref, ends_ref, col_ref, x_ref, v_ref = rest[:9]
    halo_sem, brim_sem, out_sem, x_sem = rest[9:]
    _, dates, cols = up_ref.shape
    width = cols // parts
    per = width // LANES
    pitch = x_ref.shape[3]
    rows = pitch - EDGE
    owners = sums_ref.shape[0]
    halos = [
        pltpu.make_async_copy(whole, ref, halo_sem.at[n])
        for n, (whole, ref) in enumerate(((up, up_ref), (down, down_ref), (ends, ends_ref)))
    ]
    for copy in halos:
        copy.start()
    for n in range(parts):
        pltpu.make_async_copy(brim.at[n], brim_ref.at[n], brim_sem.at[n]).start()
    middles = [
        pltpu.make_async_copy(inner[n], x_ref.at[n, :, :, pl.ds(EDGE, rows - 2 * EDGE), :], x_sem.at[n]) for n in range(parts)
    ]
    for copy in middles:
        copy.start()
    fill_columns(col_ref, taps)
    total = taps[0]
    for k in range(1, 2 * RADIUS + 1):
        total = total + taps[k]
    scale = 1.0 / jnp.full((dates, LANES), total, jnp.float32)
    flat = ends_ref.reshape(cols // LANES, dates * 2 * EDGE, LANES)

    def store(n):
        return [
            pltpu.make_async_copy(
                x_ref.at[n, :, :, pl.ds(side * (rows - EDGE), EDGE), :],
                outs[n].at[:, :, pl.ds(side * EDGE, EDGE), :], out_sem.at[n, side])
            for side in range(2)
        ]

    for copy in halos:
        copy.wait()

    mids, rims = [], []
    for n in range(parts):
        block = place[0] ^ order[n]
        start = pl.multiple_of(block * width, LANES)
        before = pl.multiple_of(jnp.maximum(start - LANES, 0), LANES)
        after = pl.multiple_of(jnp.minimum(start + width, cols - LANES), LANES)

        def both(first, span):
            at = pl.ds(first, span)
            return jnp.concatenate([up_ref[:, :, at], down_ref[:, :, at]], axis=0).reshape(2 * RADIUS * dates, span)

        mids.append(both(start, width))
        rims.append(rim_tile(both(before, LANES), both(after, LANES), block, parts))
    across = filter_columns(jnp.concatenate(mids, axis=0), jnp.concatenate(rims, axis=0), col_ref[...])
    span = 2 * RADIUS * dates
    for n in range(parts):
        for h in range(per):
            across_ref[n, h] = across[n * span:(n + 1) * span, h * LANES:(h + 1) * LANES]

    def one(n, carry):
        block = place[0] ^ chosen(n, order)
        every = x_ref.at[n].reshape(per, dates * pitch, LANES)
        pltpu.make_async_copy(brim.at[n], brim_ref.at[n], brim_sem.at[n]).wait()

        def half(h, carry):
            for side in range(2):
                held = []
                for q in range(2 * RADIUS + EDGE):
                    halo = q < RADIUS if side == 0 else q >= RADIUS + EDGE
                    if halo:
                        at = q if side == 0 else q - EDGE
                        held.append(across_ref[n, h, at * dates:(at + 1) * dates, :])
                    else:
                        at = q - RADIUS if side == 0 else 3 * EDGE - RADIUS + q
                        held.append(jnp.concatenate([
                            brim_ref[n, h, (d * 4 * EDGE + at) * EDGE:(d * 4 * EDGE + at + 1) * EDGE, :]
                            for d in range(dates // EDGE)
                        ], axis=0))
                for r in range(EDGE):
                    low = taps[0] * held[r]
                    for j in range(1, 2 * RADIUS + 1):
                        low = low + taps[j] * held[r + j]
                    at = pl.ds(side * EDGE + r, dates, stride=2 * EDGE)
                    done = flat[block * per + h, at, :] - scale * low
                    every[h, pl.ds(side * (rows - EDGE) + r, dates, stride=pitch), :] = done
            return carry

        lax.fori_loop(0, per, half, 0)
        for m in range(parts):
            @pl.when(n == m)
            def _():
                for copy in store(m):
                    copy.start()
        return carry

    lax.fori_loop(0, parts, one, 0)

    lane = lax.broadcasted_iota(jnp.int32, (dates, LANES), 1)
    both = [jnp.concatenate([ref[n:n + 1, :] for ref in vectors], axis=1) for n in range(1, 4)]
    index = lax.broadcasted_iota(jnp.int32, both[0].shape, 1)
    source = (index // feet) ^ place[0]
    named = lax.broadcasted_iota(jnp.int32, (owners, index.shape[1]), 0) == both[1]
    places = []
    for block in range(parts):
        for slot in range(PAIR_CAP):
            hit = named & (source == block) & (both[2] == slot)
            places.append(jnp.where(hit, 1.0, 0.0).astype(jnp.bfloat16))
    places = jnp.concatenate(places, axis=0)
    pixel_rows = x_ref.reshape(parts * per * dates * pitch, LANES)
    for copy in middles:
        copy.wait()
    for k in range(parts):
        base = order.index(k) * per * dates * pitch

        def take(f, carry):
            pixels = pixel_rows[pl.ds(base + meta[k][0, f], dates, stride=pitch), :]
            v_ref[k * feet + f] = jnp.where(lane < meta[k][1, f], pixels, 0.0)
            return carry

        lax.fori_loop(0, feet, take, 0, unroll=8)
    tiles = []
    for first in range(0, parts * feet, LANES):

        def add(f, total):
            one = jnp.sum(v_ref[first + f], axis=1, keepdims=True)
            return jnp.where(lane == f, one, total)

        tiles.append(lax.fori_loop(0, LANES, add, jnp.zeros((dates, LANES), jnp.float32), unroll=32))
    counts = jnp.broadcast_to(both[0].astype(jnp.float32), (dates, index.shape[1]))
    sums = jnp.concatenate([jnp.concatenate(tiles, axis=1), counts], axis=0)
    held = jnp.zeros((places.shape[0], 2 * dates), jnp.float32)
    for piece in split(sums, 3):
        held = held + lax.dot_general(places, piece, (((1,), (1,)), ((), ())), preferred_element_type=jnp.float32)
    for n in range(parts * PAIR_CAP):
        at = pl.ds(n * dates, dates)
        sums_ref[:, 0, at] = held[n * owners:(n + 1) * owners, :dates]
        sums_ref[:, 1, at] = held[n * owners:(n + 1) * owners, dates:]
    for m in range(parts):
        for copy in store(m):
            copy.wait()


def edges(ends, up, down, brim, inner, meta, taps, place, order, owners):
    parts = len(order)
    tiles, dates, _, _ = ends.shape
    per = tiles // parts
    feet = meta[0].shape[1]
    rows = inner[0].shape[2] + 2 * EDGE
    here = pl.BlockSpec(memory_space=pltpu.HBM)
    resident = pl.BlockSpec(memory_space=pltpu.VMEM)
    return pl.pallas_call(
        functools.partial(edge_kernel, order, feet),
        grid_spec=pltpu.PrefetchScalarGridSpec(
            num_scalar_prefetch=2 + parts,
            grid=(),
            in_specs=[resident] * parts + [here] * (4 + parts),
            out_specs=[here] * parts + [resident],
            scratch_shapes=[
                pltpu.VMEM((parts, per, 2 * RADIUS * dates, LANES), jnp.float32),
                pltpu.VMEM((parts, per, 4 * EDGE * dates, LANES), jnp.float32),
                pltpu.VMEM(up.shape, jnp.float32),
                pltpu.VMEM(up.shape, jnp.float32),
                pltpu.VMEM(ends.shape, jnp.float32),
                pltpu.VMEM((12 * LANES, per * LANES), jnp.bfloat16),
                pltpu.VMEM((parts, per, dates, rows + EDGE, LANES), jnp.float32),
                pltpu.VMEM((parts * feet, dates, LANES), jnp.float32),
                pltpu.SemaphoreType.DMA((3,)),
                pltpu.SemaphoreType.DMA((parts,)),
                pltpu.SemaphoreType.DMA((parts, 2)),
                pltpu.SemaphoreType.DMA((parts,)),
            ],
        ),
        out_shape=[jax.ShapeDtypeStruct((per, dates, 2 * EDGE, LANES), jnp.float32)] * parts
        + [jax.ShapeDtypeStruct((owners, 2, parts * PAIR_CAP * dates), jnp.float32)],
        compiler_params=params(63),
        cost_estimate=cost(8),
    )(place, taps, *meta, *meta, ends, up, down, brim, *inner)


def temporal_kernel(parts, with_base, first_tile, tile_step, place, taps, *rest):
    pieces = rest[:parts]
    out, z_ref, f_ref, out_ref, in_sem, out_sem = rest[parts + with_base:]
    count, total, _, _ = out_ref.shape
    per = pieces[0].shape[0]
    local = total // parts
    pad = REACH * DILATION
    step = 8

    def load(n):
        rows = pl.ds(pl.multiple_of(n * EDGE, EDGE), EDGE)
        return [
            pltpu.make_async_copy(
                pieces[k].at[:, :, rows, :],
                z_ref.at[n, :, pl.ds(REACH + (place[0] ^ k) * local, local)], in_sem.at[n, k])
            for k in range(parts)
        ]

    def store(n):
        tile = first_tile + n * tile_step
        rows = pl.ds(pl.multiple_of(tile * EDGE, EDGE), EDGE)
        return pltpu.make_async_copy(out_ref.at[n], out.at[:, rows, :], out_sem.at[n])

    for n in range(count):
        for copy in load(n):
            copy.start()
    none = jnp.zeros((REACH, EDGE, LANES), jnp.float32)
    wide = jnp.zeros((pad, EDGE, LANES), jnp.float32)
    for h in range(per):
        for n in range(count):
            z_ref[n, h, 0:REACH] = none
            z_ref[n, h, REACH + total:REACH + total + REACH] = none
        f_ref[h, 0:pad] = wide
        f_ref[h, pad + total:pad + total + pad] = wide
    own = 1.0 - taps[0, REACH]
    own_wide = 1.0 - taps[1, REACH]
    others = [k for k in range(2 * REACH + 1) if k != REACH]

    def one(n, carry):
        for copy in load(n):
            copy.wait()
        for h in range(per):
            for t in range(0, total, step):
                z = z_ref[n, h, t:t + step + 2 * REACH]
                kept = own * z[REACH:REACH + step]
                for k in others:
                    kept = kept - taps[0, k] * z[k:k + step]
                f_ref[h, pad + t:pad + t + step] = kept
            for t in range(0, total, step):
                kept = own_wide * f_ref[h, pad + t:pad + t + step]
                for k in others:
                    kept = kept - taps[1, k] * f_ref[h, t + k * DILATION:t + k * DILATION + step]
                out_ref[n, t:t + step, :, h * LANES:(h + 1) * LANES] = kept
        store(n).start()
        return carry

    lax.fori_loop(0, count, one, 0)
    for n in range(count):
        store(n).wait()


def temporal(pieces, base, taps, place, first_tile, tile_step, rows):
    parts = len(pieces)
    per, local, here, _ = pieces[0].shape
    total = local * parts
    extra = [] if base is None else [base]
    count = here // EDGE
    width = per * LANES
    return pl.pallas_call(
        functools.partial(temporal_kernel, parts, len(extra), first_tile, tile_step),
        grid_spec=pltpu.PrefetchScalarGridSpec(
            num_scalar_prefetch=2,
            grid=(),
            in_specs=[pl.BlockSpec(memory_space=pl.ANY)] * (parts + len(extra)),
            out_specs=pl.BlockSpec(memory_space=pltpu.HBM),
            scratch_shapes=[
                pltpu.VMEM((count, per, total + 2 * REACH, EDGE, LANES), jnp.float32),
                pltpu.VMEM((per, total + 2 * REACH * DILATION, EDGE, LANES), jnp.float32),
                pltpu.VMEM((count, total, EDGE, width), jnp.float32),
                pltpu.SemaphoreType.DMA((count, parts)),
                pltpu.SemaphoreType.DMA((count,)),
            ],
        ),
        out_shape=jax.ShapeDtypeStruct((total, rows, width), jnp.float32),
        input_output_aliases={} if base is None else {2 + parts: 0},
        compiler_params=params(24),
        cost_estimate=cost(2.5 + 0.4 * count),
    )(place, taps, *pieces, *extra)


def owner_kernel(parts, strips, taps, got_ref, anomaly_ref, series_ref):
    owners = parts * strips
    slots = owners * PAIR_CAP
    dates = got_ref.shape[2] // PAIR_CAP
    local = dates // parts
    sums, held = got_ref[:, 0, :], got_ref[:, 1, :]
    rows, weights = [], []
    for block in range(parts):
        for slot in range(PAIR_CAP):
            at = (block * PAIR_CAP + slot) * local
            rows.append(jnp.concatenate(
                [sums[e * strips:(e + 1) * strips, at:at + local] for e in range(parts)], axis=1))
            weights.append(held[0:strips, at:at + 1])
    sums = jnp.concatenate(rows, axis=0)
    weight = jnp.concatenate(weights, axis=0)
    shape = (dates, dates)
    lag = lax.broadcasted_iota(jnp.int32, shape, 0) - lax.broadcasted_iota(jnp.int32, shape, 1)
    for level, spacing in ((0, 1), (1, DILATION)):
        filt = jnp.where(lag == 0, 1.0, 0.0)
        for k in range(2 * REACH + 1):
            filt = filt - jnp.where(lag == (k - REACH) * spacing, taps[level, k], 0.0)
        sums = jnp.dot(sums, filt, precision=HIGHEST, preferred_element_type=jnp.float32)
    mean = sums / jnp.where(weight > 0, weight, 1.0)
    asset = jnp.sum(weight * mean, axis=0, keepdims=True) / jnp.sum(weight, axis=0, keepdims=True)
    odd = jnp.where(weight > 0, mean - asset, 0.0)
    series_ref[...] = asset
    shape = (slots, slots)
    to = lax.broadcasted_iota(jnp.int32, shape, 0)
    source = lax.broadcasted_iota(jnp.int32, shape, 1)
    block, rest = source // (PAIR_CAP * strips), source % (PAIR_CAP * strips)
    place_of = block * (PAIR_CAP * strips) + (rest % strips) * PAIR_CAP + rest // strips
    order = jnp.where(to == place_of, 1.0, 0.0)
    anomaly_ref[0] = jnp.dot(order, odd, precision=HIGHEST, preferred_element_type=jnp.float32)


def owner_series(got, taps, parts, strips):
    owners = parts * strips
    dates = got.shape[2] // PAIR_CAP
    slots = owners * PAIR_CAP
    return pl.pallas_call(
        functools.partial(owner_kernel, parts, strips),
        grid_spec=pltpu.PrefetchScalarGridSpec(
            num_scalar_prefetch=1,
            grid=(),
            in_specs=[pl.BlockSpec(memory_space=pltpu.VMEM)],
            out_specs=[pl.BlockSpec(memory_space=pltpu.VMEM)] * 2,
        ),
        out_shape=[
            jax.ShapeDtypeStruct((1, slots, dates), jnp.float32),
            jax.ShapeDtypeStruct((1, dates), jnp.float32),
        ],
        compiler_params=params(24),
        cost_estimate=cost(1.8),
    )(taps, got)


def spread_meta(meta, offset, swap):
    known = sorted(meta)
    got = swap(jnp.concatenate([meta[k] for k in known], axis=1), offset)
    width = meta[0].shape[1]
    return meta | {k ^ offset: got[:, n * width:(n + 1) * width] for n, k in enumerate(known)}


def shards(stack, spatial_taps, temporal_taps, foot_tile, foot_row, foot_count, foot_owner):
    parts, strips = lax.axis_size("date"), lax.axis_size("strip")
    place = lax.axis_index("date").astype(jnp.int32)[None]
    dates, rows, cols = stack.shape
    feet = foot_row.shape[0]
    owner = foot_owner[:, 0]
    position = jnp.arange(feet, dtype=jnp.int32)
    earlier = (owner[:, None] == owner[None, :]) & (position[None, :] < position[:, None])
    slot = jnp.sum(earlier.astype(jnp.int32), axis=1)
    own = jnp.stack([foot_tile * (dates * (rows + EDGE)) + foot_row, foot_count, owner, slot])

    def swap(value, offset):
        return lax.ppermute(value, "date", [(i, i ^ offset) for i in range(parts)])

    order = (*range(2, parts), 1, 0)
    inner, far_inner = {}, {}
    lead = order[0]
    inner[lead], brim, last_rows, first_rows, ends = interior(stack, None, spatial_taps, place, (lead,), 0, parts)
    far_inner[lead] = swap(inner[lead], lead)
    up = lax.ppermute(last_rows, "strip", [(i, i + 1) for i in range(strips - 1)])
    down = lax.ppermute(first_rows, "strip", [(i + 1, i) for i in range(strips - 1)])
    own, brim = lax.optimization_barrier((own, brim))
    meta = {0: own}
    for bit in range(parts.bit_length() - 2, 0, -1):
        meta = spread_meta(meta, 1 << bit, swap)
    *made, brim = interior(stack, brim, spatial_taps, place, order[1:], 1, parts)
    for n, offset in enumerate(order[1:]):
        inner[offset] = made[n]
        if offset > 1:
            far_inner[offset] = swap(inner[offset], offset)
    known = sorted(meta)
    *held, far_inner[lead], brim = lax.optimization_barrier((*[meta[k] for k in known], far_inner[lead], brim))
    meta = spread_meta(dict(zip(known, held)), 1, swap)
    meta = [meta[k] for k in range(parts)]
    *made, sums = edges(
        ends, up, down, brim, [inner[k] for k in order], meta, spatial_taps, place, order, parts * strips)
    rim = dict(zip(order, made))
    far_inner[1] = swap(inner[1], 1)
    got = lax.all_to_all(sums, ("date", "strip"), split_axis=0, concat_axis=0, tiled=True)
    gate, *made = lax.optimization_barrier((swap(rim[1], 1), *[rim[k] for k in order[:-2]]))
    far_rim = {k: swap(made[n], k) for n, k in enumerate(order[:-2])}
    far_rim[1] = gate
    last = rows // EDGE - 1
    residual = temporal(
        [inner[0]] + [far_inner[k] for k in range(1, parts)], None, temporal_taps, place, 1, 1, rows)
    got, residual = lax.optimization_barrier((got, residual))
    anomaly, series = owner_series(got, temporal_taps, parts, strips)
    residual = temporal(
        [rim[0]] + [far_rim[k] for k in range(1, parts)], residual, temporal_taps, place, 0, last, rows)
    return residual, anomaly, series


def solution(mesh):
    placed = (
        P("date", "strip", None),
        P(),
        P(),
        P(("date", "strip")),
        P(("date", "strip")),
        P(("date", "strip")),
        P(("date", "strip"), None),
    )
    return jax.shard_map(
        shards,
        mesh=mesh,
        in_specs=placed,
        out_specs=(
            P(None, "strip", "date"),
            P(("date", "strip"), None, None),
            P(("date", "strip"), None),
        ),
        check_vma=False,
    )
```

```python
import functools

import jax
import jax.numpy as jnp
from jax import lax
from jax.experimental import pallas as pl
from jax.experimental.pallas import tpu as pltpu
from jax.sharding import PartitionSpec as P

TILE = 128
RADIUS = 6
REACH = 2
DILATION = 8
PAIR_CAP = 2
LANES = 128
EDGE = 8
HIGHEST = lax.Precision.HIGHEST


def params(mebibytes):
    return pltpu.CompilerParams(vmem_limit_bytes=mebibytes * 1024 * 1024)


def cost(micros):
    return pl.CostEstimate(flops=int(micros * 1153.5e6), bytes_accessed=int(micros * 3.69e6), transcendentals=0)


def pick_taps(at, taps):
    count = taps.shape[0]
    total = taps[0]
    for k in range(1, count):
        total = total + taps[k]
    out = jnp.zeros(at.shape, jnp.float32)
    for k in range(count):
        out = jnp.where(at == k, taps[k], out)
    return out / jnp.full(at.shape, total, jnp.float32)


def split(value, count):
    out = []
    for _ in range(count):
        piece = value.astype(jnp.bfloat16)
        out.append(piece)
        value = value - piece.astype(jnp.float32)
    return out


def spread(value, axis):
    high, mid = split(value, 2)
    return jnp.concatenate([high, high, high, mid], axis=axis)


def fill_columns(col_ref, taps):
    shape = (LANES, LANES)
    lag = lax.broadcasted_iota(jnp.int32, shape, 0) - lax.broadcasted_iota(jnp.int32, shape, 1)
    near = split(pick_taps(lag + RADIUS, taps), 3)
    far = pick_taps(jnp.where(lag > 0, lag + RADIUS - LANES, lag + RADIUS + LANES), taps)
    above = split(jnp.where(lag > 0, far, 0.0), 3)
    below = split(jnp.where(lag > 0, 0.0, far), 3)
    for n, piece in enumerate((0, 1, 2, 0)):
        at = n * 3 * LANES
        for i, pair in enumerate(((near, above), (below, near), (above, below))):
            for j, block in enumerate(pair):
                col_ref[at + i * LANES:at + (i + 1) * LANES, j * LANES:(j + 1) * LANES] = block[piece]


def row_band(out_rows, in_rows, taps):
    shape = (out_rows, 4 * in_rows)
    lane = lax.broadcasted_iota(jnp.int32, shape, 1)
    row = lax.broadcasted_iota(jnp.int32, shape, 0)
    part = jnp.zeros(shape, jnp.int32)
    for n in range(1, 4):
        part = jnp.where(lane >= n * in_rows, n, part)
    return lane - part * in_rows, row, part


def pieces_of(values, part):
    high, mid, low = [p.astype(jnp.float32) for p in split(values, 3)]
    return jnp.where(part == 1, mid, jnp.where(part == 2, low, high)).astype(jnp.bfloat16)


def filter_columns(mid, rim, col):
    rows = mid.shape[0]
    window = jnp.concatenate([mid, rim], axis=1)
    return jnp.dot(spread(window, 1), col, preferred_element_type=jnp.float32)


def rim_tile(left, right, block, parts):
    lane = lax.broadcasted_iota(jnp.int32, left.shape, len(left.shape) - 1)
    first = lane < LANES // 2
    keep = (first & (block < parts - 1)) | (~first & (block > 0))
    return jnp.where(keep, jnp.where(first, right, left), 0.0)


def chosen(n, values):
    out = values[0]
    for m in range(1, len(values)):
        out = jnp.where(n == m, values[m], out)
    return out


def interior_kernel(offsets, slot, parts, group, place, taps, stack, *rest):
    count = len(offsets)
    first = slot == 0
    if not first:
        rest = rest[1:]
    outs, brim, rest = rest[:count], rest[count], rest[count + 1:]
    if first:
        up, down, ends, mid_ref, left_ref, right_ref, halo_ref, up_ref, down_ref, halo_sem, halo_out_sem, *rest = rest
    else:
        x_ref, *rest = rest
    out_ref, brim_ref, col_ref, row_ref, in_sem, out_sem, brim_sem = rest
    _, per, dates, inner, _ = out_ref.shape
    width = per * LANES
    rows = inner + 2 * EDGE
    cols = width * parts
    steps = dates // group

    def bounds(block):
        start = block * width
        places = start, jnp.maximum(start - LANES, 0), jnp.minimum(start + width, cols - LANES)
        return [pl.multiple_of(at, LANES) for at in places]

    def load(g):
        at = pl.ds(g * group, group)
        if not first:
            return [pltpu.make_async_copy(stack.at[at], x_ref.at[at], in_sem.at[0, g])]
        return [
            pltpu.make_async_copy(stack.at[at, :, pl.ds(start, ref.shape[2])], ref.at[at], in_sem.at[n, g])
            for n, (start, ref) in enumerate(zip(bounds(place[0] ^ offsets[0]), (mid_ref, left_ref, right_ref)))
        ]

    def store(m, g):
        at = pl.ds(g * group, group)
        return pltpu.make_async_copy(out_ref.at[m, :, at], outs[m].at[:, at], out_sem.at[m, g])

    def store_brim(n):
        return pltpu.make_async_copy(brim_ref.at[n], brim.at[slot + n], brim_sem.at[n])

    for g in range(steps):
        for copy in load(g):
            copy.start()
    halo_loads, halo_stores = [], []
    if first:
        halo_loads = [
            pltpu.make_async_copy(
                stack.at[:, pl.ds(side * (rows - EDGE), EDGE), pl.ds(c * LANES, LANES)],
                halo_ref.at[c, :, pl.ds(side * EDGE, EDGE), :], halo_sem.at[side, c])
            for side in range(2) for c in range(cols // LANES)
        ]
        halo_stores = [
            pltpu.make_async_copy(halo_ref, ends, halo_out_sem.at[0]),
            pltpu.make_async_copy(up_ref, up, halo_out_sem.at[1]),
            pltpu.make_async_copy(down_ref, down, halo_out_sem.at[2]),
        ]
        for copy in halo_loads:
            copy.start()
    fill_columns(col_ref, taps)
    q, r, part = row_band(inner, rows, taps)
    row_ref[...] = pieces_of(pick_taps(q - r - (EDGE - RADIUS), taps), part)

    def pack(c, carry):
        at = pl.ds(pl.multiple_of(c * LANES, LANES), LANES)
        rows_of = halo_ref.at[c].reshape(dates * 2 * EDGE, LANES)
        for r in range(RADIUS):
            up_ref[r, :, at] = rows_of[pl.ds(2 * EDGE - RADIUS + r, dates, stride=2 * EDGE), :]
            down_ref[r, :, at] = rows_of[pl.ds(r, dates, stride=2 * EDGE), :]
        return carry

    def step(i, carry):
        n, g = i // steps, i % steps
        block = place[0] ^ chosen(n, offsets)
        at = pl.ds(g * group, group)

        @pl.when(n == 0)
        def _():
            for copy in load(g):
                copy.wait()

        if first:
            @pl.when(i == steps - 1)
            def _():
                for copy in halo_loads:
                    copy.wait()
                lax.fori_loop(0, cols // LANES, pack, 0)
                for copy in halo_stores:
                    copy.start()

            mid, left, right = mid_ref[at], left_ref[at], right_ref[at]
        else:
            start, before, after = bounds(block)
            mid, left, right = [x_ref[at, :, pl.ds(f, w)] for f, w in ((start, width), (before, LANES), (after, LANES))]
        rim = rim_tile(left, right, block, parts)
        across = filter_columns(mid.reshape(group * rows, width), rim.reshape(group * rows, LANES), col_ref[...])
        for t in range(group):
            one = across[t * rows:(t + 1) * rows]
            low = jnp.dot(row_ref[...], spread(one, 0), preferred_element_type=jnp.float32)
            done = mid[t, EDGE:rows - EDGE, :] - low
            for h in range(per):
                out_ref[n, h, g * group + t] = done[:, h * LANES:(h + 1) * LANES]
                for side in range(2):
                    lines = one[side * (rows - 2 * EDGE):side * (rows - 2 * EDGE) + 2 * EDGE, h * LANES:(h + 1) * LANES]
                    date = g * group + t
                    at = ((date // EDGE) * 4 * EDGE + side * 2 * EDGE) * EDGE + date % EDGE
                    brim_ref[n, h, pl.ds(at, 2 * EDGE, stride=EDGE), :] = lines
        for m in range(count):
            @pl.when(n == m)
            def _():
                store(m, g).start()

        @pl.when(g == steps - 1)
        def _():
            store_brim(n).start()

        return carry

    lax.fori_loop(0, count * steps, step, 0)
    for copy in halo_stores:
        copy.wait()
    for m in range(count):
        for g in range(steps):
            store(m, g).wait()
        store_brim(m).wait()


def interior(stack, brim, taps, place, offsets, slot, parts):
    dates, rows, cols = stack.shape
    width = cols // parts
    per = width // LANES
    group = min(8, dates)
    inner = rows - 2 * EDGE
    count = len(offsets)
    first = slot == 0
    here = pl.BlockSpec(memory_space=pltpu.HBM)
    out_shape = [jax.ShapeDtypeStruct((per, dates, inner, LANES), jnp.float32)] * count
    out_shape += [jax.ShapeDtypeStruct((parts, per, 4 * EDGE * dates, LANES), jnp.float32)]
    if first:
        out_shape += [jax.ShapeDtypeStruct((RADIUS, dates, cols), jnp.float32)] * 2
        out_shape += [jax.ShapeDtypeStruct((cols // LANES, dates, 2 * EDGE, LANES), jnp.float32)]
        scratch = [pltpu.VMEM((dates, rows, span), jnp.float32) for span in (width, LANES, LANES)] + [
            pltpu.VMEM((cols // LANES, dates, 2 * EDGE, LANES), jnp.float32),
            pltpu.VMEM((RADIUS, dates, cols), jnp.float32),
            pltpu.VMEM((RADIUS, dates, cols), jnp.float32),
            pltpu.SemaphoreType.DMA((2, cols // LANES)),
            pltpu.SemaphoreType.DMA((3,)),
        ]
    else:
        scratch = [pltpu.VMEM((dates, rows, cols), jnp.float32)]
    return pl.pallas_call(
        functools.partial(interior_kernel, offsets, slot, parts, group),
        grid_spec=pltpu.PrefetchScalarGridSpec(
            num_scalar_prefetch=2,
            grid=(),
            in_specs=[here] * (1 if first else 2),
            out_specs=[here] * len(out_shape),
            scratch_shapes=scratch + [
                pltpu.VMEM((count, per, dates, inner, LANES), jnp.float32),
                pltpu.VMEM((count, per, 4 * EDGE * dates, LANES), jnp.float32),
                pltpu.VMEM((12 * LANES, width), jnp.bfloat16),
                pltpu.VMEM((inner, 4 * rows), jnp.bfloat16),
                pltpu.SemaphoreType.DMA((3, dates // group)),
                pltpu.SemaphoreType.DMA((count, dates // group)),
                pltpu.SemaphoreType.DMA((count,)),
            ],
        ),
        out_shape=out_shape,
        input_output_aliases={} if first else {3: count},
        compiler_params=params(63),
        cost_estimate=cost(2.5 + 2.5 * count),
    )(place, taps, stack, *([] if first else [brim]))


def edge_kernel(order, feet, place, taps, *rest):
    parts = len(order)
    meta, vectors, rest = rest[:parts], rest[parts:2 * parts], rest[2 * parts:]
    ends, up, down, brim, *rest = rest
    inner, outs, rest = rest[:parts], rest[parts:2 * parts], rest[2 * parts:]
    sums_ref, across_ref, brim_ref, up_ref, down_ref, ends_ref, col_ref, x_ref, v_ref = rest[:9]
    halo_sem, brim_sem, out_sem, x_sem = rest[9:]
    _, dates, cols = up_ref.shape
    width = cols // parts
    per = width // LANES
    pitch = x_ref.shape[3]
    rows = pitch - EDGE
    owners = sums_ref.shape[0]
    halos = [
        pltpu.make_async_copy(whole, ref, halo_sem.at[n])
        for n, (whole, ref) in enumerate(((up, up_ref), (down, down_ref), (ends, ends_ref)))
    ]
    for copy in halos:
        copy.start()
    for n in range(parts):
        pltpu.make_async_copy(brim.at[n], brim_ref.at[n], brim_sem.at[n]).start()
    middles = [
        pltpu.make_async_copy(inner[n], x_ref.at[n, :, :, pl.ds(EDGE, rows - 2 * EDGE), :], x_sem.at[n]) for n in range(parts)
    ]
    for copy in middles:
        copy.start()
    fill_columns(col_ref, taps)
    total = taps[0]
    for k in range(1, 2 * RADIUS + 1):
        total = total + taps[k]
    scale = 1.0 / jnp.full((dates, LANES), total, jnp.float32)
    flat = ends_ref.reshape(cols // LANES, dates * 2 * EDGE, LANES)

    def store(n):
        return [
            pltpu.make_async_copy(
                x_ref.at[n, :, :, pl.ds(side * (rows - EDGE), EDGE), :],
                outs[n].at[:, :, pl.ds(side * EDGE, EDGE), :], out_sem.at[n, side])
            for side in range(2)
        ]

    for copy in halos:
        copy.wait()

    mids, rims = [], []
    for n in range(parts):
        block = place[0] ^ order[n]
        start = pl.multiple_of(block * width, LANES)
        before = pl.multiple_of(jnp.maximum(start - LANES, 0), LANES)
        after = pl.multiple_of(jnp.minimum(start + width, cols - LANES), LANES)

        def both(first, span):
            at = pl.ds(first, span)
            return jnp.concatenate([up_ref[:, :, at], down_ref[:, :, at]], axis=0).reshape(2 * RADIUS * dates, span)

        mids.append(both(start, width))
        rims.append(rim_tile(both(before, LANES), both(after, LANES), block, parts))
    across = filter_columns(jnp.concatenate(mids, axis=0), jnp.concatenate(rims, axis=0), col_ref[...])
    span = 2 * RADIUS * dates
    for n in range(parts):
        for h in range(per):
            across_ref[n, h] = across[n * span:(n + 1) * span, h * LANES:(h + 1) * LANES]

    def one(n, carry):
        block = place[0] ^ chosen(n, order)
        every = x_ref.at[n].reshape(per, dates * pitch, LANES)
        pltpu.make_async_copy(brim.at[n], brim_ref.at[n], brim_sem.at[n]).wait()

        def half(h, carry):
            for side in range(2):
                held = []
                for q in range(2 * RADIUS + EDGE):
                    halo = q < RADIUS if side == 0 else q >= RADIUS + EDGE
                    if halo:
                        at = q if side == 0 else q - EDGE
                        held.append(across_ref[n, h, at * dates:(at + 1) * dates, :])
                    else:
                        at = q - RADIUS if side == 0 else 3 * EDGE - RADIUS + q
                        held.append(jnp.concatenate([
                            brim_ref[n, h, (d * 4 * EDGE + at) * EDGE:(d * 4 * EDGE + at + 1) * EDGE, :]
                            for d in range(dates // EDGE)
                        ], axis=0))
                for r in range(EDGE):
                    low = taps[0] * held[r]
                    for j in range(1, 2 * RADIUS + 1):
                        low = low + taps[j] * held[r + j]
                    at = pl.ds(side * EDGE + r, dates, stride=2 * EDGE)
                    done = flat[block * per + h, at, :] - scale * low
                    every[h, pl.ds(side * (rows - EDGE) + r, dates, stride=pitch), :] = done
            return carry

        lax.fori_loop(0, per, half, 0)
        for m in range(parts):
            @pl.when(n == m)
            def _():
                for copy in store(m):
                    copy.start()
        return carry

    lax.fori_loop(0, parts, one, 0)

    lane = lax.broadcasted_iota(jnp.int32, (dates, LANES), 1)
    both = [jnp.concatenate([ref[n:n + 1, :] for ref in vectors], axis=1) for n in range(1, 4)]
    index = lax.broadcasted_iota(jnp.int32, both[0].shape, 1)
    source = (index // feet) ^ place[0]
    named = lax.broadcasted_iota(jnp.int32, (owners, index.shape[1]), 0) == both[1]
    places = []
    for block in range(parts):
        for slot in range(PAIR_CAP):
            hit = named & (source == block) & (both[2] == slot)
            places.append(jnp.where(hit, 1.0, 0.0).astype(jnp.bfloat16))
    places = jnp.concatenate(places, axis=0)
    pixel_rows = x_ref.reshape(parts * per * dates * pitch, LANES)
    for copy in middles:
        copy.wait()
    for k in range(parts):
        base = order.index(k) * per * dates * pitch

        def take(f, carry):
            pixels = pixel_rows[pl.ds(base + meta[k][0, f], dates, stride=pitch), :]
            v_ref[k * feet + f] = jnp.where(lane < meta[k][1, f], pixels, 0.0)
            return carry

        lax.fori_loop(0, feet, take, 0, unroll=8)
    tiles = []
    for first in range(0, parts * feet, LANES):

        def add(f, total):
            one = jnp.sum(v_ref[first + f], axis=1, keepdims=True)
            return jnp.where(lane == f, one, total)

        tiles.append(lax.fori_loop(0, LANES, add, jnp.zeros((dates, LANES), jnp.float32), unroll=32))
    counts = jnp.broadcast_to(both[0].astype(jnp.float32), (dates, index.shape[1]))
    sums = jnp.concatenate([jnp.concatenate(tiles, axis=1), counts], axis=0)
    held = jnp.zeros((places.shape[0], 2 * dates), jnp.float32)
    for piece in split(sums, 3):
        held = held + lax.dot_general(places, piece, (((1,), (1,)), ((), ())), preferred_element_type=jnp.float32)
    for n in range(parts * PAIR_CAP):
        at = pl.ds(n * dates, dates)
        sums_ref[:, 0, at] = held[n * owners:(n + 1) * owners, :dates]
        sums_ref[:, 1, at] = held[n * owners:(n + 1) * owners, dates:]
    for m in range(parts):
        for copy in store(m):
            copy.wait()


def edges(ends, up, down, brim, inner, meta, taps, place, order, owners):
    parts = len(order)
    tiles, dates, _, _ = ends.shape
    per = tiles // parts
    feet = meta[0].shape[1]
    rows = inner[0].shape[2] + 2 * EDGE
    here = pl.BlockSpec(memory_space=pltpu.HBM)
    resident = pl.BlockSpec(memory_space=pltpu.VMEM)
    return pl.pallas_call(
        functools.partial(edge_kernel, order, feet),
        grid_spec=pltpu.PrefetchScalarGridSpec(
            num_scalar_prefetch=2 + parts,
            grid=(),
            in_specs=[resident] * parts + [here] * (4 + parts),
            out_specs=[here] * parts + [resident],
            scratch_shapes=[
                pltpu.VMEM((parts, per, 2 * RADIUS * dates, LANES), jnp.float32),
                pltpu.VMEM((parts, per, 4 * EDGE * dates, LANES), jnp.float32),
                pltpu.VMEM(up.shape, jnp.float32),
                pltpu.VMEM(up.shape, jnp.float32),
                pltpu.VMEM(ends.shape, jnp.float32),
                pltpu.VMEM((12 * LANES, per * LANES), jnp.bfloat16),
                pltpu.VMEM((parts, per, dates, rows + EDGE, LANES), jnp.float32),
                pltpu.VMEM((parts * feet, dates, LANES), jnp.float32),
                pltpu.SemaphoreType.DMA((3,)),
                pltpu.SemaphoreType.DMA((parts,)),
                pltpu.SemaphoreType.DMA((parts, 2)),
                pltpu.SemaphoreType.DMA((parts,)),
            ],
        ),
        out_shape=[jax.ShapeDtypeStruct((per, dates, 2 * EDGE, LANES), jnp.float32)] * parts
        + [jax.ShapeDtypeStruct((owners, 2, parts * PAIR_CAP * dates), jnp.float32)],
        compiler_params=params(63),
        cost_estimate=cost(9),
    )(place, taps, *meta, *meta, ends, up, down, brim, *inner)


def temporal_kernel(parts, with_base, first_tile, tile_step, place, taps, *rest):
    pieces = rest[:parts]
    out, z_ref, f_ref, out_ref, in_sem, out_sem = rest[parts + with_base:]
    count, total, _, _ = out_ref.shape
    per = pieces[0].shape[0]
    local = total // parts
    pad = REACH * DILATION
    step = 8

    def load(n):
        rows = pl.ds(pl.multiple_of(n * EDGE, EDGE), EDGE)
        return [
            pltpu.make_async_copy(
                pieces[k].at[:, :, rows, :],
                z_ref.at[n, :, pl.ds(REACH + (place[0] ^ k) * local, local)], in_sem.at[n, k])
            for k in range(parts)
        ]

    def store(n):
        tile = first_tile + n * tile_step
        rows = pl.ds(pl.multiple_of(tile * EDGE, EDGE), EDGE)
        return pltpu.make_async_copy(out_ref.at[n], out.at[:, rows, :], out_sem.at[n])

    for n in range(count):
        for copy in load(n):
            copy.start()
    none = jnp.zeros((REACH, EDGE, LANES), jnp.float32)
    wide = jnp.zeros((pad, EDGE, LANES), jnp.float32)
    for h in range(per):
        for n in range(count):
            z_ref[n, h, 0:REACH] = none
            z_ref[n, h, REACH + total:REACH + total + REACH] = none
        f_ref[h, 0:pad] = wide
        f_ref[h, pad + total:pad + total + pad] = wide
    own = 1.0 - taps[0, REACH]
    own_wide = 1.0 - taps[1, REACH]
    others = [k for k in range(2 * REACH + 1) if k != REACH]

    def one(n, carry):
        for copy in load(n):
            copy.wait()
        for h in range(per):
            for t in range(0, total, step):
                z = z_ref[n, h, t:t + step + 2 * REACH]
                kept = own * z[REACH:REACH + step]
                for k in others:
                    kept = kept - taps[0, k] * z[k:k + step]
                f_ref[h, pad + t:pad + t + step] = kept
            for t in range(0, total, step):
                kept = own_wide * f_ref[h, pad + t:pad + t + step]
                for k in others:
                    kept = kept - taps[1, k] * f_ref[h, t + k * DILATION:t + k * DILATION + step]
                out_ref[n, t:t + step, :, h * LANES:(h + 1) * LANES] = kept
        store(n).start()
        return carry

    lax.fori_loop(0, count, one, 0)
    for n in range(count):
        store(n).wait()


def temporal(pieces, base, taps, place, first_tile, tile_step, rows):
    parts = len(pieces)
    per, local, here, _ = pieces[0].shape
    total = local * parts
    extra = [] if base is None else [base]
    count = here // EDGE
    width = per * LANES
    return pl.pallas_call(
        functools.partial(temporal_kernel, parts, len(extra), first_tile, tile_step),
        grid_spec=pltpu.PrefetchScalarGridSpec(
            num_scalar_prefetch=2,
            grid=(),
            in_specs=[pl.BlockSpec(memory_space=pl.ANY)] * (parts + len(extra)),
            out_specs=pl.BlockSpec(memory_space=pltpu.HBM),
            scratch_shapes=[
                pltpu.VMEM((count, per, total + 2 * REACH, EDGE, LANES), jnp.float32),
                pltpu.VMEM((per, total + 2 * REACH * DILATION, EDGE, LANES), jnp.float32),
                pltpu.VMEM((count, total, EDGE, width), jnp.float32),
                pltpu.SemaphoreType.DMA((count, parts)),
                pltpu.SemaphoreType.DMA((count,)),
            ],
        ),
        out_shape=jax.ShapeDtypeStruct((total, rows, width), jnp.float32),
        input_output_aliases={} if base is None else {2 + parts: 0},
        compiler_params=params(24),
        cost_estimate=cost(2.5 + 0.4 * count),
    )(place, taps, *pieces, *extra)


def owner_kernel(parts, strips, taps, got_ref, anomaly_ref, series_ref):
    owners = parts * strips
    slots = owners * PAIR_CAP
    dates = got_ref.shape[2] // PAIR_CAP
    local = dates // parts
    sums, held = got_ref[:, 0, :], got_ref[:, 1, :]
    rows, weights = [], []
    for block in range(parts):
        for slot in range(PAIR_CAP):
            at = (block * PAIR_CAP + slot) * local
            rows.append(jnp.concatenate(
                [sums[e * strips:(e + 1) * strips, at:at + local] for e in range(parts)], axis=1))
            weights.append(held[0:strips, at:at + 1])
    sums = jnp.concatenate(rows, axis=0)
    weight = jnp.concatenate(weights, axis=0)
    shape = (dates, dates)
    lag = lax.broadcasted_iota(jnp.int32, shape, 0) - lax.broadcasted_iota(jnp.int32, shape, 1)
    for level, spacing in ((0, 1), (1, DILATION)):
        filt = jnp.where(lag == 0, 1.0, 0.0)
        for k in range(2 * REACH + 1):
            filt = filt - jnp.where(lag == (k - REACH) * spacing, taps[level, k], 0.0)
        sums = jnp.dot(sums, filt, precision=HIGHEST, preferred_element_type=jnp.float32)
    mean = sums / jnp.where(weight > 0, weight, 1.0)
    asset = jnp.sum(weight * mean, axis=0, keepdims=True) / jnp.sum(weight, axis=0, keepdims=True)
    odd = jnp.where(weight > 0, mean - asset, 0.0)
    series_ref[...] = asset
    shape = (slots, slots)
    to = lax.broadcasted_iota(jnp.int32, shape, 0)
    source = lax.broadcasted_iota(jnp.int32, shape, 1)
    block, rest = source // (PAIR_CAP * strips), source % (PAIR_CAP * strips)
    place_of = block * (PAIR_CAP * strips) + (rest % strips) * PAIR_CAP + rest // strips
    order = jnp.where(to == place_of, 1.0, 0.0)
    anomaly_ref[0] = jnp.dot(order, odd, precision=HIGHEST, preferred_element_type=jnp.float32)


def owner_series(got, taps, parts, strips):
    owners = parts * strips
    dates = got.shape[2] // PAIR_CAP
    slots = owners * PAIR_CAP
    return pl.pallas_call(
        functools.partial(owner_kernel, parts, strips),
        grid_spec=pltpu.PrefetchScalarGridSpec(
            num_scalar_prefetch=1,
            grid=(),
            in_specs=[pl.BlockSpec(memory_space=pltpu.VMEM)],
            out_specs=[pl.BlockSpec(memory_space=pltpu.VMEM)] * 2,
        ),
        out_shape=[
            jax.ShapeDtypeStruct((1, slots, dates), jnp.float32),
            jax.ShapeDtypeStruct((1, dates), jnp.float32),
        ],
        compiler_params=params(24),
        cost_estimate=cost(1.8),
    )(taps, got)


def spread_meta(meta, offset, swap):
    known = sorted(meta)
    got = swap(jnp.concatenate([meta[k] for k in known], axis=1), offset)
    width = meta[0].shape[1]
    return meta | {k ^ offset: got[:, n * width:(n + 1) * width] for n, k in enumerate(known)}


def shards(stack, spatial_taps, temporal_taps, foot_tile, foot_row, foot_count, foot_owner):
    parts, strips = lax.axis_size("date"), lax.axis_size("strip")
    place = lax.axis_index("date").astype(jnp.int32)[None]
    dates, rows, cols = stack.shape
    feet = foot_row.shape[0]
    owner = foot_owner[:, 0]
    position = jnp.arange(feet, dtype=jnp.int32)
    earlier = (owner[:, None] == owner[None, :]) & (position[None, :] < position[:, None])
    slot = jnp.sum(earlier.astype(jnp.int32), axis=1)
    own = jnp.stack([foot_tile * (dates * (rows + EDGE)) + foot_row, foot_count, owner, slot])

    def swap(value, offset):
        return lax.ppermute(value, "date", [(i, i ^ offset) for i in range(parts)])

    order = (*range(2, parts), 1, 0)
    inner, far_inner = {}, {}
    lead = order[0]
    inner[lead], brim, last_rows, first_rows, ends = interior(stack, None, spatial_taps, place, (lead,), 0, parts)
    far_inner[lead] = swap(inner[lead], lead)
    up = lax.ppermute(last_rows, "strip", [(i, i + 1) for i in range(strips - 1)])
    down = lax.ppermute(first_rows, "strip", [(i + 1, i) for i in range(strips - 1)])
    own, brim = lax.optimization_barrier((own, brim))
    meta = {0: own}
    for bit in range(parts.bit_length() - 2, 0, -1):
        meta = spread_meta(meta, 1 << bit, swap)
    *made, brim = interior(stack, brim, spatial_taps, place, order[1:], 1, parts)
    for n, offset in enumerate(order[1:]):
        inner[offset] = made[n]
        if offset > 1:
            far_inner[offset] = swap(inner[offset], offset)
    known = sorted(meta)
    *held, brim = lax.optimization_barrier((*[meta[k] for k in known], brim))
    far_inner[lead], ends = lax.optimization_barrier((far_inner[lead], ends))
    meta = spread_meta(dict(zip(known, held)), 1, swap)
    meta = [meta[k] for k in range(parts)]
    *made, sums = edges(
        ends, up, down, brim, [inner[k] for k in order], meta, spatial_taps, place, order, parts * strips)
    rim = dict(zip(order, made))
    far_inner[1] = swap(inner[1], 1)
    got = lax.all_to_all(sums, ("date", "strip"), split_axis=0, concat_axis=0, tiled=True)
    far_rim = {k: swap(rim[k], k) for n, k in enumerate(order[:-1])}
    last = rows // EDGE - 1
    residual = temporal(
        [inner[0]] + [far_inner[k] for k in range(1, parts)], None, temporal_taps, place, 1, 1, rows)
    got, residual = lax.optimization_barrier((got, residual))
    anomaly, series = owner_series(got, temporal_taps, parts, strips)
    residual = temporal(
        [rim[0]] + [far_rim[k] for k in range(1, parts)], residual, temporal_taps, place, 0, last, rows)
    return residual, anomaly, series


def solution(mesh):
    placed = (
        P("date", "strip", None),
        P(),
        P(),
        P(("date", "strip")),
        P(("date", "strip")),
        P(("date", "strip")),
        P(("date", "strip"), None),
    )
    return jax.shard_map(
        shards,
        mesh=mesh,
        in_specs=placed,
        out_specs=(
            P(None, "strip", "date"),
            P(("date", "strip"), None, None),
            P(("date", "strip"), None),
        ),
        check_vma=False,
    )
```

```python
import functools

import jax
import jax.numpy as jnp
from jax import lax
from jax.experimental import pallas as pl
from jax.experimental.pallas import tpu as pltpu
from jax.sharding import PartitionSpec as P

TILE = 128
RADIUS = 6
REACH = 2
DILATION = 8
PAIR_CAP = 2
LANES = 128
EDGE = 8
HIGHEST = lax.Precision.HIGHEST


def params(mebibytes):
    return pltpu.CompilerParams(vmem_limit_bytes=mebibytes * 1024 * 1024)


def cost(micros):
    return pl.CostEstimate(flops=int(micros * 1153.5e6), bytes_accessed=int(micros * 3.69e6), transcendentals=0)


def pick_taps(at, taps):
    count = taps.shape[0]
    total = taps[0]
    for k in range(1, count):
        total = total + taps[k]
    out = jnp.zeros(at.shape, jnp.float32)
    for k in range(count):
        out = jnp.where(at == k, taps[k], out)
    return out / jnp.full(at.shape, total, jnp.float32)


def split(value, count):
    out = []
    for _ in range(count):
        piece = value.astype(jnp.bfloat16)
        out.append(piece)
        value = value - piece.astype(jnp.float32)
    return out


def spread(value, axis):
    high, mid = split(value, 2)
    return jnp.concatenate([high, high, high, mid], axis=axis)


def fill_columns(col_ref, taps):
    shape = (LANES, LANES)
    lag = lax.broadcasted_iota(jnp.int32, shape, 0) - lax.broadcasted_iota(jnp.int32, shape, 1)
    near = split(pick_taps(lag + RADIUS, taps), 3)
    far = pick_taps(jnp.where(lag > 0, lag + RADIUS - LANES, lag + RADIUS + LANES), taps)
    above = split(jnp.where(lag > 0, far, 0.0), 3)
    below = split(jnp.where(lag > 0, 0.0, far), 3)
    for n, piece in enumerate((0, 1, 2, 0)):
        at = n * 3 * LANES
        for i, pair in enumerate(((near, above), (below, near), (above, below))):
            for j, block in enumerate(pair):
                col_ref[at + i * LANES:at + (i + 1) * LANES, j * LANES:(j + 1) * LANES] = block[piece]


def row_band(out_rows, in_rows, taps):
    shape = (out_rows, 4 * in_rows)
    lane = lax.broadcasted_iota(jnp.int32, shape, 1)
    row = lax.broadcasted_iota(jnp.int32, shape, 0)
    part = jnp.zeros(shape, jnp.int32)
    for n in range(1, 4):
        part = jnp.where(lane >= n * in_rows, n, part)
    return lane - part * in_rows, row, part


def pieces_of(values, part):
    high, mid, low = [p.astype(jnp.float32) for p in split(values, 3)]
    return jnp.where(part == 1, mid, jnp.where(part == 2, low, high)).astype(jnp.bfloat16)


def filter_columns(mid, rim, col):
    rows = mid.shape[0]
    window = jnp.concatenate([mid, rim], axis=1)
    return jnp.dot(spread(window, 1), col, preferred_element_type=jnp.float32)


def rim_tile(left, right, block, parts):
    lane = lax.broadcasted_iota(jnp.int32, left.shape, len(left.shape) - 1)
    first = lane < LANES // 2
    keep = (first & (block < parts - 1)) | (~first & (block > 0))
    return jnp.where(keep, jnp.where(first, right, left), 0.0)


def chosen(n, values):
    out = values[0]
    for m in range(1, len(values)):
        out = jnp.where(n == m, values[m], out)
    return out


def interior_kernel(offsets, slot, parts, group, place, taps, stack, *rest):
    count = len(offsets)
    first = slot == 0
    if not first:
        rest = rest[1:]
    outs, brim, rest = rest[:count], rest[count], rest[count + 1:]
    if first:
        up, down, ends, mid_ref, left_ref, right_ref, halo_ref, up_ref, down_ref, halo_sem, halo_out_sem, *rest = rest
    else:
        x_ref, *rest = rest
    out_ref, brim_ref, col_ref, row_ref, in_sem, out_sem, brim_sem = rest
    _, per, dates, inner, _ = out_ref.shape
    width = per * LANES
    rows = inner + 2 * EDGE
    cols = width * parts
    steps = dates // group

    def bounds(block):
        start = block * width
        places = start, jnp.maximum(start - LANES, 0), jnp.minimum(start + width, cols - LANES)
        return [pl.multiple_of(at, LANES) for at in places]

    def load(g):
        at = pl.ds(g * group, group)
        if not first:
            return [pltpu.make_async_copy(stack.at[at], x_ref.at[at], in_sem.at[0, g])]
        return [
            pltpu.make_async_copy(stack.at[at, :, pl.ds(start, ref.shape[2])], ref.at[at], in_sem.at[n, g])
            for n, (start, ref) in enumerate(zip(bounds(place[0] ^ offsets[0]), (mid_ref, left_ref, right_ref)))
        ]

    def store(m, g):
        at = pl.ds(g * group, group)
        return pltpu.make_async_copy(out_ref.at[m, :, at], outs[m].at[:, at], out_sem.at[m, g])

    def store_brim(n):
        return pltpu.make_async_copy(brim_ref.at[n], brim.at[slot + n], brim_sem.at[n])

    for g in range(steps):
        for copy in load(g):
            copy.start()
    halo_loads, halo_stores = [], []
    if first:
        halo_loads = [
            pltpu.make_async_copy(
                stack.at[:, pl.ds(side * (rows - EDGE), EDGE), pl.ds(c * LANES, LANES)],
                halo_ref.at[c, :, pl.ds(side * EDGE, EDGE), :], halo_sem.at[side, c])
            for side in range(2) for c in range(cols // LANES)
        ]
        halo_stores = [
            pltpu.make_async_copy(halo_ref, ends, halo_out_sem.at[0]),
            pltpu.make_async_copy(up_ref, up, halo_out_sem.at[1]),
            pltpu.make_async_copy(down_ref, down, halo_out_sem.at[2]),
        ]
        for copy in halo_loads:
            copy.start()
    fill_columns(col_ref, taps)
    q, r, part = row_band(inner, rows, taps)
    row_ref[...] = pieces_of(pick_taps(q - r - (EDGE - RADIUS), taps), part)

    def pack(c, carry):
        at = pl.ds(pl.multiple_of(c * LANES, LANES), LANES)
        rows_of = halo_ref.at[c].reshape(dates * 2 * EDGE, LANES)
        for r in range(RADIUS):
            up_ref[r, :, at] = rows_of[pl.ds(2 * EDGE - RADIUS + r, dates, stride=2 * EDGE), :]
            down_ref[r, :, at] = rows_of[pl.ds(r, dates, stride=2 * EDGE), :]
        return carry

    def step(i, carry):
        n, g = i // steps, i % steps
        block = place[0] ^ chosen(n, offsets)
        at = pl.ds(g * group, group)

        @pl.when(n == 0)
        def _():
            for copy in load(g):
                copy.wait()

        if first:
            @pl.when(i == steps - 1)
            def _():
                for copy in halo_loads:
                    copy.wait()
                lax.fori_loop(0, cols // LANES, pack, 0)
                for copy in halo_stores:
                    copy.start()

            mid, left, right = mid_ref[at], left_ref[at], right_ref[at]
        else:
            start, before, after = bounds(block)
            mid, left, right = [x_ref[at, :, pl.ds(f, w)] for f, w in ((start, width), (before, LANES), (after, LANES))]
        rim = rim_tile(left, right, block, parts)
        across = filter_columns(mid.reshape(group * rows, width), rim.reshape(group * rows, LANES), col_ref[...])
        for t in range(group):
            one = across[t * rows:(t + 1) * rows]
            low = jnp.dot(row_ref[...], spread(one, 0), preferred_element_type=jnp.float32)
            done = mid[t, EDGE:rows - EDGE, :] - low
            for h in range(per):
                out_ref[n, h, g * group + t] = done[:, h * LANES:(h + 1) * LANES]
                for side in range(2):
                    lines = one[side * (rows - 2 * EDGE):side * (rows - 2 * EDGE) + 2 * EDGE, h * LANES:(h + 1) * LANES]
                    date = g * group + t
                    at = ((date // EDGE) * 4 * EDGE + side * 2 * EDGE) * EDGE + date % EDGE
                    brim_ref[n, h, pl.ds(at, 2 * EDGE, stride=EDGE), :] = lines
        for m in range(count):
            @pl.when(n == m)
            def _():
                store(m, g).start()

        @pl.when(g == steps - 1)
        def _():
            store_brim(n).start()

        return carry

    lax.fori_loop(0, count * steps, step, 0)
    for copy in halo_stores:
        copy.wait()
    for m in range(count):
        for g in range(steps):
            store(m, g).wait()
        store_brim(m).wait()


def interior(stack, brim, taps, place, offsets, slot, parts):
    dates, rows, cols = stack.shape
    width = cols // parts
    per = width // LANES
    group = min(8, dates)
    inner = rows - 2 * EDGE
    count = len(offsets)
    first = slot == 0
    here = pl.BlockSpec(memory_space=pltpu.HBM)
    out_shape = [jax.ShapeDtypeStruct((per, dates, inner, LANES), jnp.float32)] * count
    out_shape += [jax.ShapeDtypeStruct((parts, per, 4 * EDGE * dates, LANES), jnp.float32)]
    if first:
        out_shape += [jax.ShapeDtypeStruct((RADIUS, dates, cols), jnp.float32)] * 2
        out_shape += [jax.ShapeDtypeStruct((cols // LANES, dates, 2 * EDGE, LANES), jnp.float32)]
        scratch = [pltpu.VMEM((dates, rows, span), jnp.float32) for span in (width, LANES, LANES)] + [
            pltpu.VMEM((cols // LANES, dates, 2 * EDGE, LANES), jnp.float32),
            pltpu.VMEM((RADIUS, dates, cols), jnp.float32),
            pltpu.VMEM((RADIUS, dates, cols), jnp.float32),
            pltpu.SemaphoreType.DMA((2, cols // LANES)),
            pltpu.SemaphoreType.DMA((3,)),
        ]
    else:
        scratch = [pltpu.VMEM((dates, rows, cols), jnp.float32)]
    return pl.pallas_call(
        functools.partial(interior_kernel, offsets, slot, parts, group),
        grid_spec=pltpu.PrefetchScalarGridSpec(
            num_scalar_prefetch=2,
            grid=(),
            in_specs=[here] * (1 if first else 2),
            out_specs=[here] * len(out_shape),
            scratch_shapes=scratch + [
                pltpu.VMEM((count, per, dates, inner, LANES), jnp.float32),
                pltpu.VMEM((count, per, 4 * EDGE * dates, LANES), jnp.float32),
                pltpu.VMEM((12 * LANES, width), jnp.bfloat16),
                pltpu.VMEM((inner, 4 * rows), jnp.bfloat16),
                pltpu.SemaphoreType.DMA((3, dates // group)),
                pltpu.SemaphoreType.DMA((count, dates // group)),
                pltpu.SemaphoreType.DMA((count,)),
            ],
        ),
        out_shape=out_shape,
        input_output_aliases={} if first else {3: count},
        compiler_params=params(63),
        cost_estimate=cost(2.5 + 2.5 * count),
    )(place, taps, stack, *([] if first else [brim]))


def edge_kernel(order, feet, place, taps, *rest):
    parts = len(order)
    meta, vectors, rest = rest[:parts], rest[parts:2 * parts], rest[2 * parts:]
    ends, up, down, brim, *rest = rest
    inner, outs, rest = rest[:parts], rest[parts:2 * parts], rest[2 * parts:]
    sums_ref, across_ref, brim_ref, up_ref, down_ref, ends_ref, col_ref, x_ref, v_ref = rest[:9]
    halo_sem, brim_sem, out_sem, x_sem = rest[9:]
    _, dates, cols = up_ref.shape
    width = cols // parts
    per = width // LANES
    pitch = x_ref.shape[3]
    rows = pitch - EDGE
    owners = sums_ref.shape[0]
    halos = [
        pltpu.make_async_copy(whole, ref, halo_sem.at[n])
        for n, (whole, ref) in enumerate(((up, up_ref), (down, down_ref), (ends, ends_ref)))
    ]
    for copy in halos:
        copy.start()
    for n in range(parts):
        pltpu.make_async_copy(brim.at[n], brim_ref.at[n], brim_sem.at[n]).start()
    middles = [
        pltpu.make_async_copy(inner[n], x_ref.at[n, :, :, pl.ds(EDGE, rows - 2 * EDGE), :], x_sem.at[n]) for n in range(parts)
    ]
    for copy in middles:
        copy.start()
    fill_columns(col_ref, taps)
    total = taps[0]
    for k in range(1, 2 * RADIUS + 1):
        total = total + taps[k]
    scale = 1.0 / jnp.full((dates, LANES), total, jnp.float32)
    flat = ends_ref.reshape(cols // LANES, dates * 2 * EDGE, LANES)

    def store(n):
        return [
            pltpu.make_async_copy(
                x_ref.at[n, :, :, pl.ds(side * (rows - EDGE), EDGE), :],
                outs[n].at[:, :, pl.ds(side * EDGE, EDGE), :], out_sem.at[n, side])
            for side in range(2)
        ]

    for copy in halos:
        copy.wait()

    mids, rims = [], []
    for n in range(parts):
        block = place[0] ^ order[n]
        start = pl.multiple_of(block * width, LANES)
        before = pl.multiple_of(jnp.maximum(start - LANES, 0), LANES)
        after = pl.multiple_of(jnp.minimum(start + width, cols - LANES), LANES)

        def both(first, span):
            at = pl.ds(first, span)
            return jnp.concatenate([up_ref[:, :, at], down_ref[:, :, at]], axis=0).reshape(2 * RADIUS * dates, span)

        mids.append(both(start, width))
        rims.append(rim_tile(both(before, LANES), both(after, LANES), block, parts))
    across = filter_columns(jnp.concatenate(mids, axis=0), jnp.concatenate(rims, axis=0), col_ref[...])
    span = 2 * RADIUS * dates
    for n in range(parts):
        for h in range(per):
            across_ref[n, h] = across[n * span:(n + 1) * span, h * LANES:(h + 1) * LANES]

    def one(n, carry):
        block = place[0] ^ chosen(n, order)
        every = x_ref.at[n].reshape(per, dates * pitch, LANES)
        pltpu.make_async_copy(brim.at[n], brim_ref.at[n], brim_sem.at[n]).wait()

        def half(h, carry):
            for side in range(2):
                held = []
                for q in range(2 * RADIUS + EDGE):
                    halo = q < RADIUS if side == 0 else q >= RADIUS + EDGE
                    if halo:
                        at = q if side == 0 else q - EDGE
                        held.append(across_ref[n, h, at * dates:(at + 1) * dates, :])
                    else:
                        at = q - RADIUS if side == 0 else 3 * EDGE - RADIUS + q
                        held.append(jnp.concatenate([
                            brim_ref[n, h, (d * 4 * EDGE + at) * EDGE:(d * 4 * EDGE + at + 1) * EDGE, :]
                            for d in range(dates // EDGE)
                        ], axis=0))
                for r in range(EDGE):
                    low = taps[0] * held[r]
                    for j in range(1, 2 * RADIUS + 1):
                        low = low + taps[j] * held[r + j]
                    at = pl.ds(side * EDGE + r, dates, stride=2 * EDGE)
                    done = flat[block * per + h, at, :] - scale * low
                    every[h, pl.ds(side * (rows - EDGE) + r, dates, stride=pitch), :] = done
            return carry

        lax.fori_loop(0, per, half, 0)
        for m in range(parts):
            @pl.when(n == m)
            def _():
                for copy in store(m):
                    copy.start()
        return carry

    lax.fori_loop(0, parts, one, 0)

    lane = lax.broadcasted_iota(jnp.int32, (dates, LANES), 1)
    both = [jnp.concatenate([ref[n:n + 1, :] for ref in vectors], axis=1) for n in range(1, 4)]
    index = lax.broadcasted_iota(jnp.int32, both[0].shape, 1)
    source = (index // feet) ^ place[0]
    named = lax.broadcasted_iota(jnp.int32, (owners, index.shape[1]), 0) == both[1]
    places = []
    for block in range(parts):
        for slot in range(PAIR_CAP):
            hit = named & (source == block) & (both[2] == slot)
            places.append(jnp.where(hit, 1.0, 0.0).astype(jnp.bfloat16))
    places = jnp.concatenate(places, axis=0)
    pixel_rows = x_ref.reshape(parts * per * dates * pitch, LANES)
    for copy in middles:
        copy.wait()
    for k in range(parts):
        base = order.index(k) * per * dates * pitch

        def take(f, carry):
            pixels = pixel_rows[pl.ds(base + meta[k][0, f], dates, stride=pitch), :]
            v_ref[k * feet + f] = jnp.where(lane < meta[k][1, f], pixels, 0.0)
            return carry

        lax.fori_loop(0, feet, take, 0, unroll=8)
    tiles = []
    for first in range(0, parts * feet, LANES):

        def add(f, total):
            one = jnp.sum(v_ref[first + f], axis=1, keepdims=True)
            return jnp.where(lane == f, one, total)

        tiles.append(lax.fori_loop(0, LANES, add, jnp.zeros((dates, LANES), jnp.float32), unroll=32))
    counts = jnp.broadcast_to(both[0].astype(jnp.float32), (dates, index.shape[1]))
    sums = jnp.concatenate([jnp.concatenate(tiles, axis=1), counts], axis=0)
    held = jnp.zeros((places.shape[0], 2 * dates), jnp.float32)
    for piece in split(sums, 3):
        held = held + lax.dot_general(places, piece, (((1,), (1,)), ((), ())), preferred_element_type=jnp.float32)
    for n in range(parts * PAIR_CAP):
        at = pl.ds(n * dates, dates)
        sums_ref[:, 0, at] = held[n * owners:(n + 1) * owners, :dates]
        sums_ref[:, 1, at] = held[n * owners:(n + 1) * owners, dates:]
    for m in range(parts):
        for copy in store(m):
            copy.wait()


def edges(ends, up, down, brim, inner, meta, taps, place, order, owners):
    parts = len(order)
    tiles, dates, _, _ = ends.shape
    per = tiles // parts
    feet = meta[0].shape[1]
    rows = inner[0].shape[2] + 2 * EDGE
    here = pl.BlockSpec(memory_space=pltpu.HBM)
    resident = pl.BlockSpec(memory_space=pltpu.VMEM)
    return pl.pallas_call(
        functools.partial(edge_kernel, order, feet),
        grid_spec=pltpu.PrefetchScalarGridSpec(
            num_scalar_prefetch=2 + parts,
            grid=(),
            in_specs=[resident] * parts + [here] * (4 + parts),
            out_specs=[here] * parts + [resident],
            scratch_shapes=[
                pltpu.VMEM((parts, per, 2 * RADIUS * dates, LANES), jnp.float32),
                pltpu.VMEM((parts, per, 4 * EDGE * dates, LANES), jnp.float32),
                pltpu.VMEM(up.shape, jnp.float32),
                pltpu.VMEM(up.shape, jnp.float32),
                pltpu.VMEM(ends.shape, jnp.float32),
                pltpu.VMEM((12 * LANES, per * LANES), jnp.bfloat16),
                pltpu.VMEM((parts, per, dates, rows + EDGE, LANES), jnp.float32),
                pltpu.VMEM((parts * feet, dates, LANES), jnp.float32),
                pltpu.SemaphoreType.DMA((3,)),
                pltpu.SemaphoreType.DMA((parts,)),
                pltpu.SemaphoreType.DMA((parts, 2)),
                pltpu.SemaphoreType.DMA((parts,)),
            ],
        ),
        out_shape=[jax.ShapeDtypeStruct((per, dates, 2 * EDGE, LANES), jnp.float32)] * parts
        + [jax.ShapeDtypeStruct((owners, 2, parts * PAIR_CAP * dates), jnp.float32)],
        compiler_params=params(63),
        cost_estimate=cost(9),
    )(place, taps, *meta, *meta, ends, up, down, brim, *inner)


def temporal_kernel(parts, with_base, first_tile, tile_step, place, taps, *rest):
    pieces = rest[:parts]
    out, z_ref, f_ref, out_ref, in_sem, out_sem = rest[parts + with_base:]
    count, total, _, _ = out_ref.shape
    per = pieces[0].shape[0]
    local = total // parts
    pad = REACH * DILATION
    step = 8

    def load(n):
        rows = pl.ds(pl.multiple_of(n * EDGE, EDGE), EDGE)
        return [
            pltpu.make_async_copy(
                pieces[k].at[:, :, rows, :],
                z_ref.at[n, :, pl.ds(REACH + (place[0] ^ k) * local, local)], in_sem.at[n, k])
            for k in range(parts)
        ]

    def store(n):
        tile = first_tile + n * tile_step
        rows = pl.ds(pl.multiple_of(tile * EDGE, EDGE), EDGE)
        return pltpu.make_async_copy(out_ref.at[n], out.at[:, rows, :], out_sem.at[n])

    for n in range(count):
        for copy in load(n):
            copy.start()
    none = jnp.zeros((REACH, EDGE, LANES), jnp.float32)
    wide = jnp.zeros((pad, EDGE, LANES), jnp.float32)
    for h in range(per):
        for n in range(count):
            z_ref[n, h, 0:REACH] = none
            z_ref[n, h, REACH + total:REACH + total + REACH] = none
        f_ref[h, 0:pad] = wide
        f_ref[h, pad + total:pad + total + pad] = wide
    own = 1.0 - taps[0, REACH]
    own_wide = 1.0 - taps[1, REACH]
    others = [k for k in range(2 * REACH + 1) if k != REACH]

    def one(n, carry):
        for copy in load(n):
            copy.wait()
        for h in range(per):
            for t in range(0, total, step):
                z = z_ref[n, h, t:t + step + 2 * REACH]
                kept = own * z[REACH:REACH + step]
                for k in others:
                    kept = kept - taps[0, k] * z[k:k + step]
                f_ref[h, pad + t:pad + t + step] = kept
            for t in range(0, total, step):
                kept = own_wide * f_ref[h, pad + t:pad + t + step]
                for k in others:
                    kept = kept - taps[1, k] * f_ref[h, t + k * DILATION:t + k * DILATION + step]
                out_ref[n, t:t + step, :, h * LANES:(h + 1) * LANES] = kept
        store(n).start()
        return carry

    lax.fori_loop(0, count, one, 0)
    for n in range(count):
        store(n).wait()


def temporal(pieces, base, taps, place, first_tile, tile_step, rows):
    parts = len(pieces)
    per, local, here, _ = pieces[0].shape
    total = local * parts
    extra = [] if base is None else [base]
    count = here // EDGE
    width = per * LANES
    return pl.pallas_call(
        functools.partial(temporal_kernel, parts, len(extra), first_tile, tile_step),
        grid_spec=pltpu.PrefetchScalarGridSpec(
            num_scalar_prefetch=2,
            grid=(),
            in_specs=[pl.BlockSpec(memory_space=pl.ANY)] * (parts + len(extra)),
            out_specs=pl.BlockSpec(memory_space=pltpu.HBM),
            scratch_shapes=[
                pltpu.VMEM((count, per, total + 2 * REACH, EDGE, LANES), jnp.float32),
                pltpu.VMEM((per, total + 2 * REACH * DILATION, EDGE, LANES), jnp.float32),
                pltpu.VMEM((count, total, EDGE, width), jnp.float32),
                pltpu.SemaphoreType.DMA((count, parts)),
                pltpu.SemaphoreType.DMA((count,)),
            ],
        ),
        out_shape=jax.ShapeDtypeStruct((total, rows, width), jnp.float32),
        input_output_aliases={} if base is None else {2 + parts: 0},
        compiler_params=params(24),
        cost_estimate=cost(0),
    )(place, taps, *pieces, *extra)


def owner_kernel(parts, strips, taps, got_ref, anomaly_ref, series_ref):
    owners = parts * strips
    slots = owners * PAIR_CAP
    dates = got_ref.shape[2] // PAIR_CAP
    local = dates // parts
    sums, held = got_ref[:, 0, :], got_ref[:, 1, :]
    rows, weights = [], []
    for block in range(parts):
        for slot in range(PAIR_CAP):
            at = (block * PAIR_CAP + slot) * local
            rows.append(jnp.concatenate(
                [sums[e * strips:(e + 1) * strips, at:at + local] for e in range(parts)], axis=1))
            weights.append(held[0:strips, at:at + 1])
    sums = jnp.concatenate(rows, axis=0)
    weight = jnp.concatenate(weights, axis=0)
    shape = (dates, dates)
    lag = lax.broadcasted_iota(jnp.int32, shape, 0) - lax.broadcasted_iota(jnp.int32, shape, 1)
    for level, spacing in ((0, 1), (1, DILATION)):
        filt = jnp.where(lag == 0, 1.0, 0.0)
        for k in range(2 * REACH + 1):
            filt = filt - jnp.where(lag == (k - REACH) * spacing, taps[level, k], 0.0)
        sums = jnp.dot(sums, filt, precision=HIGHEST, preferred_element_type=jnp.float32)
    mean = sums / jnp.where(weight > 0, weight, 1.0)
    asset = jnp.sum(weight * mean, axis=0, keepdims=True) / jnp.sum(weight, axis=0, keepdims=True)
    odd = jnp.where(weight > 0, mean - asset, 0.0)
    series_ref[...] = asset
    shape = (slots, slots)
    to = lax.broadcasted_iota(jnp.int32, shape, 0)
    source = lax.broadcasted_iota(jnp.int32, shape, 1)
    block, rest = source // (PAIR_CAP * strips), source % (PAIR_CAP * strips)
    place_of = block * (PAIR_CAP * strips) + (rest % strips) * PAIR_CAP + rest // strips
    order = jnp.where(to == place_of, 1.0, 0.0)
    anomaly_ref[0] = jnp.dot(order, odd, precision=HIGHEST, preferred_element_type=jnp.float32)


def owner_series(got, taps, parts, strips):
    owners = parts * strips
    dates = got.shape[2] // PAIR_CAP
    slots = owners * PAIR_CAP
    return pl.pallas_call(
        functools.partial(owner_kernel, parts, strips),
        grid_spec=pltpu.PrefetchScalarGridSpec(
            num_scalar_prefetch=1,
            grid=(),
            in_specs=[pl.BlockSpec(memory_space=pltpu.VMEM)],
            out_specs=[pl.BlockSpec(memory_space=pltpu.VMEM)] * 2,
        ),
        out_shape=[
            jax.ShapeDtypeStruct((1, slots, dates), jnp.float32),
            jax.ShapeDtypeStruct((1, dates), jnp.float32),
        ],
        compiler_params=params(24),
        cost_estimate=cost(0),
    )(taps, got)


def spread_meta(meta, offset, swap):
    known = sorted(meta)
    got = swap(jnp.concatenate([meta[k] for k in known], axis=1), offset)
    width = meta[0].shape[1]
    return meta | {k ^ offset: got[:, n * width:(n + 1) * width] for n, k in enumerate(known)}


def shards(stack, spatial_taps, temporal_taps, foot_tile, foot_row, foot_count, foot_owner):
    parts, strips = lax.axis_size("date"), lax.axis_size("strip")
    place = lax.axis_index("date").astype(jnp.int32)[None]
    dates, rows, cols = stack.shape
    feet = foot_row.shape[0]

    def swap(value, offset):
        return lax.ppermute(value, "date", [(i, i ^ offset) for i in range(parts)])

    order = (*range(2, parts), 1, 0)
    inner, far_inner = {}, {}
    lead = order[0]
    inner[lead], brim, last_rows, first_rows, ends = interior(stack, None, spatial_taps, place, (lead,), 0, parts)
    far_inner[lead] = swap(inner[lead], lead)
    up = lax.ppermute(last_rows, "strip", [(i, i + 1) for i in range(strips - 1)])
    down = lax.ppermute(first_rows, "strip", [(i + 1, i) for i in range(strips - 1)])
    foot_tile, foot_row, foot_count, foot_owner, brim = lax.optimization_barrier(
        (foot_tile, foot_row, foot_count, foot_owner, brim))
    owner = foot_owner[:, 0]
    position = jnp.arange(feet, dtype=jnp.int32)
    earlier = (owner[:, None] == owner[None, :]) & (position[None, :] < position[:, None])
    slot = jnp.sum(earlier.astype(jnp.int32), axis=1)
    meta = {0: jnp.stack([foot_tile * (dates * (rows + EDGE)) + foot_row, foot_count, owner, slot])}
    for bit in range(parts.bit_length() - 2, 0, -1):
        meta = spread_meta(meta, 1 << bit, swap)
    *made, brim = interior(stack, brim, spatial_taps, place, order[1:], 1, parts)
    for n, offset in enumerate(order[1:]):
        inner[offset] = made[n]
        if offset > 1:
            far_inner[offset] = swap(inner[offset], offset)
    known = sorted(meta)
    *held, brim = lax.optimization_barrier((*[meta[k] for k in known], brim))
    far_inner[lead], ends = lax.optimization_barrier((far_inner[lead], ends))
    meta = spread_meta(dict(zip(known, held)), 1, swap)
    meta = [meta[k] for k in range(parts)]
    *made, sums = edges(
        ends, up, down, brim, [inner[k] for k in order], meta, spatial_taps, place, order, parts * strips)
    rim = dict(zip(order, made))
    far_inner[1] = swap(inner[1], 1)
    got = lax.all_to_all(sums, ("date", "strip"), split_axis=0, concat_axis=0, tiled=True)
    far_rim = {k: swap(rim[k], k) for n, k in enumerate(order[:-1])}
    last = rows // EDGE - 1
    residual = temporal(
        [inner[0]] + [far_inner[k] for k in range(1, parts)], None, temporal_taps, place, 1, 1, rows)
    got, residual = lax.optimization_barrier((got, residual))
    anomaly, series = owner_series(got, temporal_taps, parts, strips)
    residual = temporal(
        [rim[0]] + [far_rim[k] for k in range(1, parts)], residual, temporal_taps, place, 0, last, rows)
    return residual, anomaly, series


def solution(mesh):
    placed = (
        P("date", "strip", None),
        P(),
        P(),
        P(("date", "strip")),
        P(("date", "strip")),
        P(("date", "strip")),
        P(("date", "strip"), None),
    )
    return jax.shard_map(
        shards,
        mesh=mesh,
        in_specs=placed,
        out_specs=(
            P(None, "strip", "date"),
            P(("date", "strip"), None, None),
            P(("date", "strip"), None),
        ),
        check_vma=False,
    )
```

```python
import functools

import jax
import jax.numpy as jnp
from jax import lax
from jax.experimental import pallas as pl
from jax.experimental.pallas import tpu as pltpu
from jax.sharding import PartitionSpec as P

TILE = 128
RADIUS = 6
REACH = 2
DILATION = 8
PAIR_CAP = 2
LANES = 128
EDGE = 8
HIGHEST = lax.Precision.HIGHEST


def params(mebibytes):
    return pltpu.CompilerParams(vmem_limit_bytes=mebibytes * 1024 * 1024)


def cost(micros):
    return pl.CostEstimate(flops=0, bytes_accessed=int(micros * 3.69e6), transcendentals=0)


def pick_taps(at, taps):
    count = taps.shape[0]
    total = taps[0]
    for k in range(1, count):
        total = total + taps[k]
    out = jnp.zeros(at.shape, jnp.float32)
    for k in range(count):
        out = jnp.where(at == k, taps[k], out)
    return out / jnp.full(at.shape, total, jnp.float32)


def split(value, count):
    out = []
    for _ in range(count):
        piece = value.astype(jnp.bfloat16)
        out.append(piece)
        value = value - piece.astype(jnp.float32)
    return out


def spread(value, axis):
    high, mid = split(value, 2)
    return jnp.concatenate([high, high, high, mid], axis=axis)


def fill_columns(col_ref, taps):
    shape = (LANES, LANES)
    lag = lax.broadcasted_iota(jnp.int32, shape, 0) - lax.broadcasted_iota(jnp.int32, shape, 1)
    near = split(pick_taps(lag + RADIUS, taps), 3)
    far = pick_taps(jnp.where(lag > 0, lag + RADIUS - LANES, lag + RADIUS + LANES), taps)
    above = split(jnp.where(lag > 0, far, 0.0), 3)
    below = split(jnp.where(lag > 0, 0.0, far), 3)
    for n, piece in enumerate((0, 1, 2, 0)):
        at = n * 3 * LANES
        for i, pair in enumerate(((near, above), (below, near), (above, below))):
            for j, block in enumerate(pair):
                col_ref[at + i * LANES:at + (i + 1) * LANES, j * LANES:(j + 1) * LANES] = block[piece]


def row_band(out_rows, in_rows, taps):
    shape = (out_rows, 4 * in_rows)
    lane = lax.broadcasted_iota(jnp.int32, shape, 1)
    row = lax.broadcasted_iota(jnp.int32, shape, 0)
    part = jnp.zeros(shape, jnp.int32)
    for n in range(1, 4):
        part = jnp.where(lane >= n * in_rows, n, part)
    return lane - part * in_rows, row, part


def pieces_of(values, part):
    high, mid, low = [p.astype(jnp.float32) for p in split(values, 3)]
    return jnp.where(part == 1, mid, jnp.where(part == 2, low, high)).astype(jnp.bfloat16)


def filter_columns(mid, rim, col):
    rows = mid.shape[0]
    window = jnp.concatenate([mid, rim], axis=1)
    return jnp.dot(spread(window, 1), col, preferred_element_type=jnp.float32)


def rim_tile(left, right, block, parts):
    lane = lax.broadcasted_iota(jnp.int32, left.shape, len(left.shape) - 1)
    first = lane < LANES // 2
    keep = (first & (block < parts - 1)) | (~first & (block > 0))
    return jnp.where(keep, jnp.where(first, right, left), 0.0)


def chosen(n, values):
    out = values[0]
    for m in range(1, len(values)):
        out = jnp.where(n == m, values[m], out)
    return out


def interior_kernel(offsets, slot, parts, group, place, taps, stack, *rest):
    count = len(offsets)
    first = slot == 0
    if not first:
        rest = rest[1:]
    outs, brim, rest = rest[:count], rest[count], rest[count + 1:]
    if first:
        up, down, ends, mid_ref, left_ref, right_ref, halo_ref, up_ref, down_ref, halo_sem, halo_out_sem, *rest = rest
    else:
        x_ref, *rest = rest
    out_ref, brim_ref, col_ref, row_ref, in_sem, out_sem, brim_sem = rest
    _, per, dates, inner, _ = out_ref.shape
    width = per * LANES
    rows = inner + 2 * EDGE
    cols = width * parts
    steps = dates // group

    def bounds(block):
        start = block * width
        places = start, jnp.maximum(start - LANES, 0), jnp.minimum(start + width, cols - LANES)
        return [pl.multiple_of(at, LANES) for at in places]

    def load(g):
        at = pl.ds(g * group, group)
        if not first:
            return [pltpu.make_async_copy(stack.at[at], x_ref.at[at], in_sem.at[0, g])]
        return [
            pltpu.make_async_copy(stack.at[at, :, pl.ds(start, ref.shape[2])], ref.at[at], in_sem.at[n, g])
            for n, (start, ref) in enumerate(zip(bounds(place[0] ^ offsets[0]), (mid_ref, left_ref, right_ref)))
        ]

    def store(m, g):
        at = pl.ds(g * group, group)
        return pltpu.make_async_copy(out_ref.at[m, :, at], outs[m].at[:, at], out_sem.at[m, g])

    def store_brim(n):
        return pltpu.make_async_copy(brim_ref.at[n], brim.at[slot + n], brim_sem.at[n])

    for g in range(steps):
        for copy in load(g):
            copy.start()
    halo_loads, halo_stores = [], []
    if first:
        halo_loads = [
            pltpu.make_async_copy(
                stack.at[:, pl.ds(side * (rows - EDGE), EDGE), pl.ds(c * LANES, LANES)],
                halo_ref.at[c, :, pl.ds(side * EDGE, EDGE), :], halo_sem.at[side, c])
            for side in range(2) for c in range(cols // LANES)
        ]
        halo_stores = [
            pltpu.make_async_copy(halo_ref, ends, halo_out_sem.at[0]),
            pltpu.make_async_copy(up_ref, up, halo_out_sem.at[1]),
            pltpu.make_async_copy(down_ref, down, halo_out_sem.at[2]),
        ]
        for copy in halo_loads:
            copy.start()
    fill_columns(col_ref, taps)
    q, r, part = row_band(inner, rows, taps)
    row_ref[...] = pieces_of(pick_taps(q - r - (EDGE - RADIUS), taps), part)

    def pack(c, carry):
        at = pl.ds(pl.multiple_of(c * LANES, LANES), LANES)
        rows_of = halo_ref.at[c].reshape(dates * 2 * EDGE, LANES)
        for r in range(RADIUS):
            up_ref[r, :, at] = rows_of[pl.ds(2 * EDGE - RADIUS + r, dates, stride=2 * EDGE), :]
            down_ref[r, :, at] = rows_of[pl.ds(r, dates, stride=2 * EDGE), :]
        return carry

    def step(i, carry):
        n, g = i // steps, i % steps
        block = place[0] ^ chosen(n, offsets)
        at = pl.ds(g * group, group)

        @pl.when(n == 0)
        def _():
            for copy in load(g):
                copy.wait()

        if first:
            @pl.when(i == steps - 1)
            def _():
                for copy in halo_loads:
                    copy.wait()
                lax.fori_loop(0, cols // LANES, pack, 0)
                for copy in halo_stores:
                    copy.start()

            mid, left, right = mid_ref[at], left_ref[at], right_ref[at]
        else:
            start, before, after = bounds(block)
            mid, left, right = [x_ref[at, :, pl.ds(f, w)] for f, w in ((start, width), (before, LANES), (after, LANES))]
        rim = rim_tile(left, right, block, parts)
        across = filter_columns(mid.reshape(group * rows, width), rim.reshape(group * rows, LANES), col_ref[...])
        for t in range(group):
            one = across[t * rows:(t + 1) * rows]
            low = jnp.dot(row_ref[...], spread(one, 0), preferred_element_type=jnp.float32)
            done = mid[t, EDGE:rows - EDGE, :] - low
            for h in range(per):
                out_ref[n, h, g * group + t] = done[:, h * LANES:(h + 1) * LANES]
                for side in range(2):
                    lines = one[side * (rows - 2 * EDGE):side * (rows - 2 * EDGE) + 2 * EDGE, h * LANES:(h + 1) * LANES]
                    date = g * group + t
                    at = ((date // EDGE) * 4 * EDGE + side * 2 * EDGE) * EDGE + date % EDGE
                    brim_ref[n, h, pl.ds(at, 2 * EDGE, stride=EDGE), :] = lines
        for m in range(count):
            @pl.when(n == m)
            def _():
                store(m, g).start()

        @pl.when(g == steps - 1)
        def _():
            store_brim(n).start()

        return carry

    lax.fori_loop(0, count * steps, step, 0)
    for copy in halo_stores:
        copy.wait()
    for m in range(count):
        for g in range(steps):
            store(m, g).wait()
        store_brim(m).wait()


def interior(stack, brim, taps, place, offsets, slot, parts):
    dates, rows, cols = stack.shape
    width = cols // parts
    per = width // LANES
    group = min(8, dates)
    inner = rows - 2 * EDGE
    count = len(offsets)
    first = slot == 0
    here = pl.BlockSpec(memory_space=pltpu.HBM)
    out_shape = [jax.ShapeDtypeStruct((per, dates, inner, LANES), jnp.float32)] * count
    out_shape += [jax.ShapeDtypeStruct((parts, per, 4 * EDGE * dates, LANES), jnp.float32)]
    if first:
        out_shape += [jax.ShapeDtypeStruct((RADIUS, dates, cols), jnp.float32)] * 2
        out_shape += [jax.ShapeDtypeStruct((cols // LANES, dates, 2 * EDGE, LANES), jnp.float32)]
        scratch = [pltpu.VMEM((dates, rows, span), jnp.float32) for span in (width, LANES, LANES)] + [
            pltpu.VMEM((cols // LANES, dates, 2 * EDGE, LANES), jnp.float32),
            pltpu.VMEM((RADIUS, dates, cols), jnp.float32),
            pltpu.VMEM((RADIUS, dates, cols), jnp.float32),
            pltpu.SemaphoreType.DMA((2, cols // LANES)),
            pltpu.SemaphoreType.DMA((3,)),
        ]
    else:
        scratch = [pltpu.VMEM((dates, rows, cols), jnp.float32)]
    return pl.pallas_call(
        functools.partial(interior_kernel, offsets, slot, parts, group),
        grid_spec=pltpu.PrefetchScalarGridSpec(
            num_scalar_prefetch=2,
            grid=(),
            in_specs=[here] * (1 if first else 2),
            out_specs=[here] * len(out_shape),
            scratch_shapes=scratch + [
                pltpu.VMEM((count, per, dates, inner, LANES), jnp.float32),
                pltpu.VMEM((count, per, 4 * EDGE * dates, LANES), jnp.float32),
                pltpu.VMEM((12 * LANES, width), jnp.bfloat16),
                pltpu.VMEM((inner, 4 * rows), jnp.bfloat16),
                pltpu.SemaphoreType.DMA((3, dates // group)),
                pltpu.SemaphoreType.DMA((count, dates // group)),
                pltpu.SemaphoreType.DMA((count,)),
            ],
        ),
        out_shape=out_shape,
        input_output_aliases={} if first else {3: count},
        compiler_params=params(63),
        cost_estimate=cost(2.5 + 2.5 * count),
    )(place, taps, stack, *([] if first else [brim]))


def edge_kernel(order, feet, place, taps, *rest):
    parts = len(order)
    meta, vectors, rest = rest[:parts], rest[parts:2 * parts], rest[2 * parts:]
    ends, up, down, brim, *rest = rest
    inner, outs, rest = rest[:parts], rest[parts:2 * parts], rest[2 * parts:]
    sums_ref, across_ref, brim_ref, up_ref, down_ref, ends_ref, col_ref, x_ref, v_ref = rest[:9]
    halo_sem, brim_sem, out_sem, x_sem = rest[9:]
    _, dates, cols = up_ref.shape
    width = cols // parts
    per = width // LANES
    pitch = x_ref.shape[3]
    rows = pitch - EDGE
    owners = sums_ref.shape[0]
    halos = [
        pltpu.make_async_copy(whole, ref, halo_sem.at[n])
        for n, (whole, ref) in enumerate(((up, up_ref), (down, down_ref), (ends, ends_ref)))
    ]
    for copy in halos:
        copy.start()
    for n in range(parts):
        pltpu.make_async_copy(brim.at[n], brim_ref.at[n], brim_sem.at[n]).start()
    middles = [
        pltpu.make_async_copy(inner[n], x_ref.at[n, :, :, pl.ds(EDGE, rows - 2 * EDGE), :], x_sem.at[n]) for n in range(parts)
    ]
    for copy in middles:
        copy.start()
    fill_columns(col_ref, taps)
    total = taps[0]
    for k in range(1, 2 * RADIUS + 1):
        total = total + taps[k]
    scale = 1.0 / jnp.full((dates, LANES), total, jnp.float32)
    flat = ends_ref.reshape(cols // LANES, dates * 2 * EDGE, LANES)

    def store(n):
        return [
            pltpu.make_async_copy(
                x_ref.at[n, :, :, pl.ds(side * (rows - EDGE), EDGE), :],
                outs[n].at[:, :, pl.ds(side * EDGE, EDGE), :], out_sem.at[n, side])
            for side in range(2)
        ]

    for copy in halos:
        copy.wait()

    mids, rims = [], []
    for n in range(parts):
        block = place[0] ^ order[n]
        start = pl.multiple_of(block * width, LANES)
        before = pl.multiple_of(jnp.maximum(start - LANES, 0), LANES)
        after = pl.multiple_of(jnp.minimum(start + width, cols - LANES), LANES)

        def both(first, span):
            at = pl.ds(first, span)
            return jnp.concatenate([up_ref[:, :, at], down_ref[:, :, at]], axis=0).reshape(2 * RADIUS * dates, span)

        mids.append(both(start, width))
        rims.append(rim_tile(both(before, LANES), both(after, LANES), block, parts))
    across = filter_columns(jnp.concatenate(mids, axis=0), jnp.concatenate(rims, axis=0), col_ref[...])
    span = 2 * RADIUS * dates
    for n in range(parts):
        for h in range(per):
            across_ref[n, h] = across[n * span:(n + 1) * span, h * LANES:(h + 1) * LANES]

    def one(n, carry):
        block = place[0] ^ chosen(n, order)
        every = x_ref.at[n].reshape(per, dates * pitch, LANES)
        pltpu.make_async_copy(brim.at[n], brim_ref.at[n], brim_sem.at[n]).wait()

        def half(h, carry):
            for side in range(2):
                held = []
                for q in range(2 * RADIUS + EDGE):
                    halo = q < RADIUS if side == 0 else q >= RADIUS + EDGE
                    if halo:
                        at = q if side == 0 else q - EDGE
                        held.append(across_ref[n, h, at * dates:(at + 1) * dates, :])
                    else:
                        at = q - RADIUS if side == 0 else 3 * EDGE - RADIUS + q
                        held.append(jnp.concatenate([
                            brim_ref[n, h, (d * 4 * EDGE + at) * EDGE:(d * 4 * EDGE + at + 1) * EDGE, :]
                            for d in range(dates // EDGE)
                        ], axis=0))
                for r in range(EDGE):
                    low = taps[0] * held[r]
                    for j in range(1, 2 * RADIUS + 1):
                        low = low + taps[j] * held[r + j]
                    at = pl.ds(side * EDGE + r, dates, stride=2 * EDGE)
                    done = flat[block * per + h, at, :] - scale * low
                    every[h, pl.ds(side * (rows - EDGE) + r, dates, stride=pitch), :] = done
            return carry

        lax.fori_loop(0, per, half, 0)
        for m in range(parts):
            @pl.when(n == m)
            def _():
                for copy in store(m):
                    copy.start()
        return carry

    lax.fori_loop(0, parts, one, 0)

    lane = lax.broadcasted_iota(jnp.int32, (dates, LANES), 1)
    both = [jnp.concatenate([ref[n:n + 1, :] for ref in vectors], axis=1) for n in range(1, 4)]
    index = lax.broadcasted_iota(jnp.int32, both[0].shape, 1)
    source = (index // feet) ^ place[0]
    named = lax.broadcasted_iota(jnp.int32, (owners, index.shape[1]), 0) == both[1]
    places = []
    for block in range(parts):
        for slot in range(PAIR_CAP):
            hit = named & (source == block) & (both[2] == slot)
            places.append(jnp.where(hit, 1.0, 0.0).astype(jnp.bfloat16))
    places = jnp.concatenate(places, axis=0)
    pixel_rows = x_ref.reshape(parts * per * dates * pitch, LANES)
    for copy in middles:
        copy.wait()
    for k in range(parts):
        base = order.index(k) * per * dates * pitch

        def take(f, carry):
            pixels = pixel_rows[pl.ds(base + meta[k][0, f], dates, stride=pitch), :]
            v_ref[k * feet + f] = jnp.where(lane < meta[k][1, f], pixels, 0.0)
            return carry

        lax.fori_loop(0, feet, take, 0, unroll=8)
    tiles = []
    for first in range(0, parts * feet, LANES):

        def add(f, total):
            one = jnp.sum(v_ref[first + f], axis=1, keepdims=True)
            return jnp.where(lane == f, one, total)

        tiles.append(lax.fori_loop(0, LANES, add, jnp.zeros((dates, LANES), jnp.float32), unroll=32))
    counts = jnp.broadcast_to(both[0].astype(jnp.float32), (dates, index.shape[1]))
    sums = jnp.concatenate([jnp.concatenate(tiles, axis=1), counts], axis=0)
    held = jnp.zeros((places.shape[0], 2 * dates), jnp.float32)
    for piece in split(sums, 3):
        held = held + lax.dot_general(places, piece, (((1,), (1,)), ((), ())), preferred_element_type=jnp.float32)
    for n in range(parts * PAIR_CAP):
        at = pl.ds(n * dates, dates)
        sums_ref[:, 0, at] = held[n * owners:(n + 1) * owners, :dates]
        sums_ref[:, 1, at] = held[n * owners:(n + 1) * owners, dates:]
    for m in range(parts):
        for copy in store(m):
            copy.wait()


def edges(ends, up, down, brim, inner, meta, taps, place, order, owners):
    parts = len(order)
    tiles, dates, _, _ = ends.shape
    per = tiles // parts
    feet = meta[0].shape[1]
    rows = inner[0].shape[2] + 2 * EDGE
    here = pl.BlockSpec(memory_space=pltpu.HBM)
    resident = pl.BlockSpec(memory_space=pltpu.VMEM)
    return pl.pallas_call(
        functools.partial(edge_kernel, order, feet),
        grid_spec=pltpu.PrefetchScalarGridSpec(
            num_scalar_prefetch=2 + parts,
            grid=(),
            in_specs=[resident] * parts + [here] * (4 + parts),
            out_specs=[here] * parts + [resident],
            scratch_shapes=[
                pltpu.VMEM((parts, per, 2 * RADIUS * dates, LANES), jnp.float32),
                pltpu.VMEM((parts, per, 4 * EDGE * dates, LANES), jnp.float32),
                pltpu.VMEM(up.shape, jnp.float32),
                pltpu.VMEM(up.shape, jnp.float32),
                pltpu.VMEM(ends.shape, jnp.float32),
                pltpu.VMEM((12 * LANES, per * LANES), jnp.bfloat16),
                pltpu.VMEM((parts, per, dates, rows + EDGE, LANES), jnp.float32),
                pltpu.VMEM((parts * feet, dates, LANES), jnp.float32),
                pltpu.SemaphoreType.DMA((3,)),
                pltpu.SemaphoreType.DMA((parts,)),
                pltpu.SemaphoreType.DMA((parts, 2)),
                pltpu.SemaphoreType.DMA((parts,)),
            ],
        ),
        out_shape=[jax.ShapeDtypeStruct((per, dates, 2 * EDGE, LANES), jnp.float32)] * parts
        + [jax.ShapeDtypeStruct((owners, 2, parts * PAIR_CAP * dates), jnp.float32)],
        compiler_params=params(63),
        cost_estimate=cost(8),
    )(place, taps, *meta, *meta, ends, up, down, brim, *inner)


def temporal_kernel(parts, strips, first_tile, tile_step, place, taps, *rest):
    pieces, rest = rest[:parts], rest[parts:]
    if strips:
        _, got_ref, out, anomaly, series, anomaly_ref, series_ref, owner_sem, *rest = rest
    else:
        out, *rest = rest
    z_ref, f_ref, out_ref, in_sem, out_sem = rest
    count, total, _, _ = out_ref.shape
    per = pieces[0].shape[0]
    local = total // parts
    pad = REACH * DILATION
    step = 8

    def load(n):
        rows = pl.ds(pl.multiple_of(n * EDGE, EDGE), EDGE)
        return [
            pltpu.make_async_copy(
                pieces[k].at[:, :, rows, :],
                z_ref.at[n, :, pl.ds(REACH + (place[0] ^ k) * local, local)], in_sem.at[n, k])
            for k in range(parts)
        ]

    def store(n):
        tile = first_tile + n * tile_step
        rows = pl.ds(pl.multiple_of(tile * EDGE, EDGE), EDGE)
        return pltpu.make_async_copy(out_ref.at[n], out.at[:, rows, :], out_sem.at[n])

    for n in range(count):
        for copy in load(n):
            copy.start()
    owner_copies = []
    if strips:
        series_ref[...], anomaly_ref[0] = owner_values(parts, strips, taps, got_ref)
        owner_copies = [
            pltpu.make_async_copy(series_ref, series, owner_sem.at[0]),
            pltpu.make_async_copy(anomaly_ref, anomaly, owner_sem.at[1]),
        ]
        for copy in owner_copies:
            copy.start()
    none = jnp.zeros((REACH, EDGE, LANES), jnp.float32)
    wide = jnp.zeros((pad, EDGE, LANES), jnp.float32)
    for h in range(per):
        for n in range(count):
            z_ref[n, h, 0:REACH] = none
            z_ref[n, h, REACH + total:REACH + total + REACH] = none
        f_ref[h, 0:pad] = wide
        f_ref[h, pad + total:pad + total + pad] = wide
    own = 1.0 - taps[0, REACH]
    own_wide = 1.0 - taps[1, REACH]
    others = [k for k in range(2 * REACH + 1) if k != REACH]

    def one(n, carry):
        for copy in load(n):
            copy.wait()
        for h in range(per):
            for t in range(0, total, step):
                z = z_ref[n, h, t:t + step + 2 * REACH]
                kept = own * z[REACH:REACH + step]
                for k in others:
                    kept = kept - taps[0, k] * z[k:k + step]
                f_ref[h, pad + t:pad + t + step] = kept
            for t in range(0, total, step):
                kept = own_wide * f_ref[h, pad + t:pad + t + step]
                for k in others:
                    kept = kept - taps[1, k] * f_ref[h, t + k * DILATION:t + k * DILATION + step]
                out_ref[n, t:t + step, :, h * LANES:(h + 1) * LANES] = kept
        store(n).start()
        return carry

    lax.fori_loop(0, count, one, 0)
    for n in range(count):
        store(n).wait()
    for copy in owner_copies:
        copy.wait()


def temporal(pieces, taps, place, first_tile, tile_step, rows, base=None, got=None, strips=0):
    parts = len(pieces)
    per, local, here, _ = pieces[0].shape
    total = local * parts
    count = here // EDGE
    width = per * LANES
    anywhere = pl.BlockSpec(memory_space=pl.ANY)
    whole = pl.BlockSpec(memory_space=pltpu.HBM)
    in_specs, out_specs, scratch = [anywhere] * parts, [whole], []
    out_shape = [jax.ShapeDtypeStruct((total, rows, width), jnp.float32)]
    extra = []
    if strips:
        extra = [base, got]
        in_specs += [anywhere, pl.BlockSpec(memory_space=pltpu.VMEM)]
        out_specs += [whole] * 2
        shapes = [(1, parts * strips * PAIR_CAP, total), (1, total)]
        out_shape += [jax.ShapeDtypeStruct(shape, jnp.float32) for shape in shapes]
        scratch = [pltpu.VMEM(shape, jnp.float32) for shape in shapes] + [pltpu.SemaphoreType.DMA((2,))]
    return pl.pallas_call(
        functools.partial(temporal_kernel, parts, strips, first_tile, tile_step),
        grid_spec=pltpu.PrefetchScalarGridSpec(
            num_scalar_prefetch=2,
            grid=(),
            in_specs=in_specs,
            out_specs=out_specs,
            scratch_shapes=scratch + [
                pltpu.VMEM((count, per, total + 2 * REACH, EDGE, LANES), jnp.float32),
                pltpu.VMEM((per, total + 2 * REACH * DILATION, EDGE, LANES), jnp.float32),
                pltpu.VMEM((count, total, EDGE, width), jnp.float32),
                pltpu.SemaphoreType.DMA((count, parts)),
                pltpu.SemaphoreType.DMA((count,)),
            ],
        ),
        out_shape=out_shape,
        input_output_aliases={2 + parts: 0} if strips else {},
        compiler_params=params(24),
        cost_estimate=cost(2.5 + 0.4 * count),
    )(place, taps, *pieces, *extra)


def owner_values(parts, strips, taps, got_ref):
    owners = parts * strips
    slots = owners * PAIR_CAP
    dates = got_ref.shape[2] // PAIR_CAP
    local = dates // parts
    sums, held = got_ref[:, 0, :], got_ref[:, 1, :]
    rows, weights = [], []
    for block in range(parts):
        for slot in range(PAIR_CAP):
            at = (block * PAIR_CAP + slot) * local
            rows.append(jnp.concatenate(
                [sums[e * strips:(e + 1) * strips, at:at + local] for e in range(parts)], axis=1))
            weights.append(held[0:strips, at:at + 1])
    sums = jnp.concatenate(rows, axis=0)
    weight = jnp.concatenate(weights, axis=0)
    shape = (dates, dates)
    lag = lax.broadcasted_iota(jnp.int32, shape, 0) - lax.broadcasted_iota(jnp.int32, shape, 1)
    for level, spacing in ((0, 1), (1, DILATION)):
        filt = jnp.where(lag == 0, 1.0, 0.0)
        for k in range(2 * REACH + 1):
            filt = filt - jnp.where(lag == (k - REACH) * spacing, taps[level, k], 0.0)
        sums = jnp.dot(sums, filt, precision=HIGHEST, preferred_element_type=jnp.float32)
    mean = sums / jnp.where(weight > 0, weight, 1.0)
    asset = jnp.sum(weight * mean, axis=0, keepdims=True) / jnp.sum(weight, axis=0, keepdims=True)
    odd = jnp.where(weight > 0, mean - asset, 0.0)
    shape = (slots, slots)
    to = lax.broadcasted_iota(jnp.int32, shape, 0)
    source = lax.broadcasted_iota(jnp.int32, shape, 1)
    block, rest = source // (PAIR_CAP * strips), source % (PAIR_CAP * strips)
    place_of = block * (PAIR_CAP * strips) + (rest % strips) * PAIR_CAP + rest // strips
    order = jnp.where(to == place_of, 1.0, 0.0)
    return asset, jnp.dot(order, odd, precision=HIGHEST, preferred_element_type=jnp.float32)


def spread_meta(meta, offset, swap):
    known = sorted(meta)
    got = swap(jnp.concatenate([meta[k] for k in known], axis=1), offset)
    width = meta[0].shape[1]
    return meta | {k ^ offset: got[:, n * width:(n + 1) * width] for n, k in enumerate(known)}


def shards(stack, spatial_taps, temporal_taps, foot_tile, foot_row, foot_count, foot_owner):
    parts, strips = lax.axis_size("date"), lax.axis_size("strip")
    place = lax.axis_index("date").astype(jnp.int32)[None]
    dates, rows, cols = stack.shape
    feet = foot_row.shape[0]
    owner = foot_owner[:, 0]
    position = jnp.arange(feet, dtype=jnp.int32)
    earlier = (owner[:, None] == owner[None, :]) & (position[None, :] < position[:, None])
    slot = jnp.sum(earlier.astype(jnp.int32), axis=1)
    own = jnp.stack([foot_tile * (dates * (rows + EDGE)) + foot_row, foot_count, owner, slot])

    def swap(value, offset):
        return lax.ppermute(value, "date", [(i, i ^ offset) for i in range(parts)])

    order = (*range(2, parts), 1, 0)
    inner, far_inner = {}, {}
    lead = order[0]
    inner[lead], brim, last_rows, first_rows, ends = interior(stack, None, spatial_taps, place, (lead,), 0, parts)
    far_inner[lead] = swap(inner[lead], lead)
    up = lax.ppermute(last_rows, "strip", [(i, i + 1) for i in range(strips - 1)])
    down = lax.ppermute(first_rows, "strip", [(i + 1, i) for i in range(strips - 1)])
    own, brim = lax.optimization_barrier((own, brim))
    meta = {0: own}
    for bit in range(parts.bit_length() - 2, 0, -1):
        meta = spread_meta(meta, 1 << bit, swap)
    *made, brim = interior(stack, brim, spatial_taps, place, order[1:], 1, parts)
    for n, offset in enumerate(order[1:]):
        inner[offset] = made[n]
        if offset > 1:
            far_inner[offset] = swap(inner[offset], offset)
    known = sorted(meta)
    *held, far_inner[lead], brim = lax.optimization_barrier((*[meta[k] for k in known], far_inner[lead], brim))
    meta = spread_meta(dict(zip(known, held)), 1, swap)
    meta = [meta[k] for k in range(parts)]
    *made, sums = edges(
        ends, up, down, brim, [inner[k] for k in order], meta, spatial_taps, place, order, parts * strips)
    rim = dict(zip(order, made))
    far_inner[1] = swap(inner[1], 1)
    got = lax.all_to_all(sums, ("date", "strip"), split_axis=0, concat_axis=0, tiled=True)
    gate, *made = lax.optimization_barrier((swap(rim[1], 1), *[rim[k] for k in order[:-2]]))
    far_rim = {k: swap(made[n], k) for n, k in enumerate(order[:-2])}
    far_rim[1] = gate
    last = rows // EDGE - 1
    residual, = temporal(
        [inner[0]] + [far_inner[k] for k in range(1, parts)], temporal_taps, place, 1, 1, rows)
    got, residual = lax.optimization_barrier((got, residual))
    return temporal(
        [rim[0]] + [far_rim[k] for k in range(1, parts)], temporal_taps, place, 0, last, rows, residual, got, strips)


def solution(mesh):
    placed = (
        P("date", "strip", None),
        P(),
        P(),
        P(("date", "strip")),
        P(("date", "strip")),
        P(("date", "strip")),
        P(("date", "strip"), None),
    )
    return jax.shard_map(
        shards,
        mesh=mesh,
        in_specs=placed,
        out_specs=(
            P(None, "strip", "date"),
            P(("date", "strip"), None, None),
            P(("date", "strip"), None),
        ),
        check_vma=False,
    )
```

```python
import functools

import jax
import jax.numpy as jnp
from jax import lax
from jax.experimental import pallas as pl
from jax.experimental.pallas import tpu as pltpu
from jax.sharding import PartitionSpec as P

TILE = 128
RADIUS = 6
REACH = 2
DILATION = 8
PAIR_CAP = 2
LANES = 128
EDGE = 8
HIGHEST = lax.Precision.HIGHEST


def params(mebibytes):
    return pltpu.CompilerParams(vmem_limit_bytes=int(mebibytes * 1024 * 1024))


def cost(micros):
    return pl.CostEstimate(flops=0, bytes_accessed=int(micros * 3.69e6), transcendentals=0)


def pick_taps(at, taps):
    count = taps.shape[0]
    total = taps[0]
    for k in range(1, count):
        total = total + taps[k]
    out = jnp.zeros(at.shape, jnp.float32)
    for k in range(count):
        out = jnp.where(at == k, taps[k], out)
    return out / jnp.full(at.shape, total, jnp.float32)


def split(value, count):
    out = []
    for _ in range(count):
        piece = value.astype(jnp.bfloat16)
        out.append(piece)
        value = value - piece.astype(jnp.float32)
    return out


def spread(value, axis):
    high, mid = split(value, 2)
    return jnp.concatenate([high, high, mid], axis=axis)


def fill_columns(col_ref, taps):
    shape = (LANES, LANES)
    lag = lax.broadcasted_iota(jnp.int32, shape, 0) - lax.broadcasted_iota(jnp.int32, shape, 1)
    near = split(pick_taps(lag + RADIUS, taps), 2)
    far = pick_taps(jnp.where(lag > 0, lag + RADIUS - LANES, lag + RADIUS + LANES), taps)
    above = split(jnp.where(lag > 0, far, 0.0), 2)
    below = split(jnp.where(lag > 0, 0.0, far), 2)
    for n, piece in enumerate((0, 1, 0)):
        at = n * 3 * LANES
        for i, pair in enumerate(((near, above), (below, near), (above, below))):
            for j, block in enumerate(pair):
                col_ref[at + i * LANES:at + (i + 1) * LANES, j * LANES:(j + 1) * LANES] = block[piece]


def row_band(out_rows, in_rows, taps):
    shape = (out_rows, 3 * in_rows)
    lane = lax.broadcasted_iota(jnp.int32, shape, 1)
    row = lax.broadcasted_iota(jnp.int32, shape, 0)
    part = jnp.zeros(shape, jnp.int32)
    for n in range(1, 3):
        part = jnp.where(lane >= n * in_rows, n, part)
    return lane - part * in_rows, row, part


def pieces_of(values, part):
    high, mid = [p.astype(jnp.float32) for p in split(values, 2)]
    return jnp.where(part == 1, mid, high).astype(jnp.bfloat16)


def filter_columns(mid, rim, col):
    rows = mid.shape[0]
    window = jnp.concatenate([mid, rim], axis=1)
    return jnp.dot(spread(window, 1), col, preferred_element_type=jnp.float32)


def rim_tile(left, right, block, parts):
    lane = lax.broadcasted_iota(jnp.int32, left.shape, len(left.shape) - 1)
    first = lane < LANES // 2
    keep = (first & (block < parts - 1)) | (~first & (block > 0))
    return jnp.where(keep, jnp.where(first, right, left), 0.0)


def chosen(n, values):
    out = values[0]
    for m in range(1, len(values)):
        out = jnp.where(n == m, values[m], out)
    return out


def interior_kernel(offsets, slot, parts, group, place, taps, stack, *rest):
    count = len(offsets)
    first = slot == 0
    if not first:
        rest = rest[1:]
    outs, brim, rest = rest[:count], rest[count], rest[count + 1:]
    if first:
        up, down, mid_ref, left_ref, right_ref, halo_ref, up_ref, down_ref, halo_sem, halo_out_sem, *rest = rest
    else:
        x_ref, *rest = rest
    out_ref, brim_ref, col_ref, row_ref, in_sem, out_sem, brim_sem = rest
    _, per, dates, inner, _ = out_ref.shape
    width = per * LANES
    rows = inner + 2 * EDGE
    cols = width * parts
    steps = dates // group

    def bounds(block):
        start = block * width
        places = start, jnp.maximum(start - LANES, 0), jnp.minimum(start + width, cols - LANES)
        return [pl.multiple_of(at, LANES) for at in places]

    def load(g):
        at = pl.ds(g * group, group)
        if not first:
            return [pltpu.make_async_copy(stack.at[at], x_ref.at[at], in_sem.at[0, g])]
        return [
            pltpu.make_async_copy(stack.at[at, :, pl.ds(start, ref.shape[2])], ref.at[at], in_sem.at[n, g])
            for n, (start, ref) in enumerate(zip(bounds(place[0] ^ offsets[0]), (mid_ref, left_ref, right_ref)))
        ]

    def store(m, g):
        at = pl.ds(g * group, group)
        return pltpu.make_async_copy(out_ref.at[m, :, at], outs[m].at[:, at], out_sem.at[m, g])

    def store_brim(n, g):
        at = pl.ds(g * group * 4 * EDGE, group * 4 * EDGE)
        return pltpu.make_async_copy(brim_ref.at[n, :, at], brim.at[slot + n, :, at], brim_sem.at[n, g])

    for g in range(steps):
        for copy in load(g):
            copy.start()
    halo_loads, halo_stores = [], []
    if first:
        halo_loads = [
            pltpu.make_async_copy(
                stack.at[:, pl.ds(side * (rows - EDGE), EDGE), pl.ds(c * LANES, LANES)],
                halo_ref.at[c, :, pl.ds(side * EDGE, EDGE), :], halo_sem.at[side, c])
            for side in range(2) for c in range(cols // LANES)
        ]
        halo_stores = [
            pltpu.make_async_copy(up_ref, up, halo_out_sem.at[0]),
            pltpu.make_async_copy(down_ref, down, halo_out_sem.at[1]),
        ]
        for copy in halo_loads:
            copy.start()
    fill_columns(col_ref, taps)
    q, r, part = row_band(inner, rows, taps)
    row_ref[...] = pieces_of(pick_taps(q - r - (EDGE - RADIUS), taps), part)

    def pack(c, carry):
        at = pl.ds(pl.multiple_of(c * LANES, LANES), LANES)
        rows_of = halo_ref.at[c].reshape(dates * 2 * EDGE, LANES)
        for r in range(RADIUS):
            up_ref[r, :, at] = rows_of[pl.ds(2 * EDGE - RADIUS + r, dates, stride=2 * EDGE), :]
            down_ref[r, :, at] = rows_of[pl.ds(r, dates, stride=2 * EDGE), :]
        return carry

    def step(i, carry):
        n, g = i // steps, i % steps
        block = place[0] ^ chosen(n, offsets)
        at = pl.ds(g * group, group)

        @pl.when(n == 0)
        def _():
            for copy in load(g):
                copy.wait()

        if first:
            @pl.when(i == steps - 1)
            def _():
                for copy in halo_loads:
                    copy.wait()
                lax.fori_loop(0, cols // LANES, pack, 0)
                for copy in halo_stores:
                    copy.start()

            mid, left, right = mid_ref[at], left_ref[at], right_ref[at]
        else:
            start, before, after = bounds(block)
            mid, left, right = [x_ref[at, :, pl.ds(f, w)] for f, w in ((start, width), (before, LANES), (after, LANES))]
        rim = rim_tile(left, right, block, parts)
        across = filter_columns(mid.reshape(group * rows, width), rim.reshape(group * rows, LANES), col_ref[...])
        for t in range(group):
            one = across[t * rows:(t + 1) * rows]
            low = jnp.dot(row_ref[...], spread(one, 0), preferred_element_type=jnp.float32)
            done = mid[t, EDGE:rows - EDGE, :] - low
            for h in range(per):
                out_ref[n, h, g * group + t] = done[:, h * LANES:(h + 1) * LANES]
                for side in range(2):
                    lines = one[side * (rows - 2 * EDGE):side * (rows - 2 * EDGE) + 2 * EDGE, h * LANES:(h + 1) * LANES]
                    date = g * group + t
                    at = ((date // EDGE) * 4 * EDGE + side * 2 * EDGE) * EDGE + date % EDGE
                    brim_ref[n, h, pl.ds(at, 2 * EDGE, stride=EDGE), :] = lines
        for m in range(count):
            @pl.when(n == m)
            def _():
                store(m, g).start()

        store_brim(n, g).start()
        return carry

    lax.fori_loop(0, count * steps, step, 0)
    for copy in halo_stores:
        copy.wait()
    for m in range(count):
        for g in range(steps):
            store(m, g).wait()
            store_brim(m, g).wait()


def interior(stack, brim, taps, place, offsets, slot, parts):
    dates, rows, cols = stack.shape
    width = cols // parts
    per = width // LANES
    group = min(8, dates)
    inner = rows - 2 * EDGE
    count = len(offsets)
    first = slot == 0
    here = pl.BlockSpec(memory_space=pltpu.HBM)
    out_shape = [jax.ShapeDtypeStruct((per, dates, inner, LANES), jnp.float32)] * count
    out_shape += [jax.ShapeDtypeStruct((parts, per, 4 * EDGE * dates, LANES), jnp.float32)]
    if first:
        out_shape += [jax.ShapeDtypeStruct((RADIUS, dates, cols), jnp.float32)] * 2
        scratch = [pltpu.VMEM((dates, rows, span), jnp.float32) for span in (width, LANES, LANES)] + [
            pltpu.VMEM((cols // LANES, dates, 2 * EDGE, LANES), jnp.float32),
            pltpu.VMEM((RADIUS, dates, cols), jnp.float32),
            pltpu.VMEM((RADIUS, dates, cols), jnp.float32),
            pltpu.SemaphoreType.DMA((2, cols // LANES)),
            pltpu.SemaphoreType.DMA((2,)),
        ]
    else:
        scratch = [pltpu.VMEM((dates, rows, cols), jnp.float32)]
    return pl.pallas_call(
        functools.partial(interior_kernel, offsets, slot, parts, group),
        grid_spec=pltpu.PrefetchScalarGridSpec(
            num_scalar_prefetch=2,
            grid=(),
            in_specs=[here] * (1 if first else 2),
            out_specs=[here] * len(out_shape),
            scratch_shapes=scratch + [
                pltpu.VMEM((count, per, dates, inner, LANES), jnp.float32),
                pltpu.VMEM((count, per, 4 * EDGE * dates, LANES), jnp.float32),
                pltpu.VMEM((9 * LANES, width), jnp.bfloat16),
                pltpu.VMEM((inner, 3 * rows), jnp.bfloat16),
                pltpu.SemaphoreType.DMA((3, dates // group)),
                pltpu.SemaphoreType.DMA((count, dates // group)),
                pltpu.SemaphoreType.DMA((count, dates // group)),
            ],
        ),
        out_shape=out_shape,
        input_output_aliases={} if first else {3: count},
        compiler_params=params(63.5),
        cost_estimate=cost(2.5 + 2.5 * count),
    )(place, taps, stack, *([] if first else [brim]))


def edge_kernel(order, feet, place, taps, *rest):
    parts = len(order)
    meta, vectors, rest = rest[:parts], rest[parts:2 * parts], rest[2 * parts:]
    stack, up, down, brim, *rest = rest
    inner, outs, rest = rest[:parts], rest[parts:2 * parts], rest[2 * parts:]
    sums_ref, across_ref, brim_ref, up_ref, down_ref, ends_ref, col_ref, x_ref, v_ref = rest[:9]
    halo_sem, ends_sem, brim_sem, out_sem, x_sem = rest[9:]
    _, dates, cols = up_ref.shape
    width = cols // parts
    per = width // LANES
    pitch = x_ref.shape[3]
    rows = pitch - EDGE
    owners = sums_ref.shape[0]
    halos = [
        pltpu.make_async_copy(whole, ref, halo_sem.at[n])
        for n, (whole, ref) in enumerate(((up, up_ref), (down, down_ref)))
    ]
    ends = [
        pltpu.make_async_copy(
            stack.at[:, pl.ds(side * (rows - EDGE), EDGE), pl.ds(c * LANES, LANES)],
            ends_ref.at[c, :, pl.ds(side * EDGE, EDGE), :], ends_sem.at[side, c])
        for side in range(2) for c in range(cols // LANES)
    ]
    for copy in halos + ends:
        copy.start()
    for n in range(parts):
        pltpu.make_async_copy(brim.at[n], brim_ref.at[n], brim_sem.at[n]).start()
    middles = [
        pltpu.make_async_copy(inner[n], x_ref.at[n, :, :, pl.ds(EDGE, rows - 2 * EDGE), :], x_sem.at[n]) for n in range(parts)
    ]
    for copy in middles:
        copy.start()
    fill_columns(col_ref, taps)
    total = taps[0]
    for k in range(1, 2 * RADIUS + 1):
        total = total + taps[k]
    scale = 1.0 / jnp.full((dates, LANES), total, jnp.float32)
    flat = ends_ref.reshape(cols // LANES, dates * 2 * EDGE, LANES)

    def store(n):
        return [
            pltpu.make_async_copy(
                x_ref.at[n, :, :, pl.ds(side * (rows - EDGE), EDGE), :],
                outs[n].at[:, :, pl.ds(side * EDGE, EDGE), :], out_sem.at[n, side])
            for side in range(2)
        ]

    for copy in halos:
        copy.wait()

    mids, rims = [], []
    for n in range(parts):
        block = place[0] ^ order[n]
        start = pl.multiple_of(block * width, LANES)
        before = pl.multiple_of(jnp.maximum(start - LANES, 0), LANES)
        after = pl.multiple_of(jnp.minimum(start + width, cols - LANES), LANES)

        def both(first, span):
            at = pl.ds(first, span)
            return jnp.concatenate([up_ref[:, :, at], down_ref[:, :, at]], axis=0).reshape(2 * RADIUS * dates, span)

        mids.append(both(start, width))
        rims.append(rim_tile(both(before, LANES), both(after, LANES), block, parts))
    across = filter_columns(jnp.concatenate(mids, axis=0), jnp.concatenate(rims, axis=0), col_ref[...])
    span = 2 * RADIUS * dates
    for n in range(parts):
        for h in range(per):
            across_ref[n, h] = across[n * span:(n + 1) * span, h * LANES:(h + 1) * LANES]
    for copy in ends:
        copy.wait()

    def one(n, carry):
        block = place[0] ^ chosen(n, order)
        every = x_ref.at[n].reshape(per, dates * pitch, LANES)
        pltpu.make_async_copy(brim.at[n], brim_ref.at[n], brim_sem.at[n]).wait()

        def half(h, carry):
            for side in range(2):
                held = []
                for q in range(2 * RADIUS + EDGE):
                    halo = q < RADIUS if side == 0 else q >= RADIUS + EDGE
                    if halo:
                        at = q if side == 0 else q - EDGE
                        held.append(across_ref[n, h, at * dates:(at + 1) * dates, :])
                    else:
                        at = q - RADIUS if side == 0 else 3 * EDGE - RADIUS + q
                        held.append(jnp.concatenate([
                            brim_ref[n, h, (d * 4 * EDGE + at) * EDGE:(d * 4 * EDGE + at + 1) * EDGE, :]
                            for d in range(dates // EDGE)
                        ], axis=0))
                for r in range(EDGE):
                    low = taps[0] * held[r]
                    for j in range(1, 2 * RADIUS + 1):
                        low = low + taps[j] * held[r + j]
                    at = pl.ds(side * EDGE + r, dates, stride=2 * EDGE)
                    done = flat[block * per + h, at, :] - scale * low
                    every[h, pl.ds(side * (rows - EDGE) + r, dates, stride=pitch), :] = done
            return carry

        lax.fori_loop(0, per, half, 0)
        for m in range(parts):
            @pl.when(n == m)
            def _():
                for copy in store(m):
                    copy.start()
        return carry

    lax.fori_loop(0, parts, one, 0)

    lane = lax.broadcasted_iota(jnp.int32, (dates, LANES), 1)
    both = [jnp.concatenate([ref[n:n + 1, :] for ref in vectors], axis=1) for n in range(1, 4)]
    index = lax.broadcasted_iota(jnp.int32, both[0].shape, 1)
    source = (index // feet) ^ place[0]
    named = lax.broadcasted_iota(jnp.int32, (owners, index.shape[1]), 0) == both[1]
    places = []
    for block in range(parts):
        for slot in range(PAIR_CAP):
            hit = named & (source == block) & (both[2] == slot)
            places.append(jnp.where(hit, 1.0, 0.0).astype(jnp.bfloat16))
    places = jnp.concatenate(places, axis=0)
    pixel_rows = x_ref.reshape(parts * per * dates * pitch, LANES)
    for copy in middles:
        copy.wait()
    for k in range(parts):
        base = order.index(k) * per * dates * pitch

        def take(f, carry):
            pixels = pixel_rows[pl.ds(base + meta[k][0, f], dates, stride=pitch), :]
            v_ref[k * feet + f] = jnp.where(lane < meta[k][1, f], pixels, 0.0)
            return carry

        lax.fori_loop(0, feet, take, 0, unroll=8)
    tiles = []
    for first in range(0, parts * feet, LANES):

        def add(f, total):
            one = jnp.sum(v_ref[first + f], axis=1, keepdims=True)
            return jnp.where(lane == f, one, total)

        tiles.append(lax.fori_loop(0, LANES, add, jnp.zeros((dates, LANES), jnp.float32), unroll=32))
    counts = jnp.broadcast_to(both[0].astype(jnp.float32), (dates, index.shape[1]))
    sums = jnp.concatenate([jnp.concatenate(tiles, axis=1), counts], axis=0)
    held = jnp.zeros((places.shape[0], 2 * dates), jnp.float32)
    for piece in split(sums, 3):
        held = held + lax.dot_general(places, piece, (((1,), (1,)), ((), ())), preferred_element_type=jnp.float32)
    for n in range(parts * PAIR_CAP):
        at = pl.ds(n * dates, dates)
        sums_ref[:, 0, at] = held[n * owners:(n + 1) * owners, :dates]
        sums_ref[:, 1, at] = held[n * owners:(n + 1) * owners, dates:]
    for m in range(parts):
        for copy in store(m):
            copy.wait()


def edges(stack, up, down, brim, inner, meta, taps, place, order, owners):
    parts = len(order)
    dates, rows, cols = stack.shape
    tiles = cols // LANES
    per = tiles // parts
    feet = meta[0].shape[1]
    here = pl.BlockSpec(memory_space=pltpu.HBM)
    resident = pl.BlockSpec(memory_space=pltpu.VMEM)
    return pl.pallas_call(
        functools.partial(edge_kernel, order, feet),
        grid_spec=pltpu.PrefetchScalarGridSpec(
            num_scalar_prefetch=2 + parts,
            grid=(),
            in_specs=[resident] * parts + [here] * (4 + parts),
            out_specs=[here] * parts + [resident],
            scratch_shapes=[
                pltpu.VMEM((parts, per, 2 * RADIUS * dates, LANES), jnp.float32),
                pltpu.VMEM((parts, per, 4 * EDGE * dates, LANES), jnp.float32),
                pltpu.VMEM(up.shape, jnp.float32),
                pltpu.VMEM(up.shape, jnp.float32),
                pltpu.VMEM((tiles, dates, 2 * EDGE, LANES), jnp.float32),
                pltpu.VMEM((9 * LANES, per * LANES), jnp.bfloat16),
                pltpu.VMEM((parts, per, dates, rows + EDGE, LANES), jnp.float32),
                pltpu.VMEM((parts * feet, dates, LANES), jnp.float32),
                pltpu.SemaphoreType.DMA((2,)),
                pltpu.SemaphoreType.DMA((2, tiles)),
                pltpu.SemaphoreType.DMA((parts,)),
                pltpu.SemaphoreType.DMA((parts, 2)),
                pltpu.SemaphoreType.DMA((parts,)),
            ],
        ),
        out_shape=[jax.ShapeDtypeStruct((per, dates, 2 * EDGE, LANES), jnp.float32)] * parts
        + [jax.ShapeDtypeStruct((owners, 2, parts * PAIR_CAP * dates), jnp.float32)],
        compiler_params=params(63.5),
        cost_estimate=cost(8),
    )(place, taps, *meta, *meta, stack, up, down, brim, *inner)


def temporal_kernel(parts, strips, first_tile, tile_step, place, taps, *rest):
    pieces, rest = rest[:parts], rest[parts:]
    if strips:
        _, got_ref, out, anomaly, series, anomaly_ref, series_ref, owner_sem, *rest = rest
    else:
        out, *rest = rest
    z_ref, f_ref, out_ref, in_sem, out_sem = rest
    count, total, _, _ = out_ref.shape
    per = pieces[0].shape[0]
    local = total // parts
    pad = REACH * DILATION
    step = 8

    def load(n):
        rows = pl.ds(pl.multiple_of(n * EDGE, EDGE), EDGE)
        return [
            pltpu.make_async_copy(
                pieces[k].at[:, :, rows, :],
                z_ref.at[n, :, pl.ds(REACH + (place[0] ^ k) * local, local)], in_sem.at[n, k])
            for k in range(parts)
        ]

    def store(n):
        tile = first_tile + n * tile_step
        rows = pl.ds(pl.multiple_of(tile * EDGE, EDGE), EDGE)
        return pltpu.make_async_copy(out_ref.at[n], out.at[:, rows, :], out_sem.at[n])

    for n in range(count):
        for copy in load(n):
            copy.start()
    owner_copies = []
    if strips:
        series_ref[...], anomaly_ref[0] = owner_values(parts, strips, taps, got_ref)
        owner_copies = [
            pltpu.make_async_copy(series_ref, series, owner_sem.at[0]),
            pltpu.make_async_copy(anomaly_ref, anomaly, owner_sem.at[1]),
        ]
        for copy in owner_copies:
            copy.start()
    none = jnp.zeros((REACH, EDGE, LANES), jnp.float32)
    wide = jnp.zeros((pad, EDGE, LANES), jnp.float32)
    for h in range(per):
        for n in range(count):
            z_ref[n, h, 0:REACH] = none
            z_ref[n, h, REACH + total:REACH + total + REACH] = none
        f_ref[h, 0:pad] = wide
        f_ref[h, pad + total:pad + total + pad] = wide
    own = 1.0 - taps[0, REACH]
    own_wide = 1.0 - taps[1, REACH]
    others = [k for k in range(2 * REACH + 1) if k != REACH]

    def one(n, carry):
        for copy in load(n):
            copy.wait()
        for h in range(per):
            for t in range(0, total, step):
                z = z_ref[n, h, t:t + step + 2 * REACH]
                kept = own * z[REACH:REACH + step]
                for k in others:
                    kept = kept - taps[0, k] * z[k:k + step]
                f_ref[h, pad + t:pad + t + step] = kept
            for t in range(0, total, step):
                kept = own_wide * f_ref[h, pad + t:pad + t + step]
                for k in others:
                    kept = kept - taps[1, k] * f_ref[h, t + k * DILATION:t + k * DILATION + step]
                out_ref[n, t:t + step, :, h * LANES:(h + 1) * LANES] = kept
        store(n).start()
        return carry

    lax.fori_loop(0, count, one, 0)
    for n in range(count):
        store(n).wait()
    for copy in owner_copies:
        copy.wait()


def temporal(pieces, taps, place, first_tile, tile_step, rows, base=None, got=None, strips=0):
    parts = len(pieces)
    per, local, here, _ = pieces[0].shape
    total = local * parts
    count = here // EDGE
    width = per * LANES
    anywhere = pl.BlockSpec(memory_space=pl.ANY)
    whole = pl.BlockSpec(memory_space=pltpu.HBM)
    in_specs, out_specs, scratch = [anywhere] * parts, [whole], []
    out_shape = [jax.ShapeDtypeStruct((total, rows, width), jnp.float32)]
    extra = []
    if strips:
        extra = [base, got]
        in_specs += [anywhere, pl.BlockSpec(memory_space=pltpu.VMEM)]
        out_specs += [whole] * 2
        shapes = [(1, parts * strips * PAIR_CAP, total), (1, total)]
        out_shape += [jax.ShapeDtypeStruct(shape, jnp.float32) for shape in shapes]
        scratch = [pltpu.VMEM(shape, jnp.float32) for shape in shapes] + [pltpu.SemaphoreType.DMA((2,))]
    return pl.pallas_call(
        functools.partial(temporal_kernel, parts, strips, first_tile, tile_step),
        grid_spec=pltpu.PrefetchScalarGridSpec(
            num_scalar_prefetch=2,
            grid=(),
            in_specs=in_specs,
            out_specs=out_specs,
            scratch_shapes=scratch + [
                pltpu.VMEM((count, per, total + 2 * REACH, EDGE, LANES), jnp.float32),
                pltpu.VMEM((per, total + 2 * REACH * DILATION, EDGE, LANES), jnp.float32),
                pltpu.VMEM((count, total, EDGE, width), jnp.float32),
                pltpu.SemaphoreType.DMA((count, parts)),
                pltpu.SemaphoreType.DMA((count,)),
            ],
        ),
        out_shape=out_shape,
        input_output_aliases={2 + parts: 0} if strips else {},
        compiler_params=params(24),
        cost_estimate=cost(2.5 + 0.4 * count),
    )(place, taps, *pieces, *extra)


def owner_values(parts, strips, taps, got_ref):
    owners = parts * strips
    slots = owners * PAIR_CAP
    dates = got_ref.shape[2] // PAIR_CAP
    local = dates // parts
    sums, held = got_ref[:, 0, :], got_ref[:, 1, :]
    rows, weights = [], []
    for block in range(parts):
        for slot in range(PAIR_CAP):
            at = (block * PAIR_CAP + slot) * local
            rows.append(jnp.concatenate(
                [sums[e * strips:(e + 1) * strips, at:at + local] for e in range(parts)], axis=1))
            weights.append(held[0:strips, at:at + 1])
    sums = jnp.concatenate(rows, axis=0)
    weight = jnp.concatenate(weights, axis=0)
    shape = (dates, dates)
    lag = lax.broadcasted_iota(jnp.int32, shape, 0) - lax.broadcasted_iota(jnp.int32, shape, 1)
    for level, spacing in ((0, 1), (1, DILATION)):
        filt = jnp.where(lag == 0, 1.0, 0.0)
        for k in range(2 * REACH + 1):
            filt = filt - jnp.where(lag == (k - REACH) * spacing, taps[level, k], 0.0)
        sums = jnp.dot(sums, filt, precision=HIGHEST, preferred_element_type=jnp.float32)
    mean = sums / jnp.where(weight > 0, weight, 1.0)
    asset = jnp.sum(weight * mean, axis=0, keepdims=True) / jnp.sum(weight, axis=0, keepdims=True)
    odd = jnp.where(weight > 0, mean - asset, 0.0)
    shape = (slots, slots)
    to = lax.broadcasted_iota(jnp.int32, shape, 0)
    source = lax.broadcasted_iota(jnp.int32, shape, 1)
    block, rest = source // (PAIR_CAP * strips), source % (PAIR_CAP * strips)
    place_of = block * (PAIR_CAP * strips) + (rest % strips) * PAIR_CAP + rest // strips
    order = jnp.where(to == place_of, 1.0, 0.0)
    return asset, jnp.dot(order, odd, precision=HIGHEST, preferred_element_type=jnp.float32)


def spread_meta(meta, offset, swap):
    known = sorted(meta)
    got = swap(jnp.concatenate([meta[k] for k in known], axis=1), offset)
    width = meta[0].shape[1]
    return meta | {k ^ offset: got[:, n * width:(n + 1) * width] for n, k in enumerate(known)}


def shards(stack, spatial_taps, temporal_taps, foot_tile, foot_row, foot_count, foot_owner):
    parts, strips = lax.axis_size("date"), lax.axis_size("strip")
    place = lax.axis_index("date").astype(jnp.int32)[None]
    dates, rows, cols = stack.shape
    feet = foot_row.shape[0]
    owner = foot_owner[:, 0]
    position = jnp.arange(feet, dtype=jnp.int32)
    earlier = (owner[:, None] == owner[None, :]) & (position[None, :] < position[:, None])
    slot = jnp.sum(earlier.astype(jnp.int32), axis=1)
    own = jnp.stack([foot_tile * (dates * (rows + EDGE)) + foot_row, foot_count, owner, slot])

    def swap(value, offset):
        return lax.ppermute(value, "date", [(i, i ^ offset) for i in range(parts)])

    order = (*range(2, parts), 1, 0)
    inner, far_inner = {}, {}
    lead = order[0]
    inner[lead], brim, last_rows, first_rows = interior(stack, None, spatial_taps, place, (lead,), 0, parts)
    far_inner[lead] = swap(inner[lead], lead)
    up = lax.ppermute(last_rows, "strip", [(i, i + 1) for i in range(strips - 1)])
    down = lax.ppermute(first_rows, "strip", [(i + 1, i) for i in range(strips - 1)])
    own, brim = lax.optimization_barrier((own, brim))
    meta = {0: own}
    for bit in range(parts.bit_length() - 2, 0, -1):
        meta = spread_meta(meta, 1 << bit, swap)
    *made, brim = interior(stack, brim, spatial_taps, place, order[1:], 1, parts)
    for n, offset in enumerate(order[1:]):
        inner[offset] = made[n]
        if offset > 1:
            far_inner[offset] = swap(inner[offset], offset)
    known = sorted(meta)
    *held, far_inner[lead], brim = lax.optimization_barrier((*[meta[k] for k in known], far_inner[lead], brim))
    meta = spread_meta(dict(zip(known, held)), 1, swap)
    meta = [meta[k] for k in range(parts)]
    *made, sums = edges(
        stack, up, down, brim, [inner[k] for k in order], meta, spatial_taps, place, order, parts * strips)
    rim = dict(zip(order, made))
    far_inner[1] = swap(inner[1], 1)
    got = lax.all_to_all(sums, ("date", "strip"), split_axis=0, concat_axis=0, tiled=True)
    gate, *made = lax.optimization_barrier((swap(rim[1], 1), *[rim[k] for k in order[:-2]]))
    far_rim = {k: swap(made[n], k) for n, k in enumerate(order[:-2])}
    far_rim[1] = gate
    last = rows // EDGE - 1
    residual, = temporal(
        [inner[0]] + [far_inner[k] for k in range(1, parts)], temporal_taps, place, 1, 1, rows)
    got, residual = lax.optimization_barrier((got, residual))
    return temporal(
        [rim[0]] + [far_rim[k] for k in range(1, parts)], temporal_taps, place, 0, last, rows, residual, got, strips)


def solution(mesh):
    placed = (
        P("date", "strip", None),
        P(),
        P(),
        P(("date", "strip")),
        P(("date", "strip")),
        P(("date", "strip")),
        P(("date", "strip"), None),
    )
    return jax.shard_map(
        shards,
        mesh=mesh,
        in_specs=placed,
        out_specs=(
            P(None, "strip", "date"),
            P(("date", "strip"), None, None),
            P(("date", "strip"), None),
        ),
        check_vma=False,
    )
```

```python
import functools

import jax
import jax.numpy as jnp
from jax import lax
from jax.experimental import pallas as pl
from jax.experimental.pallas import tpu as pltpu
from jax.sharding import PartitionSpec as P

TILE = 128
RADIUS = 6
REACH = 2
DILATION = 8
PAIR_CAP = 2
LANES = 128
EDGE = 8
HIGHEST = lax.Precision.HIGHEST


def params(mebibytes):
    return pltpu.CompilerParams(vmem_limit_bytes=int(mebibytes * 1024 * 1024))


def cost(micros):
    return pl.CostEstimate(flops=0, bytes_accessed=int(micros * 3.69e6), transcendentals=0)


def pick_taps(at, taps):
    count = taps.shape[0]
    total = taps[0]
    for k in range(1, count):
        total = total + taps[k]
    out = jnp.zeros(at.shape, jnp.float32)
    for k in range(count):
        out = jnp.where(at == k, taps[k], out)
    return out / jnp.full(at.shape, total, jnp.float32)


def split(value, count):
    out = []
    for _ in range(count):
        piece = value.astype(jnp.bfloat16)
        out.append(piece)
        value = value - piece.astype(jnp.float32)
    return out


def spread(value, axis):
    high, mid = split(value, 2)
    return jnp.concatenate([high, high, mid], axis=axis)


def fill_columns(col_ref, taps):
    shape = (LANES, LANES)
    lag = lax.broadcasted_iota(jnp.int32, shape, 0) - lax.broadcasted_iota(jnp.int32, shape, 1)
    near = split(pick_taps(lag + RADIUS, taps), 2)
    far = pick_taps(jnp.where(lag > 0, lag + RADIUS - LANES, lag + RADIUS + LANES), taps)
    above = split(jnp.where(lag > 0, far, 0.0), 2)
    below = split(jnp.where(lag > 0, 0.0, far), 2)
    for n, piece in enumerate((0, 1, 0)):
        at = n * 3 * LANES
        for i, pair in enumerate(((near, above), (below, near), (above, below))):
            for j, block in enumerate(pair):
                col_ref[at + i * LANES:at + (i + 1) * LANES, j * LANES:(j + 1) * LANES] = block[piece]


def row_band(out_rows, in_rows, taps):
    shape = (out_rows, 3 * in_rows)
    lane = lax.broadcasted_iota(jnp.int32, shape, 1)
    row = lax.broadcasted_iota(jnp.int32, shape, 0)
    part = jnp.zeros(shape, jnp.int32)
    for n in range(1, 3):
        part = jnp.where(lane >= n * in_rows, n, part)
    return lane - part * in_rows, row, part


def pieces_of(values, part):
    high, mid = [p.astype(jnp.float32) for p in split(values, 2)]
    return jnp.where(part == 1, mid, high).astype(jnp.bfloat16)


def filter_columns(mid, rim, col):
    rows = mid.shape[0]
    window = jnp.concatenate([mid, rim], axis=1)
    return jnp.dot(spread(window, 1), col, preferred_element_type=jnp.float32)


def rim_tile(left, right, block, parts):
    lane = lax.broadcasted_iota(jnp.int32, left.shape, len(left.shape) - 1)
    first = lane < LANES // 2
    keep = (first & (block < parts - 1)) | (~first & (block > 0))
    return jnp.where(keep, jnp.where(first, right, left), 0.0)


def chosen(n, values):
    out = values[0]
    for m in range(1, len(values)):
        out = jnp.where(n == m, values[m], out)
    return out


def interior_kernel(offsets, slot, parts, group, place, taps, stack, *rest):
    count = len(offsets)
    first = slot == 0
    if not first:
        rest = rest[1:]
    outs, brim, rest = rest[:count], rest[count], rest[count + 1:]
    if first:
        mid_ref, left_ref, right_ref, *rest = rest
    else:
        x_ref, *rest = rest
    out_ref, brim_ref, col_ref, row_ref, in_sem, out_sem, brim_sem = rest
    _, per, dates, inner, _ = out_ref.shape
    width = per * LANES
    rows = inner + 2 * EDGE
    cols = width * parts
    steps = dates // group

    def bounds(block):
        start = block * width
        places = start, jnp.maximum(start - LANES, 0), jnp.minimum(start + width, cols - LANES)
        return [pl.multiple_of(at, LANES) for at in places]

    def load(g):
        at = pl.ds(g * group, group)
        if not first:
            return [pltpu.make_async_copy(stack.at[at], x_ref.at[at], in_sem.at[0, g])]
        return [
            pltpu.make_async_copy(stack.at[at, :, pl.ds(start, ref.shape[2])], ref.at[at], in_sem.at[n, g])
            for n, (start, ref) in enumerate(zip(bounds(place[0] ^ offsets[0]), (mid_ref, left_ref, right_ref)))
        ]

    def store(m, g):
        at = pl.ds(g * group, group)
        return pltpu.make_async_copy(out_ref.at[m, :, at], outs[m].at[:, at], out_sem.at[m, g])

    def store_brim(n, g):
        at = pl.ds(g * group * 4 * EDGE, group * 4 * EDGE)
        return pltpu.make_async_copy(brim_ref.at[n, :, at], brim.at[slot + n, :, at], brim_sem.at[n, g])

    for g in range(steps):
        for copy in load(g):
            copy.start()
    fill_columns(col_ref, taps)
    q, r, part = row_band(inner, rows, taps)
    row_ref[...] = pieces_of(pick_taps(q - r - (EDGE - RADIUS), taps), part)

    def step(i, carry):
        n, g = i // steps, i % steps
        block = place[0] ^ chosen(n, offsets)
        at = pl.ds(g * group, group)

        @pl.when(n == 0)
        def _():
            for copy in load(g):
                copy.wait()

        if first:
            mid, left, right = mid_ref[at], left_ref[at], right_ref[at]
        else:
            start, before, after = bounds(block)
            mid, left, right = [x_ref[at, :, pl.ds(f, w)] for f, w in ((start, width), (before, LANES), (after, LANES))]
        rim = rim_tile(left, right, block, parts)
        across = filter_columns(mid.reshape(group * rows, width), rim.reshape(group * rows, LANES), col_ref[...])
        for t in range(group):
            one = across[t * rows:(t + 1) * rows]
            low = jnp.dot(row_ref[...], spread(one, 0), preferred_element_type=jnp.float32)
            done = mid[t, EDGE:rows - EDGE, :] - low
            for h in range(per):
                out_ref[n, h, g * group + t] = done[:, h * LANES:(h + 1) * LANES]
                for side in range(2):
                    lines = one[side * (rows - 2 * EDGE):side * (rows - 2 * EDGE) + 2 * EDGE, h * LANES:(h + 1) * LANES]
                    date = g * group + t
                    at = ((date // EDGE) * 4 * EDGE + side * 2 * EDGE) * EDGE + date % EDGE
                    brim_ref[n, h, pl.ds(at, 2 * EDGE, stride=EDGE), :] = lines
        for m in range(count):
            @pl.when(n == m)
            def _():
                store(m, g).start()

        store_brim(n, g).start()
        return carry

    lax.fori_loop(0, count * steps, step, 0)
    for m in range(count):
        for g in range(steps):
            store(m, g).wait()
            store_brim(m, g).wait()


def interior(stack, brim, taps, place, offsets, slot, parts):
    dates, rows, cols = stack.shape
    width = cols // parts
    per = width // LANES
    group = min(8, dates)
    inner = rows - 2 * EDGE
    count = len(offsets)
    first = slot == 0
    here = pl.BlockSpec(memory_space=pltpu.HBM)
    out_shape = [jax.ShapeDtypeStruct((per, dates, inner, LANES), jnp.float32)] * count
    out_shape += [jax.ShapeDtypeStruct((parts, per, 4 * EDGE * dates, LANES), jnp.float32)]
    scratch = [pltpu.VMEM((dates, rows, span), jnp.float32) for span in ((width, LANES, LANES) if first else (cols,))]
    return pl.pallas_call(
        functools.partial(interior_kernel, offsets, slot, parts, group),
        grid_spec=pltpu.PrefetchScalarGridSpec(
            num_scalar_prefetch=2,
            grid=(),
            in_specs=[here] * (1 if first else 2),
            out_specs=[here] * len(out_shape),
            scratch_shapes=scratch + [
                pltpu.VMEM((count, per, dates, inner, LANES), jnp.float32),
                pltpu.VMEM((count, per, 4 * EDGE * dates, LANES), jnp.float32),
                pltpu.VMEM((9 * LANES, width), jnp.bfloat16),
                pltpu.VMEM((inner, 3 * rows), jnp.bfloat16),
                pltpu.SemaphoreType.DMA((3, dates // group)),
                pltpu.SemaphoreType.DMA((count, dates // group)),
                pltpu.SemaphoreType.DMA((count, dates // group)),
            ],
        ),
        out_shape=out_shape,
        input_output_aliases={} if first else {3: count},
        compiler_params=params(63.5),
        cost_estimate=cost(2.5 + 2.5 * count),
    )(place, taps, stack, *([] if first else [brim]))


def halo_kernel(place, stack, up, down, halo_ref, up_ref, down_ref, halo_sem, out_sem):
    tiles, dates, _, _ = halo_ref.shape
    rows = stack.shape[1]

    def load(c):
        lanes = pl.ds(pl.multiple_of(c * LANES, LANES), LANES)
        return [
            pltpu.make_async_copy(
                stack.at[:, pl.ds(side * (rows - EDGE), EDGE), lanes],
                halo_ref.at[c, :, pl.ds(side * EDGE, EDGE), :], halo_sem.at[side, c])
            for side in range(2)
        ]

    for c in range(tiles):
        for copy in load(c):
            copy.start()

    def pack(c, carry):
        for copy in load(c):
            copy.wait()
        at = pl.ds(pl.multiple_of(c * LANES, LANES), LANES)
        rows_of = halo_ref.at[c].reshape(dates * 2 * EDGE, LANES)
        for r in range(RADIUS):
            up_ref[r, :, at] = rows_of[pl.ds(2 * EDGE - RADIUS + r, dates, stride=2 * EDGE), :]
            down_ref[r, :, at] = rows_of[pl.ds(r, dates, stride=2 * EDGE), :]
        return carry

    lax.fori_loop(0, tiles, pack, 0)
    copies = [
        pltpu.make_async_copy(up_ref, up, out_sem.at[0]),
        pltpu.make_async_copy(down_ref, down, out_sem.at[1]),
    ]
    for copy in copies:
        copy.start()
    for copy in copies:
        copy.wait()


def halo_rows(stack, place):
    dates, _, cols = stack.shape
    here = pl.BlockSpec(memory_space=pltpu.HBM)
    return pl.pallas_call(
        halo_kernel,
        grid_spec=pltpu.PrefetchScalarGridSpec(
            num_scalar_prefetch=1,
            grid=(),
            in_specs=[here],
            out_specs=[here] * 2,
            scratch_shapes=[
                pltpu.VMEM((cols // LANES, dates, 2 * EDGE, LANES), jnp.float32),
                pltpu.VMEM((RADIUS, dates, cols), jnp.float32),
                pltpu.VMEM((RADIUS, dates, cols), jnp.float32),
                pltpu.SemaphoreType.DMA((2, cols // LANES)),
                pltpu.SemaphoreType.DMA((2,)),
            ],
        ),
        out_shape=[jax.ShapeDtypeStruct((RADIUS, dates, cols), jnp.float32)] * 2,
        compiler_params=params(63.5),
        cost_estimate=cost(2.5),
    )(place, stack)


def edge_kernel(order, feet, place, taps, *rest):
    parts = len(order)
    meta, vectors, rest = rest[:parts], rest[parts:2 * parts], rest[2 * parts:]
    stack, up, down, brim, *rest = rest
    inner, outs, rest = rest[:parts], rest[parts:2 * parts], rest[2 * parts:]
    sums_ref, across_ref, brim_ref, up_ref, down_ref, ends_ref, col_ref, x_ref, v_ref = rest[:9]
    halo_sem, ends_sem, brim_sem, out_sem, x_sem = rest[9:]
    _, dates, cols = up_ref.shape
    width = cols // parts
    per = width // LANES
    pitch = x_ref.shape[3]
    rows = pitch - EDGE
    owners = sums_ref.shape[0]
    halos = [
        pltpu.make_async_copy(whole, ref, halo_sem.at[n])
        for n, (whole, ref) in enumerate(((up, up_ref), (down, down_ref)))
    ]
    ends = [
        pltpu.make_async_copy(
            stack.at[:, pl.ds(side * (rows - EDGE), EDGE), pl.ds(c * LANES, LANES)],
            ends_ref.at[c, :, pl.ds(side * EDGE, EDGE), :], ends_sem.at[side, c])
        for side in range(2) for c in range(cols // LANES)
    ]
    for copy in halos + ends:
        copy.start()
    for n in range(parts):
        pltpu.make_async_copy(brim.at[n], brim_ref.at[n], brim_sem.at[n]).start()
    middles = [
        pltpu.make_async_copy(inner[n], x_ref.at[n, :, :, pl.ds(EDGE, rows - 2 * EDGE), :], x_sem.at[n]) for n in range(parts)
    ]
    for copy in middles:
        copy.start()
    fill_columns(col_ref, taps)
    total = taps[0]
    for k in range(1, 2 * RADIUS + 1):
        total = total + taps[k]
    scale = 1.0 / jnp.full((dates, LANES), total, jnp.float32)
    flat = ends_ref.reshape(cols // LANES, dates * 2 * EDGE, LANES)

    def store(n):
        return [
            pltpu.make_async_copy(
                x_ref.at[n, :, :, pl.ds(side * (rows - EDGE), EDGE), :],
                outs[n].at[:, :, pl.ds(side * EDGE, EDGE), :], out_sem.at[n, side])
            for side in range(2)
        ]

    for copy in halos:
        copy.wait()

    mids, rims = [], []
    for n in range(parts):
        block = place[0] ^ order[n]
        start = pl.multiple_of(block * width, LANES)
        before = pl.multiple_of(jnp.maximum(start - LANES, 0), LANES)
        after = pl.multiple_of(jnp.minimum(start + width, cols - LANES), LANES)

        def both(first, span):
            at = pl.ds(first, span)
            return jnp.concatenate([up_ref[:, :, at], down_ref[:, :, at]], axis=0).reshape(2 * RADIUS * dates, span)

        mids.append(both(start, width))
        rims.append(rim_tile(both(before, LANES), both(after, LANES), block, parts))
    across = filter_columns(jnp.concatenate(mids, axis=0), jnp.concatenate(rims, axis=0), col_ref[...])
    span = 2 * RADIUS * dates
    for n in range(parts):
        for h in range(per):
            across_ref[n, h] = across[n * span:(n + 1) * span, h * LANES:(h + 1) * LANES]
    for copy in ends:
        copy.wait()

    def one(n, carry):
        block = place[0] ^ chosen(n, order)
        every = x_ref.at[n].reshape(per, dates * pitch, LANES)
        pltpu.make_async_copy(brim.at[n], brim_ref.at[n], brim_sem.at[n]).wait()

        def half(h, carry):
            for side in range(2):
                held = []
                for q in range(2 * RADIUS + EDGE):
                    halo = q < RADIUS if side == 0 else q >= RADIUS + EDGE
                    if halo:
                        at = q if side == 0 else q - EDGE
                        held.append(across_ref[n, h, at * dates:(at + 1) * dates, :])
                    else:
                        at = q - RADIUS if side == 0 else 3 * EDGE - RADIUS + q
                        held.append(jnp.concatenate([
                            brim_ref[n, h, (d * 4 * EDGE + at) * EDGE:(d * 4 * EDGE + at + 1) * EDGE, :]
                            for d in range(dates // EDGE)
                        ], axis=0))
                for r in range(EDGE):
                    low = taps[0] * held[r]
                    for j in range(1, 2 * RADIUS + 1):
                        low = low + taps[j] * held[r + j]
                    at = pl.ds(side * EDGE + r, dates, stride=2 * EDGE)
                    done = flat[block * per + h, at, :] - scale * low
                    every[h, pl.ds(side * (rows - EDGE) + r, dates, stride=pitch), :] = done
            return carry

        lax.fori_loop(0, per, half, 0)
        for m in range(parts):
            @pl.when(n == m)
            def _():
                for copy in store(m):
                    copy.start()
        return carry

    lax.fori_loop(0, parts, one, 0)

    lane = lax.broadcasted_iota(jnp.int32, (dates, LANES), 1)
    both = [jnp.concatenate([ref[n:n + 1, :] for ref in vectors], axis=1) for n in range(1, 4)]
    index = lax.broadcasted_iota(jnp.int32, both[0].shape, 1)
    source = (index // feet) ^ place[0]
    named = lax.broadcasted_iota(jnp.int32, (owners, index.shape[1]), 0) == both[1]
    places = []
    for block in range(parts):
        for slot in range(PAIR_CAP):
            hit = named & (source == block) & (both[2] == slot)
            places.append(jnp.where(hit, 1.0, 0.0).astype(jnp.bfloat16))
    places = jnp.concatenate(places, axis=0)
    pixel_rows = x_ref.reshape(parts * per * dates * pitch, LANES)
    for copy in middles:
        copy.wait()
    for k in range(parts):
        base = order.index(k) * per * dates * pitch

        def take(f, carry):
            pixels = pixel_rows[pl.ds(base + meta[k][0, f], dates, stride=pitch), :]
            v_ref[k * feet + f] = jnp.where(lane < meta[k][1, f], pixels, 0.0)
            return carry

        lax.fori_loop(0, feet, take, 0, unroll=8)
    tiles = []
    for first in range(0, parts * feet, LANES):

        def add(f, total):
            one = jnp.sum(v_ref[first + f], axis=1, keepdims=True)
            return jnp.where(lane == f, one, total)

        tiles.append(lax.fori_loop(0, LANES, add, jnp.zeros((dates, LANES), jnp.float32), unroll=32))
    counts = jnp.broadcast_to(both[0].astype(jnp.float32), (dates, index.shape[1]))
    sums = jnp.concatenate([jnp.concatenate(tiles, axis=1), counts], axis=0)
    held = jnp.zeros((places.shape[0], 2 * dates), jnp.float32)
    for piece in split(sums, 3):
        held = held + lax.dot_general(places, piece, (((1,), (1,)), ((), ())), preferred_element_type=jnp.float32)
    for n in range(parts * PAIR_CAP):
        at = pl.ds(n * dates, dates)
        sums_ref[:, 0, at] = held[n * owners:(n + 1) * owners, :dates]
        sums_ref[:, 1, at] = held[n * owners:(n + 1) * owners, dates:]
    for m in range(parts):
        for copy in store(m):
            copy.wait()


def edges(stack, up, down, brim, inner, meta, taps, place, order, owners):
    parts = len(order)
    dates, rows, cols = stack.shape
    tiles = cols // LANES
    per = tiles // parts
    feet = meta[0].shape[1]
    here = pl.BlockSpec(memory_space=pltpu.HBM)
    resident = pl.BlockSpec(memory_space=pltpu.VMEM)
    return pl.pallas_call(
        functools.partial(edge_kernel, order, feet),
        grid_spec=pltpu.PrefetchScalarGridSpec(
            num_scalar_prefetch=2 + parts,
            grid=(),
            in_specs=[resident] * parts + [here] * (4 + parts),
            out_specs=[here] * parts + [resident],
            scratch_shapes=[
                pltpu.VMEM((parts, per, 2 * RADIUS * dates, LANES), jnp.float32),
                pltpu.VMEM((parts, per, 4 * EDGE * dates, LANES), jnp.float32),
                pltpu.VMEM(up.shape, jnp.float32),
                pltpu.VMEM(up.shape, jnp.float32),
                pltpu.VMEM((tiles, dates, 2 * EDGE, LANES), jnp.float32),
                pltpu.VMEM((9 * LANES, per * LANES), jnp.bfloat16),
                pltpu.VMEM((parts, per, dates, rows + EDGE, LANES), jnp.float32),
                pltpu.VMEM((parts * feet, dates, LANES), jnp.float32),
                pltpu.SemaphoreType.DMA((2,)),
                pltpu.SemaphoreType.DMA((2, tiles)),
                pltpu.SemaphoreType.DMA((parts,)),
                pltpu.SemaphoreType.DMA((parts, 2)),
                pltpu.SemaphoreType.DMA((parts,)),
            ],
        ),
        out_shape=[jax.ShapeDtypeStruct((per, dates, 2 * EDGE, LANES), jnp.float32)] * parts
        + [jax.ShapeDtypeStruct((owners, 2, parts * PAIR_CAP * dates), jnp.float32)],
        compiler_params=params(63.5),
        cost_estimate=cost(8),
    )(place, taps, *meta, *meta, stack, up, down, brim, *inner)


def temporal_kernel(parts, strips, first_tile, tile_step, place, taps, *rest):
    pieces, rest = rest[:parts], rest[parts:]
    if strips:
        _, got_ref, out, anomaly, series, anomaly_ref, series_ref, owner_sem, *rest = rest
    else:
        out, *rest = rest
    z_ref, f_ref, out_ref, in_sem, out_sem = rest
    count, total, _, _ = out_ref.shape
    per = pieces[0].shape[0]
    local = total // parts
    pad = REACH * DILATION
    step = 8

    def load(n):
        rows = pl.ds(pl.multiple_of(n * EDGE, EDGE), EDGE)
        return [
            pltpu.make_async_copy(
                pieces[k].at[:, :, rows, :],
                z_ref.at[n, :, pl.ds(REACH + (place[0] ^ k) * local, local)], in_sem.at[n, k])
            for k in range(parts)
        ]

    def store(n):
        tile = first_tile + n * tile_step
        rows = pl.ds(pl.multiple_of(tile * EDGE, EDGE), EDGE)
        return pltpu.make_async_copy(out_ref.at[n], out.at[:, rows, :], out_sem.at[n])

    for n in range(count):
        for copy in load(n):
            copy.start()
    owner_copies = []
    if strips:
        series_ref[...], anomaly_ref[0] = owner_values(parts, strips, taps, got_ref)
        owner_copies = [
            pltpu.make_async_copy(series_ref, series, owner_sem.at[0]),
            pltpu.make_async_copy(anomaly_ref, anomaly, owner_sem.at[1]),
        ]
        for copy in owner_copies:
            copy.start()
    none = jnp.zeros((REACH, EDGE, LANES), jnp.float32)
    wide = jnp.zeros((pad, EDGE, LANES), jnp.float32)
    for h in range(per):
        for n in range(count):
            z_ref[n, h, 0:REACH] = none
            z_ref[n, h, REACH + total:REACH + total + REACH] = none
        f_ref[h, 0:pad] = wide
        f_ref[h, pad + total:pad + total + pad] = wide
    own = 1.0 - taps[0, REACH]
    own_wide = 1.0 - taps[1, REACH]
    others = [k for k in range(2 * REACH + 1) if k != REACH]

    def one(n, carry):
        for copy in load(n):
            copy.wait()
        for h in range(per):
            for t in range(0, total, step):
                z = z_ref[n, h, t:t + step + 2 * REACH]
                kept = own * z[REACH:REACH + step]
                for k in others:
                    kept = kept - taps[0, k] * z[k:k + step]
                f_ref[h, pad + t:pad + t + step] = kept
            for t in range(0, total, step):
                kept = own_wide * f_ref[h, pad + t:pad + t + step]
                for k in others:
                    kept = kept - taps[1, k] * f_ref[h, t + k * DILATION:t + k * DILATION + step]
                out_ref[n, t:t + step, :, h * LANES:(h + 1) * LANES] = kept
        store(n).start()
        return carry

    lax.fori_loop(0, count, one, 0)
    for n in range(count):
        store(n).wait()
    for copy in owner_copies:
        copy.wait()


def temporal(pieces, taps, place, first_tile, tile_step, rows, base=None, got=None, strips=0):
    parts = len(pieces)
    per, local, here, _ = pieces[0].shape
    total = local * parts
    count = here // EDGE
    width = per * LANES
    anywhere = pl.BlockSpec(memory_space=pl.ANY)
    whole = pl.BlockSpec(memory_space=pltpu.HBM)
    in_specs, out_specs, scratch = [anywhere] * parts, [whole], []
    out_shape = [jax.ShapeDtypeStruct((total, rows, width), jnp.float32)]
    extra = []
    if strips:
        extra = [base, got]
        in_specs += [anywhere, pl.BlockSpec(memory_space=pltpu.VMEM)]
        out_specs += [whole] * 2
        shapes = [(1, parts * strips * PAIR_CAP, total), (1, total)]
        out_shape += [jax.ShapeDtypeStruct(shape, jnp.float32) for shape in shapes]
        scratch = [pltpu.VMEM(shape, jnp.float32) for shape in shapes] + [pltpu.SemaphoreType.DMA((2,))]
    return pl.pallas_call(
        functools.partial(temporal_kernel, parts, strips, first_tile, tile_step),
        grid_spec=pltpu.PrefetchScalarGridSpec(
            num_scalar_prefetch=2,
            grid=(),
            in_specs=in_specs,
            out_specs=out_specs,
            scratch_shapes=scratch + [
                pltpu.VMEM((count, per, total + 2 * REACH, EDGE, LANES), jnp.float32),
                pltpu.VMEM((per, total + 2 * REACH * DILATION, EDGE, LANES), jnp.float32),
                pltpu.VMEM((count, total, EDGE, width), jnp.float32),
                pltpu.SemaphoreType.DMA((count, parts)),
                pltpu.SemaphoreType.DMA((count,)),
            ],
        ),
        out_shape=out_shape,
        input_output_aliases={2 + parts: 0} if strips else {},
        compiler_params=params(24),
        cost_estimate=cost(2.5 + 0.4 * count),
    )(place, taps, *pieces, *extra)


def owner_values(parts, strips, taps, got_ref):
    owners = parts * strips
    slots = owners * PAIR_CAP
    dates = got_ref.shape[2] // PAIR_CAP
    local = dates // parts
    sums, held = got_ref[:, 0, :], got_ref[:, 1, :]
    rows, weights = [], []
    for block in range(parts):
        for slot in range(PAIR_CAP):
            at = (block * PAIR_CAP + slot) * local
            rows.append(jnp.concatenate(
                [sums[e * strips:(e + 1) * strips, at:at + local] for e in range(parts)], axis=1))
            weights.append(held[0:strips, at:at + 1])
    sums = jnp.concatenate(rows, axis=0)
    weight = jnp.concatenate(weights, axis=0)
    shape = (dates, dates)
    lag = lax.broadcasted_iota(jnp.int32, shape, 0) - lax.broadcasted_iota(jnp.int32, shape, 1)
    for level, spacing in ((0, 1), (1, DILATION)):
        filt = jnp.where(lag == 0, 1.0, 0.0)
        for k in range(2 * REACH + 1):
            filt = filt - jnp.where(lag == (k - REACH) * spacing, taps[level, k], 0.0)
        sums = jnp.dot(sums, filt, precision=HIGHEST, preferred_element_type=jnp.float32)
    mean = sums / jnp.where(weight > 0, weight, 1.0)
    asset = jnp.sum(weight * mean, axis=0, keepdims=True) / jnp.sum(weight, axis=0, keepdims=True)
    odd = jnp.where(weight > 0, mean - asset, 0.0)
    shape = (slots, slots)
    to = lax.broadcasted_iota(jnp.int32, shape, 0)
    source = lax.broadcasted_iota(jnp.int32, shape, 1)
    block, rest = source // (PAIR_CAP * strips), source % (PAIR_CAP * strips)
    place_of = block * (PAIR_CAP * strips) + (rest % strips) * PAIR_CAP + rest // strips
    order = jnp.where(to == place_of, 1.0, 0.0)
    return asset, jnp.dot(order, odd, precision=HIGHEST, preferred_element_type=jnp.float32)


def spread_meta(meta, offset, swap):
    known = sorted(meta)
    got = swap(jnp.concatenate([meta[k] for k in known], axis=1), offset)
    width = meta[0].shape[1]
    return meta | {k ^ offset: got[:, n * width:(n + 1) * width] for n, k in enumerate(known)}


def shards(stack, spatial_taps, temporal_taps, foot_tile, foot_row, foot_count, foot_owner):
    parts, strips = lax.axis_size("date"), lax.axis_size("strip")
    place = lax.axis_index("date").astype(jnp.int32)[None]
    dates, rows, cols = stack.shape
    feet = foot_row.shape[0]
    owner = foot_owner[:, 0]
    position = jnp.arange(feet, dtype=jnp.int32)
    earlier = (owner[:, None] == owner[None, :]) & (position[None, :] < position[:, None])
    slot = jnp.sum(earlier.astype(jnp.int32), axis=1)
    own = jnp.stack([foot_tile * (dates * (rows + EDGE)) + foot_row, foot_count, owner, slot])

    def swap(value, offset):
        return lax.ppermute(value, "date", [(i, i ^ offset) for i in range(parts)])

    order = (*range(2, parts), 1, 0)
    inner, far_inner = {}, {}
    lead = order[0]
    inner[lead], brim = interior(stack, None, spatial_taps, place, (lead,), 0, parts)
    far_inner[lead] = swap(inner[lead], lead)
    later, brim = lax.optimization_barrier((place, brim))
    last_rows, first_rows = halo_rows(stack, later)
    up = lax.ppermute(last_rows, "strip", [(i, i + 1) for i in range(strips - 1)])
    down = lax.ppermute(first_rows, "strip", [(i + 1, i) for i in range(strips - 1)])
    own, brim = lax.optimization_barrier((own, brim))
    meta = {0: own}
    for bit in range(parts.bit_length() - 2, 0, -1):
        meta = spread_meta(meta, 1 << bit, swap)
    *made, brim = interior(stack, brim, spatial_taps, place, order[1:], 1, parts)
    for n, offset in enumerate(order[1:]):
        inner[offset] = made[n]
        if offset > 1:
            far_inner[offset] = swap(inner[offset], offset)
    known = sorted(meta)
    *held, far_inner[lead], brim = lax.optimization_barrier((*[meta[k] for k in known], far_inner[lead], brim))
    meta = spread_meta(dict(zip(known, held)), 1, swap)
    meta = [meta[k] for k in range(parts)]
    *made, sums = edges(
        stack, up, down, brim, [inner[k] for k in order], meta, spatial_taps, place, order, parts * strips)
    rim = dict(zip(order, made))
    far_inner[1] = swap(inner[1], 1)
    got = lax.all_to_all(sums, ("date", "strip"), split_axis=0, concat_axis=0, tiled=True)
    gate, *made = lax.optimization_barrier((swap(rim[1], 1), *[rim[k] for k in order[:-2]]))
    far_rim = {k: swap(made[n], k) for n, k in enumerate(order[:-2])}
    far_rim[1] = gate
    last = rows // EDGE - 1
    residual, = temporal(
        [inner[0]] + [far_inner[k] for k in range(1, parts)], temporal_taps, place, 1, 1, rows)
    got, residual = lax.optimization_barrier((got, residual))
    return temporal(
        [rim[0]] + [far_rim[k] for k in range(1, parts)], temporal_taps, place, 0, last, rows, residual, got, strips)


def solution(mesh):
    placed = (
        P("date", "strip", None),
        P(),
        P(),
        P(("date", "strip")),
        P(("date", "strip")),
        P(("date", "strip")),
        P(("date", "strip"), None),
    )
    return jax.shard_map(
        shards,
        mesh=mesh,
        in_specs=placed,
        out_specs=(
            P(None, "strip", "date"),
            P(("date", "strip"), None, None),
            P(("date", "strip"), None),
        ),
        check_vma=False,
    )
```

```python
import functools

import jax
import jax.numpy as jnp
from jax import lax
from jax.experimental import pallas as pl
from jax.experimental.pallas import tpu as pltpu
from jax.sharding import PartitionSpec as P

TILE = 128
RADIUS = 6
REACH = 2
DILATION = 8
PAIR_CAP = 2
LANES = 128
EDGE = 8
HIGHEST = lax.Precision.HIGHEST


def params(mebibytes):
    return pltpu.CompilerParams(vmem_limit_bytes=int(mebibytes * 1024 * 1024))


def cost(micros):
    return pl.CostEstimate(flops=int(micros * 1153.5e6), bytes_accessed=int(micros * 3.69e6), transcendentals=0)


def pick_taps(at, taps):
    count = taps.shape[0]
    total = taps[0]
    for k in range(1, count):
        total = total + taps[k]
    out = jnp.zeros(at.shape, jnp.float32)
    for k in range(count):
        out = jnp.where(at == k, taps[k], out)
    return out / jnp.full(at.shape, total, jnp.float32)


def split(value, count):
    out = []
    for _ in range(count):
        piece = value.astype(jnp.bfloat16)
        out.append(piece)
        value = value - piece.astype(jnp.float32)
    return out


def spread(value, axis):
    high, mid = split(value, 2)
    return jnp.concatenate([high, high, mid], axis=axis)


def fill_columns(col_ref, taps):
    shape = (LANES, LANES)
    lag = lax.broadcasted_iota(jnp.int32, shape, 0) - lax.broadcasted_iota(jnp.int32, shape, 1)
    near = split(pick_taps(lag + RADIUS, taps), 2)
    far = pick_taps(jnp.where(lag > 0, lag + RADIUS - LANES, lag + RADIUS + LANES), taps)
    above = split(jnp.where(lag > 0, far, 0.0), 2)
    below = split(jnp.where(lag > 0, 0.0, far), 2)
    for n, piece in enumerate((0, 1, 0)):
        at = n * 3 * LANES
        for i, pair in enumerate(((near, above), (below, near), (above, below))):
            for j, block in enumerate(pair):
                col_ref[at + i * LANES:at + (i + 1) * LANES, j * LANES:(j + 1) * LANES] = block[piece]


def row_band(out_rows, in_rows, taps):
    shape = (out_rows, 3 * in_rows)
    lane = lax.broadcasted_iota(jnp.int32, shape, 1)
    row = lax.broadcasted_iota(jnp.int32, shape, 0)
    part = jnp.zeros(shape, jnp.int32)
    for n in range(1, 3):
        part = jnp.where(lane >= n * in_rows, n, part)
    return lane - part * in_rows, row, part


def pieces_of(values, part):
    high, mid = [p.astype(jnp.float32) for p in split(values, 2)]
    return jnp.where(part == 1, mid, high).astype(jnp.bfloat16)


def filter_columns(mid, rim, col):
    rows = mid.shape[0]
    window = jnp.concatenate([mid, rim], axis=1)
    return jnp.dot(spread(window, 1), col, preferred_element_type=jnp.float32)


def rim_tile(left, right, block, parts):
    lane = lax.broadcasted_iota(jnp.int32, left.shape, len(left.shape) - 1)
    first = lane < LANES // 2
    keep = (first & (block < parts - 1)) | (~first & (block > 0))
    return jnp.where(keep, jnp.where(first, right, left), 0.0)


def chosen(n, values):
    out = values[0]
    for m in range(1, len(values)):
        out = jnp.where(n == m, values[m], out)
    return out


def interior_kernel(offsets, slot, parts, group, place, taps, stack, *rest):
    count = len(offsets)
    first = slot == 0
    if not first:
        rest = rest[1:]
    outs, brim, rest = rest[:count], rest[count], rest[count + 1:]
    if first:
        mid_ref, left_ref, right_ref, *rest = rest
    else:
        x_ref, *rest = rest
    out_ref, brim_ref, col_ref, row_ref, in_sem, out_sem, brim_sem = rest
    _, per, dates, inner, _ = out_ref.shape
    width = per * LANES
    rows = inner + 2 * EDGE
    cols = width * parts
    steps = dates // group

    def bounds(block):
        start = block * width
        places = start, jnp.maximum(start - LANES, 0), jnp.minimum(start + width, cols - LANES)
        return [pl.multiple_of(at, LANES) for at in places]

    def load(g):
        at = pl.ds(g * group, group)
        if not first:
            return [pltpu.make_async_copy(stack.at[at], x_ref.at[at], in_sem.at[0, g])]
        return [
            pltpu.make_async_copy(stack.at[at, :, pl.ds(start, ref.shape[2])], ref.at[at], in_sem.at[n, g])
            for n, (start, ref) in enumerate(zip(bounds(place[0] ^ offsets[0]), (mid_ref, left_ref, right_ref)))
        ]

    def store(m, g):
        at = pl.ds(g * group, group)
        return pltpu.make_async_copy(out_ref.at[m, :, at], outs[m].at[:, at], out_sem.at[m, g])

    def store_brim(n, g):
        at = pl.ds(g * group * 4 * EDGE, group * 4 * EDGE)
        return pltpu.make_async_copy(brim_ref.at[n, :, at], brim.at[slot + n, :, at], brim_sem.at[n, g])

    for g in range(steps):
        for copy in load(g):
            copy.start()
    fill_columns(col_ref, taps)
    q, r, part = row_band(inner, rows, taps)
    row_ref[...] = pieces_of(pick_taps(q - r - (EDGE - RADIUS), taps), part)

    def step(i, carry):
        n, g = i // steps, i % steps
        block = place[0] ^ chosen(n, offsets)
        at = pl.ds(g * group, group)

        @pl.when(n == 0)
        def _():
            for copy in load(g):
                copy.wait()

        if first:
            mid, left, right = mid_ref[at], left_ref[at], right_ref[at]
        else:
            start, before, after = bounds(block)
            mid, left, right = [x_ref[at, :, pl.ds(f, w)] for f, w in ((start, width), (before, LANES), (after, LANES))]
        rim = rim_tile(left, right, block, parts)
        across = filter_columns(mid.reshape(group * rows, width), rim.reshape(group * rows, LANES), col_ref[...])
        for t in range(group):
            one = across[t * rows:(t + 1) * rows]
            low = jnp.dot(row_ref[...], spread(one, 0), preferred_element_type=jnp.float32)
            done = mid[t, EDGE:rows - EDGE, :] - low
            for h in range(per):
                out_ref[n, h, g * group + t] = done[:, h * LANES:(h + 1) * LANES]
                for side in range(2):
                    lines = one[side * (rows - 2 * EDGE):side * (rows - 2 * EDGE) + 2 * EDGE, h * LANES:(h + 1) * LANES]
                    date = g * group + t
                    at = ((date // EDGE) * 4 * EDGE + side * 2 * EDGE) * EDGE + date % EDGE
                    brim_ref[n, h, pl.ds(at, 2 * EDGE, stride=EDGE), :] = lines
        for m in range(count):
            @pl.when(n == m)
            def _():
                store(m, g).start()

        store_brim(n, g).start()
        return carry

    lax.fori_loop(0, count * steps, step, 0)
    for m in range(count):
        for g in range(steps):
            store(m, g).wait()
            store_brim(m, g).wait()


def interior(stack, brim, taps, place, offsets, slot, parts):
    dates, rows, cols = stack.shape
    width = cols // parts
    per = width // LANES
    group = min(8, dates)
    inner = rows - 2 * EDGE
    count = len(offsets)
    first = slot == 0
    here = pl.BlockSpec(memory_space=pltpu.HBM)
    out_shape = [jax.ShapeDtypeStruct((per, dates, inner, LANES), jnp.float32)] * count
    out_shape += [jax.ShapeDtypeStruct((parts, per, 4 * EDGE * dates, LANES), jnp.float32)]
    scratch = [pltpu.VMEM((dates, rows, span), jnp.float32) for span in ((width, LANES, LANES) if first else (cols,))]
    return pl.pallas_call(
        functools.partial(interior_kernel, offsets, slot, parts, group),
        grid_spec=pltpu.PrefetchScalarGridSpec(
            num_scalar_prefetch=2,
            grid=(),
            in_specs=[here] * (1 if first else 2),
            out_specs=[here] * len(out_shape),
            scratch_shapes=scratch + [
                pltpu.VMEM((count, per, dates, inner, LANES), jnp.float32),
                pltpu.VMEM((count, per, 4 * EDGE * dates, LANES), jnp.float32),
                pltpu.VMEM((9 * LANES, width), jnp.bfloat16),
                pltpu.VMEM((inner, 3 * rows), jnp.bfloat16),
                pltpu.SemaphoreType.DMA((3, dates // group)),
                pltpu.SemaphoreType.DMA((count, dates // group)),
                pltpu.SemaphoreType.DMA((count, dates // group)),
            ],
        ),
        out_shape=out_shape,
        input_output_aliases={} if first else {3: count},
        compiler_params=params(63.5),
        cost_estimate=cost(5 if count == 1 else 4),
    )(place, taps, stack, *([] if first else [brim]))


def halo_kernel(place, stack, up, down, halo_ref, up_ref, down_ref, halo_sem, out_sem):
    tiles, dates, _, _ = halo_ref.shape
    rows = stack.shape[1]

    def load(c):
        lanes = pl.ds(pl.multiple_of(c * LANES, LANES), LANES)
        return [
            pltpu.make_async_copy(
                stack.at[:, pl.ds(side * (rows - EDGE), EDGE), lanes],
                halo_ref.at[c, :, pl.ds(side * EDGE, EDGE), :], halo_sem.at[side, c])
            for side in range(2)
        ]

    for c in range(tiles):
        for copy in load(c):
            copy.start()

    def pack(c, carry):
        for copy in load(c):
            copy.wait()
        at = pl.ds(pl.multiple_of(c * LANES, LANES), LANES)
        rows_of = halo_ref.at[c].reshape(dates * 2 * EDGE, LANES)
        for r in range(RADIUS):
            up_ref[r, :, at] = rows_of[pl.ds(2 * EDGE - RADIUS + r, dates, stride=2 * EDGE), :]
            down_ref[r, :, at] = rows_of[pl.ds(r, dates, stride=2 * EDGE), :]
        return carry

    lax.fori_loop(0, tiles, pack, 0)
    copies = [
        pltpu.make_async_copy(up_ref, up, out_sem.at[0]),
        pltpu.make_async_copy(down_ref, down, out_sem.at[1]),
    ]
    for copy in copies:
        copy.start()
    for copy in copies:
        copy.wait()


def halo_rows(stack, place):
    dates, _, cols = stack.shape
    here = pl.BlockSpec(memory_space=pltpu.HBM)
    return pl.pallas_call(
        halo_kernel,
        grid_spec=pltpu.PrefetchScalarGridSpec(
            num_scalar_prefetch=1,
            grid=(),
            in_specs=[here],
            out_specs=[here] * 2,
            scratch_shapes=[
                pltpu.VMEM((cols // LANES, dates, 2 * EDGE, LANES), jnp.float32),
                pltpu.VMEM((RADIUS, dates, cols), jnp.float32),
                pltpu.VMEM((RADIUS, dates, cols), jnp.float32),
                pltpu.SemaphoreType.DMA((2, cols // LANES)),
                pltpu.SemaphoreType.DMA((2,)),
            ],
        ),
        out_shape=[jax.ShapeDtypeStruct((RADIUS, dates, cols), jnp.float32)] * 2,
        compiler_params=params(63.5),
        cost_estimate=cost(2.5),
    )(place, stack)


def edge_kernel(order, feet, place, taps, *rest):
    parts = len(order)
    meta, vectors, rest = rest[:parts], rest[parts:2 * parts], rest[2 * parts:]
    stack, up, down, brim, *rest = rest
    inner, outs, rest = rest[:parts], rest[parts:2 * parts], rest[2 * parts:]
    sums_ref, across_ref, brim_ref, up_ref, down_ref, ends_ref, col_ref, x_ref, v_ref = rest[:9]
    halo_sem, ends_sem, brim_sem, out_sem, x_sem = rest[9:]
    _, dates, cols = up_ref.shape
    width = cols // parts
    per = width // LANES
    pitch = x_ref.shape[3]
    rows = pitch - EDGE
    owners = sums_ref.shape[0]
    halos = [
        pltpu.make_async_copy(whole, ref, halo_sem.at[n])
        for n, (whole, ref) in enumerate(((up, up_ref), (down, down_ref)))
    ]
    ends = [
        pltpu.make_async_copy(
            stack.at[:, pl.ds(side * (rows - EDGE), EDGE), pl.ds(c * LANES, LANES)],
            ends_ref.at[c, :, pl.ds(side * EDGE, EDGE), :], ends_sem.at[side, c])
        for side in range(2) for c in range(cols // LANES)
    ]
    for copy in halos + ends:
        copy.start()
    for n in range(parts):
        pltpu.make_async_copy(brim.at[n], brim_ref.at[n], brim_sem.at[n]).start()
    middles = [
        pltpu.make_async_copy(inner[n], x_ref.at[n, :, :, pl.ds(EDGE, rows - 2 * EDGE), :], x_sem.at[n]) for n in range(parts)
    ]
    for copy in middles:
        copy.start()
    fill_columns(col_ref, taps)
    total = taps[0]
    for k in range(1, 2 * RADIUS + 1):
        total = total + taps[k]
    scale = 1.0 / jnp.full((dates, LANES), total, jnp.float32)
    flat = ends_ref.reshape(cols // LANES, dates * 2 * EDGE, LANES)

    def store(n):
        return [
            pltpu.make_async_copy(
                x_ref.at[n, :, :, pl.ds(side * (rows - EDGE), EDGE), :],
                outs[n].at[:, :, pl.ds(side * EDGE, EDGE), :], out_sem.at[n, side])
            for side in range(2)
        ]

    for copy in halos:
        copy.wait()

    mids, rims = [], []
    for n in range(parts):
        block = place[0] ^ order[n]
        start = pl.multiple_of(block * width, LANES)
        before = pl.multiple_of(jnp.maximum(start - LANES, 0), LANES)
        after = pl.multiple_of(jnp.minimum(start + width, cols - LANES), LANES)

        def both(first, span):
            at = pl.ds(first, span)
            return jnp.concatenate([up_ref[:, :, at], down_ref[:, :, at]], axis=0).reshape(2 * RADIUS * dates, span)

        mids.append(both(start, width))
        rims.append(rim_tile(both(before, LANES), both(after, LANES), block, parts))
    across = filter_columns(jnp.concatenate(mids, axis=0), jnp.concatenate(rims, axis=0), col_ref[...])
    span = 2 * RADIUS * dates
    for n in range(parts):
        for h in range(per):
            across_ref[n, h] = across[n * span:(n + 1) * span, h * LANES:(h + 1) * LANES]
    for copy in ends:
        copy.wait()

    def one(n, carry):
        block = place[0] ^ chosen(n, order)
        every = x_ref.at[n].reshape(per, dates * pitch, LANES)
        pltpu.make_async_copy(brim.at[n], brim_ref.at[n], brim_sem.at[n]).wait()

        def half(h, carry):
            for side in range(2):
                held = []
                for q in range(2 * RADIUS + EDGE):
                    halo = q < RADIUS if side == 0 else q >= RADIUS + EDGE
                    if halo:
                        at = q if side == 0 else q - EDGE
                        held.append(across_ref[n, h, at * dates:(at + 1) * dates, :])
                    else:
                        at = q - RADIUS if side == 0 else 3 * EDGE - RADIUS + q
                        held.append(jnp.concatenate([
                            brim_ref[n, h, (d * 4 * EDGE + at) * EDGE:(d * 4 * EDGE + at + 1) * EDGE, :]
                            for d in range(dates // EDGE)
                        ], axis=0))
                for r in range(EDGE):
                    low = taps[0] * held[r]
                    for j in range(1, 2 * RADIUS + 1):
                        low = low + taps[j] * held[r + j]
                    at = pl.ds(side * EDGE + r, dates, stride=2 * EDGE)
                    done = flat[block * per + h, at, :] - scale * low
                    every[h, pl.ds(side * (rows - EDGE) + r, dates, stride=pitch), :] = done
            return carry

        lax.fori_loop(0, per, half, 0)
        for m in range(parts):
            @pl.when(n == m)
            def _():
                for copy in store(m):
                    copy.start()
        return carry

    lax.fori_loop(0, parts, one, 0)

    lane = lax.broadcasted_iota(jnp.int32, (dates, LANES), 1)
    both = [jnp.concatenate([ref[n:n + 1, :] for ref in vectors], axis=1) for n in range(1, 4)]
    index = lax.broadcasted_iota(jnp.int32, both[0].shape, 1)
    source = (index // feet) ^ place[0]
    named = lax.broadcasted_iota(jnp.int32, (owners, index.shape[1]), 0) == both[1]
    places = []
    for block in range(parts):
        for slot in range(PAIR_CAP):
            hit = named & (source == block) & (both[2] == slot)
            places.append(jnp.where(hit, 1.0, 0.0).astype(jnp.bfloat16))
    places = jnp.concatenate(places, axis=0)
    pixel_rows = x_ref.reshape(parts * per * dates * pitch, LANES)
    for copy in middles:
        copy.wait()
    for k in range(parts):
        base = order.index(k) * per * dates * pitch

        def take(f, carry):
            pixels = pixel_rows[pl.ds(base + meta[k][0, f], dates, stride=pitch), :]
            v_ref[k * feet + f] = jnp.where(lane < meta[k][1, f], pixels, 0.0)
            return carry

        lax.fori_loop(0, feet, take, 0, unroll=8)
    tiles = []
    for first in range(0, parts * feet, LANES):

        def add(f, total):
            one = jnp.sum(v_ref[first + f], axis=1, keepdims=True)
            return jnp.where(lane == f, one, total)

        tiles.append(lax.fori_loop(0, LANES, add, jnp.zeros((dates, LANES), jnp.float32), unroll=32))
    counts = jnp.broadcast_to(both[0].astype(jnp.float32), (dates, index.shape[1]))
    sums = jnp.concatenate([jnp.concatenate(tiles, axis=1), counts], axis=0)
    held = jnp.zeros((places.shape[0], 2 * dates), jnp.float32)
    for piece in split(sums, 3):
        held = held + lax.dot_general(places, piece, (((1,), (1,)), ((), ())), preferred_element_type=jnp.float32)
    for n in range(parts * PAIR_CAP):
        at = pl.ds(n * dates, dates)
        sums_ref[:, 0, at] = held[n * owners:(n + 1) * owners, :dates]
        sums_ref[:, 1, at] = held[n * owners:(n + 1) * owners, dates:]
    for m in range(parts):
        for copy in store(m):
            copy.wait()


def edges(stack, up, down, brim, inner, meta, taps, place, order, owners):
    parts = len(order)
    dates, rows, cols = stack.shape
    tiles = cols // LANES
    per = tiles // parts
    feet = meta[0].shape[1]
    here = pl.BlockSpec(memory_space=pltpu.HBM)
    resident = pl.BlockSpec(memory_space=pltpu.VMEM)
    return pl.pallas_call(
        functools.partial(edge_kernel, order, feet),
        grid_spec=pltpu.PrefetchScalarGridSpec(
            num_scalar_prefetch=2 + parts,
            grid=(),
            in_specs=[resident] * parts + [here] * (4 + parts),
            out_specs=[here] * parts + [resident],
            scratch_shapes=[
                pltpu.VMEM((parts, per, 2 * RADIUS * dates, LANES), jnp.float32),
                pltpu.VMEM((parts, per, 4 * EDGE * dates, LANES), jnp.float32),
                pltpu.VMEM(up.shape, jnp.float32),
                pltpu.VMEM(up.shape, jnp.float32),
                pltpu.VMEM((tiles, dates, 2 * EDGE, LANES), jnp.float32),
                pltpu.VMEM((9 * LANES, per * LANES), jnp.bfloat16),
                pltpu.VMEM((parts, per, dates, rows + EDGE, LANES), jnp.float32),
                pltpu.VMEM((parts * feet, dates, LANES), jnp.float32),
                pltpu.SemaphoreType.DMA((2,)),
                pltpu.SemaphoreType.DMA((2, tiles)),
                pltpu.SemaphoreType.DMA((parts,)),
                pltpu.SemaphoreType.DMA((parts, 2)),
                pltpu.SemaphoreType.DMA((parts,)),
            ],
        ),
        out_shape=[jax.ShapeDtypeStruct((per, dates, 2 * EDGE, LANES), jnp.float32)] * parts
        + [jax.ShapeDtypeStruct((owners, 2, parts * PAIR_CAP * dates), jnp.float32)],
        compiler_params=params(63.5),
        cost_estimate=cost(2),
    )(place, taps, *meta, *meta, stack, up, down, brim, *inner)


def temporal_kernel(parts, strips, first_tile, tile_step, place, taps, *rest):
    pieces, rest = rest[:parts], rest[parts:]
    if strips:
        _, got_ref, out, anomaly, series, anomaly_ref, series_ref, owner_sem, *rest = rest
    else:
        out, *rest = rest
    z_ref, f_ref, out_ref, in_sem, out_sem = rest
    count, total, _, _ = out_ref.shape
    per = pieces[0].shape[0]
    local = total // parts
    pad = REACH * DILATION
    step = 8

    def load(n):
        rows = pl.ds(pl.multiple_of(n * EDGE, EDGE), EDGE)
        return [
            pltpu.make_async_copy(
                pieces[k].at[:, :, rows, :],
                z_ref.at[n, :, pl.ds(REACH + (place[0] ^ k) * local, local)], in_sem.at[n, k])
            for k in range(parts)
        ]

    def store(n):
        tile = first_tile + n * tile_step
        rows = pl.ds(pl.multiple_of(tile * EDGE, EDGE), EDGE)
        return pltpu.make_async_copy(out_ref.at[n], out.at[:, rows, :], out_sem.at[n])

    for n in range(count):
        for copy in load(n):
            copy.start()
    owner_copies = []
    if strips:
        series_ref[...], anomaly_ref[0] = owner_values(parts, strips, taps, got_ref)
        owner_copies = [
            pltpu.make_async_copy(series_ref, series, owner_sem.at[0]),
            pltpu.make_async_copy(anomaly_ref, anomaly, owner_sem.at[1]),
        ]
        for copy in owner_copies:
            copy.start()
    none = jnp.zeros((REACH, EDGE, LANES), jnp.float32)
    wide = jnp.zeros((pad, EDGE, LANES), jnp.float32)
    for h in range(per):
        for n in range(count):
            z_ref[n, h, 0:REACH] = none
            z_ref[n, h, REACH + total:REACH + total + REACH] = none
        f_ref[h, 0:pad] = wide
        f_ref[h, pad + total:pad + total + pad] = wide
    own = 1.0 - taps[0, REACH]
    own_wide = 1.0 - taps[1, REACH]
    others = [k for k in range(2 * REACH + 1) if k != REACH]

    def one(n, carry):
        for copy in load(n):
            copy.wait()
        for h in range(per):
            for t in range(0, total, step):
                z = z_ref[n, h, t:t + step + 2 * REACH]
                kept = own * z[REACH:REACH + step]
                for k in others:
                    kept = kept - taps[0, k] * z[k:k + step]
                f_ref[h, pad + t:pad + t + step] = kept
            for t in range(0, total, step):
                kept = own_wide * f_ref[h, pad + t:pad + t + step]
                for k in others:
                    kept = kept - taps[1, k] * f_ref[h, t + k * DILATION:t + k * DILATION + step]
                out_ref[n, t:t + step, :, h * LANES:(h + 1) * LANES] = kept
        store(n).start()
        return carry

    lax.fori_loop(0, count, one, 0)
    for n in range(count):
        store(n).wait()
    for copy in owner_copies:
        copy.wait()


def temporal(pieces, taps, place, first_tile, tile_step, rows, base=None, got=None, strips=0):
    parts = len(pieces)
    per, local, here, _ = pieces[0].shape
    total = local * parts
    count = here // EDGE
    width = per * LANES
    anywhere = pl.BlockSpec(memory_space=pl.ANY)
    whole = pl.BlockSpec(memory_space=pltpu.HBM)
    in_specs, out_specs, scratch = [anywhere] * parts, [whole], []
    out_shape = [jax.ShapeDtypeStruct((total, rows, width), jnp.float32)]
    extra = []
    if strips:
        extra = [base, got]
        in_specs += [anywhere, pl.BlockSpec(memory_space=pltpu.VMEM)]
        out_specs += [whole] * 2
        shapes = [(1, parts * strips * PAIR_CAP, total), (1, total)]
        out_shape += [jax.ShapeDtypeStruct(shape, jnp.float32) for shape in shapes]
        scratch = [pltpu.VMEM(shape, jnp.float32) for shape in shapes] + [pltpu.SemaphoreType.DMA((2,))]
    return pl.pallas_call(
        functools.partial(temporal_kernel, parts, strips, first_tile, tile_step),
        grid_spec=pltpu.PrefetchScalarGridSpec(
            num_scalar_prefetch=2,
            grid=(),
            in_specs=in_specs,
            out_specs=out_specs,
            scratch_shapes=scratch + [
                pltpu.VMEM((count, per, total + 2 * REACH, EDGE, LANES), jnp.float32),
                pltpu.VMEM((per, total + 2 * REACH * DILATION, EDGE, LANES), jnp.float32),
                pltpu.VMEM((count, total, EDGE, width), jnp.float32),
                pltpu.SemaphoreType.DMA((count, parts)),
                pltpu.SemaphoreType.DMA((count,)),
            ],
        ),
        out_shape=out_shape,
        input_output_aliases={2 + parts: 0} if strips else {},
        compiler_params=params(24),
        cost_estimate=cost(0),
    )(place, taps, *pieces, *extra)


def owner_values(parts, strips, taps, got_ref):
    owners = parts * strips
    slots = owners * PAIR_CAP
    dates = got_ref.shape[2] // PAIR_CAP
    local = dates // parts
    sums, held = got_ref[:, 0, :], got_ref[:, 1, :]
    rows, weights = [], []
    for block in range(parts):
        for slot in range(PAIR_CAP):
            at = (block * PAIR_CAP + slot) * local
            rows.append(jnp.concatenate(
                [sums[e * strips:(e + 1) * strips, at:at + local] for e in range(parts)], axis=1))
            weights.append(held[0:strips, at:at + 1])
    sums = jnp.concatenate(rows, axis=0)
    weight = jnp.concatenate(weights, axis=0)
    shape = (dates, dates)
    lag = lax.broadcasted_iota(jnp.int32, shape, 0) - lax.broadcasted_iota(jnp.int32, shape, 1)
    for level, spacing in ((0, 1), (1, DILATION)):
        filt = jnp.where(lag == 0, 1.0, 0.0)
        for k in range(2 * REACH + 1):
            filt = filt - jnp.where(lag == (k - REACH) * spacing, taps[level, k], 0.0)
        sums = jnp.dot(sums, filt, precision=HIGHEST, preferred_element_type=jnp.float32)
    mean = sums / jnp.where(weight > 0, weight, 1.0)
    asset = jnp.sum(weight * mean, axis=0, keepdims=True) / jnp.sum(weight, axis=0, keepdims=True)
    odd = jnp.where(weight > 0, mean - asset, 0.0)
    shape = (slots, slots)
    to = lax.broadcasted_iota(jnp.int32, shape, 0)
    source = lax.broadcasted_iota(jnp.int32, shape, 1)
    block, rest = source // (PAIR_CAP * strips), source % (PAIR_CAP * strips)
    place_of = block * (PAIR_CAP * strips) + (rest % strips) * PAIR_CAP + rest // strips
    order = jnp.where(to == place_of, 1.0, 0.0)
    return asset, jnp.dot(order, odd, precision=HIGHEST, preferred_element_type=jnp.float32)


def spread_meta(meta, offset, swap):
    known = sorted(meta)
    got = swap(jnp.concatenate([meta[k] for k in known], axis=1), offset)
    width = meta[0].shape[1]
    return meta | {k ^ offset: got[:, n * width:(n + 1) * width] for n, k in enumerate(known)}


def shards(stack, spatial_taps, temporal_taps, foot_tile, foot_row, foot_count, foot_owner):
    parts, strips = lax.axis_size("date"), lax.axis_size("strip")
    place = lax.axis_index("date").astype(jnp.int32)[None]
    dates, rows, cols = stack.shape
    feet = foot_row.shape[0]
    owner = foot_owner[:, 0]
    position = jnp.arange(feet, dtype=jnp.int32)
    earlier = (owner[:, None] == owner[None, :]) & (position[None, :] < position[:, None])
    slot = jnp.sum(earlier.astype(jnp.int32), axis=1)
    own = jnp.stack([foot_tile * (dates * (rows + EDGE)) + foot_row, foot_count, owner, slot])

    def swap(value, offset):
        return lax.ppermute(value, "date", [(i, i ^ offset) for i in range(parts)])

    order = (*range(2, parts), 1, 0)
    inner, far_inner = {}, {}
    lead = order[0]
    inner[lead], brim = interior(stack, None, spatial_taps, place, (lead,), 0, parts)
    far_inner[lead] = swap(inner[lead], lead)
    later, brim = lax.optimization_barrier((place, brim))
    last_rows, first_rows = halo_rows(stack, later)
    up = lax.ppermute(last_rows, "strip", [(i, i + 1) for i in range(strips - 1)])
    down = lax.ppermute(first_rows, "strip", [(i + 1, i) for i in range(strips - 1)])
    own, brim = lax.optimization_barrier((own, brim))
    meta = {0: own}
    for bit in range(parts.bit_length() - 2, 0, -1):
        meta = spread_meta(meta, 1 << bit, swap)
    *made, brim = interior(stack, brim, spatial_taps, place, order[1:], 1, parts)
    for n, offset in enumerate(order[1:]):
        inner[offset] = made[n]
        if offset > 1:
            far_inner[offset] = swap(inner[offset], offset)
    known = sorted(meta)
    *held, far_inner[lead], brim = lax.optimization_barrier((*[meta[k] for k in known], far_inner[lead], brim))
    meta = spread_meta(dict(zip(known, held)), 1, swap)
    meta = [meta[k] for k in range(parts)]
    *made, sums = edges(
        stack, up, down, brim, [inner[k] for k in order], meta, spatial_taps, place, order, parts * strips)
    rim = dict(zip(order, made))
    far_inner[1] = swap(inner[1], 1)
    got = lax.all_to_all(sums, ("date", "strip"), split_axis=0, concat_axis=0, tiled=True)
    far_rim = {k: swap(rim[k], k) for k in order[:-1]}
    last = rows // EDGE - 1
    residual, = temporal(
        [inner[0]] + [far_inner[k] for k in range(1, parts)], temporal_taps, place, 1, 1, rows)
    got, residual = lax.optimization_barrier((got, residual))
    return temporal(
        [rim[0]] + [far_rim[k] for k in range(1, parts)], temporal_taps, place, 0, last, rows, residual, got, strips)


def solution(mesh):
    placed = (
        P("date", "strip", None),
        P(),
        P(),
        P(("date", "strip")),
        P(("date", "strip")),
        P(("date", "strip")),
        P(("date", "strip"), None),
    )
    return jax.shard_map(
        shards,
        mesh=mesh,
        in_specs=placed,
        out_specs=(
            P(None, "strip", "date"),
            P(("date", "strip"), None, None),
            P(("date", "strip"), None),
        ),
        check_vma=False,
    )
```

```python
import functools

import jax
import jax.numpy as jnp
from jax import lax
from jax.experimental import pallas as pl
from jax.experimental.pallas import tpu as pltpu
from jax.sharding import PartitionSpec as P

TILE = 128
RADIUS = 6
REACH = 2
DILATION = 8
PAIR_CAP = 2
LANES = 128
EDGE = 8
HIGHEST = lax.Precision.HIGHEST


def params(mebibytes):
    return pltpu.CompilerParams(vmem_limit_bytes=int(mebibytes * 1024 * 1024))


def cost(micros):
    return pl.CostEstimate(flops=int(micros * 1153.5e6), bytes_accessed=int(micros * 3.69e6), transcendentals=0)


def pick_taps(at, taps):
    count = taps.shape[0]
    total = taps[0]
    for k in range(1, count):
        total = total + taps[k]
    out = jnp.zeros(at.shape, jnp.float32)
    for k in range(count):
        out = jnp.where(at == k, taps[k], out)
    return out / jnp.full(at.shape, total, jnp.float32)


def split(value, count):
    out = []
    for _ in range(count):
        piece = value.astype(jnp.bfloat16)
        out.append(piece)
        value = value - piece.astype(jnp.float32)
    return out


def spread(value, axis):
    high, mid = split(value, 2)
    return jnp.concatenate([high, high, mid], axis=axis)


def fill_columns(col_ref, taps):
    shape = (LANES, LANES)
    lag = lax.broadcasted_iota(jnp.int32, shape, 0) - lax.broadcasted_iota(jnp.int32, shape, 1)
    near = split(pick_taps(lag + RADIUS, taps), 2)
    far = pick_taps(jnp.where(lag > 0, lag + RADIUS - LANES, lag + RADIUS + LANES), taps)
    above = split(jnp.where(lag > 0, far, 0.0), 2)
    below = split(jnp.where(lag > 0, 0.0, far), 2)
    for n, piece in enumerate((0, 1, 0)):
        at = n * 3 * LANES
        for i, pair in enumerate(((near, above), (below, near), (above, below))):
            for j, block in enumerate(pair):
                col_ref[at + i * LANES:at + (i + 1) * LANES, j * LANES:(j + 1) * LANES] = block[piece]


def row_band(out_rows, in_rows, taps):
    shape = (out_rows, 3 * in_rows)
    lane = lax.broadcasted_iota(jnp.int32, shape, 1)
    row = lax.broadcasted_iota(jnp.int32, shape, 0)
    part = jnp.zeros(shape, jnp.int32)
    for n in range(1, 3):
        part = jnp.where(lane >= n * in_rows, n, part)
    return lane - part * in_rows, row, part


def pieces_of(values, part):
    high, mid = [p.astype(jnp.float32) for p in split(values, 2)]
    return jnp.where(part == 1, mid, high).astype(jnp.bfloat16)


def filter_columns(mid, rim, col):
    rows = mid.shape[0]
    window = jnp.concatenate([mid, rim], axis=1)
    return jnp.dot(spread(window, 1), col, preferred_element_type=jnp.float32)


def rim_tile(left, right, block, parts):
    lane = lax.broadcasted_iota(jnp.int32, left.shape, len(left.shape) - 1)
    first = lane < LANES // 2
    keep = (first & (block < parts - 1)) | (~first & (block > 0))
    return jnp.where(keep, jnp.where(first, right, left), 0.0)


def chosen(n, values):
    out = values[0]
    for m in range(1, len(values)):
        out = jnp.where(n == m, values[m], out)
    return out


def interior_kernel(offsets, slot, parts, group, place, taps, stack, *rest):
    count = len(offsets)
    first = slot == 0
    if not first:
        rest = rest[1:]
    outs, brim, rest = rest[:count], rest[count], rest[count + 1:]
    if first:
        mid_ref, left_ref, right_ref, *rest = rest
    else:
        x_ref, *rest = rest
    out_ref, brim_ref, col_ref, row_ref, in_sem, out_sem, brim_sem = rest
    _, per, dates, inner, _ = out_ref.shape
    width = per * LANES
    rows = inner + 2 * EDGE
    cols = width * parts
    steps = dates // group

    def bounds(block):
        start = block * width
        places = start, jnp.maximum(start - LANES, 0), jnp.minimum(start + width, cols - LANES)
        return [pl.multiple_of(at, LANES) for at in places]

    def load(g):
        at = pl.ds(g * group, group)
        if not first:
            return [pltpu.make_async_copy(stack.at[at], x_ref.at[at], in_sem.at[0, g])]
        return [
            pltpu.make_async_copy(stack.at[at, :, pl.ds(start, ref.shape[2])], ref.at[at], in_sem.at[n, g])
            for n, (start, ref) in enumerate(zip(bounds(place[0] ^ offsets[0]), (mid_ref, left_ref, right_ref)))
        ]

    def store(m, g):
        at = pl.ds(g * group, group)
        return pltpu.make_async_copy(out_ref.at[m, :, at], outs[m].at[:, at], out_sem.at[m, g])

    def store_brim(n, g):
        at = pl.ds(g * group * 4 * EDGE, group * 4 * EDGE)
        return pltpu.make_async_copy(brim_ref.at[n, :, at], brim.at[slot + n, :, at], brim_sem.at[n, g])

    for g in range(steps):
        for copy in load(g):
            copy.start()
    fill_columns(col_ref, taps)
    q, r, part = row_band(inner, rows, taps)
    row_ref[...] = pieces_of(pick_taps(q - r - (EDGE - RADIUS), taps), part)

    def step(i, carry):
        n, g = i // steps, i % steps
        block = place[0] ^ chosen(n, offsets)
        at = pl.ds(g * group, group)

        @pl.when(n == 0)
        def _():
            for copy in load(g):
                copy.wait()

        if first:
            mid, left, right = mid_ref[at], left_ref[at], right_ref[at]
        else:
            start, before, after = bounds(block)
            mid, left, right = [x_ref[at, :, pl.ds(f, w)] for f, w in ((start, width), (before, LANES), (after, LANES))]
        rim = rim_tile(left, right, block, parts)
        across = filter_columns(mid.reshape(group * rows, width), rim.reshape(group * rows, LANES), col_ref[...])
        for t in range(group):
            one = across[t * rows:(t + 1) * rows]
            low = jnp.dot(row_ref[...], spread(one, 0), preferred_element_type=jnp.float32)
            done = mid[t, EDGE:rows - EDGE, :] - low
            for h in range(per):
                out_ref[n, h, g * group + t] = done[:, h * LANES:(h + 1) * LANES]
                for side in range(2):
                    lines = one[side * (rows - 2 * EDGE):side * (rows - 2 * EDGE) + 2 * EDGE, h * LANES:(h + 1) * LANES]
                    date = g * group + t
                    at = ((date // EDGE) * 4 * EDGE + side * 2 * EDGE) * EDGE + date % EDGE
                    brim_ref[n, h, pl.ds(at, 2 * EDGE, stride=EDGE), :] = lines
        for m in range(count):
            @pl.when(n == m)
            def _():
                store(m, g).start()

        store_brim(n, g).start()
        return carry

    lax.fori_loop(0, count * steps, step, 0)
    for m in range(count):
        for g in range(steps):
            store(m, g).wait()
            store_brim(m, g).wait()


def interior(stack, brim, taps, place, offsets, slot, parts):
    dates, rows, cols = stack.shape
    width = cols // parts
    per = width // LANES
    group = min(8, dates)
    inner = rows - 2 * EDGE
    count = len(offsets)
    first = slot == 0
    here = pl.BlockSpec(memory_space=pltpu.HBM)
    out_shape = [jax.ShapeDtypeStruct((per, dates, inner, LANES), jnp.float32)] * count
    out_shape += [jax.ShapeDtypeStruct((parts, per, 4 * EDGE * dates, LANES), jnp.float32)]
    scratch = [pltpu.VMEM((dates, rows, span), jnp.float32) for span in ((width, LANES, LANES) if first else (cols,))]
    return pl.pallas_call(
        functools.partial(interior_kernel, offsets, slot, parts, group),
        grid_spec=pltpu.PrefetchScalarGridSpec(
            num_scalar_prefetch=2,
            grid=(),
            in_specs=[here] * (1 if first else 2),
            out_specs=[here] * len(out_shape),
            scratch_shapes=scratch + [
                pltpu.VMEM((count, per, dates, inner, LANES), jnp.float32),
                pltpu.VMEM((count, per, 4 * EDGE * dates, LANES), jnp.float32),
                pltpu.VMEM((9 * LANES, width), jnp.bfloat16),
                pltpu.VMEM((inner, 3 * rows), jnp.bfloat16),
                pltpu.SemaphoreType.DMA((3, dates // group)),
                pltpu.SemaphoreType.DMA((count, dates // group)),
                pltpu.SemaphoreType.DMA((count, dates // group)),
            ],
        ),
        out_shape=out_shape,
        input_output_aliases={} if first else {3: count},
        compiler_params=params(63.75),
        cost_estimate=cost(5 if count == 1 else 4),
    )(place, taps, stack, *([] if first else [brim]))


def halo_kernel(place, stack, up, down, halo_ref, up_ref, down_ref, halo_sem, out_sem):
    tiles, dates, _, _ = halo_ref.shape
    rows = stack.shape[1]

    def load(c):
        lanes = pl.ds(pl.multiple_of(c * LANES, LANES), LANES)
        return [
            pltpu.make_async_copy(
                stack.at[:, pl.ds(side * (rows - EDGE), EDGE), lanes],
                halo_ref.at[c, :, pl.ds(side * EDGE, EDGE), :], halo_sem.at[side, c])
            for side in range(2)
        ]

    for c in range(tiles):
        for copy in load(c):
            copy.start()

    def pack(c, carry):
        for copy in load(c):
            copy.wait()
        at = pl.ds(pl.multiple_of(c * LANES, LANES), LANES)
        rows_of = halo_ref.at[c].reshape(dates * 2 * EDGE, LANES)
        for r in range(RADIUS):
            up_ref[r, :, at] = rows_of[pl.ds(2 * EDGE - RADIUS + r, dates, stride=2 * EDGE), :]
            down_ref[r, :, at] = rows_of[pl.ds(r, dates, stride=2 * EDGE), :]
        return carry

    lax.fori_loop(0, tiles, pack, 0)
    copies = [
        pltpu.make_async_copy(up_ref, up, out_sem.at[0]),
        pltpu.make_async_copy(down_ref, down, out_sem.at[1]),
    ]
    for copy in copies:
        copy.start()
    for copy in copies:
        copy.wait()


def halo_rows(stack, place):
    dates, _, cols = stack.shape
    here = pl.BlockSpec(memory_space=pltpu.HBM)
    return pl.pallas_call(
        halo_kernel,
        grid_spec=pltpu.PrefetchScalarGridSpec(
            num_scalar_prefetch=1,
            grid=(),
            in_specs=[here],
            out_specs=[here] * 2,
            scratch_shapes=[
                pltpu.VMEM((cols // LANES, dates, 2 * EDGE, LANES), jnp.float32),
                pltpu.VMEM((RADIUS, dates, cols), jnp.float32),
                pltpu.VMEM((RADIUS, dates, cols), jnp.float32),
                pltpu.SemaphoreType.DMA((2, cols // LANES)),
                pltpu.SemaphoreType.DMA((2,)),
            ],
        ),
        out_shape=[jax.ShapeDtypeStruct((RADIUS, dates, cols), jnp.float32)] * 2,
        compiler_params=params(63.75),
        cost_estimate=cost(2.5),
    )(place, stack)


def edge_kernel(order, feet, place, taps, *rest):
    parts = len(order)
    meta, vectors, rest = rest[:parts], rest[parts:2 * parts], rest[2 * parts:]
    stack, up, down, brim, *rest = rest
    inner, outs, rest = rest[:parts], rest[parts:2 * parts], rest[2 * parts:]
    sums_ref, across_ref, brim_ref, up_ref, down_ref, ends_ref, col_ref, x_ref, v_ref = rest[:9]
    halo_sem, ends_sem, brim_sem, out_sem, x_sem = rest[9:]
    _, dates, cols = up_ref.shape
    width = cols // parts
    per = width // LANES
    pitch = x_ref.shape[3]
    rows = pitch - EDGE
    owners = sums_ref.shape[0]
    halos = [
        pltpu.make_async_copy(whole, ref, halo_sem.at[n])
        for n, (whole, ref) in enumerate(((up, up_ref), (down, down_ref)))
    ]
    ends = [
        pltpu.make_async_copy(
            stack.at[:, pl.ds(side * (rows - EDGE), EDGE), pl.ds(c * LANES, LANES)],
            ends_ref.at[c, :, pl.ds(side * EDGE, EDGE), :], ends_sem.at[side, c])
        for side in range(2) for c in range(cols // LANES)
    ]
    for copy in halos + ends:
        copy.start()
    for n in range(parts):
        pltpu.make_async_copy(brim.at[n], brim_ref.at[n], brim_sem.at[n]).start()
    middles = [
        pltpu.make_async_copy(inner[n], x_ref.at[n, :, :, pl.ds(EDGE, rows - 2 * EDGE), :], x_sem.at[n]) for n in range(parts)
    ]
    for copy in middles:
        copy.start()
    fill_columns(col_ref, taps)
    total = taps[0]
    for k in range(1, 2 * RADIUS + 1):
        total = total + taps[k]
    scale = 1.0 / jnp.full((dates, LANES), total, jnp.float32)
    flat = ends_ref.reshape(cols // LANES, dates * 2 * EDGE, LANES)

    def store(n):
        return [
            pltpu.make_async_copy(
                x_ref.at[n, :, :, pl.ds(side * (rows - EDGE), EDGE), :],
                outs[n].at[:, :, pl.ds(side * EDGE, EDGE), :], out_sem.at[n, side])
            for side in range(2)
        ]

    for copy in halos:
        copy.wait()

    mids, rims = [], []
    for n in range(parts):
        block = place[0] ^ order[n]
        start = pl.multiple_of(block * width, LANES)
        before = pl.multiple_of(jnp.maximum(start - LANES, 0), LANES)
        after = pl.multiple_of(jnp.minimum(start + width, cols - LANES), LANES)

        def both(first, span):
            at = pl.ds(first, span)
            return jnp.concatenate([up_ref[:, :, at], down_ref[:, :, at]], axis=0).reshape(2 * RADIUS * dates, span)

        mids.append(both(start, width))
        rims.append(rim_tile(both(before, LANES), both(after, LANES), block, parts))
    across = filter_columns(jnp.concatenate(mids, axis=0), jnp.concatenate(rims, axis=0), col_ref[...])
    span = 2 * RADIUS * dates
    for n in range(parts):
        for h in range(per):
            across_ref[n, h] = across[n * span:(n + 1) * span, h * LANES:(h + 1) * LANES]
    for copy in ends:
        copy.wait()

    def one(n, carry):
        block = place[0] ^ chosen(n, order)
        every = x_ref.at[n].reshape(per, dates * pitch, LANES)
        pltpu.make_async_copy(brim.at[n], brim_ref.at[n], brim_sem.at[n]).wait()

        def half(h, carry):
            for side in range(2):
                held = []
                for q in range(2 * RADIUS + EDGE):
                    halo = q < RADIUS if side == 0 else q >= RADIUS + EDGE
                    if halo:
                        at = q if side == 0 else q - EDGE
                        held.append(across_ref[n, h, at * dates:(at + 1) * dates, :])
                    else:
                        at = q - RADIUS if side == 0 else 3 * EDGE - RADIUS + q
                        held.append(jnp.concatenate([
                            brim_ref[n, h, (d * 4 * EDGE + at) * EDGE:(d * 4 * EDGE + at + 1) * EDGE, :]
                            for d in range(dates // EDGE)
                        ], axis=0))
                for r in range(EDGE):
                    low = taps[0] * held[r]
                    for j in range(1, 2 * RADIUS + 1):
                        low = low + taps[j] * held[r + j]
                    at = pl.ds(side * EDGE + r, dates, stride=2 * EDGE)
                    done = flat[block * per + h, at, :] - scale * low
                    every[h, pl.ds(side * (rows - EDGE) + r, dates, stride=pitch), :] = done
            return carry

        lax.fori_loop(0, per, half, 0)
        for m in range(parts):
            @pl.when(n == m)
            def _():
                for copy in store(m):
                    copy.start()
        return carry

    lax.fori_loop(0, parts, one, 0)

    lane = lax.broadcasted_iota(jnp.int32, (dates, LANES), 1)
    both = [jnp.concatenate([ref[n:n + 1, :] for ref in vectors], axis=1) for n in range(1, 4)]
    index = lax.broadcasted_iota(jnp.int32, both[0].shape, 1)
    source = (index // feet) ^ place[0]
    named = lax.broadcasted_iota(jnp.int32, (owners, index.shape[1]), 0) == both[1]
    places = []
    for block in range(parts):
        for slot in range(PAIR_CAP):
            hit = named & (source == block) & (both[2] == slot)
            places.append(jnp.where(hit, 1.0, 0.0).astype(jnp.bfloat16))
    places = jnp.concatenate(places, axis=0)
    pixel_rows = x_ref.reshape(parts * per * dates * pitch, LANES)
    for copy in middles:
        copy.wait()
    for k in range(parts):
        base = order.index(k) * per * dates * pitch

        def take(f, carry):
            pixels = pixel_rows[pl.ds(base + meta[k][0, f], dates, stride=pitch), :]
            v_ref[k * feet + f] = jnp.where(lane < meta[k][1, f], pixels, 0.0)
            return carry

        lax.fori_loop(0, feet, take, 0, unroll=8)
    tiles = []
    for first in range(0, parts * feet, LANES):

        def add(f, total):
            one = jnp.sum(v_ref[first + f], axis=1, keepdims=True)
            return jnp.where(lane == f, one, total)

        tiles.append(lax.fori_loop(0, LANES, add, jnp.zeros((dates, LANES), jnp.float32), unroll=32))
    counts = jnp.broadcast_to(both[0].astype(jnp.float32), (dates, index.shape[1]))
    sums = jnp.concatenate([jnp.concatenate(tiles, axis=1), counts], axis=0)
    held = jnp.zeros((places.shape[0], 2 * dates), jnp.float32)
    for piece in split(sums, 3):
        held = held + lax.dot_general(places, piece, (((1,), (1,)), ((), ())), preferred_element_type=jnp.float32)
    for n in range(parts * PAIR_CAP):
        at = pl.ds(n * dates, dates)
        sums_ref[:, 0, at] = held[n * owners:(n + 1) * owners, :dates]
        sums_ref[:, 1, at] = held[n * owners:(n + 1) * owners, dates:]
    for m in range(parts):
        for copy in store(m):
            copy.wait()


def edges(stack, up, down, brim, inner, meta, taps, place, order, owners):
    parts = len(order)
    dates, rows, cols = stack.shape
    tiles = cols // LANES
    per = tiles // parts
    feet = meta[0].shape[1]
    here = pl.BlockSpec(memory_space=pltpu.HBM)
    resident = pl.BlockSpec(memory_space=pltpu.VMEM)
    return pl.pallas_call(
        functools.partial(edge_kernel, order, feet),
        grid_spec=pltpu.PrefetchScalarGridSpec(
            num_scalar_prefetch=2 + parts,
            grid=(),
            in_specs=[resident] * parts + [here] * (4 + parts),
            out_specs=[here] * parts + [resident],
            scratch_shapes=[
                pltpu.VMEM((parts, per, 2 * RADIUS * dates, LANES), jnp.float32),
                pltpu.VMEM((parts, per, 4 * EDGE * dates, LANES), jnp.float32),
                pltpu.VMEM(up.shape, jnp.float32),
                pltpu.VMEM(up.shape, jnp.float32),
                pltpu.VMEM((tiles, dates, 2 * EDGE, LANES), jnp.float32),
                pltpu.VMEM((9 * LANES, per * LANES), jnp.bfloat16),
                pltpu.VMEM((parts, per, dates, rows + EDGE, LANES), jnp.float32),
                pltpu.VMEM((parts * feet, dates, LANES), jnp.float32),
                pltpu.SemaphoreType.DMA((2,)),
                pltpu.SemaphoreType.DMA((2, tiles)),
                pltpu.SemaphoreType.DMA((parts,)),
                pltpu.SemaphoreType.DMA((parts, 2)),
                pltpu.SemaphoreType.DMA((parts,)),
            ],
        ),
        out_shape=[jax.ShapeDtypeStruct((per, dates, 2 * EDGE, LANES), jnp.float32)] * parts
        + [jax.ShapeDtypeStruct((owners, 2, parts * PAIR_CAP * dates), jnp.float32)],
        compiler_params=params(63.75),
        cost_estimate=cost(2),
    )(place, taps, *meta, *meta, stack, up, down, brim, *inner)


def temporal_kernel(parts, strips, first_tile, tile_step, place, taps, *rest):
    pieces, rest = rest[:parts], rest[parts:]
    if strips:
        _, got_ref, out, anomaly, series, anomaly_ref, series_ref, owner_sem, *rest = rest
    else:
        out, *rest = rest
    z_ref, f_ref, out_ref, in_sem, out_sem = rest
    count, total, _, _ = out_ref.shape
    per = pieces[0].shape[0]
    local = total // parts
    pad = REACH * DILATION
    step = 8

    def load(n):
        rows = pl.ds(pl.multiple_of(n * EDGE, EDGE), EDGE)
        return [
            pltpu.make_async_copy(
                pieces[k].at[:, :, rows, :],
                z_ref.at[n, :, pl.ds(REACH + (place[0] ^ k) * local, local)], in_sem.at[n, k])
            for k in range(parts)
        ]

    def store(n):
        tile = first_tile + n * tile_step
        rows = pl.ds(pl.multiple_of(tile * EDGE, EDGE), EDGE)
        return pltpu.make_async_copy(out_ref.at[n], out.at[:, rows, :], out_sem.at[n])

    for n in range(count):
        for copy in load(n):
            copy.start()
    owner_copies = []
    if strips:
        series_ref[...], anomaly_ref[0] = owner_values(parts, strips, taps, got_ref)
        owner_copies = [
            pltpu.make_async_copy(series_ref, series, owner_sem.at[0]),
            pltpu.make_async_copy(anomaly_ref, anomaly, owner_sem.at[1]),
        ]
        for copy in owner_copies:
            copy.start()
    none = jnp.zeros((REACH, EDGE, LANES), jnp.float32)
    wide = jnp.zeros((pad, EDGE, LANES), jnp.float32)
    for h in range(per):
        for n in range(count):
            z_ref[n, h, 0:REACH] = none
            z_ref[n, h, REACH + total:REACH + total + REACH] = none
        f_ref[h, 0:pad] = wide
        f_ref[h, pad + total:pad + total + pad] = wide
    own = 1.0 - taps[0, REACH]
    own_wide = 1.0 - taps[1, REACH]
    others = [k for k in range(2 * REACH + 1) if k != REACH]

    def one(n, carry):
        for copy in load(n):
            copy.wait()
        for h in range(per):
            for t in range(0, total, step):
                z = z_ref[n, h, t:t + step + 2 * REACH]
                kept = own * z[REACH:REACH + step]
                for k in others:
                    kept = kept - taps[0, k] * z[k:k + step]
                f_ref[h, pad + t:pad + t + step] = kept
            for t in range(0, total, step):
                kept = own_wide * f_ref[h, pad + t:pad + t + step]
                for k in others:
                    kept = kept - taps[1, k] * f_ref[h, t + k * DILATION:t + k * DILATION + step]
                out_ref[n, t:t + step, :, h * LANES:(h + 1) * LANES] = kept
        store(n).start()
        return carry

    lax.fori_loop(0, count, one, 0)
    for n in range(count):
        store(n).wait()
    for copy in owner_copies:
        copy.wait()


def temporal(pieces, taps, place, first_tile, tile_step, rows, base=None, got=None, strips=0):
    parts = len(pieces)
    per, local, here, _ = pieces[0].shape
    total = local * parts
    count = here // EDGE
    width = per * LANES
    anywhere = pl.BlockSpec(memory_space=pl.ANY)
    whole = pl.BlockSpec(memory_space=pltpu.HBM)
    in_specs, out_specs, scratch = [anywhere] * parts, [whole], []
    out_shape = [jax.ShapeDtypeStruct((total, rows, width), jnp.float32)]
    extra = []
    if strips:
        extra = [base, got]
        in_specs += [anywhere, pl.BlockSpec(memory_space=pltpu.VMEM)]
        out_specs += [whole] * 2
        shapes = [(1, parts * strips * PAIR_CAP, total), (1, total)]
        out_shape += [jax.ShapeDtypeStruct(shape, jnp.float32) for shape in shapes]
        scratch = [pltpu.VMEM(shape, jnp.float32) for shape in shapes] + [pltpu.SemaphoreType.DMA((2,))]
    return pl.pallas_call(
        functools.partial(temporal_kernel, parts, strips, first_tile, tile_step),
        grid_spec=pltpu.PrefetchScalarGridSpec(
            num_scalar_prefetch=2,
            grid=(),
            in_specs=in_specs,
            out_specs=out_specs,
            scratch_shapes=scratch + [
                pltpu.VMEM((count, per, total + 2 * REACH, EDGE, LANES), jnp.float32),
                pltpu.VMEM((per, total + 2 * REACH * DILATION, EDGE, LANES), jnp.float32),
                pltpu.VMEM((count, total, EDGE, width), jnp.float32),
                pltpu.SemaphoreType.DMA((count, parts)),
                pltpu.SemaphoreType.DMA((count,)),
            ],
        ),
        out_shape=out_shape,
        input_output_aliases={2 + parts: 0} if strips else {},
        compiler_params=params(24),
        cost_estimate=cost(0),
    )(place, taps, *pieces, *extra)


def owner_values(parts, strips, taps, got_ref):
    owners = parts * strips
    slots = owners * PAIR_CAP
    dates = got_ref.shape[2] // PAIR_CAP
    local = dates // parts
    sums, held = got_ref[:, 0, :], got_ref[:, 1, :]
    rows, weights = [], []
    for block in range(parts):
        for slot in range(PAIR_CAP):
            at = (block * PAIR_CAP + slot) * local
            rows.append(jnp.concatenate(
                [sums[e * strips:(e + 1) * strips, at:at + local] for e in range(parts)], axis=1))
            weights.append(held[0:strips, at:at + 1])
    sums = jnp.concatenate(rows, axis=0)
    weight = jnp.concatenate(weights, axis=0)
    shape = (dates, dates)
    lag = lax.broadcasted_iota(jnp.int32, shape, 0) - lax.broadcasted_iota(jnp.int32, shape, 1)
    for level, spacing in ((0, 1), (1, DILATION)):
        filt = jnp.where(lag == 0, 1.0, 0.0)
        for k in range(2 * REACH + 1):
            filt = filt - jnp.where(lag == (k - REACH) * spacing, taps[level, k], 0.0)
        sums = jnp.dot(sums, filt, precision=HIGHEST, preferred_element_type=jnp.float32)
    mean = sums / jnp.where(weight > 0, weight, 1.0)
    asset = jnp.sum(weight * mean, axis=0, keepdims=True) / jnp.sum(weight, axis=0, keepdims=True)
    odd = jnp.where(weight > 0, mean - asset, 0.0)
    shape = (slots, slots)
    to = lax.broadcasted_iota(jnp.int32, shape, 0)
    source = lax.broadcasted_iota(jnp.int32, shape, 1)
    block, rest = source // (PAIR_CAP * strips), source % (PAIR_CAP * strips)
    place_of = block * (PAIR_CAP * strips) + (rest % strips) * PAIR_CAP + rest // strips
    order = jnp.where(to == place_of, 1.0, 0.0)
    return asset, jnp.dot(order, odd, precision=HIGHEST, preferred_element_type=jnp.float32)


def spread_meta(meta, offset, swap):
    known = sorted(meta)
    got = swap(jnp.concatenate([meta[k] for k in known], axis=1), offset)
    width = meta[0].shape[1]
    return meta | {k ^ offset: got[:, n * width:(n + 1) * width] for n, k in enumerate(known)}


def shards(stack, spatial_taps, temporal_taps, foot_tile, foot_row, foot_count, foot_owner):
    parts, strips = lax.axis_size("date"), lax.axis_size("strip")
    place = lax.axis_index("date").astype(jnp.int32)[None]
    dates, rows, cols = stack.shape
    feet = foot_row.shape[0]
    owner = foot_owner[:, 0]
    position = jnp.arange(feet, dtype=jnp.int32)
    earlier = (owner[:, None] == owner[None, :]) & (position[None, :] < position[:, None])
    slot = jnp.sum(earlier.astype(jnp.int32), axis=1)
    own = jnp.stack([foot_tile * (dates * (rows + EDGE)) + foot_row, foot_count, owner, slot])

    def swap(value, offset):
        return lax.ppermute(value, "date", [(i, i ^ offset) for i in range(parts)])

    order = (*range(2, parts), 1, 0)
    inner, far_inner = {}, {}
    lead = order[0]
    inner[lead], brim = interior(stack, None, spatial_taps, place, (lead,), 0, parts)
    far_inner[lead] = swap(inner[lead], lead)
    later, brim = lax.optimization_barrier((place, brim))
    last_rows, first_rows = halo_rows(stack, later)
    up = lax.ppermute(last_rows, "strip", [(i, i + 1) for i in range(strips - 1)])
    down = lax.ppermute(first_rows, "strip", [(i + 1, i) for i in range(strips - 1)])
    own, brim = lax.optimization_barrier((own, brim))
    meta = {0: own}
    for bit in range(parts.bit_length() - 2, 0, -1):
        meta = spread_meta(meta, 1 << bit, swap)
    *made, brim = interior(stack, brim, spatial_taps, place, order[1:], 1, parts)
    for n, offset in enumerate(order[1:]):
        inner[offset] = made[n]
        if offset > 1:
            far_inner[offset] = swap(inner[offset], offset)
    known = sorted(meta)
    *held, far_inner[lead], brim = lax.optimization_barrier((*[meta[k] for k in known], far_inner[lead], brim))
    meta = spread_meta(dict(zip(known, held)), 1, swap)
    meta = [meta[k] for k in range(parts)]
    *made, sums = edges(
        stack, up, down, brim, [inner[k] for k in order], meta, spatial_taps, place, order, parts * strips)
    rim = dict(zip(order, made))
    far_inner[1] = swap(inner[1], 1)
    got = lax.all_to_all(sums, ("date", "strip"), split_axis=0, concat_axis=0, tiled=True)
    far_rim = {k: swap(rim[k], k) for k in order[:-1]}
    last = rows // EDGE - 1
    residual, = temporal(
        [inner[0]] + [far_inner[k] for k in range(1, parts)], temporal_taps, place, 1, 1, rows)
    got, residual = lax.optimization_barrier((got, residual))
    return temporal(
        [rim[0]] + [far_rim[k] for k in range(1, parts)], temporal_taps, place, 0, last, rows, residual, got, strips)


def solution(mesh):
    placed = (
        P("date", "strip", None),
        P(),
        P(),
        P(("date", "strip")),
        P(("date", "strip")),
        P(("date", "strip")),
        P(("date", "strip"), None),
    )
    return jax.shard_map(
        shards,
        mesh=mesh,
        in_specs=placed,
        out_specs=(
            P(None, "strip", "date"),
            P(("date", "strip"), None, None),
            P(("date", "strip"), None),
        ),
        check_vma=False,
    )
```

```python
import functools

import jax
import jax.numpy as jnp
from jax import lax
from jax.experimental import pallas as pl
from jax.experimental.pallas import tpu as pltpu
from jax.sharding import PartitionSpec as P

TILE = 128
RADIUS = 6
REACH = 2
DILATION = 8
PAIR_CAP = 2
LANES = 128
EDGE = 8
HIGHEST = lax.Precision.HIGHEST


def params(mebibytes):
    return pltpu.CompilerParams(vmem_limit_bytes=mebibytes * 1024 * 1024)


def cost(micros):
    return pl.CostEstimate(flops=0, bytes_accessed=int(micros * 3.69e6), transcendentals=0)


def pick_taps(at, taps):
    count = taps.shape[0]
    total = taps[0]
    for k in range(1, count):
        total = total + taps[k]
    out = jnp.zeros(at.shape, jnp.float32)
    for k in range(count):
        out = jnp.where(at == k, taps[k], out)
    return out / jnp.full(at.shape, total, jnp.float32)


def split(value, count):
    out = []
    for _ in range(count):
        piece = value.astype(jnp.bfloat16)
        out.append(piece)
        value = value - piece.astype(jnp.float32)
    return out


def spread(value, axis):
    high, mid = split(value, 2)
    return jnp.concatenate([high, high, high, mid], axis=axis)


def fill_columns(col_ref, taps):
    shape = (LANES, LANES)
    lag = lax.broadcasted_iota(jnp.int32, shape, 0) - lax.broadcasted_iota(jnp.int32, shape, 1)
    near = split(pick_taps(lag + RADIUS, taps), 3)
    far = pick_taps(jnp.where(lag > 0, lag + RADIUS - LANES, lag + RADIUS + LANES), taps)
    above = split(jnp.where(lag > 0, far, 0.0), 3)
    below = split(jnp.where(lag > 0, 0.0, far), 3)
    for n, piece in enumerate((0, 1, 2, 0)):
        at = n * 3 * LANES
        for i, pair in enumerate(((near, above), (below, near), (above, below))):
            for j, block in enumerate(pair):
                col_ref[at + i * LANES:at + (i + 1) * LANES, j * LANES:(j + 1) * LANES] = block[piece]


def row_band(out_rows, in_rows, taps):
    shape = (out_rows, 4 * in_rows)
    lane = lax.broadcasted_iota(jnp.int32, shape, 1)
    row = lax.broadcasted_iota(jnp.int32, shape, 0)
    part = jnp.zeros(shape, jnp.int32)
    for n in range(1, 4):
        part = jnp.where(lane >= n * in_rows, n, part)
    return lane - part * in_rows, row, part


def pieces_of(values, part):
    high, mid, low = [p.astype(jnp.float32) for p in split(values, 3)]
    return jnp.where(part == 1, mid, jnp.where(part == 2, low, high)).astype(jnp.bfloat16)


def filter_columns(mid, rim, col):
    rows = mid.shape[0]
    window = jnp.concatenate([mid, rim], axis=1)
    return jnp.dot(spread(window, 1), col, preferred_element_type=jnp.float32)


def rim_tile(left, right, block, parts):
    lane = lax.broadcasted_iota(jnp.int32, left.shape, len(left.shape) - 1)
    first = lane < LANES // 2
    keep = (first & (block < parts - 1)) | (~first & (block > 0))
    return jnp.where(keep, jnp.where(first, right, left), 0.0)


def chosen(n, values):
    out = values[0]
    for m in range(1, len(values)):
        out = jnp.where(n == m, values[m], out)
    return out


def interior_kernel(offsets, slot, parts, group, place, taps, stack, *rest):
    count = len(offsets)
    first = slot == 0
    if not first:
        rest = rest[1:]
    outs, brim, rest = rest[:count], rest[count], rest[count + 1:]
    if first:
        up, down, ends, mid_ref, left_ref, right_ref, halo_ref, up_ref, down_ref, halo_sem, halo_out_sem, *rest = rest
    else:
        x_ref, *rest = rest
    out_ref, brim_ref, col_ref, row_ref, in_sem, out_sem, brim_sem = rest
    _, per, dates, inner, _ = out_ref.shape
    width = per * LANES
    rows = inner + 2 * EDGE
    cols = width * parts
    steps = dates // group

    def bounds(block):
        start = block * width
        places = start, jnp.maximum(start - LANES, 0), jnp.minimum(start + width, cols - LANES)
        return [pl.multiple_of(at, LANES) for at in places]

    def load(g):
        at = pl.ds(g * group, group)
        if not first:
            return [pltpu.make_async_copy(stack.at[at], x_ref.at[at], in_sem.at[0, g])]
        return [
            pltpu.make_async_copy(stack.at[at, :, pl.ds(start, ref.shape[2])], ref.at[at], in_sem.at[n, g])
            for n, (start, ref) in enumerate(zip(bounds(place[0] ^ offsets[0]), (mid_ref, left_ref, right_ref)))
        ]

    def store(m, g):
        at = pl.ds(g * group, group)
        return pltpu.make_async_copy(out_ref.at[m, :, at], outs[m].at[:, at], out_sem.at[m, g])

    def store_brim(n):
        return pltpu.make_async_copy(brim_ref.at[n], brim.at[slot + n], brim_sem.at[n])

    for g in range(steps):
        for copy in load(g):
            copy.start()
    halo_loads, halo_stores = [], []
    if first:
        halo_loads = [
            pltpu.make_async_copy(
                stack.at[:, pl.ds(side * (rows - EDGE), EDGE), pl.ds(c * LANES, LANES)],
                halo_ref.at[c, :, pl.ds(side * EDGE, EDGE), :], halo_sem.at[side, c])
            for side in range(2) for c in range(cols // LANES)
        ]
        halo_stores = [
            pltpu.make_async_copy(halo_ref, ends, halo_out_sem.at[0]),
            pltpu.make_async_copy(up_ref, up, halo_out_sem.at[1]),
            pltpu.make_async_copy(down_ref, down, halo_out_sem.at[2]),
        ]
        for copy in halo_loads:
            copy.start()
    fill_columns(col_ref, taps)
    q, r, part = row_band(inner, rows, taps)
    row_ref[...] = pieces_of(pick_taps(q - r - (EDGE - RADIUS), taps), part)

    def pack(c, carry):
        at = pl.ds(pl.multiple_of(c * LANES, LANES), LANES)
        rows_of = halo_ref.at[c].reshape(dates * 2 * EDGE, LANES)
        for r in range(RADIUS):
            up_ref[r, :, at] = rows_of[pl.ds(2 * EDGE - RADIUS + r, dates, stride=2 * EDGE), :]
            down_ref[r, :, at] = rows_of[pl.ds(r, dates, stride=2 * EDGE), :]
        return carry

    def step(i, carry):
        n, g = i // steps, i % steps
        block = place[0] ^ chosen(n, offsets)
        at = pl.ds(g * group, group)

        @pl.when(n == 0)
        def _():
            for copy in load(g):
                copy.wait()

        if first:
            @pl.when(i == steps - 1)
            def _():
                for copy in halo_loads:
                    copy.wait()
                lax.fori_loop(0, cols // LANES, pack, 0)
                for copy in halo_stores:
                    copy.start()

            mid, left, right = mid_ref[at], left_ref[at], right_ref[at]
        else:
            start, before, after = bounds(block)
            mid, left, right = [x_ref[at, :, pl.ds(f, w)] for f, w in ((start, width), (before, LANES), (after, LANES))]
        rim = rim_tile(left, right, block, parts)
        across = filter_columns(mid.reshape(group * rows, width), rim.reshape(group * rows, LANES), col_ref[...])
        for t in range(group):
            one = across[t * rows:(t + 1) * rows]
            low = jnp.dot(row_ref[...], spread(one, 0), preferred_element_type=jnp.float32)
            done = mid[t, EDGE:rows - EDGE, :] - low
            for h in range(per):
                out_ref[n, h, g * group + t] = done[:, h * LANES:(h + 1) * LANES]
                for side in range(2):
                    lines = one[side * (rows - 2 * EDGE):side * (rows - 2 * EDGE) + 2 * EDGE, h * LANES:(h + 1) * LANES]
                    date = g * group + t
                    at = ((date // EDGE) * 4 * EDGE + side * 2 * EDGE) * EDGE + date % EDGE
                    brim_ref[n, h, pl.ds(at, 2 * EDGE, stride=EDGE), :] = lines
        for m in range(count):
            @pl.when(n == m)
            def _():
                store(m, g).start()

        @pl.when(g == steps - 1)
        def _():
            store_brim(n).start()

        return carry

    lax.fori_loop(0, count * steps, step, 0)
    for copy in halo_stores:
        copy.wait()
    for m in range(count):
        for g in range(steps):
            store(m, g).wait()
        store_brim(m).wait()


def interior(stack, brim, taps, place, offsets, slot, parts):
    dates, rows, cols = stack.shape
    width = cols // parts
    per = width // LANES
    group = min(8, dates)
    inner = rows - 2 * EDGE
    count = len(offsets)
    first = slot == 0
    here = pl.BlockSpec(memory_space=pltpu.HBM)
    out_shape = [jax.ShapeDtypeStruct((per, dates, inner, LANES), jnp.float32)] * count
    out_shape += [jax.ShapeDtypeStruct((parts, per, 4 * EDGE * dates, LANES), jnp.float32)]
    if first:
        out_shape += [jax.ShapeDtypeStruct((RADIUS, dates, cols), jnp.float32)] * 2
        out_shape += [jax.ShapeDtypeStruct((cols // LANES, dates, 2 * EDGE, LANES), jnp.float32)]
        scratch = [pltpu.VMEM((dates, rows, span), jnp.float32) for span in (width, LANES, LANES)] + [
            pltpu.VMEM((cols // LANES, dates, 2 * EDGE, LANES), jnp.float32),
            pltpu.VMEM((RADIUS, dates, cols), jnp.float32),
            pltpu.VMEM((RADIUS, dates, cols), jnp.float32),
            pltpu.SemaphoreType.DMA((2, cols // LANES)),
            pltpu.SemaphoreType.DMA((3,)),
        ]
    else:
        scratch = [pltpu.VMEM((dates, rows, cols), jnp.float32)]
    return pl.pallas_call(
        functools.partial(interior_kernel, offsets, slot, parts, group),
        grid_spec=pltpu.PrefetchScalarGridSpec(
            num_scalar_prefetch=2,
            grid=(),
            in_specs=[here] * (1 if first else 2),
            out_specs=[here] * len(out_shape),
            scratch_shapes=scratch + [
                pltpu.VMEM((count, per, dates, inner, LANES), jnp.float32),
                pltpu.VMEM((count, per, 4 * EDGE * dates, LANES), jnp.float32),
                pltpu.VMEM((12 * LANES, width), jnp.bfloat16),
                pltpu.VMEM((inner, 4 * rows), jnp.bfloat16),
                pltpu.SemaphoreType.DMA((3, dates // group)),
                pltpu.SemaphoreType.DMA((count, dates // group)),
                pltpu.SemaphoreType.DMA((count,)),
            ],
        ),
        out_shape=out_shape,
        input_output_aliases={} if first else {3: count},
        compiler_params=params(63),
        cost_estimate=cost(2.5 + 2.5 * count),
    )(place, taps, stack, *([] if first else [brim]))


def edge_kernel(order, feet, place, taps, *rest):
    parts = len(order)
    meta, vectors, rest = rest[:parts], rest[parts:2 * parts], rest[2 * parts:]
    ends, up, down, brim, *rest = rest
    inner, outs, rest = rest[:parts], rest[parts:2 * parts], rest[2 * parts:]
    sums_ref, across_ref, brim_ref, up_ref, down_ref, ends_ref, col_ref, x_ref, v_ref = rest[:9]
    halo_sem, brim_sem, out_sem, x_sem = rest[9:]
    _, dates, cols = up_ref.shape
    width = cols // parts
    per = width // LANES
    pitch = x_ref.shape[3]
    rows = pitch - EDGE
    owners = sums_ref.shape[0]
    halos = [
        pltpu.make_async_copy(whole, ref, halo_sem.at[n])
        for n, (whole, ref) in enumerate(((up, up_ref), (down, down_ref), (ends, ends_ref)))
    ]
    for copy in halos:
        copy.start()
    for n in range(parts):
        pltpu.make_async_copy(brim.at[n], brim_ref.at[n], brim_sem.at[n]).start()
    middles = [
        pltpu.make_async_copy(inner[n], x_ref.at[n, :, :, pl.ds(EDGE, rows - 2 * EDGE), :], x_sem.at[n]) for n in range(parts)
    ]
    for copy in middles:
        copy.start()
    fill_columns(col_ref, taps)
    total = taps[0]
    for k in range(1, 2 * RADIUS + 1):
        total = total + taps[k]
    scale = 1.0 / jnp.full((dates, LANES), total, jnp.float32)
    flat = ends_ref.reshape(cols // LANES, dates * 2 * EDGE, LANES)

    def store(n):
        return [
            pltpu.make_async_copy(
                x_ref.at[n, :, :, pl.ds(side * (rows - EDGE), EDGE), :],
                outs[n].at[:, :, pl.ds(side * EDGE, EDGE), :], out_sem.at[n, side])
            for side in range(2)
        ]

    for copy in halos:
        copy.wait()

    mids, rims = [], []
    for n in range(parts):
        block = place[0] ^ order[n]
        start = pl.multiple_of(block * width, LANES)
        before = pl.multiple_of(jnp.maximum(start - LANES, 0), LANES)
        after = pl.multiple_of(jnp.minimum(start + width, cols - LANES), LANES)

        def both(first, span):
            at = pl.ds(first, span)
            return jnp.concatenate([up_ref[:, :, at], down_ref[:, :, at]], axis=0).reshape(2 * RADIUS * dates, span)

        mids.append(both(start, width))
        rims.append(rim_tile(both(before, LANES), both(after, LANES), block, parts))
    across = filter_columns(jnp.concatenate(mids, axis=0), jnp.concatenate(rims, axis=0), col_ref[...])
    span = 2 * RADIUS * dates
    for n in range(parts):
        for h in range(per):
            across_ref[n, h] = across[n * span:(n + 1) * span, h * LANES:(h + 1) * LANES]

    def one(n, carry):
        block = place[0] ^ chosen(n, order)
        every = x_ref.at[n].reshape(per, dates * pitch, LANES)
        pltpu.make_async_copy(brim.at[n], brim_ref.at[n], brim_sem.at[n]).wait()

        def half(h, carry):
            for side in range(2):
                held = []
                for q in range(2 * RADIUS + EDGE):
                    halo = q < RADIUS if side == 0 else q >= RADIUS + EDGE
                    if halo:
                        at = q if side == 0 else q - EDGE
                        held.append(across_ref[n, h, at * dates:(at + 1) * dates, :])
                    else:
                        at = q - RADIUS if side == 0 else 3 * EDGE - RADIUS + q
                        held.append(jnp.concatenate([
                            brim_ref[n, h, (d * 4 * EDGE + at) * EDGE:(d * 4 * EDGE + at + 1) * EDGE, :]
                            for d in range(dates // EDGE)
                        ], axis=0))
                for r in range(EDGE):
                    low = taps[0] * held[r]
                    for j in range(1, 2 * RADIUS + 1):
                        low = low + taps[j] * held[r + j]
                    at = pl.ds(side * EDGE + r, dates, stride=2 * EDGE)
                    done = flat[block * per + h, at, :] - scale * low
                    every[h, pl.ds(side * (rows - EDGE) + r, dates, stride=pitch), :] = done
            return carry

        lax.fori_loop(0, per, half, 0)
        for m in range(parts):
            @pl.when(n == m)
            def _():
                for copy in store(m):
                    copy.start()
        return carry

    lax.fori_loop(0, parts, one, 0)

    lane = lax.broadcasted_iota(jnp.int32, (dates, LANES), 1)
    both = [jnp.concatenate([ref[n:n + 1, :] for ref in vectors], axis=1) for n in range(1, 4)]
    index = lax.broadcasted_iota(jnp.int32, both[0].shape, 1)
    source = (index // feet) ^ place[0]
    named = lax.broadcasted_iota(jnp.int32, (owners, index.shape[1]), 0) == both[1]
    places = []
    for block in range(parts):
        for slot in range(PAIR_CAP):
            hit = named & (source == block) & (both[2] == slot)
            places.append(jnp.where(hit, 1.0, 0.0).astype(jnp.bfloat16))
    places = jnp.concatenate(places, axis=0)
    pixel_rows = x_ref.reshape(parts * per * dates * pitch, LANES)
    for copy in middles:
        copy.wait()
    for k in range(parts):
        base = order.index(k) * per * dates * pitch

        def take(f, carry):
            pixels = pixel_rows[pl.ds(base + meta[k][0, f], dates, stride=pitch), :]
            v_ref[k * feet + f] = jnp.where(lane < meta[k][1, f], pixels, 0.0)
            return carry

        lax.fori_loop(0, feet, take, 0, unroll=8)
    tiles = []
    for first in range(0, parts * feet, LANES):

        def add(f, total):
            one = jnp.sum(v_ref[first + f], axis=1, keepdims=True)
            return jnp.where(lane == f, one, total)

        tiles.append(lax.fori_loop(0, LANES, add, jnp.zeros((dates, LANES), jnp.float32), unroll=32))
    counts = jnp.broadcast_to(both[0].astype(jnp.float32), (dates, index.shape[1]))
    sums = jnp.concatenate([jnp.concatenate(tiles, axis=1), counts], axis=0)
    held = jnp.zeros((places.shape[0], 2 * dates), jnp.float32)
    for piece in split(sums, 3):
        held = held + lax.dot_general(places, piece, (((1,), (1,)), ((), ())), preferred_element_type=jnp.float32)
    for n in range(parts * PAIR_CAP):
        at = pl.ds(n * dates, dates)
        sums_ref[:, 0, at] = held[n * owners:(n + 1) * owners, :dates]
        sums_ref[:, 1, at] = held[n * owners:(n + 1) * owners, dates:]
    for m in range(parts):
        for copy in store(m):
            copy.wait()


def edges(ends, up, down, brim, inner, meta, taps, place, order, owners):
    parts = len(order)
    tiles, dates, _, _ = ends.shape
    per = tiles // parts
    feet = meta[0].shape[1]
    rows = inner[0].shape[2] + 2 * EDGE
    here = pl.BlockSpec(memory_space=pltpu.HBM)
    resident = pl.BlockSpec(memory_space=pltpu.VMEM)
    return pl.pallas_call(
        functools.partial(edge_kernel, order, feet),
        grid_spec=pltpu.PrefetchScalarGridSpec(
            num_scalar_prefetch=2 + parts,
            grid=(),
            in_specs=[resident] * parts + [here] * (4 + parts),
            out_specs=[here] * parts + [resident],
            scratch_shapes=[
                pltpu.VMEM((parts, per, 2 * RADIUS * dates, LANES), jnp.float32),
                pltpu.VMEM((parts, per, 4 * EDGE * dates, LANES), jnp.float32),
                pltpu.VMEM(up.shape, jnp.float32),
                pltpu.VMEM(up.shape, jnp.float32),
                pltpu.VMEM(ends.shape, jnp.float32),
                pltpu.VMEM((12 * LANES, per * LANES), jnp.bfloat16),
                pltpu.VMEM((parts, per, dates, rows + EDGE, LANES), jnp.float32),
                pltpu.VMEM((parts * feet, dates, LANES), jnp.float32),
                pltpu.SemaphoreType.DMA((3,)),
                pltpu.SemaphoreType.DMA((parts,)),
                pltpu.SemaphoreType.DMA((parts, 2)),
                pltpu.SemaphoreType.DMA((parts,)),
            ],
        ),
        out_shape=[jax.ShapeDtypeStruct((per, dates, 2 * EDGE, LANES), jnp.float32)] * parts
        + [jax.ShapeDtypeStruct((owners, 2, parts * PAIR_CAP * dates), jnp.float32)],
        compiler_params=params(63),
        cost_estimate=cost(8),
    )(place, taps, *meta, *meta, ends, up, down, brim, *inner)


def temporal_kernel(parts, strips, first_tile, tile_step, place, taps, *rest):
    pieces, rest = rest[:parts], rest[parts:]
    if strips:
        _, got_ref, out, anomaly, series, anomaly_ref, series_ref, owner_sem, *rest = rest
    else:
        out, *rest = rest
    z_ref, f_ref, out_ref, in_sem, out_sem = rest
    count, total, _, _ = out_ref.shape
    per = pieces[0].shape[0]
    local = total // parts
    pad = REACH * DILATION
    step = 8

    def load(n):
        rows = pl.ds(pl.multiple_of(n * EDGE, EDGE), EDGE)
        return [
            pltpu.make_async_copy(
                pieces[k].at[:, :, rows, :],
                z_ref.at[n, :, pl.ds(REACH + (place[0] ^ k) * local, local)], in_sem.at[n, k])
            for k in range(parts)
        ]

    def store(n, h):
        tile = first_tile + n * tile_step
        rows = pl.ds(pl.multiple_of(tile * EDGE, EDGE), EDGE)
        lanes = pl.ds(h * LANES, LANES)
        return pltpu.make_async_copy(out_ref.at[n, :, :, lanes], out.at[:, rows, lanes], out_sem.at[n, h])

    for n in range(count):
        for copy in load(n):
            copy.start()
    owner_copies = []
    if strips:
        series_ref[...], anomaly_ref[0] = owner_values(parts, strips, taps, got_ref)
        owner_copies = [
            pltpu.make_async_copy(series_ref, series, owner_sem.at[0]),
            pltpu.make_async_copy(anomaly_ref, anomaly, owner_sem.at[1]),
        ]
        for copy in owner_copies:
            copy.start()
    none = jnp.zeros((REACH, EDGE, LANES), jnp.float32)
    wide = jnp.zeros((pad, EDGE, LANES), jnp.float32)
    for h in range(per):
        for n in range(count):
            z_ref[n, h, 0:REACH] = none
            z_ref[n, h, REACH + total:REACH + total + REACH] = none
        f_ref[h, 0:pad] = wide
        f_ref[h, pad + total:pad + total + pad] = wide
    own = 1.0 - taps[0, REACH]
    own_wide = 1.0 - taps[1, REACH]
    others = [k for k in range(2 * REACH + 1) if k != REACH]

    def one(n, carry):
        for copy in load(n):
            copy.wait()
        for h in range(per):
            for t in range(0, total, step):
                z = z_ref[n, h, t:t + step + 2 * REACH]
                kept = own * z[REACH:REACH + step]
                for k in others:
                    kept = kept - taps[0, k] * z[k:k + step]
                f_ref[h, pad + t:pad + t + step] = kept
            for t in range(0, total, step):
                kept = own_wide * f_ref[h, pad + t:pad + t + step]
                for k in others:
                    kept = kept - taps[1, k] * f_ref[h, t + k * DILATION:t + k * DILATION + step]
                out_ref[n, t:t + step, :, h * LANES:(h + 1) * LANES] = kept
            store(n, h).start()
        return carry

    lax.fori_loop(0, count, one, 0)
    for n in range(count):
        for h in range(per):
            store(n, h).wait()
    for copy in owner_copies:
        copy.wait()


def temporal(pieces, taps, place, first_tile, tile_step, rows, base=None, got=None, strips=0):
    parts = len(pieces)
    per, local, here, _ = pieces[0].shape
    total = local * parts
    count = here // EDGE
    width = per * LANES
    anywhere = pl.BlockSpec(memory_space=pl.ANY)
    whole = pl.BlockSpec(memory_space=pltpu.HBM)
    in_specs, out_specs, scratch = [anywhere] * parts, [whole], []
    out_shape = [jax.ShapeDtypeStruct((total, rows, width), jnp.float32)]
    extra = []
    if strips:
        extra = [base, got]
        in_specs += [anywhere, pl.BlockSpec(memory_space=pltpu.VMEM)]
        out_specs += [whole] * 2
        shapes = [(1, parts * strips * PAIR_CAP, total), (1, total)]
        out_shape += [jax.ShapeDtypeStruct(shape, jnp.float32) for shape in shapes]
        scratch = [pltpu.VMEM(shape, jnp.float32) for shape in shapes] + [pltpu.SemaphoreType.DMA((2,))]
    return pl.pallas_call(
        functools.partial(temporal_kernel, parts, strips, first_tile, tile_step),
        grid_spec=pltpu.PrefetchScalarGridSpec(
            num_scalar_prefetch=2,
            grid=(),
            in_specs=in_specs,
            out_specs=out_specs,
            scratch_shapes=scratch + [
                pltpu.VMEM((count, per, total + 2 * REACH, EDGE, LANES), jnp.float32),
                pltpu.VMEM((per, total + 2 * REACH * DILATION, EDGE, LANES), jnp.float32),
                pltpu.VMEM((count, total, EDGE, width), jnp.float32),
                pltpu.SemaphoreType.DMA((count, parts)),
                pltpu.SemaphoreType.DMA((count, per)),
            ],
        ),
        out_shape=out_shape,
        input_output_aliases={2 + parts: 0} if strips else {},
        compiler_params=params(24),
        cost_estimate=cost(2.5 + 0.4 * count),
    )(place, taps, *pieces, *extra)


def owner_values(parts, strips, taps, got_ref):
    owners = parts * strips
    slots = owners * PAIR_CAP
    dates = got_ref.shape[2] // PAIR_CAP
    local = dates // parts
    sums, held = got_ref[:, 0, :], got_ref[:, 1, :]
    rows, weights = [], []
    for block in range(parts):
        for slot in range(PAIR_CAP):
            at = (block * PAIR_CAP + slot) * local
            rows.append(jnp.concatenate(
                [sums[e * strips:(e + 1) * strips, at:at + local] for e in range(parts)], axis=1))
            weights.append(held[0:strips, at:at + 1])
    sums = jnp.concatenate(rows, axis=0)
    weight = jnp.concatenate(weights, axis=0)
    shape = (dates, dates)
    lag = lax.broadcasted_iota(jnp.int32, shape, 0) - lax.broadcasted_iota(jnp.int32, shape, 1)
    for level, spacing in ((0, 1), (1, DILATION)):
        filt = jnp.where(lag == 0, 1.0, 0.0)
        for k in range(2 * REACH + 1):
            filt = filt - jnp.where(lag == (k - REACH) * spacing, taps[level, k], 0.0)
        sums = jnp.dot(sums, filt, precision=HIGHEST, preferred_element_type=jnp.float32)
    mean = sums / jnp.where(weight > 0, weight, 1.0)
    asset = jnp.sum(weight * mean, axis=0, keepdims=True) / jnp.sum(weight, axis=0, keepdims=True)
    odd = jnp.where(weight > 0, mean - asset, 0.0)
    shape = (slots, slots)
    to = lax.broadcasted_iota(jnp.int32, shape, 0)
    source = lax.broadcasted_iota(jnp.int32, shape, 1)
    block, rest = source // (PAIR_CAP * strips), source % (PAIR_CAP * strips)
    place_of = block * (PAIR_CAP * strips) + (rest % strips) * PAIR_CAP + rest // strips
    order = jnp.where(to == place_of, 1.0, 0.0)
    return asset, jnp.dot(order, odd, precision=HIGHEST, preferred_element_type=jnp.float32)


def spread_meta(meta, offset, swap):
    known = sorted(meta)
    got = swap(jnp.concatenate([meta[k] for k in known], axis=1), offset)
    width = meta[0].shape[1]
    return meta | {k ^ offset: got[:, n * width:(n + 1) * width] for n, k in enumerate(known)}


def shards(stack, spatial_taps, temporal_taps, foot_tile, foot_row, foot_count, foot_owner):
    parts, strips = lax.axis_size("date"), lax.axis_size("strip")
    place = lax.axis_index("date").astype(jnp.int32)[None]
    dates, rows, cols = stack.shape
    feet = foot_row.shape[0]
    owner = foot_owner[:, 0]
    position = jnp.arange(feet, dtype=jnp.int32)
    earlier = (owner[:, None] == owner[None, :]) & (position[None, :] < position[:, None])
    slot = jnp.sum(earlier.astype(jnp.int32), axis=1)
    own = jnp.stack([foot_tile * (dates * (rows + EDGE)) + foot_row, foot_count, owner, slot])

    def swap(value, offset):
        return lax.ppermute(value, "date", [(i, i ^ offset) for i in range(parts)])

    order = (*range(2, parts), 1, 0)
    inner, far_inner = {}, {}
    lead = order[0]
    inner[lead], brim, last_rows, first_rows, ends = interior(stack, None, spatial_taps, place, (lead,), 0, parts)
    far_inner[lead] = swap(inner[lead], lead)
    up = lax.ppermute(last_rows, "strip", [(i, i + 1) for i in range(strips - 1)])
    down = lax.ppermute(first_rows, "strip", [(i + 1, i) for i in range(strips - 1)])
    own, brim = lax.optimization_barrier((own, brim))
    meta = {0: own}
    for bit in range(parts.bit_length() - 2, 0, -1):
        meta = spread_meta(meta, 1 << bit, swap)
    *made, brim = interior(stack, brim, spatial_taps, place, order[1:], 1, parts)
    for n, offset in enumerate(order[1:]):
        inner[offset] = made[n]
        if offset > 1:
            far_inner[offset] = swap(inner[offset], offset)
    known = sorted(meta)
    *held, far_inner[lead], brim = lax.optimization_barrier((*[meta[k] for k in known], far_inner[lead], brim))
    meta = spread_meta(dict(zip(known, held)), 1, swap)
    meta = [meta[k] for k in range(parts)]
    *made, sums = edges(
        ends, up, down, brim, [inner[k] for k in order], meta, spatial_taps, place, order, parts * strips)
    rim = dict(zip(order, made))
    far_inner[1] = swap(inner[1], 1)
    got = lax.all_to_all(sums, ("date", "strip"), split_axis=0, concat_axis=0, tiled=True)
    gate, *made = lax.optimization_barrier((swap(rim[1], 1), *[rim[k] for k in order[:-2]]))
    far_rim = {k: swap(made[n], k) for n, k in enumerate(order[:-2])}
    far_rim[1] = gate
    last = rows // EDGE - 1
    residual, = temporal(
        [inner[0]] + [far_inner[k] for k in range(1, parts)], temporal_taps, place, 1, 1, rows)
    got, residual = lax.optimization_barrier((got, residual))
    return temporal(
        [rim[0]] + [far_rim[k] for k in range(1, parts)], temporal_taps, place, 0, last, rows, residual, got, strips)


def solution(mesh):
    placed = (
        P("date", "strip", None),
        P(),
        P(),
        P(("date", "strip")),
        P(("date", "strip")),
        P(("date", "strip")),
        P(("date", "strip"), None),
    )
    return jax.shard_map(
        shards,
        mesh=mesh,
        in_specs=placed,
        out_specs=(
            P(None, "strip", "date"),
            P(("date", "strip"), None, None),
            P(("date", "strip"), None),
        ),
        check_vma=False,
    )
```
